32 devices in a mesh: seq: 4 (over y, x), tm: 8 (over z, core).
Axes of the slice: x: 2, y: 2, z: 4, core: 2. Of those that a mesh axis runs over, the one named last changes fastest.
Arguments:
- tokens: float32 [4, 3584, 768], P('seq', 'tm'), may hold values from -6 to 6
- cotangent: float32 [4, 3584, 768], P('seq', 'tm'), may hold values from -6 to 6
- qkv_weights: bfloat16 [11520, 768], P(('seq', 'tm')), may hold values from -0.21875 to 0.21875
- out_weights: bfloat16 [3840, 768], P(('seq', 'tm')), may hold values from -0.875 to 0.875
- up_weights: bfloat16 [2304, 3072], P(('seq', 'tm')), may hold values from -0.21875 to 0.21875
- down_weights: bfloat16 [9216, 768], P(('seq', 'tm')), may hold values from -0.109375 to 0.109375
- gains: bfloat16 [7680], P(('seq', 'tm')), may hold values from 0.5 to 1.5
Outputs:
- layer_out: float32 [4, 3584, 768], P('seq', 'tm')
- token_grad: float32 [4, 3584, 768], P('seq', 'tm')
- qkv_grad: float32 [11520, 768], P(('seq', 'tm'))
- out_grad: float32 [3840, 768], P(('seq', 'tm'))
- up_grad: float32 [2304, 3072], P(('seq', 'tm'))
- down_grad: float32 [9216, 768], P(('seq', 'tm'))
- gain_grad: float32 [7680], P(('seq', 'tm'))
The draws below stay inside these ranges and needn't reach their ends.
All inputs are finite; a program needn't handle non-finite values.
Results may differ from the reference program's by a relative error of at most 0.015.
Values may be sent and summed in bfloat16 or wider, within the bound.
A program may use at most 320 MiB of HBM per device.

```python
import jax
import jax.numpy as jnp
from jax import lax

D = 768
HEADS = 12
FF = 3072
SLAB = 448
CLIPS = 4
N_TM = 8


def shard_levels(stream_key, extent, shards, smallest, high):
    loudness = 1.0
    for axis_at, shards_of in shards:
        steps = jax.random.uniform(jax.random.fold_in(jax.random.fold_in(stream_key, 6), axis_at), (shards_of,), jnp.float32, smallest / len(shards), high / len(shards))
        loudness = loudness * jnp.repeat(jnp.exp(steps), extent[axis_at] // shards_of).reshape((-1,) + (1,) * (len(extent) - 1 - axis_at))
    return loudness


def gaussian(own_key, extent, deviation, most, split=(), kind=jnp.bfloat16):
    level = shard_levels(own_key, extent, split, -0.22, 0.18) if split else 1.0
    array = jax.random.normal(own_key, extent, jnp.float32) * deviation * level
    return jnp.minimum(jnp.maximum(array, -most), most).astype(kind)


def setup_inputs(seed: int = 0) -> dict:
    key_of = jax.random.split(jax.random.key(seed), 8)
    tokens = gaussian(key_of[0], (CLIPS, N_TM * SLAB, D), 1.0, 6.0, ((0, 4), (1, 8)), jnp.float32)
    cotangent = gaussian(key_of[1], (CLIPS, N_TM * SLAB, D), 1.0, 6.0, ((0, 4), (1, 8)), jnp.float32)
    qkv_weights = gaussian(key_of[2], (15 * D, D), D ** -0.5, 0.21875, ((0, 32),))
    out_weights = gaussian(key_of[3], (5 * D, D), (D // 16) ** -0.5, 0.875, ((0, 32),))
    up_weights = gaussian(key_of[4], (3 * D, FF), D ** -0.5, 0.21875, ((0, 32),))
    down_weights = gaussian(key_of[5], (3 * FF, D), FF ** -0.5, 0.109375, ((0, 32),))
    gains = jnp.clip(1.0 + 0.1 * jax.random.normal(key_of[6], (10 * D,), jnp.float32), 0.5, 1.5).astype(jnp.bfloat16)
    return dict(tokens=tokens, cotangent=cotangent, qkv_weights=qkv_weights, out_weights=out_weights, up_weights=up_weights, down_weights=down_weights, gains=gains)


EPS = 1e-06
FAR = -1e+30

@jax.custom_vjp
def low(v):
    return lax.optimization_barrier(v.astype(jnp.bfloat16)).astype(jnp.float32)

@jax.custom_vjp
def low_back(v):
    return v

def low_keep(v):
    return (low(v), None)

def low_pass(kept, grad):
    return (grad,)

def back_keep(v):
    return (v, None)

def back_low(kept, grad):
    return (low(grad),)
low.defvjp(low_keep, low_pass)
low_back.defvjp(back_keep, back_low)

def rounded(v):
    return low(low_back(v))

def norm_rows(x, gain):
    mean = lax.optimization_barrier(jnp.mean(x, axis=-1, keepdims=True))
    centered = x - mean
    spread = lax.optimization_barrier(jnp.mean(centered * centered, axis=-1, keepdims=True))
    return centered * lax.rsqrt(spread + EPS) * gain

def project(x, weight):
    return jnp.einsum('nld,de->nle', x, weight, precision=lax.Precision.HIGHEST)

def attend(query, keys, values, bias):
    slabs, rows, width = query.shape
    depth = width // HEADS
    qh = query.reshape(slabs, rows, HEADS, depth)
    kh = keys.reshape(slabs, keys.shape[1], HEADS, depth)
    vh = values.reshape(slabs, values.shape[1], HEADS, depth)
    raw = jnp.einsum('nqhd,nkhd->nhqk', qh, kh, precision=lax.Precision.HIGHEST)
    scores = low_back(raw * depth ** (-0.5)) + bias[:, None, None, :]
    top = lax.optimization_barrier(jnp.max(scores, axis=-1, keepdims=True))
    expo = jnp.exp(scores - top)
    probs = low(expo / lax.optimization_barrier(jnp.sum(expo, axis=-1, keepdims=True)))
    mixed = jnp.einsum('nhqk,nkhd->nqhd', probs, vh, precision=lax.Precision.HIGHEST)
    return rounded(mixed.reshape(slabs, rows, width))

def widen(field, spatial):
    blank = jnp.zeros((1, spatial, field.shape[2]), jnp.float32)
    below = jnp.concatenate([blank, field[:-1, -spatial:]], axis=0)
    above = jnp.concatenate([field[1:, :spatial], blank], axis=0)
    return jnp.concatenate([below, field, above], axis=1)

def clip_forward(x, qkv, outw, upw, downw, gain):
    slabs = x.shape[0]
    spatial = x.shape[1] // 7
    bounds = ((0, 4 * spatial), (4 * spatial, 6 * spatial), (6 * spatial, 7 * spatial))
    views = [x[:, start:stop] for start, stop in bounds]
    joined = []
    for view in range(2):
        first = low(norm_rows(views[view], gain[3 + view, 0]))
        second = low(norm_rows(views[view + 1], gain[3 + view, 1]))
        query = rounded(project(first, qkv[3 + view, 0]))
        keys = rounded(project(second, qkv[3 + view, 1]))
        values = rounded(project(second, qkv[3 + view, 2]))
        flat_bias = jnp.zeros((slabs, keys.shape[1]), jnp.float32)
        mixed = attend(query, keys, values, flat_bias)
        joined.append(views[view] + low_back(project(mixed, outw[3 + view])))
    joined.append(views[2])
    place = jnp.arange(slabs)
    below_bias = jnp.where(place > 0, 0.0, FAR).astype(jnp.float32)
    above_bias = jnp.where(place < slabs - 1, 0.0, FAR).astype(jnp.float32)
    outputs = []
    for view in range(3):
        current = joined[view]
        length = current.shape[1]
        normed = low(norm_rows(current, gain[view, 0]))
        query = rounded(project(normed, qkv[view, 0]))
        keys = rounded(project(normed, qkv[view, 1]))
        values = rounded(project(normed, qkv[view, 2]))
        bias = jnp.concatenate([jnp.broadcast_to(below_bias[:, None], (slabs, spatial)), jnp.zeros((slabs, length), jnp.float32), jnp.broadcast_to(above_bias[:, None], (slabs, spatial))], axis=1)
        mixed = attend(query, widen(keys, spatial), widen(values, spatial), bias)
        middle = current + low_back(project(mixed, outw[view]))
        normed_two = low(norm_rows(middle, gain[view, 1]))
        hidden_pre = low_back(project(normed_two, upw[view]))
        active = low(jax.nn.gelu(hidden_pre, approximate=False))
        outputs.append(middle + low_back(project(active, downw[view])))
    return jnp.concatenate(outputs, axis=1)

def reference(tokens, cotangent, qkv_weights, out_weights, up_weights, down_weights, gains):
    params = tuple((w.astype(jnp.float32) for w in (qkv_weights, out_weights, up_weights, down_weights, gains)))
    clips = tokens.shape[0]

    def forward(x, qkv_flat, out_flat, up_flat, down_flat, gain_flat):
        qkv = qkv_flat.reshape(5, 3, D, D)
        outw = out_flat.reshape(5, D, D)
        upw = up_flat.reshape(3, D, FF)
        downw = down_flat.reshape(3, FF, D)
        gain = gain_flat.reshape(5, 2, D)
        shaped = x.reshape(clips, N_TM, -1, x.shape[-1])
        step = jax.checkpoint(lambda piece: clip_forward(piece, qkv, outw, upw, downw, gain))
        return lax.map(step, shaped).reshape(x.shape)
    layer_out, pull = jax.vjp(forward, tokens, *params)
    grads = pull(cotangent)
    return (layer_out, grads[0], grads[1], grads[2], grads[3], grads[4], grads[5])
```

```python
import functools

import jax
import jax.numpy as jnp
from jax import lax
from jax.experimental import pallas as pl
from jax.experimental.pallas import tpu as pltpu
from jax.sharding import PartitionSpec as P

D = 768
HEADS = 12
FF = 3072

EPS = 1e-06
FAR = -1e30
MESH = pl.DeviceIdType.MESH
BF = jnp.bfloat16
F32 = jnp.float32
BLOCK = D // 2
ROWS = 48
LAG = 0.5
SLOTS = 36
COPIES = 480


def extended(cells, sides, width):
    for axis, dim in sides:
        count = lax.axis_size(axis)
        ends = count - 1
        head = lax.slice_in_dim(cells, 0, width, axis=dim)
        tail = lax.slice_in_dim(cells, cells.shape[dim] - width, cells.shape[dim], axis=dim)
        cells = jnp.concatenate(
            [
                lax.ppermute(tail, axis, [(i, (i + 1) % count) for i in range(ends)]),
                cells,
                lax.ppermute(head, axis, [((i + 1) % count, i) for i in range(ends)]),
            ],
            axis=dim,
        )
    return cells


def from_behind(block, axis, distance):
    devices = range(lax.axis_size(axis))
    route = [(i - distance, i) for i in devices if i - distance in devices]
    return lax.ppermute(block, axis, route)


def norm_rows(x, gain):
    mean = jnp.mean(x, axis=-1, keepdims=True)
    centered = x - mean
    spread = jnp.mean(centered * centered, axis=-1, keepdims=True)
    return centered * lax.rsqrt(spread + EPS) * gain


def norm_back(x, gain, grad):
    unused, pull = jax.vjp(norm_rows, x, gain)
    return pull(grad)


def gelu_back(hidden_pre, grad):
    unused, pull = jax.vjp(lambda value: jax.nn.gelu(value, approximate=False), hidden_pre)
    return pull(grad)[0]


def lowered(value):
    return value.astype(jnp.bfloat16)


def product(left, right):
    return jnp.dot(left, right, preferred_element_type=jnp.float32)


def product_tn(left, right):
    return lax.dot_general(
        left, right, (((0,), (0,)), ((), ())), preferred_element_type=jnp.float32
    )


def product_nt(left, right):
    return lax.dot_general(
        left, right, (((1,), (1,)), ((), ())), preferred_element_type=jnp.float32
    )


def unstack(parts):
    qkv_flat, out_flat, up_flat, down_flat, gain_flat = parts
    return (
        qkv_flat.reshape(5, 3, D, D),
        out_flat.reshape(5, D, D),
        up_flat.reshape(3, D, FF),
        down_flat.reshape(3, FF, D),
        gain_flat.reshape(5, 2, D),
    )


def attend(query, keys, values, bias):
    rows, width = query.shape
    depth = width // HEADS
    qh = query.reshape(rows, HEADS, depth)
    kh = keys.reshape(keys.shape[0], HEADS, depth)
    vh = values.reshape(values.shape[0], HEADS, depth)
    scores = (
        jnp.einsum("qhd,khd->hqk", qh, kh, preferred_element_type=jnp.float32) * depth ** (-0.5)
        + bias
    )
    top = jnp.max(scores, axis=-1, keepdims=True)
    expo = jnp.exp(scores - top)
    probs = expo / jnp.sum(expo, axis=-1, keepdims=True)
    mixed = jnp.einsum("hqk,khd->qhd", lowered(probs), vh, preferred_element_type=jnp.float32)
    return (lowered(mixed.reshape(rows, width)), probs)


def attend_back(query, keys, values, probs, grad_mixed):
    rows, width = query.shape
    depth = width // HEADS
    qh = query.reshape(rows, HEADS, depth)
    kh = keys.reshape(keys.shape[0], HEADS, depth)
    vh = values.reshape(values.shape[0], HEADS, depth)
    gh = grad_mixed.reshape(rows, HEADS, depth)
    dprobs = jnp.einsum("qhd,khd->hqk", gh, vh, preferred_element_type=jnp.float32)
    dvalues = jnp.einsum("hqk,qhd->khd", lowered(probs), gh, preferred_element_type=jnp.float32)
    inner = jnp.sum(dprobs * probs, axis=-1, keepdims=True)
    dscores = lowered(probs * (dprobs - inner))
    scale = depth ** (-0.5)
    dquery = jnp.einsum("hqk,khd->qhd", dscores, kh, preferred_element_type=jnp.float32) * scale
    dkeys = jnp.einsum("hqk,qhd->khd", dscores, qh, preferred_element_type=jnp.float32) * scale
    return (dquery.reshape(rows, width), dkeys.reshape(-1, width), dvalues.reshape(-1, width))


class Place:
    def __init__(self, dims):
        self.dims = dims
        s = lax.axis_index("seq")
        t = lax.axis_index("tm")
        self.at = (s // dims[1], s % dims[1], t // 2)
        self.core = t % 2

    def device(self, at, core):
        return (at[0] * self.dims[1] + at[1], at[2] * 2 + core)

    def along(self, dim, value):
        at = list(self.at)
        at[dim] = value
        return self.device(at, self.core)

    def sibling(self):
        return self.device(self.at, 1 - self.core)


def meet(place):
    barrier = pltpu.get_barrier_semaphore()
    count = 1
    pl.semaphore_signal(barrier, inc=1, device_id=place.sibling(), device_id_type=MESH)
    for dim, n in enumerate(place.dims):
        me = place.at[dim]
        for step in (1, -1):
            ok = (me + step >= 0) & (me + step < n)

            @pl.when(ok)
            def _():
                pl.semaphore_signal(barrier, inc=1, device_id=place.along(dim, me + step), device_id_type=MESH)

            count = count + jnp.where(ok, 1, 0)
    pl.semaphore_wait(barrier, count)


class Copies:
    def __init__(self, send, recv):
        self.send, self.recv = send, recv
        self.used = 0
        self.sent = []

    def start(self, src, dst, device, ok=None):
        copy = pltpu.make_async_remote_copy(
            src_ref=src,
            dst_ref=dst,
            send_sem=self.send.at[self.used],
            recv_sem=self.recv.at[self.used],
            device_id=device,
            device_id_type=MESH,
        )
        self.used += 1
        when(ok, copy.start)
        self.sent.append((copy, ok))
        return copy

    def drain(self):
        for copy, ok in self.sent:
            when(ok, copy.wait_send)
        self.sent = []


def when(ok, action):
    if ok is None:
        action()
    else:

        @pl.when(ok)
        def _():
            action()


def gather_line(copies, place, dim, pick):
    n = place.dims[dim]
    me = place.at[dim]
    if n == 2:
        part = pick(me)
        copy = copies.start(part, part, place.along(dim, 1 - me))
        yield
        copy.wait_recv()
        return
    before = {}
    for hop in range(1, n):
        for step in (1, -1):
            origin = me - step * (hop - 1)
            held = (origin >= 0) & (origin < n)
            if hop > 1:
                when(held, before[step].wait_recv)
            ok = held & (me + step >= 0) & (me + step < n)
            part = pick(jnp.clip(origin, 0, n - 1))
            before[step] = copies.start(part, part, place.along(dim, jnp.clip(me + step, 0, n - 1)), ok)
        yield
    for step in (1, -1):
        origin = me - step * (n - 1)
        when((origin >= 0) & (origin < n), before[step].wait_recv)


def gather_piece(copies, place, full, rows, cols, order, pair):
    done = set()
    for dim in order:

        def pick(value):
            index = [slice(None) if d in done else place.at[d] for d in range(3)]
            index[dim] = value
            return full.at[(*index, pl.ds(*rows), cols)]

        yield from gather_line(copies, place, dim, pick)
        done.add(dim)
    if pair is not None:
        part = full.at[:, :, :, pl.ds(*rows), cols]
        pair.append(copies.start(part, part, place.sibling()))


ZXY, ZYX, XZY, YZX = (2, 1, 0), (2, 0, 1), (1, 2, 0), (0, 2, 1)
CYCLE = (XZY, YZX, ZXY, XZY, YZX, ZYX)


def pieces_of(slabs, arrays):
    flat = []
    for array in arrays:
        rows, width = slabs[array]
        for block in range(width // 2 // BLOCK):
            for row in range(0, rows, ROWS):
                flat.append((array, row, block, CYCLE[len(flat) % 6]))
    return [flat[i : i + 3] for i in range(0, len(flat), 3)]


def march(sets, begin, extra=(), between=None):
    waiting = list(sets)
    active = list(extra)
    step = 0
    while active or waiting:
        while waiting and step >= LAG * (len(sets) - len(waiting)):
            for piece in waiting.pop(0):
                active.append(begin(piece))
        still = []
        for one in active:
            try:
                next(one)
                still.append(one)
            except StopIteration:
                pass
        active = still
        if between is not None:
            between(step)
        step += 1


def gather_kernel(dims, qkv, out, up, down, gain, fqkv, fout, fup, fdown, fgain, *scratch):
    place = Place(dims)
    shards = (qkv, out, up, down)
    fulls = (fqkv, fout, fup, fdown)
    theirs = scratch[:4]
    merged = scratch[4:8]
    gain_pair, send, recv, local = scratch[8:]
    copies = Copies(send, recv)
    core = place.core
    meet(place)
    width = [s.shape[1] // 2 for s in shards]
    mine = [pl.ds(pl.multiple_of(core * w, 128), w) for w in width]
    other = [pl.ds(pl.multiple_of((1 - core) * w, 128), w) for w in width]
    swaps = []
    for a in range(4):
        swaps.append(copies.start(shards[a].at[:, other[a]], theirs[a], place.sibling()))
    gain_pair[core] = gain[...]
    part = gain_pair.at[core]
    swap_gain = copies.start(part, part, place.sibling())
    at = place.at

    def prepare(a):
        swaps[a].wait_recv()
        w = width[a]
        own = jnp.where(core == 0, shards[a][:, :w].astype(F32), shards[a][:, w:].astype(F32))
        got = theirs[a][...].astype(F32)
        upper = jnp.where(core == 0, own, got)
        lower = jnp.where(core == 0, got, own)
        merged[a][...] = jnp.concatenate([upper, lower], axis=0).astype(BF)
        copy = pltpu.make_async_copy(merged[a], fulls[a].at[at[0], at[1], at[2], :, mine[a]], local.at[a])
        copy.start()
        copy.wait()

    pair = []
    ready = set()

    def begin(piece):
        a, row, block, order = piece
        if a not in ready:
            prepare(a)
            ready.add(a)
        cols = pl.ds(pl.multiple_of(core * width[a] + block * BLOCK, 128), BLOCK)
        return gather_piece(copies, place, fulls[a], (row, ROWS), cols, order, pair)

    def gains():
        swap_gain.wait_recv()
        copy = pltpu.make_async_copy(gain_pair, fgain.at[at[0], at[1], at[2]], local.at[4])
        copy.start()
        copy.wait()
        done = set()
        for dim in ZXY:

            def pick(value):
                index = [slice(None) if d in done else at[d] for d in range(3)]
                index[dim] = value
                return fgain.at[tuple(index)]

            yield from gather_line(copies, place, dim, pick)
            done.add(dim)

    march(pieces_of([m.shape[:1] + (2 * m.shape[1],) for m in merged], range(4)), begin, (gains(),))
    for copy in pair:
        copy.wait_recv()
    copies.drain()


def gather_all(dims, qkv, out, up, down, gain):
    shards = (qkv, out, up, down)
    slabs = [(2 * s.shape[0], s.shape[1]) for s in shards]
    anywhere = pl.BlockSpec(memory_space=pl.ANY)
    vmem = pl.BlockSpec(memory_space=pltpu.VMEM)
    return pl.pallas_call(
        functools.partial(gather_kernel, dims),
        out_shape=[jax.ShapeDtypeStruct((*dims, *s), BF) for s in slabs]
        + [jax.ShapeDtypeStruct((*dims, 2, 8, 128), F32)],
        in_specs=[vmem] * 5,
        out_specs=[anywhere] * 5,
        scratch_shapes=[pltpu.VMEM((r // 2, w // 2), BF) for r, w in slabs]
        + [pltpu.VMEM((r, w // 2), BF) for r, w in slabs]
        + [
            pltpu.VMEM((2, 8, 128), F32),
            pltpu.SemaphoreType.DMA((COPIES,)),
            pltpu.SemaphoreType.DMA((COPIES,)),
            pltpu.SemaphoreType.DMA((5,)),
        ],
        compiler_params=pltpu.CompilerParams(
            collective_id=0, has_side_effects=True, vmem_limit_bytes=48 << 20
        ),
    )(qkv, out, up, down, gain)


def add_to(total, term):
    total[...] = (total[...].astype(F32) + term[...].astype(F32)).astype(total.dtype)


def reduce_line(copies, place, pick, slots):
    n = place.dims[2]
    z = place.at[2]
    before = {}
    for turn in range(n):
        for step in (1, -1):
            far = z if step == 1 else n - 1 - z
            goal = far + n - 1 - turn
            goal = jnp.minimum(goal if step == 1 else n - 1 - goal, n - 1)
            goal = jnp.maximum(goal, 0)
            if turn > 0:

                def take(step=step, turn=turn, goal=goal):
                    before[step].wait_recv()
                    add_to(pick(goal), slots(turn - 1, step))

                when((far >= 1) & (far <= turn), take)
            if turn < n - 1:
                before[step] = copies.start(
                    pick(goal), slots(turn, step), place.along(2, jnp.clip(z + step, 0, n - 1)), far <= turn
                )
        if turn < n - 1:
            yield


def reduce_piece(copies, place, source, order, acc, first, turns, last, local, finish):
    lead = order[0]
    rest = 1 - lead
    me, mine = place.at[lead], place.at[rest]
    z = place.at[2]
    copy = copies.start(source(lead, 1 - me), first, place.along(lead, 1 - me))
    load = pltpu.make_async_copy(source(lead, me), acc, local)
    load.start()
    yield
    load.wait()
    copy.wait_recv()
    add_to(acc, first)
    slots = lambda turn, step: turns.at[turn, (1 - step) // 2]
    if order[1] == 2:
        yield from reduce_line(copies, place, lambda v: acc.at[:, v], slots)
        copy = copies.start(acc.at[1 - mine, z], last, place.along(rest, 1 - mine))
        yield
        copy.wait_recv()
        finish(acc[mine, z].astype(F32) + last[...].astype(F32))
    else:
        copy = copies.start(acc.at[1 - mine], last, place.along(rest, 1 - mine))
        yield
        copy.wait_recv()
        add_to(acc.at[mine], last)
        yield from reduce_line(copies, place, lambda v: acc.at[mine, v], slots)
        finish(acc[mine, z].astype(F32))


LEFTS = ("active", "normed_two", "mixed", "normed", "first", "second", "cross_mixed")
RIGHTS = ("d_out", "d_pre", "d_attn", "dq", "dk", "dv", "d_cross", "cq", "ck", "cv")


def jobs_of(spatial):
    rows = {0: (0, 4 * spatial), 1: (4 * spatial, 2 * spatial), 2: (6 * spatial, spatial)}
    late = {0: (0, 2 * spatial), 1: (2 * spatial, spatial)}
    jobs = {a: [] for a in range(4)}
    for view in range(3):
        for block in range(FF // D):
            jobs[3].append((view * FF + block * D, 0, "active", block, rows[view], "d_out", 0, rows[view]))
        for block in range(FF // 2 // BLOCK):
            jobs[2].append((view * D, block, "normed_two", 0, rows[view], "d_pre", block, rows[view]))
        jobs[1].append((view * D, 0, "mixed", 0, rows[view], "d_attn", 0, rows[view]))
        for j, name in enumerate(("dq", "dk", "dv")):
            jobs[0].append(((3 * view + j) * D, 0, "normed", 0, rows[view], name, 0, rows[view]))
    for view in range(2):
        jobs[1].append(((3 + view) * D, 0, "cross_mixed", 0, rows[view], "d_cross", 0, rows[view]))
        jobs[0].append(((9 + 3 * view) * D, 0, "first", 0, rows[view], "cq", 0, rows[view]))
        for j, name in enumerate(("ck", "cv")):
            jobs[0].append(((10 + 3 * view + j) * D, 0, "second", 0, late[view], name, 0, late[view]))
    return jobs


def reduce_kernel(dims, slabs, sets, count, spatial, *refs):
    refs = list(refs)
    take = lambda n: [refs.pop(0) for _ in range(n)]
    lefts, rights = dict(zip(LEFTS, take(7))), dict(zip(RIGHTS, take(10)))
    (gain,) = take(1)
    results = take(4)
    (gain_out,) = take(1)
    parts = take(4)
    far_lefts, far_rights = dict(zip(LEFTS, take(7))), dict(zip(RIGHTS, take(10)))
    acc, first, turns_a, turns_b, last_a, last_b = take(6)
    finals = take(4)
    xs, ys, made = take(3)
    g_far, g_acc, g_first, g_turns, g_last = take(5)
    send, recv, local, load_sem, store_sem, final_sem = take(6)
    place = Place(dims)
    core = place.core
    copies = Copies(send, recv)
    meet(place)
    half_of = lambda ref, c: pl.ds(pl.multiple_of(c * (ref.shape[1] // 2), 128), ref.shape[1] // 2)
    coming = {}
    for name in ("active", "d_out", "normed_two", "d_pre", "mixed", "d_attn", "normed", "dq", "dk", "dv", "cross_mixed", "d_cross", "first", "cq", "second", "ck", "cv"):
        if name in lefts:
            coming[name] = copies.start(lefts[name], far_lefts[name], place.sibling())
        else:
            ref = rights[name]
            coming[name] = copies.start(ref.at[:, half_of(ref, 1 - core)], far_rights[name], place.sibling())
    swap_gain = copies.start(gain, g_far, place.sibling())

    arrived = set()

    def arrive(name):
        if name not in arrived:
            coming[name].wait_recv()
            arrived.add(name)

    order = [(a, job) for a in (3, 2, 1, 0) for job in jobs_of(spatial)[a]]

    def load(i):
        a, (row, block, left, lcol, lrows, right, rcol, rrows) = order[i]
        slot = i % 2
        arrive(left)
        arrive(right)
        n = lrows[1]
        ref = rights[right]
        own = pl.ds(pl.multiple_of(core * (ref.shape[1] // 2) + rcol * BLOCK, 128), BLOCK)
        pairs = [
            (lefts[left].at[pl.ds(*lrows), pl.ds(lcol * D, D)], xs.at[slot, pl.ds(0, n)]),
            (far_lefts[left].at[pl.ds(*lrows), pl.ds(lcol * D, D)], xs.at[slot, pl.ds(n, n)]),
            (ref.at[pl.ds(*rrows), own], ys.at[slot, pl.ds(0, n)]),
            (far_rights[right].at[pl.ds(*rrows), pl.ds(rcol * BLOCK, BLOCK)], ys.at[slot, pl.ds(n, n)]),
        ]
        loads = [pltpu.make_async_copy(s, d, load_sem.at[slot, j]) for j, (s, d) in enumerate(pairs)]
        for one in loads:
            one.start()
        return loads

    loading = {0: load(0)}
    storing = {}
    done = {"jobs": 0}

    def store(i):
        a, job = order[i]
        row, block = job[0], job[1]
        slab = slabs[a][0]
        slot = i % 2
        stores = []
        at, end = row, row + D
        while at < end:
            chip, off = at // slab, at % slab
            n = min(end - at, slab - off)
            p, q, z = chip // (dims[1] * dims[2]), chip // dims[2] % dims[1], chip % dims[2]
            stores.append(
                pltpu.make_async_copy(
                    made.at[slot, pl.ds(at - row, n)],
                    parts[a].at[p, q, z, pl.ds(off, n), pl.ds(block * BLOCK, BLOCK)],
                    store_sem.at[slot, len(stores)],
                )
            )
            at += n
        for one in stores:
            one.start()
        return stores

    def finish_stores(i):
        for one in storing.pop(i, ()):
            one.wait()

    def multiply(upto):
        while done["jobs"] < upto:
            i = done["jobs"]
            for one in loading.pop(i):
                one.wait()
            if i + 1 < len(order):
                loading[i + 1] = load(i + 1)
            finish_stores(i - 2)
            n = 2 * order[i][1][4][1]
            slot = i % 2
            made[slot] = lax.dot_general(
                xs[slot, :n], ys[slot, :n], (((0,), (0,)), ((), ())), preferred_element_type=F32
            ).astype(BF)
            storing[i] = store(i)
            done["jobs"] += 1

    upto = {}
    for a in (3, 2, 1, 0):
        upto[a] = max(i for i, one in enumerate(order) if one[0] == a) + 1

    used = {"n": 0, 0: 0, 1: 0}
    owners = []
    left_in = {a: sum(1 for s in sets for piece in s if piece[0] == a) for a in range(4)}
    ending = []

    def begin(piece):
        a, row, block, order_ = piece
        multiply(upto[a])
        for i in list(storing):
            finish_stores(i)
        i = used["n"]
        used["n"] += 1
        kind = 0 if order_[1] == 0 or order_[1] == 2 else 1
        way = order_[::-1]
        kind = 0 if way[1] == 2 else 1
        k = used[kind]
        used[kind] += 1
        slot = i % SLOTS
        if i >= SLOTS:
            owners[i - SLOTS].drain()
        mine = Copies(send, recv)
        mine.used = copies.used
        copies.used += 9
        owners.append(mine)
        cols = pl.ds(block * BLOCK, BLOCK)

        def source(dim, value):
            index = [slice(None)] * 3
            index[dim] = value
            return parts[a].at[(*index, pl.ds(row, ROWS), cols)]

        def finish(value):
            finals[a][pl.ds(row, ROWS), cols] = value
            left_in[a] -= 1
            if left_in[a] == 0:
                deliver(a)

        turns, last = ((turns_a, last_a), (turns_b, last_b))[kind]
        return reduce_piece(
            mine, place, source, way, acc.at[slot], first.at[i], turns.at[k], last.at[k], local.at[slot], finish
        )

    def deliver(a):
        rows, width = slabs[a][0] // 2, slabs[a][1] // 2
        cols = pl.ds(pl.multiple_of(core * width, 128), width)
        ending.append(
            copies.start(
                finals[a].at[pl.ds(pl.multiple_of((1 - core) * rows, 8), rows)], results[a].at[:, cols], place.sibling()
            )
        )
        keep = pltpu.make_async_copy(
            finals[a].at[pl.ds(pl.multiple_of(core * rows, 8), rows)], results[a].at[:, cols], final_sem.at[a]
        )
        keep.start()
        keep.wait()

    def gains():
        swap_gain.wait_recv()
        add_to(g_far, gain)
        source = lambda dim, value: g_far.at[(*[value if d == dim else slice(None) for d in range(3)], core)]

        def finish(value):
            gain_out[...] = value

        yield from reduce_piece(copies, place, source, (0, 1, 2), g_acc, g_first, g_turns, g_last, local.at[SLOTS], finish)

    def between(step):
        multiply(min(len(order), done["jobs"] + 6))

    march(sets, begin, (gains(),), between)
    for one in ending:
        one.wait_recv()
    copies.drain()
    for one in owners:
        one.drain()


def reduce_all(dims, slabs, lefts, rights, gain):
    anywhere = pl.BlockSpec(memory_space=pl.ANY)
    vmem = pl.BlockSpec(memory_space=pltpu.VMEM)
    sets = pieces_of(slabs, (3, 2, 1, 0))
    flat = [piece for group in sets for piece in group]
    count = len(flat)
    bundled = sum(1 for piece in flat if piece[3][1] == 2)
    single = count - bundled
    z = dims[2]
    spatial = lefts[0].shape[0] // 7
    longest = 2 * 4 * spatial
    tile = (ROWS, BLOCK)
    segments = max(D // slab[0] + 2 for slab in slabs)
    halves = lambda ref: jax.ShapeDtypeStruct((ref.shape[0], ref.shape[1] // 2), BF)
    outs = pl.pallas_call(
        functools.partial(reduce_kernel, dims, slabs, sets, count, spatial),
        out_shape=[jax.ShapeDtypeStruct((s[0] // 2, s[1]), F32) for s in slabs]
        + [jax.ShapeDtypeStruct((8, 128), F32)]
        + [jax.ShapeDtypeStruct((*dims, s[0], s[1] // 2), BF) for s in slabs]
        + [jax.ShapeDtypeStruct(x.shape, BF) for x in lefts]
        + [halves(y) for y in rights],
        in_specs=[anywhere] * 17 + [vmem],
        out_specs=[vmem] * 5 + [anywhere] * 21,
        scratch_shapes=[
            pltpu.VMEM((SLOTS, 2, z, *tile), BF),
            pltpu.VMEM((count, 2, z, *tile), BF),
            pltpu.VMEM((bundled, z - 1, 2, 2, *tile), BF),
            pltpu.VMEM((single, z - 1, 2, *tile), BF),
            pltpu.VMEM((bundled, *tile), BF),
            pltpu.VMEM((single, z, *tile), BF),
        ]
        + [pltpu.VMEM((s[0], s[1] // 2), F32) for s in slabs]
        + [
            pltpu.VMEM((2, longest, D), BF),
            pltpu.VMEM((2, longest, BLOCK), BF),
            pltpu.VMEM((2, D, BLOCK), BF),
            pltpu.VMEM((*dims, 2, 8, 128), F32),
            pltpu.VMEM((2, z, 8, 128), F32),
            pltpu.VMEM((2, z, 8, 128), F32),
            pltpu.VMEM((z - 1, 2, 8, 128), F32),
            pltpu.VMEM((z, 8, 128), F32),
            pltpu.SemaphoreType.DMA((COPIES,)),
            pltpu.SemaphoreType.DMA((COPIES,)),
            pltpu.SemaphoreType.DMA((SLOTS + 1,)),
            pltpu.SemaphoreType.DMA((2, 4)),
            pltpu.SemaphoreType.DMA((2, segments)),
            pltpu.SemaphoreType.DMA((4,)),
        ],
        compiler_params=pltpu.CompilerParams(
            collective_id=1, has_side_effects=True, vmem_limit_bytes=60 << 20
        ),
    )(*lefts, *rights, gain)
    return outs[:5]


def plain_device(tokens, cotangent, qkv_weights, out_weights, up_weights, down_weights, gains):
    rows = tokens[0]
    incoming = cotangent[0]
    spatial = rows.shape[0] // 7
    bounds = ((0, 4 * spatial), (4 * spatial, 6 * spatial), (6 * spatial, 7 * spatial))
    qkv, outw, upw, downw, gain_low = unstack(
        (
            lax.all_gather(qkv_weights, ("seq", "tm"), axis=0, tiled=True),
            lax.all_gather(out_weights, ("seq", "tm"), axis=0, tiled=True),
            lax.all_gather(up_weights, ("seq", "tm"), axis=0, tiled=True),
            lax.all_gather(down_weights, ("seq", "tm"), axis=0, tiled=True),
            lax.all_gather(gains, ("seq", "tm"), axis=0, tiled=True),
        )
    )
    gain = gain_low.astype(jnp.float32)
    place = lax.axis_index("tm")
    count = lax.axis_size("tm")
    below_bias = jnp.where(place > 0, 0.0, FAR).astype(jnp.float32)
    above_bias = jnp.where(place < count - 1, 0.0, FAR).astype(jnp.float32)
    views = [rows[start:stop] for start, stop in bounds]
    cross_keep = []
    joined = []
    for view in range(2):
        first = lowered(norm_rows(views[view], gain[3 + view, 0]))
        second = lowered(norm_rows(views[view + 1], gain[3 + view, 1]))
        query = lowered(product(first, qkv[3 + view, 0]))
        keys = lowered(product(second, qkv[3 + view, 1]))
        values = lowered(product(second, qkv[3 + view, 2]))
        mixed, probs = attend(query, keys, values, 0.0)
        joined.append(views[view] + product(mixed, outw[3 + view]))
        cross_keep.append((first, second, query, keys, values, mixed, probs))
    joined.append(views[2])
    local_keep = []
    edges = []
    for view in range(3):
        normed = lowered(norm_rows(joined[view], gain[view, 0]))
        query = lowered(product(normed, qkv[view, 0]))
        keys = lowered(product(normed, qkv[view, 1]))
        values = lowered(product(normed, qkv[view, 2]))
        local_keep.append((normed, query, keys, values))
        paired = jnp.stack([keys, values])
        edges.append(jnp.concatenate([paired[:, :spatial], paired[:, -spatial:]], axis=1))
    rim = extended(jnp.stack(edges, axis=1), (("tm", 2),), spatial)
    self_keep = []
    outputs = []
    for view in range(3):
        normed, query, keys, values = local_keep[view]
        length = keys.shape[0]
        keys_all = jnp.concatenate(
            [rim[0, view, :spatial], keys, rim[0, view, 3 * spatial :]], axis=0
        )
        values_all = jnp.concatenate(
            [rim[1, view, :spatial], values, rim[1, view, 3 * spatial :]], axis=0
        )
        bias = jnp.concatenate(
            [
                jnp.broadcast_to(below_bias, (spatial,)),
                jnp.zeros((length,), jnp.float32),
                jnp.broadcast_to(above_bias, (spatial,)),
            ]
        )
        mixed, probs = attend(query, keys_all, values_all, bias)
        middle = joined[view] + product(mixed, outw[view])
        normed_two = lowered(norm_rows(middle, gain[view, 1]))
        hidden_pre = product(normed_two, upw[view])
        active = lowered(jax.nn.gelu(hidden_pre, approximate=False))
        outputs.append(middle + product(active, downw[view]))
        self_keep.append(
            (
                normed,
                query,
                keys_all,
                values_all,
                mixed,
                probs,
                middle,
                normed_two,
                hidden_pre,
                active,
            )
        )
    layer_out = jnp.concatenate(outputs, axis=0)[None]
    qkv, outw, upw, downw, gain_low = unstack(
        (
            lax.all_gather(qkv_weights, ("seq", "tm"), axis=0, tiled=True),
            lax.all_gather(out_weights, ("seq", "tm"), axis=0, tiled=True),
            lax.all_gather(up_weights, ("seq", "tm"), axis=0, tiled=True),
            lax.all_gather(down_weights, ("seq", "tm"), axis=0, tiled=True),
            lax.all_gather(gains, ("seq", "tm"), axis=0, tiled=True),
        )
    )
    grad_qkv = [[None, None, None] for index in range(5)]
    grad_out = [None] * 5
    grad_up = [None] * 3
    grad_down = [None] * 3
    grad_gain = [[None, None] for index in range(5)]
    halves = []
    for view in range(3):
        (
            normed,
            query,
            keys_all,
            values_all,
            mixed,
            probs,
            middle,
            normed_two,
            hidden_pre,
            active,
        ) = self_keep[view]
        start, stop = bounds[view]
        dfinal = incoming[start:stop]
        dbranch = lowered(dfinal)
        grad_down[view] = product_tn(active, dbranch)
        dactive = product_nt(dbranch, downw[view])
        dpre_low = lowered(gelu_back(hidden_pre, dactive))
        grad_up[view] = product_tn(normed_two, dpre_low)
        dnormed_two = product_nt(dpre_low, upw[view])
        dmid_norm, grad_gain[view][1] = norm_back(middle, gain[view, 1], dnormed_two)
        dmiddle = dfinal + dmid_norm
        dattn = lowered(dmiddle)
        grad_out[view] = product_tn(mixed, dattn)
        dmixed = lowered(product_nt(dattn, outw[view]))
        dquery, dkeys, dvalues = attend_back(query, keys_all, values_all, probs, dmixed)
        halves.append((dmiddle, dquery, dkeys, dvalues))
    lower_part = jnp.stack(
        [jnp.stack([half[2][:spatial], half[3][:spatial]]) for half in halves], axis=1
    )
    upper_part = jnp.stack(
        [jnp.stack([half[2][-spatial:], half[3][-spatial:]]) for half in halves], axis=1
    )
    from_above = from_behind(lower_part.astype(jnp.bfloat16), "tm", -1).astype(lower_part.dtype)
    from_below = from_behind(upper_part.astype(jnp.bfloat16), "tm", 1).astype(upper_part.dtype)
    dfused = []
    for view in range(3):
        dmiddle, dquery, dkeys, dvalues = halves[view]
        normed = self_keep[view][0]
        length = dquery.shape[0]
        own_keys = dkeys[spatial : spatial + length]
        own_values = dvalues[spatial : spatial + length]
        own_keys = (
            own_keys.at[:spatial]
            .add(from_below[0, view])
            .at[length - spatial :]
            .add(from_above[0, view])
        )
        own_values = (
            own_values.at[:spatial]
            .add(from_below[1, view])
            .at[length - spatial :]
            .add(from_above[1, view])
        )
        dq_low = lowered(dquery)
        dk_low = lowered(own_keys)
        dv_low = lowered(own_values)
        grad_qkv[view] = [
            product_tn(normed, dq_low),
            product_tn(normed, dk_low),
            product_tn(normed, dv_low),
        ]
        dnormed = (
            product_nt(dq_low, qkv[view, 0])
            + product_nt(dk_low, qkv[view, 1])
            + product_nt(dv_low, qkv[view, 2])
        )
        dfused_norm, grad_gain[view][0] = norm_back(joined[view], gain[view, 0], dnormed)
        dfused.append(dmiddle + dfused_norm)
    dviews = list(dfused)
    for view in range(2):
        first, second, query, keys, values, mixed, probs = cross_keep[view]
        dbranch = lowered(dfused[view])
        grad_out[3 + view] = product_tn(mixed, dbranch)
        dmixed = lowered(product_nt(dbranch, outw[3 + view]))
        dquery, dkeys, dvalues = attend_back(query, keys, values, probs, dmixed)
        dq_low = lowered(dquery)
        dk_low = lowered(dkeys)
        dv_low = lowered(dvalues)
        grad_qkv[3 + view] = [
            product_tn(first, dq_low),
            product_tn(second, dk_low),
            product_tn(second, dv_low),
        ]
        dfirst = product_nt(dq_low, qkv[3 + view, 0])
        dsecond = product_nt(dk_low, qkv[3 + view, 1]) + product_nt(dv_low, qkv[3 + view, 2])
        dx_first, grad_gain[3 + view][0] = norm_back(views[view], gain[3 + view, 0], dfirst)
        dx_second, grad_gain[3 + view][1] = norm_back(views[view + 1], gain[3 + view, 1], dsecond)
        dviews[view] = dviews[view] + dx_first
        dviews[view + 1] = dviews[view + 1] + dx_second
    token_grad = jnp.concatenate(dviews, axis=0)[None]
    qkv_total = jnp.stack([jnp.stack(entry) for entry in grad_qkv]).reshape(15 * D, D)
    out_total = jnp.stack(grad_out).reshape(5 * D, D)
    gain_total = jnp.stack([jnp.stack(entry) for entry in grad_gain]).reshape(10 * D)
    totals = (
        qkv_total,
        out_total,
        jnp.stack(grad_up).reshape(3 * D, FF),
        jnp.stack(grad_down).reshape(3 * FF, D),
        gain_total,
    )
    shares = (
        lax.psum_scatter(totals[0], ("seq", "tm"), scatter_dimension=0, tiled=True),
        lax.psum_scatter(totals[1], ("seq", "tm"), scatter_dimension=0, tiled=True),
        lax.psum_scatter(totals[2], ("seq", "tm"), scatter_dimension=0, tiled=True),
        lax.psum_scatter(totals[3], ("seq", "tm"), scatter_dimension=0, tiled=True),
        lax.psum_scatter(totals[4], ("seq", "tm"), scatter_dimension=0, tiled=True),
    )
    return (layer_out, token_grad, shares[0], shares[1], shares[2], shares[3], shares[4])


def per_device(dims, tokens, cotangent, qkv_weights, out_weights, up_weights, down_weights, gains):
    rows = tokens[0]
    incoming = cotangent[0]
    spatial = rows.shape[0] // 7
    bounds = ((0, 4 * spatial), (4 * spatial, 6 * spatial), (6 * spatial, 7 * spatial))
    own_gains = gains.shape[0]
    tile = jnp.pad(gains.astype(F32), (0, 1024 - own_gains)).reshape(8, 128)
    shards = (qkv_weights, out_weights, up_weights, down_weights)
    slabs = tuple((2 * w.shape[0], w.shape[1]) for w in shards)
    wholes = gather_all(dims, *shards, tile)
    gain = wholes[4].reshape(-1, 1024)[:, :own_gains].reshape(5, 2, D)
    qkv = wholes[0].reshape(5, 3, D, D)
    outw = wholes[1].reshape(5, D, D)
    upw = wholes[2].reshape(3, D, FF)
    downw = wholes[3].reshape(3, FF, D)
    place = lax.axis_index("tm")
    count = lax.axis_size("tm")
    below_bias = jnp.where(place > 0, 0.0, FAR).astype(jnp.float32)
    above_bias = jnp.where(place < count - 1, 0.0, FAR).astype(jnp.float32)
    views = [rows[start:stop] for start, stop in bounds]
    cross_keep = []
    joined = []
    for view in range(2):
        first = lowered(norm_rows(views[view], gain[3 + view, 0]))
        second = lowered(norm_rows(views[view + 1], gain[3 + view, 1]))
        query = lowered(product(first, qkv[3 + view, 0]))
        keys = lowered(product(second, qkv[3 + view, 1]))
        values = lowered(product(second, qkv[3 + view, 2]))
        mixed, probs = attend(query, keys, values, 0.0)
        joined.append(views[view] + product(mixed, outw[3 + view]))
        cross_keep.append((first, second, query, keys, values, mixed, probs))
    joined.append(views[2])
    local_keep = []
    edges = []
    for view in range(3):
        normed = lowered(norm_rows(joined[view], gain[view, 0]))
        query = lowered(product(normed, qkv[view, 0]))
        keys = lowered(product(normed, qkv[view, 1]))
        values = lowered(product(normed, qkv[view, 2]))
        local_keep.append((normed, query, keys, values))
        paired = jnp.stack([keys, values])
        edges.append(jnp.concatenate([paired[:, :spatial], paired[:, -spatial:]], axis=1))
    rim = extended(jnp.stack(edges, axis=1), (("tm", 2),), spatial)
    self_keep = []
    outputs = []
    for view in range(3):
        normed, query, keys, values = local_keep[view]
        length = keys.shape[0]
        keys_all = jnp.concatenate([rim[0, view, :spatial], keys, rim[0, view, 3 * spatial :]], axis=0)
        values_all = jnp.concatenate([rim[1, view, :spatial], values, rim[1, view, 3 * spatial :]], axis=0)
        bias = jnp.concatenate(
            [
                jnp.broadcast_to(below_bias, (spatial,)),
                jnp.zeros((length,), jnp.float32),
                jnp.broadcast_to(above_bias, (spatial,)),
            ]
        )
        mixed, probs = attend(query, keys_all, values_all, bias)
        middle = joined[view] + product(mixed, outw[view])
        normed_two = lowered(norm_rows(middle, gain[view, 1]))
        hidden_pre = product(normed_two, upw[view])
        active = lowered(jax.nn.gelu(hidden_pre, approximate=False))
        outputs.append(middle + product(active, downw[view]))
        self_keep.append((normed, query, keys_all, values_all, mixed, probs, middle, normed_two, hidden_pre, active))
    layer_out = jnp.concatenate(outputs, axis=0)[None]
    grad_gain = [[None, None] for index in range(5)]
    halves = []
    d_pre, d_attn = [], []
    d_out = lowered(incoming)
    for view in range(3):
        normed, query, keys_all, values_all, mixed, probs, middle, normed_two, hidden_pre, active = self_keep[view]
        start, stop = bounds[view]
        dfinal = incoming[start:stop]
        dactive = product_nt(d_out[start:stop], downw[view])
        d_pre.append(lowered(gelu_back(hidden_pre, dactive)))
        dnormed_two = product_nt(d_pre[view], upw[view])
        dmid_norm, grad_gain[view][1] = norm_back(middle, gain[view, 1], dnormed_two)
        dmiddle = dfinal + dmid_norm
        d_attn.append(lowered(dmiddle))
        dmixed = lowered(product_nt(d_attn[view], outw[view]))
        dquery, dkeys, dvalues = attend_back(query, keys_all, values_all, probs, dmixed)
        halves.append((dmiddle, dquery, dkeys, dvalues))
    lower_part = jnp.stack([jnp.stack([half[2][:spatial], half[3][:spatial]]) for half in halves], axis=1)
    upper_part = jnp.stack([jnp.stack([half[2][-spatial:], half[3][-spatial:]]) for half in halves], axis=1)
    from_above = from_behind(lower_part.astype(jnp.bfloat16), "tm", -1).astype(lower_part.dtype)
    from_below = from_behind(upper_part.astype(jnp.bfloat16), "tm", 1).astype(upper_part.dtype)
    dfused = []
    d_self = [[], [], []]
    for view in range(3):
        dmiddle, dquery, dkeys, dvalues = halves[view]
        length = dquery.shape[0]
        own = [dquery]
        for index, whole in ((0, dkeys), (1, dvalues)):
            part = whole[spatial : spatial + length]
            part = part.at[:spatial].add(from_below[index, view]).at[length - spatial :].add(from_above[index, view])
            own.append(part)
        own = [lowered(part) for part in own]
        for index in range(3):
            d_self[index].append(own[index])
        dnormed = (
            product_nt(own[0], qkv[view, 0]) + product_nt(own[1], qkv[view, 1]) + product_nt(own[2], qkv[view, 2])
        )
        dfused_norm, grad_gain[view][0] = norm_back(joined[view], gain[view, 0], dnormed)
        dfused.append(dmiddle + dfused_norm)
    dviews = list(dfused)
    d_cross = []
    d_join = [[], [], []]
    for view in range(2):
        first, second, query, keys, values, mixed, probs = cross_keep[view]
        d_cross.append(lowered(dfused[view]))
        dmixed = lowered(product_nt(d_cross[view], outw[3 + view]))
        own = [lowered(part) for part in attend_back(query, keys, values, probs, dmixed)]
        for index in range(3):
            d_join[index].append(own[index])
        dfirst = product_nt(own[0], qkv[3 + view, 0])
        dsecond = product_nt(own[1], qkv[3 + view, 1]) + product_nt(own[2], qkv[3 + view, 2])
        dx_first, grad_gain[3 + view][0] = norm_back(views[view], gain[3 + view, 0], dfirst)
        dx_second, grad_gain[3 + view][1] = norm_back(views[view + 1], gain[3 + view, 1], dsecond)
        dviews[view] = dviews[view] + dx_first
        dviews[view + 1] = dviews[view + 1] + dx_second
    token_grad = jnp.concatenate(dviews, axis=0)[None]
    gain_total = jnp.stack([jnp.stack(entry) for entry in grad_gain]).reshape(-1, own_gains)
    gain_total = jnp.pad(gain_total, ((0, 0), (0, 1024 - own_gains))).reshape(*dims, 2, 8, 128)
    tall = lambda parts: jnp.concatenate(parts, axis=0)
    kept = lambda index: tall([entry[index] for entry in self_keep])
    lefts = (
        kept(9),
        kept(7),
        kept(4),
        kept(0),
        tall([entry[0] for entry in cross_keep]),
        tall([entry[1] for entry in cross_keep]),
        tall([entry[5] for entry in cross_keep]),
    )
    rights = (d_out, tall(d_pre), tall(d_attn), *[tall(part) for part in d_self], tall(d_cross), *[tall(part) for part in d_join])
    shares = reduce_all(dims, slabs, lefts, rights, gain_total)
    gain_share = shares[4].reshape(-1)[:own_gains]
    return (layer_out, token_grad, shares[0], shares[1], shares[2], shares[3], gain_share)


def fits(mesh, dims):
    chips = dims[0] * dims[1] * dims[2]
    rows = (15 * D, 5 * D, 3 * D, 3 * FF)
    return dims[:2] == (2, 2) and all(r % (chips * ROWS) == 0 for r in rows) and 10 * D // (2 * chips) <= 1024


def solution(mesh):
    seq, tm = mesh.shape["seq"], mesh.shape["tm"]
    dims = (2, seq // 2, tm // 2)
    body = functools.partial(per_device, dims) if fits(mesh, dims) else plain_device
    placed = (
        P("seq", "tm", None),
        P("seq", "tm", None),
        P(("seq", "tm"), None),
        P(("seq", "tm"), None),
        P(("seq", "tm"), None),
        P(("seq", "tm"), None),
        P(("seq", "tm")),
    )
    return jax.shard_map(body, mesh=mesh, in_specs=placed, out_specs=placed, check_vma=False)
```

```python
import functools

import jax
import jax.numpy as jnp
from jax import lax
from jax.experimental import pallas as pl
from jax.experimental.pallas import tpu as pltpu
from jax.sharding import PartitionSpec as P

D = 768
HEADS = 12
FF = 3072

EPS = 1e-06
FAR = -1e30
MESH = pl.DeviceIdType.MESH
BF = jnp.bfloat16
F32 = jnp.float32
BLOCK = D // 2
ROWS = 48
LAG = 0.5
SLOTS = 36
COPIES = 480


def extended(cells, sides, width):
    for axis, dim in sides:
        count = lax.axis_size(axis)
        ends = count - 1
        head = lax.slice_in_dim(cells, 0, width, axis=dim)
        tail = lax.slice_in_dim(cells, cells.shape[dim] - width, cells.shape[dim], axis=dim)
        cells = jnp.concatenate(
            [
                lax.ppermute(tail, axis, [(i, (i + 1) % count) for i in range(ends)]),
                cells,
                lax.ppermute(head, axis, [((i + 1) % count, i) for i in range(ends)]),
            ],
            axis=dim,
        )
    return cells


def from_behind(block, axis, distance):
    devices = range(lax.axis_size(axis))
    route = [(i - distance, i) for i in devices if i - distance in devices]
    return lax.ppermute(block, axis, route)


def norm_rows(x, gain):
    mean = jnp.mean(x, axis=-1, keepdims=True)
    centered = x - mean
    spread = jnp.mean(centered * centered, axis=-1, keepdims=True)
    return centered * lax.rsqrt(spread + EPS) * gain


def norm_back(x, gain, grad):
    unused, pull = jax.vjp(norm_rows, x, gain)
    return pull(grad)


def gelu_back(hidden_pre, grad):
    unused, pull = jax.vjp(lambda value: jax.nn.gelu(value, approximate=False), hidden_pre)
    return pull(grad)[0]


def lowered(value):
    return value.astype(jnp.bfloat16)


def product(left, right):
    return jnp.dot(left, right, preferred_element_type=jnp.float32)


def product_tn(left, right):
    return lax.dot_general(
        left, right, (((0,), (0,)), ((), ())), preferred_element_type=jnp.float32
    )


def product_nt(left, right):
    return lax.dot_general(
        left, right, (((1,), (1,)), ((), ())), preferred_element_type=jnp.float32
    )


def unstack(parts):
    qkv_flat, out_flat, up_flat, down_flat, gain_flat = parts
    return (
        qkv_flat.reshape(5, 3, D, D),
        out_flat.reshape(5, D, D),
        up_flat.reshape(3, D, FF),
        down_flat.reshape(3, FF, D),
        gain_flat.reshape(5, 2, D),
    )


def attend(query, keys, values, bias):
    rows, width = query.shape
    depth = width // HEADS
    qh = query.reshape(rows, HEADS, depth)
    kh = keys.reshape(keys.shape[0], HEADS, depth)
    vh = values.reshape(values.shape[0], HEADS, depth)
    scores = (
        jnp.einsum("qhd,khd->hqk", qh, kh, preferred_element_type=jnp.float32) * depth ** (-0.5)
        + bias
    )
    top = jnp.max(scores, axis=-1, keepdims=True)
    expo = jnp.exp(scores - top)
    probs = expo / jnp.sum(expo, axis=-1, keepdims=True)
    mixed = jnp.einsum("hqk,khd->qhd", lowered(probs), vh, preferred_element_type=jnp.float32)
    return (lowered(mixed.reshape(rows, width)), probs)


def attend_back(query, keys, values, probs, grad_mixed):
    rows, width = query.shape
    depth = width // HEADS
    qh = query.reshape(rows, HEADS, depth)
    kh = keys.reshape(keys.shape[0], HEADS, depth)
    vh = values.reshape(values.shape[0], HEADS, depth)
    gh = grad_mixed.reshape(rows, HEADS, depth)
    dprobs = jnp.einsum("qhd,khd->hqk", gh, vh, preferred_element_type=jnp.float32)
    dvalues = jnp.einsum("hqk,qhd->khd", lowered(probs), gh, preferred_element_type=jnp.float32)
    inner = jnp.sum(dprobs * probs, axis=-1, keepdims=True)
    dscores = lowered(probs * (dprobs - inner))
    scale = depth ** (-0.5)
    dquery = jnp.einsum("hqk,khd->qhd", dscores, kh, preferred_element_type=jnp.float32) * scale
    dkeys = jnp.einsum("hqk,qhd->khd", dscores, qh, preferred_element_type=jnp.float32) * scale
    return (dquery.reshape(rows, width), dkeys.reshape(-1, width), dvalues.reshape(-1, width))


class Place:
    def __init__(self, dims):
        self.dims = dims
        s = lax.axis_index("seq")
        t = lax.axis_index("tm")
        self.at = (s // dims[1], s % dims[1], t // 2)
        self.core = t % 2
        self.slab = t

    def device(self, at, core):
        return (at[0] * self.dims[1] + at[1], at[2] * 2 + core)

    def along(self, dim, value):
        at = list(self.at)
        at[dim] = value
        return self.device(at, self.core)

    def sibling(self):
        return self.device(self.at, 1 - self.core)


def meet(place):
    barrier = pltpu.get_barrier_semaphore()
    count = 1
    pl.semaphore_signal(barrier, inc=1, device_id=place.sibling(), device_id_type=MESH)
    for dim, n in enumerate(place.dims):
        me = place.at[dim]
        for step in (1, -1):
            ok = (me + step >= 0) & (me + step < n)

            @pl.when(ok)
            def _():
                pl.semaphore_signal(barrier, inc=1, device_id=place.along(dim, me + step), device_id_type=MESH)

            count = count + jnp.where(ok, 1, 0)
    step = 2 * place.core - 1
    ok = (place.at[2] + step >= 0) & (place.at[2] + step < place.dims[2])

    @pl.when(ok)
    def _():
        beside = (place.at[0], place.at[1], place.at[2] + step)
        pl.semaphore_signal(barrier, inc=1, device_id=place.device(beside, 1 - place.core), device_id_type=MESH)

    count = count + jnp.where(ok, 1, 0)
    pl.semaphore_wait(barrier, count)


class Copies:
    def __init__(self, send, recv):
        self.send, self.recv = send, recv
        self.used = 0
        self.sent = []

    def start(self, src, dst, device, ok=None):
        copy = pltpu.make_async_remote_copy(
            src_ref=src,
            dst_ref=dst,
            send_sem=self.send.at[self.used],
            recv_sem=self.recv.at[self.used],
            device_id=device,
            device_id_type=MESH,
        )
        self.used += 1
        when(ok, copy.start)
        self.sent.append((copy, ok))
        return copy

    def drain(self):
        for copy, ok in self.sent:
            when(ok, copy.wait_send)
        self.sent = []


def when(ok, action):
    if ok is None:
        action()
    else:

        @pl.when(ok)
        def _():
            action()


def gather_line(copies, place, dim, pick):
    n = place.dims[dim]
    me = place.at[dim]
    if n == 2:
        part = pick(me)
        copy = copies.start(part, part, place.along(dim, 1 - me))
        yield
        copy.wait_recv()
        return
    before = {}
    for hop in range(1, n):
        for step in (1, -1):
            origin = me - step * (hop - 1)
            held = (origin >= 0) & (origin < n)
            if hop > 1:
                when(held, before[step].wait_recv)
            ok = held & (me + step >= 0) & (me + step < n)
            part = pick(jnp.clip(origin, 0, n - 1))
            before[step] = copies.start(part, part, place.along(dim, jnp.clip(me + step, 0, n - 1)), ok)
        yield
    for step in (1, -1):
        origin = me - step * (n - 1)
        when((origin >= 0) & (origin < n), before[step].wait_recv)


def gather_piece(copies, place, full, rows, cols, order, pair):
    done = set()
    for dim in order:

        def pick(value):
            index = [slice(None) if d in done else place.at[d] for d in range(3)]
            index[dim] = value
            return full.at[(*index, pl.ds(*rows), cols)]

        yield from gather_line(copies, place, dim, pick)
        done.add(dim)
    if pair is not None:
        part = full.at[:, :, :, pl.ds(*rows), cols]
        pair.append(copies.start(part, part, place.sibling()))


ZXY, ZYX, XZY, YZX = (2, 1, 0), (2, 0, 1), (1, 2, 0), (0, 2, 1)
CYCLE = (XZY, YZX, ZXY, XZY, YZX, ZYX)


def pieces_of(slabs, arrays):
    flat = []
    for array in arrays:
        rows, width = slabs[array]
        for block in range(width // 2 // BLOCK):
            for row in range(0, rows, ROWS):
                flat.append((array, row, block, CYCLE[len(flat) % 6]))
    return [flat[i : i + 3] for i in range(0, len(flat), 3)]


def march(sets, begin, extra=()):
    waiting = list(sets)
    active = list(extra)
    step = 0
    while active or waiting:
        while waiting and step >= LAG * (len(sets) - len(waiting)):
            for piece in waiting.pop(0):
                active.append(begin(piece))
        still = []
        for one in active:
            try:
                yield next(one)
                still.append(one)
            except StopIteration:
                pass
        active = still
        step += 1


def weave(comm, work, each):
    live = [True, True]
    gate = [None, None]
    sources = (comm, work)

    def advance(k):
        if not live[k]:
            return None
        if gate[k] is not None:
            if not gate[k]():
                return None
            gate[k] = None
        try:
            item = next(sources[k])
        except StopIteration:
            live[k] = False
            return None
        if callable(item):
            gate[k] = item
            return 0.0
        return item or 0.0

    credit = 0.0
    while live[0] or live[1]:
        moved = advance(0)
        if moved is not None:
            credit = min(credit + each, 4.0)
        stuck = moved is None
        while live[1] and (credit > 0 or stuck):
            cost = advance(1)
            if cost is None:
                break
            credit = max(credit - cost, -8.0)
            if stuck and live[0] and (gate[0] is None or gate[0]()):
                break


def matmul(left, right):
    return jnp.dot(left, right, preferred_element_type=F32)


def matmul_nt(left, right):
    return lax.dot_general(left, right, (((1,), (1,)), ((), ())), preferred_element_type=F32)


def matmul_tn(left, right):
    return lax.dot_general(left, right, (((0,), (0,)), ((), ())), preferred_element_type=F32)


def halves_of(pair):
    low = lax.broadcasted_iota(jnp.int32, pair.shape, 1) < pair.shape[1] // 2
    zero = jnp.zeros_like(pair)
    return jnp.where(low, pair, zero), jnp.where(low, zero, pair)


def softmax_rows(scores):
    expo = jnp.exp(scores - jnp.max(scores, axis=-1, keepdims=True))
    return expo * (1.0 / jnp.sum(expo, axis=-1, keepdims=True))


def attend_pair(query, keys, values, bias):
    outs = []
    for part in halves_of(query):
        scores = matmul_nt(part, keys) * 0.125
        if bias is not None:
            scores = scores + bias
        outs.append(matmul(softmax_rows(scores).astype(BF), values))
    low = lax.broadcasted_iota(jnp.int32, outs[0].shape, 1) < outs[0].shape[1] // 2
    return jnp.where(low, outs[0], outs[1]).astype(BF)


def gain_table(tiles, own):
    rows = tiles.shape[0]
    filled = own // 48
    r = lax.broadcasted_iota(jnp.int32, (rows, D), 0)
    c = lax.broadcasted_iota(jnp.int32, (rows, D), 1)
    spread = (lax.broadcasted_iota(jnp.int32, (128, D), 0) == lax.broadcasted_iota(jnp.int32, (128, D), 1) % 48)
    wide = matmul(tiles.astype(BF), spread.astype(BF))
    flat = (r // 8) * filled + r % 8
    wide = jnp.where((r % 8 < filled) & (c // 48 == flat % 16), wide, 0.0).astype(BF)
    rr = lax.broadcasted_iota(jnp.int32, (16, rows), 1)
    vv = lax.broadcasted_iota(jnp.int32, (16, rows), 0)
    pick = (rr % 8 < filled) & (((rr // 8) * filled + rr % 8) // 16 == vv)
    return matmul(pick.astype(BF), wide)


class Weights:
    def __init__(self, dims, slabs, wholes, ring, sems, blocks):
        self.dims, self.slabs, self.wholes, self.ring, self.sems, self.blocks = dims, slabs, wholes, ring, sems, blocks
        self.depth = ring.shape[0]
        self.loading = {}
        self.next_load = 0
        self.next_use = 0
        self.ready = set()

    def fetch(self):
        while self.next_load < min(len(self.blocks), self.next_use + self.depth):
            i = self.next_load
            a, row, block = self.blocks[i]
            if a not in self.ready:
                return
            slot = i % self.depth
            copies = []
            at, end = row, row + D
            slab = self.slabs[a][0]
            while at < end:
                chip, off = at // slab, at % slab
                n = min(end - at, slab - off)
                p, q, z = chip // (self.dims[1] * self.dims[2]), chip // self.dims[2] % self.dims[1], chip % self.dims[2]
                copies.append(
                    pltpu.make_async_copy(
                        self.wholes[a].at[p, q, z, pl.ds(off, n), pl.ds(block * D, D)],
                        self.ring.at[slot, pl.ds(at - row, n)],
                        self.sems.at[slot, len(copies)],
                    )
                )
                at += n
            for one in copies:
                one.start()
            self.loading[i] = copies
            self.next_load += 1

    def take(self, expected):
        i = self.next_use
        assert self.blocks[i] == expected, (self.blocks[i], expected)
        self.fetch()
        for one in self.loading.pop(i):
            one.wait()
        return self.ring.at[i % self.depth]

    def give_back(self):
        self.next_use += 1
        self.fetch()


def forward_blocks():
    blocks = [(0, (9 + i) * D, 0) for i in range(6)]
    blocks += [(1, 3 * D, 0), (1, 4 * D, 0)]
    blocks += [(0, i * D, 0) for i in range(9)]
    blocks += [(1, i * D, 0) for i in range(3)]
    blocks += [(2, v * D, j) for v in range(3) for j in range(FF // D)]
    blocks += [(3, v * FF + j * D, 0) for v in range(3) for j in range(FF // D)]
    return blocks


KEPT = ("first", "second", "cq", "ck", "cv", "cmixed", "joined", "normed", "q", "kx", "vx", "mixed", "middle", "normed_two", "hidden", "active")


def forward_shapes(rows):
    u = rows // 7
    sizes = dict(
        first=(6 * u, D), second=(3 * u, D), cq=(6 * u, D), ck=(3 * u, D), cv=(3 * u, D), cmixed=(6 * u, D),
        joined=(rows, D), normed=(rows, D), q=(rows, D), kx=(rows + 6 * u, D), vx=(rows + 6 * u, D),
        mixed=(rows, D), middle=(rows, D), normed_two=(rows, D), hidden=(rows, FF), active=(rows, FF),
    )
    return {k: (sizes[k], F32 if k in ("joined", "middle", "hidden") else BF) for k in KEPT}


def halo_device(place, count, step):
    t = jnp.clip(place.slab + step, 0, count - 1)
    return (place.at[0] * place.dims[1] + place.at[1], t)


def slab_bias(place, count, width, spatial):
    col = lax.broadcasted_iota(jnp.int32, (1, width), 1)
    below = (col < spatial) & (place.slab == 0)
    above = (col >= width - spatial) & (place.slab == count - 1)
    return jnp.where(below | above, FAR, 0.0).astype(F32)


def forward_work(place, copies, weights, need, gain, x, layer, v, save):
    u = x.shape[0] // 7
    count = 2 * place.dims[2]
    spans = ((0, 4 * u), (4 * u, 2 * u), (6 * u, u))
    bases = (0, 6 * u, 10 * u)
    yield need("gain")
    for c in range(2):
        r0, n = spans[c]
        k0, m = spans[c + 1]
        rows, keys = pl.ds(r0, n), pl.ds(k0 - 4 * u, m)
        g = lambda j: gain[pl.ds(2 * (3 + c) + j, 1), :]
        v["first"][rows] = norm_rows(x[rows], g(0)).astype(BF)
        v["second"][keys] = norm_rows(x[pl.ds(k0, m)], g(1)).astype(BF)
        yield 0.5
    save("first")
    save("second")
    yield need(0)
    for c in range(2):
        r0, n = spans[c]
        k0, m = spans[c + 1]
        rows, keys = pl.ds(r0, n), pl.ds(k0 - 4 * u, m)
        for j, (src, dst, part) in enumerate((("first", "cq", rows), ("second", "ck", keys), ("second", "cv", keys))):
            w = weights.take((0, (9 + 3 * c + j) * D, 0))
            v[dst][part] = matmul(v[src][part], w[...]).astype(BF)
            weights.give_back()
            yield 0.8
        for h in range(HEADS // 2):
            cols = pl.ds(h * 128, 128)
            v["cmixed"][rows, cols] = attend_pair(v["cq"][rows, cols], v["ck"][keys, cols], v["cv"][keys, cols], None)
            yield 0.8 if c == 0 else 0.3
    for name in ("cq", "ck", "cv", "cmixed"):
        save(name)
    yield need(1)
    for c in range(2):
        rows = pl.ds(*spans[c])
        w = weights.take((1, (3 + c) * D, 0))
        v["joined"][rows] = x[rows] + matmul(v["cmixed"][rows], w[...])
        weights.give_back()
        yield 0.8
    v["joined"][pl.ds(*spans[2])] = x[pl.ds(*spans[2])]
    save("joined")
    for name in ("kx", "vx"):
        for view in range(3):
            base, n = bases[view], spans[view][1]

            @pl.when(place.slab == 0)
            def _():
                v[name][pl.ds(base, u)] = jnp.zeros((u, D), BF)

            @pl.when(place.slab == count - 1)
            def _():
                v[name][pl.ds(base + u + n, u)] = jnp.zeros((u, D), BF)

    halo = {0: [], 1: [], 2: []}
    for view in range(3):
        r0, n = spans[view]
        rows = pl.ds(r0, n)
        base = bases[view]
        v["normed"][rows] = norm_rows(v["joined"][rows], gain[pl.ds(2 * view, 1), :]).astype(BF)
        for j, (dst, part) in enumerate((("q", rows), ("kx", pl.ds(base + u, n)), ("vx", pl.ds(base + u, n)))):
            w = weights.take((0, (3 * view + j) * D, 0))
            v[dst][part] = matmul(v["normed"][rows], w[...]).astype(BF)
            weights.give_back()
            if j > 0:
                ref = v[dst]
                up, down = place.slab < count - 1, place.slab > 0
                halo[view].append(
                    (copies.start(ref.at[pl.ds(base + n, u)], ref.at[pl.ds(base, u)], halo_device(place, count, 1), up), down)
                )
                halo[view].append(
                    (
                        copies.start(
                            ref.at[pl.ds(base + u, u)], ref.at[pl.ds(base + u + n, u)], halo_device(place, count, -1), down
                        ),
                        up,
                    )
                )
            yield 0.8
    save("normed")
    save("q")
    for view in range(3):
        r0, n = spans[view]
        rows, keys = pl.ds(r0, n), pl.ds(bases[view], n + 2 * u)
        for one, ok in halo[view]:
            when(ok, one.wait_recv)
        bias = slab_bias(place, count, n + 2 * u, u)
        for h in range(HEADS // 2):
            cols = pl.ds(h * 128, 128)
            v["mixed"][rows, cols] = attend_pair(v["q"][rows, cols], v["kx"][keys, cols], v["vx"][keys, cols], bias)
            yield (1.4, 0.6, 0.3)[view]
        w = weights_later = None
    save("kx")
    save("vx")
    save("mixed")
    for view in range(3):
        rows = pl.ds(*spans[view])
        w = weights.take((1, view * D, 0))
        v["middle"][rows] = v["joined"][rows] + matmul(v["mixed"][rows], w[...])
        weights.give_back()
        v["normed_two"][rows] = norm_rows(v["middle"][rows], gain[pl.ds(2 * view + 1, 1), :]).astype(BF)
        yield 1.0
    save("middle")
    save("normed_two")
    yield need(2)
    for view in range(3):
        rows = pl.ds(*spans[view])
        for j in range(FF // D):
            cols = pl.ds(j * D, D)
            w = weights.take((2, view * D, j))
            pre = matmul(v["normed_two"][rows], w[...])
            weights.give_back()
            v["hidden"][rows, cols] = pre
            v["active"][rows, cols] = (0.5 * pre * (1.0 + lax.erf(pre * (0.5**0.5)))).astype(BF)
            yield 1.2
    save("hidden")
    save("active")
    yield need(3)
    for view in range(3):
        rows = pl.ds(*spans[view])
        for j in range(FF // D):
            w = weights.take((3, view * FF + j * D, 0))
            term = matmul(v["active"][rows, pl.ds(j * D, D)], w[...])
            weights.give_back()
            layer[rows] = (v["middle"][rows] if j == 0 else layer[rows]) + term
            yield 0.8
    save("layer")


def gather_kernel(dims, own_gains, *refs):
    refs = list(refs)
    take = lambda n: [refs.pop(0) for _ in range(n)]
    shards = take(4)
    gain_tile, x = take(2)
    fulls = take(4)
    gain_out, layer_out = take(2)
    kept_out = dict(zip(KEPT, take(len(KEPT))))
    theirs, merged = take(4), take(4)
    gain_all, gain, layer = take(3)
    v = dict(zip(KEPT, take(len(KEPT))))
    ring, send, recv, local, ring_sem, save_sem = take(6)
    place = Place(dims)
    copies = Copies(send, recv)
    core = place.core
    at = place.at
    meet(place)
    width = [s.shape[1] // 2 for s in shards]
    mine = [pl.ds(pl.multiple_of(core * w, 128), w) for w in width]
    other = [pl.ds(pl.multiple_of((1 - core) * w, 128), w) for w in width]
    swaps = []
    for a in range(4):
        swaps.append(copies.start(shards[a].at[:, other[a]], theirs[a], place.sibling()))
    own_tile = gain_all.at[at[0], at[1], at[2], core]
    own_tile[...] = gain_tile[...]
    swap_gain = copies.start(own_tile, own_tile, place.sibling())
    slabs = [(m.shape[0], 2 * m.shape[1]) for m in merged]
    sets = pieces_of(slabs, range(4))
    left = {a: sum(1 for s in sets for piece in s if piece[0] == a) for a in range(4)}
    pair = {a: [] for a in range(4)}
    ready = set()
    state = {"gain": False}

    def prepare(a):
        swaps[a].wait_recv()
        w = width[a]
        own = jnp.where(core == 0, shards[a][:, :w].astype(F32), shards[a][:, w:].astype(F32))
        got = theirs[a][...].astype(F32)
        upper = jnp.where(core == 0, own, got)
        lower = jnp.where(core == 0, got, own)
        merged[a][...] = jnp.concatenate([upper, lower], axis=0).astype(BF)
        copy = pltpu.make_async_copy(merged[a], fulls[a].at[at[0], at[1], at[2], :, mine[a]], local.at[a])
        copy.start()
        copy.wait()

    def begin(piece):
        a, row, block, order = piece
        if a not in ready:
            prepare(a)
            ready.add(a)
        cols = pl.ds(pl.multiple_of(core * width[a] + block * BLOCK, 128), BLOCK)
        yield from gather_piece(copies, place, fulls[a], (row, ROWS), cols, order, pair[a])
        left[a] -= 1

    def gains():
        swap_gain.wait_recv()
        done = set()
        for dim in ZXY:

            def pick(value):
                index = [slice(None) if d in done else at[d] for d in range(3)]
                index[dim] = value
                return gain_all.at[tuple(index)]

            yield from gather_line(copies, place, dim, pick)
            done.add(dim)
        gain[...] = gain_table(gain_all[...].reshape(-1, 128), own_gains)
        copy = pltpu.make_async_copy(gain, gain_out, local.at[4])
        copy.start()
        copy.wait()
        state["gain"] = True

    weights = Weights(dims, slabs, fulls, ring, ring_sem, forward_blocks())

    def need(what):
        def gate():
            if what == "gain":
                return state["gain"]
            if left[what]:
                return False
            if what not in weights.ready:
                for copy in pair[what]:
                    copy.wait_recv()
                weights.ready.add(what)
                weights.fetch()
            return True

        return gate

    saves = []

    def save(name):
        src, dst = (layer, layer_out) if name == "layer" else (v[name], kept_out[name])
        copy = pltpu.make_async_copy(src, dst, save_sem.at[len(saves)])
        copy.start()
        saves.append(copy)

    work = forward_work(place, copies, weights, need, gain, x, layer, v, save)
    weave(march(sets, begin, (gains(),)), work, 0.8)
    for copy in saves:
        copy.wait()
    copies.drain()


def gather_all(dims, own_gains, shards, tile, x):
    slabs = [(2 * s.shape[0], s.shape[1]) for s in shards]
    anywhere = pl.BlockSpec(memory_space=pl.ANY)
    vmem = pl.BlockSpec(memory_space=pltpu.VMEM)
    kept = forward_shapes(x.shape[0])
    segments = max(D // s[0] + 2 for s in slabs)
    outs = pl.pallas_call(
        functools.partial(gather_kernel, dims, own_gains),
        out_shape=[jax.ShapeDtypeStruct((*dims, *s), BF) for s in slabs]
        + [jax.ShapeDtypeStruct((16, D), F32), jax.ShapeDtypeStruct(x.shape, F32)]
        + [jax.ShapeDtypeStruct(*kept[k]) for k in KEPT],
        in_specs=[vmem] * 6,
        out_specs=[anywhere] * (6 + len(KEPT)),
        scratch_shapes=[pltpu.VMEM((r // 2, w // 2), BF) for r, w in slabs]
        + [pltpu.VMEM((r, w // 2), BF) for r, w in slabs]
        + [pltpu.VMEM((*dims, 2, 8, 128), F32), pltpu.VMEM((16, D), F32), pltpu.VMEM(x.shape, F32)]
        + [pltpu.VMEM(*kept[k]) for k in KEPT]
        + [
            pltpu.VMEM((4, D, D), BF),
            pltpu.SemaphoreType.DMA((COPIES,)),
            pltpu.SemaphoreType.DMA((COPIES,)),
            pltpu.SemaphoreType.DMA((5,)),
            pltpu.SemaphoreType.DMA((4, segments)),
            pltpu.SemaphoreType.DMA((1 + len(KEPT),)),
        ],
        compiler_params=pltpu.CompilerParams(collective_id=0, has_side_effects=True, vmem_limit_bytes=60 << 20),
    )(*shards, tile, x)
    return outs[:4], outs[4], outs[5], dict(zip(KEPT, outs[6:]))


def add_to(total, term):
    total[...] = (total[...].astype(F32) + term[...].astype(F32)).astype(total.dtype)


def reduce_line(copies, place, pick, slots):
    n = place.dims[2]
    z = place.at[2]
    before = {}
    for turn in range(n):
        for step in (1, -1):
            far = z if step == 1 else n - 1 - z
            goal = far + n - 1 - turn
            goal = jnp.minimum(goal if step == 1 else n - 1 - goal, n - 1)
            goal = jnp.maximum(goal, 0)
            if turn > 0:

                def take(step=step, turn=turn, goal=goal):
                    before[step].wait_recv()
                    add_to(pick(goal), slots(turn - 1, step))

                when((far >= 1) & (far <= turn), take)
            if turn < n - 1:
                before[step] = copies.start(
                    pick(goal), slots(turn, step), place.along(2, jnp.clip(z + step, 0, n - 1)), far <= turn
                )
        if turn < n - 1:
            yield


def reduce_piece(copies, place, source, order, acc, first, turns, last, local, finish):
    lead = order[0]
    rest = 1 - lead
    me, mine = place.at[lead], place.at[rest]
    z = place.at[2]
    copy = copies.start(source(lead, 1 - me), first, place.along(lead, 1 - me))
    load = pltpu.make_async_copy(source(lead, me), acc, local)
    load.start()
    yield
    load.wait()
    copy.wait_recv()
    add_to(acc, first)
    slots = lambda turn, step: turns.at[turn, (1 - step) // 2]
    if order[1] == 2:
        yield from reduce_line(copies, place, lambda v: acc.at[:, v], slots)
        copy = copies.start(acc.at[1 - mine, z], last, place.along(rest, 1 - mine))
        yield
        copy.wait_recv()
        finish(acc[mine, z].astype(F32) + last[...].astype(F32))
    else:
        copy = copies.start(acc.at[1 - mine], last, place.along(rest, 1 - mine))
        yield
        copy.wait_recv()
        add_to(acc.at[mine], last)
        yield from reduce_line(copies, place, lambda v: acc.at[mine, v], slots)
        finish(acc[mine, z].astype(F32))


LEFTS = ("active", "normed_two", "mixed", "normed", "first", "second", "cross_mixed")
RIGHTS = ("d_out", "d_pre", "d_attn", "dq", "dk", "dv", "d_cross", "cq", "ck", "cv")


def jobs_of(spatial):
    rows = {0: (0, 4 * spatial), 1: (4 * spatial, 2 * spatial), 2: (6 * spatial, spatial)}
    late = {0: (0, 2 * spatial), 1: (2 * spatial, spatial)}
    jobs = {a: [] for a in range(4)}
    for view in range(3):
        for block in range(FF // D):
            jobs[3].append((view * FF + block * D, 0, "active", block, rows[view], "d_out", 0, rows[view]))
        for block in range(FF // 2 // BLOCK):
            jobs[2].append((view * D, block, "normed_two", 0, rows[view], "d_pre", block, rows[view]))
        jobs[1].append((view * D, 0, "mixed", 0, rows[view], "d_attn", 0, rows[view]))
        for j, name in enumerate(("dq", "dk", "dv")):
            jobs[0].append(((3 * view + j) * D, 0, "normed", 0, rows[view], name, 0, rows[view]))
    for view in range(2):
        jobs[1].append(((3 + view) * D, 0, "cross_mixed", 0, rows[view], "d_cross", 0, rows[view]))
        jobs[0].append(((9 + 3 * view) * D, 0, "first", 0, rows[view], "cq", 0, rows[view]))
        for j, name in enumerate(("ck", "cv")):
            jobs[0].append(((10 + 3 * view + j) * D, 0, "second", 0, late[view], name, 0, late[view]))
    return jobs


def reduce_kernel(dims, slabs, sets, count, spatial, *refs):
    refs = list(refs)
    take = lambda n: [refs.pop(0) for _ in range(n)]
    lefts, rights = dict(zip(LEFTS, take(7))), dict(zip(RIGHTS, take(10)))
    (gain,) = take(1)
    results = take(4)
    (gain_out,) = take(1)
    parts = take(4)
    far_lefts, far_rights = dict(zip(LEFTS, take(7))), dict(zip(RIGHTS, take(10)))
    acc, first, turns_a, turns_b, last_a, last_b = take(6)
    finals = take(4)
    xs, ys, made = take(3)
    g_far, g_acc, g_first, g_turns, g_last = take(5)
    send, recv, local, load_sem, store_sem, final_sem = take(6)
    place = Place(dims)
    core = place.core
    copies = Copies(send, recv)
    meet(place)
    half_of = lambda ref, c: pl.ds(pl.multiple_of(c * (ref.shape[1] // 2), 128), ref.shape[1] // 2)
    coming = {}
    for name in ("active", "d_out", "normed_two", "d_pre", "mixed", "d_attn", "normed", "dq", "dk", "dv", "cross_mixed", "d_cross", "first", "cq", "second", "ck", "cv"):
        if name in lefts:
            coming[name] = copies.start(lefts[name], far_lefts[name], place.sibling())
        else:
            ref = rights[name]
            coming[name] = copies.start(ref.at[:, half_of(ref, 1 - core)], far_rights[name], place.sibling())
    swap_gain = copies.start(gain, g_far, place.sibling())

    arrived = set()

    def arrive(name):
        if name not in arrived:
            coming[name].wait_recv()
            arrived.add(name)

    order = [(a, job) for a in (3, 2, 1, 0) for job in jobs_of(spatial)[a]]

    def load(i):
        a, (row, block, left, lcol, lrows, right, rcol, rrows) = order[i]
        slot = i % 2
        arrive(left)
        arrive(right)
        n = lrows[1]
        ref = rights[right]
        own = pl.ds(pl.multiple_of(core * (ref.shape[1] // 2) + rcol * BLOCK, 128), BLOCK)
        pairs = [
            (lefts[left].at[pl.ds(*lrows), pl.ds(lcol * D, D)], xs.at[slot, pl.ds(0, n)]),
            (far_lefts[left].at[pl.ds(*lrows), pl.ds(lcol * D, D)], xs.at[slot, pl.ds(n, n)]),
            (ref.at[pl.ds(*rrows), own], ys.at[slot, pl.ds(0, n)]),
            (far_rights[right].at[pl.ds(*rrows), pl.ds(rcol * BLOCK, BLOCK)], ys.at[slot, pl.ds(n, n)]),
        ]
        loads = [pltpu.make_async_copy(s, d, load_sem.at[slot, j]) for j, (s, d) in enumerate(pairs)]
        for one in loads:
            one.start()
        return loads

    loading = {0: load(0)}
    storing = {}
    done = {"jobs": 0}

    def store(i):
        a, job = order[i]
        row, block = job[0], job[1]
        slab = slabs[a][0]
        slot = i % 2
        stores = []
        at, end = row, row + D
        while at < end:
            chip, off = at // slab, at % slab
            n = min(end - at, slab - off)
            p, q, z = chip // (dims[1] * dims[2]), chip // dims[2] % dims[1], chip % dims[2]
            stores.append(
                pltpu.make_async_copy(
                    made.at[slot, pl.ds(at - row, n)],
                    parts[a].at[p, q, z, pl.ds(off, n), pl.ds(block * BLOCK, BLOCK)],
                    store_sem.at[slot, len(stores)],
                )
            )
            at += n
        for one in stores:
            one.start()
        return stores

    def finish_stores(i):
        for one in storing.pop(i, ()):
            one.wait()

    def multiply(upto):
        while done["jobs"] < upto:
            i = done["jobs"]
            for one in loading.pop(i):
                one.wait()
            if i + 1 < len(order):
                loading[i + 1] = load(i + 1)
            finish_stores(i - 2)
            n = 2 * order[i][1][4][1]
            slot = i % 2
            made[slot] = lax.dot_general(
                xs[slot, :n], ys[slot, :n], (((0,), (0,)), ((), ())), preferred_element_type=F32
            ).astype(BF)
            storing[i] = store(i)
            done["jobs"] += 1

    upto = {}
    for a in (3, 2, 1, 0):
        upto[a] = max(i for i, one in enumerate(order) if one[0] == a) + 1

    used = {"n": 0, 0: 0, 1: 0}
    owners = []
    left_in = {a: sum(1 for s in sets for piece in s if piece[0] == a) for a in range(4)}
    ending = []

    def begin(piece):
        a, row, block, order_ = piece
        multiply(upto[a])
        for i in list(storing):
            finish_stores(i)
        i = used["n"]
        used["n"] += 1
        kind = 0 if order_[1] == 0 or order_[1] == 2 else 1
        way = order_[::-1]
        kind = 0 if way[1] == 2 else 1
        k = used[kind]
        used[kind] += 1
        slot = i % SLOTS
        if i >= SLOTS:
            owners[i - SLOTS].drain()
        mine = Copies(send, recv)
        mine.used = copies.used
        copies.used += 9
        owners.append(mine)
        cols = pl.ds(block * BLOCK, BLOCK)

        def source(dim, value):
            index = [slice(None)] * 3
            index[dim] = value
            return parts[a].at[(*index, pl.ds(row, ROWS), cols)]

        def finish(value):
            finals[a][pl.ds(row, ROWS), cols] = value
            left_in[a] -= 1
            if left_in[a] == 0:
                deliver(a)

        turns, last = ((turns_a, last_a), (turns_b, last_b))[kind]
        return reduce_piece(
            mine, place, source, way, acc.at[slot], first.at[i], turns.at[k], last.at[k], local.at[slot], finish
        )

    def deliver(a):
        rows, width = slabs[a][0] // 2, slabs[a][1] // 2
        cols = pl.ds(pl.multiple_of(core * width, 128), width)
        ending.append(
            copies.start(
                finals[a].at[pl.ds(pl.multiple_of((1 - core) * rows, 8), rows)], results[a].at[:, cols], place.sibling()
            )
        )
        keep = pltpu.make_async_copy(
            finals[a].at[pl.ds(pl.multiple_of(core * rows, 8), rows)], results[a].at[:, cols], final_sem.at[a]
        )
        keep.start()
        keep.wait()

    def gains():
        swap_gain.wait_recv()
        add_to(g_far, gain)
        source = lambda dim, value: g_far.at[(*[value if d == dim else slice(None) for d in range(3)], core)]

        def finish(value):
            gain_out[...] = value

        yield from reduce_piece(copies, place, source, (0, 1, 2), g_acc, g_first, g_turns, g_last, local.at[SLOTS], finish)

    for step, _ in enumerate(march(sets, begin, (gains(),))):
        if step % 8 == 7:
            multiply(min(len(order), done["jobs"] + 2))
    for one in ending:
        one.wait_recv()
    copies.drain()
    for one in owners:
        one.drain()


def reduce_all(dims, slabs, lefts, rights, gain):
    anywhere = pl.BlockSpec(memory_space=pl.ANY)
    vmem = pl.BlockSpec(memory_space=pltpu.VMEM)
    sets = pieces_of(slabs, (3, 2, 1, 0))
    flat = [piece for group in sets for piece in group]
    count = len(flat)
    bundled = sum(1 for piece in flat if piece[3][1] == 2)
    single = count - bundled
    z = dims[2]
    spatial = lefts[0].shape[0] // 7
    longest = 2 * 4 * spatial
    tile = (ROWS, BLOCK)
    segments = max(D // slab[0] + 2 for slab in slabs)
    halves = lambda ref: jax.ShapeDtypeStruct((ref.shape[0], ref.shape[1] // 2), BF)
    outs = pl.pallas_call(
        functools.partial(reduce_kernel, dims, slabs, sets, count, spatial),
        out_shape=[jax.ShapeDtypeStruct((s[0] // 2, s[1]), F32) for s in slabs]
        + [jax.ShapeDtypeStruct((8, 128), F32)]
        + [jax.ShapeDtypeStruct((*dims, s[0], s[1] // 2), BF) for s in slabs]
        + [jax.ShapeDtypeStruct(x.shape, BF) for x in lefts]
        + [halves(y) for y in rights],
        in_specs=[anywhere] * 17 + [vmem],
        out_specs=[vmem] * 5 + [anywhere] * 21,
        scratch_shapes=[
            pltpu.VMEM((SLOTS, 2, z, *tile), BF),
            pltpu.VMEM((count, 2, z, *tile), BF),
            pltpu.VMEM((bundled, z - 1, 2, 2, *tile), BF),
            pltpu.VMEM((single, z - 1, 2, *tile), BF),
            pltpu.VMEM((bundled, *tile), BF),
            pltpu.VMEM((single, z, *tile), BF),
        ]
        + [pltpu.VMEM((s[0], s[1] // 2), F32) for s in slabs]
        + [
            pltpu.VMEM((2, longest, D), BF),
            pltpu.VMEM((2, longest, BLOCK), BF),
            pltpu.VMEM((2, D, BLOCK), BF),
            pltpu.VMEM((*dims, 2, 8, 128), F32),
            pltpu.VMEM((2, z, 8, 128), F32),
            pltpu.VMEM((2, z, 8, 128), F32),
            pltpu.VMEM((z - 1, 2, 8, 128), F32),
            pltpu.VMEM((z, 8, 128), F32),
            pltpu.SemaphoreType.DMA((COPIES,)),
            pltpu.SemaphoreType.DMA((COPIES,)),
            pltpu.SemaphoreType.DMA((SLOTS + 1,)),
            pltpu.SemaphoreType.DMA((2, 4)),
            pltpu.SemaphoreType.DMA((2, segments)),
            pltpu.SemaphoreType.DMA((4,)),
        ],
        compiler_params=pltpu.CompilerParams(
            collective_id=1, has_side_effects=True, vmem_limit_bytes=60 << 20
        ),
    )(*lefts, *rights, gain)
    return outs[:5]


def plain_device(tokens, cotangent, qkv_weights, out_weights, up_weights, down_weights, gains):
    rows = tokens[0]
    incoming = cotangent[0]
    spatial = rows.shape[0] // 7
    bounds = ((0, 4 * spatial), (4 * spatial, 6 * spatial), (6 * spatial, 7 * spatial))
    qkv, outw, upw, downw, gain_low = unstack(
        (
            lax.all_gather(qkv_weights, ("seq", "tm"), axis=0, tiled=True),
            lax.all_gather(out_weights, ("seq", "tm"), axis=0, tiled=True),
            lax.all_gather(up_weights, ("seq", "tm"), axis=0, tiled=True),
            lax.all_gather(down_weights, ("seq", "tm"), axis=0, tiled=True),
            lax.all_gather(gains, ("seq", "tm"), axis=0, tiled=True),
        )
    )
    gain = gain_low.astype(jnp.float32)
    place = lax.axis_index("tm")
    count = lax.axis_size("tm")
    below_bias = jnp.where(place > 0, 0.0, FAR).astype(jnp.float32)
    above_bias = jnp.where(place < count - 1, 0.0, FAR).astype(jnp.float32)
    views = [rows[start:stop] for start, stop in bounds]
    cross_keep = []
    joined = []
    for view in range(2):
        first = lowered(norm_rows(views[view], gain[3 + view, 0]))
        second = lowered(norm_rows(views[view + 1], gain[3 + view, 1]))
        query = lowered(product(first, qkv[3 + view, 0]))
        keys = lowered(product(second, qkv[3 + view, 1]))
        values = lowered(product(second, qkv[3 + view, 2]))
        mixed, probs = attend(query, keys, values, 0.0)
        joined.append(views[view] + product(mixed, outw[3 + view]))
        cross_keep.append((first, second, query, keys, values, mixed, probs))
    joined.append(views[2])
    local_keep = []
    edges = []
    for view in range(3):
        normed = lowered(norm_rows(joined[view], gain[view, 0]))
        query = lowered(product(normed, qkv[view, 0]))
        keys = lowered(product(normed, qkv[view, 1]))
        values = lowered(product(normed, qkv[view, 2]))
        local_keep.append((normed, query, keys, values))
        paired = jnp.stack([keys, values])
        edges.append(jnp.concatenate([paired[:, :spatial], paired[:, -spatial:]], axis=1))
    rim = extended(jnp.stack(edges, axis=1), (("tm", 2),), spatial)
    self_keep = []
    outputs = []
    for view in range(3):
        normed, query, keys, values = local_keep[view]
        length = keys.shape[0]
        keys_all = jnp.concatenate(
            [rim[0, view, :spatial], keys, rim[0, view, 3 * spatial :]], axis=0
        )
        values_all = jnp.concatenate(
            [rim[1, view, :spatial], values, rim[1, view, 3 * spatial :]], axis=0
        )
        bias = jnp.concatenate(
            [
                jnp.broadcast_to(below_bias, (spatial,)),
                jnp.zeros((length,), jnp.float32),
                jnp.broadcast_to(above_bias, (spatial,)),
            ]
        )
        mixed, probs = attend(query, keys_all, values_all, bias)
        middle = joined[view] + product(mixed, outw[view])
        normed_two = lowered(norm_rows(middle, gain[view, 1]))
        hidden_pre = product(normed_two, upw[view])
        active = lowered(jax.nn.gelu(hidden_pre, approximate=False))
        outputs.append(middle + product(active, downw[view]))
        self_keep.append(
            (
                normed,
                query,
                keys_all,
                values_all,
                mixed,
                probs,
                middle,
                normed_two,
                hidden_pre,
                active,
            )
        )
    layer_out = jnp.concatenate(outputs, axis=0)[None]
    qkv, outw, upw, downw, gain_low = unstack(
        (
            lax.all_gather(qkv_weights, ("seq", "tm"), axis=0, tiled=True),
            lax.all_gather(out_weights, ("seq", "tm"), axis=0, tiled=True),
            lax.all_gather(up_weights, ("seq", "tm"), axis=0, tiled=True),
            lax.all_gather(down_weights, ("seq", "tm"), axis=0, tiled=True),
            lax.all_gather(gains, ("seq", "tm"), axis=0, tiled=True),
        )
    )
    grad_qkv = [[None, None, None] for index in range(5)]
    grad_out = [None] * 5
    grad_up = [None] * 3
    grad_down = [None] * 3
    grad_gain = [[None, None] for index in range(5)]
    halves = []
    for view in range(3):
        (
            normed,
            query,
            keys_all,
            values_all,
            mixed,
            probs,
            middle,
            normed_two,
            hidden_pre,
            active,
        ) = self_keep[view]
        start, stop = bounds[view]
        dfinal = incoming[start:stop]
        dbranch = lowered(dfinal)
        grad_down[view] = product_tn(active, dbranch)
        dactive = product_nt(dbranch, downw[view])
        dpre_low = lowered(gelu_back(hidden_pre, dactive))
        grad_up[view] = product_tn(normed_two, dpre_low)
        dnormed_two = product_nt(dpre_low, upw[view])
        dmid_norm, grad_gain[view][1] = norm_back(middle, gain[view, 1], dnormed_two)
        dmiddle = dfinal + dmid_norm
        dattn = lowered(dmiddle)
        grad_out[view] = product_tn(mixed, dattn)
        dmixed = lowered(product_nt(dattn, outw[view]))
        dquery, dkeys, dvalues = attend_back(query, keys_all, values_all, probs, dmixed)
        halves.append((dmiddle, dquery, dkeys, dvalues))
    lower_part = jnp.stack(
        [jnp.stack([half[2][:spatial], half[3][:spatial]]) for half in halves], axis=1
    )
    upper_part = jnp.stack(
        [jnp.stack([half[2][-spatial:], half[3][-spatial:]]) for half in halves], axis=1
    )
    from_above = from_behind(lower_part.astype(jnp.bfloat16), "tm", -1).astype(lower_part.dtype)
    from_below = from_behind(upper_part.astype(jnp.bfloat16), "tm", 1).astype(upper_part.dtype)
    dfused = []
    for view in range(3):
        dmiddle, dquery, dkeys, dvalues = halves[view]
        normed = self_keep[view][0]
        length = dquery.shape[0]
        own_keys = dkeys[spatial : spatial + length]
        own_values = dvalues[spatial : spatial + length]
        own_keys = (
            own_keys.at[:spatial]
            .add(from_below[0, view])
            .at[length - spatial :]
            .add(from_above[0, view])
        )
        own_values = (
            own_values.at[:spatial]
            .add(from_below[1, view])
            .at[length - spatial :]
            .add(from_above[1, view])
        )
        dq_low = lowered(dquery)
        dk_low = lowered(own_keys)
        dv_low = lowered(own_values)
        grad_qkv[view] = [
            product_tn(normed, dq_low),
            product_tn(normed, dk_low),
            product_tn(normed, dv_low),
        ]
        dnormed = (
            product_nt(dq_low, qkv[view, 0])
            + product_nt(dk_low, qkv[view, 1])
            + product_nt(dv_low, qkv[view, 2])
        )
        dfused_norm, grad_gain[view][0] = norm_back(joined[view], gain[view, 0], dnormed)
        dfused.append(dmiddle + dfused_norm)
    dviews = list(dfused)
    for view in range(2):
        first, second, query, keys, values, mixed, probs = cross_keep[view]
        dbranch = lowered(dfused[view])
        grad_out[3 + view] = product_tn(mixed, dbranch)
        dmixed = lowered(product_nt(dbranch, outw[3 + view]))
        dquery, dkeys, dvalues = attend_back(query, keys, values, probs, dmixed)
        dq_low = lowered(dquery)
        dk_low = lowered(dkeys)
        dv_low = lowered(dvalues)
        grad_qkv[3 + view] = [
            product_tn(first, dq_low),
            product_tn(second, dk_low),
            product_tn(second, dv_low),
        ]
        dfirst = product_nt(dq_low, qkv[3 + view, 0])
        dsecond = product_nt(dk_low, qkv[3 + view, 1]) + product_nt(dv_low, qkv[3 + view, 2])
        dx_first, grad_gain[3 + view][0] = norm_back(views[view], gain[3 + view, 0], dfirst)
        dx_second, grad_gain[3 + view][1] = norm_back(views[view + 1], gain[3 + view, 1], dsecond)
        dviews[view] = dviews[view] + dx_first
        dviews[view + 1] = dviews[view + 1] + dx_second
    token_grad = jnp.concatenate(dviews, axis=0)[None]
    qkv_total = jnp.stack([jnp.stack(entry) for entry in grad_qkv]).reshape(15 * D, D)
    out_total = jnp.stack(grad_out).reshape(5 * D, D)
    gain_total = jnp.stack([jnp.stack(entry) for entry in grad_gain]).reshape(10 * D)
    totals = (
        qkv_total,
        out_total,
        jnp.stack(grad_up).reshape(3 * D, FF),
        jnp.stack(grad_down).reshape(3 * FF, D),
        gain_total,
    )
    shares = (
        lax.psum_scatter(totals[0], ("seq", "tm"), scatter_dimension=0, tiled=True),
        lax.psum_scatter(totals[1], ("seq", "tm"), scatter_dimension=0, tiled=True),
        lax.psum_scatter(totals[2], ("seq", "tm"), scatter_dimension=0, tiled=True),
        lax.psum_scatter(totals[3], ("seq", "tm"), scatter_dimension=0, tiled=True),
        lax.psum_scatter(totals[4], ("seq", "tm"), scatter_dimension=0, tiled=True),
    )
    return (layer_out, token_grad, shares[0], shares[1], shares[2], shares[3], shares[4])


def per_device(dims, tokens, cotangent, qkv_weights, out_weights, up_weights, down_weights, gains):
    rows = tokens[0]
    incoming = cotangent[0]
    spatial = rows.shape[0] // 7
    bounds = ((0, 4 * spatial), (4 * spatial, 6 * spatial), (6 * spatial, 7 * spatial))
    own_gains = gains.shape[0]
    tile = jnp.pad(gains.astype(F32).reshape(-1, 48), ((0, 8 - own_gains // 48), (0, 80)))
    shards = (qkv_weights, out_weights, up_weights, down_weights)
    slabs = tuple((2 * w.shape[0], w.shape[1]) for w in shards)
    wholes, gain_rows, layer_out, kept = gather_all(dims, own_gains, shards, tile, rows)
    layer_out = layer_out[None]
    gain = gain_rows[:10].reshape(5, 2, D)
    qkv = wholes[0].reshape(5, 3, D, D)
    outw = wholes[1].reshape(5, D, D)
    upw = wholes[2].reshape(3, D, FF)
    downw = wholes[3].reshape(3, FF, D)
    place = lax.axis_index("tm")
    count = lax.axis_size("tm")
    below_bias = jnp.where(place > 0, 0.0, FAR).astype(jnp.float32)
    above_bias = jnp.where(place < count - 1, 0.0, FAR).astype(jnp.float32)
    views = [rows[start:stop] for start, stop in bounds]
    starts = (0, 6 * spatial, 10 * spatial, 13 * spatial)
    cross_keep = []
    for view in range(2):
        qs = slice(*bounds[view])
        ks = slice(bounds[view + 1][0] - 4 * spatial, bounds[view + 1][1] - 4 * spatial)
        query, keys, values = kept["cq"][qs], kept["ck"][ks], kept["cv"][ks]
        probs = attend(query, keys, values, 0.0)[1]
        cross_keep.append((None, None, query, keys, values, None, probs))
    joined = [kept["joined"][start:stop] for start, stop in bounds]
    self_keep = []
    for view in range(3):
        rs = slice(*bounds[view])
        ks = slice(starts[view], starts[view + 1])
        length = bounds[view][1] - bounds[view][0]
        query, keys_all, values_all = kept["q"][rs], kept["kx"][ks], kept["vx"][ks]
        bias = jnp.concatenate(
            [
                jnp.broadcast_to(below_bias, (spatial,)),
                jnp.zeros((length,), jnp.float32),
                jnp.broadcast_to(above_bias, (spatial,)),
            ]
        )
        probs = attend(query, keys_all, values_all, bias)[1]
        self_keep.append((None, query, keys_all, values_all, None, probs, kept["middle"][rs], None, kept["hidden"][rs], None))
    grad_gain = [[None, None] for index in range(5)]
    halves = []
    d_pre, d_attn = [], []
    d_out = lowered(incoming)
    for view in range(3):
        normed, query, keys_all, values_all, mixed, probs, middle, normed_two, hidden_pre, active = self_keep[view]
        start, stop = bounds[view]
        dfinal = incoming[start:stop]
        dactive = product_nt(d_out[start:stop], downw[view])
        d_pre.append(lowered(gelu_back(hidden_pre, dactive)))
        dnormed_two = product_nt(d_pre[view], upw[view])
        dmid_norm, grad_gain[view][1] = norm_back(middle, gain[view, 1], dnormed_two)
        dmiddle = dfinal + dmid_norm
        d_attn.append(lowered(dmiddle))
        dmixed = lowered(product_nt(d_attn[view], outw[view]))
        dquery, dkeys, dvalues = attend_back(query, keys_all, values_all, probs, dmixed)
        halves.append((dmiddle, dquery, dkeys, dvalues))
    lower_part = jnp.stack([jnp.stack([half[2][:spatial], half[3][:spatial]]) for half in halves], axis=1)
    upper_part = jnp.stack([jnp.stack([half[2][-spatial:], half[3][-spatial:]]) for half in halves], axis=1)
    from_above = from_behind(lower_part.astype(jnp.bfloat16), "tm", -1).astype(lower_part.dtype)
    from_below = from_behind(upper_part.astype(jnp.bfloat16), "tm", 1).astype(upper_part.dtype)
    dfused = []
    d_self = [[], [], []]
    for view in range(3):
        dmiddle, dquery, dkeys, dvalues = halves[view]
        length = dquery.shape[0]
        own = [dquery]
        for index, whole in ((0, dkeys), (1, dvalues)):
            part = whole[spatial : spatial + length]
            part = part.at[:spatial].add(from_below[index, view]).at[length - spatial :].add(from_above[index, view])
            own.append(part)
        own = [lowered(part) for part in own]
        for index in range(3):
            d_self[index].append(own[index])
        dnormed = (
            product_nt(own[0], qkv[view, 0]) + product_nt(own[1], qkv[view, 1]) + product_nt(own[2], qkv[view, 2])
        )
        dfused_norm, grad_gain[view][0] = norm_back(joined[view], gain[view, 0], dnormed)
        dfused.append(dmiddle + dfused_norm)
    dviews = list(dfused)
    d_cross = []
    d_join = [[], [], []]
    for view in range(2):
        first, second, query, keys, values, mixed, probs = cross_keep[view]
        d_cross.append(lowered(dfused[view]))
        dmixed = lowered(product_nt(d_cross[view], outw[3 + view]))
        own = [lowered(part) for part in attend_back(query, keys, values, probs, dmixed)]
        for index in range(3):
            d_join[index].append(own[index])
        dfirst = product_nt(own[0], qkv[3 + view, 0])
        dsecond = product_nt(own[1], qkv[3 + view, 1]) + product_nt(own[2], qkv[3 + view, 2])
        dx_first, grad_gain[3 + view][0] = norm_back(views[view], gain[3 + view, 0], dfirst)
        dx_second, grad_gain[3 + view][1] = norm_back(views[view + 1], gain[3 + view, 1], dsecond)
        dviews[view] = dviews[view] + dx_first
        dviews[view + 1] = dviews[view + 1] + dx_second
    token_grad = jnp.concatenate(dviews, axis=0)[None]
    gain_total = jnp.stack([jnp.stack(entry) for entry in grad_gain]).reshape(-1, own_gains)
    gain_total = jnp.pad(gain_total, ((0, 0), (0, 1024 - own_gains))).reshape(*dims, 2, 8, 128)
    tall = lambda parts: jnp.concatenate(parts, axis=0)
    lefts = tuple(kept[name] for name in ("active", "normed_two", "mixed", "normed", "first", "second", "cmixed"))
    rights = (d_out, tall(d_pre), tall(d_attn), *[tall(part) for part in d_self], tall(d_cross), *[tall(part) for part in d_join])
    shares = reduce_all(dims, slabs, lefts, rights, gain_total)
    gain_share = shares[4].reshape(-1)[:own_gains]
    return (layer_out, token_grad, shares[0], shares[1], shares[2], shares[3], gain_share)


def fits(mesh, dims):
    chips = dims[0] * dims[1] * dims[2]
    rows = (15 * D, 5 * D, 3 * D, 3 * FF)
    return dims[:2] == (2, 2) and all(r % (chips * ROWS) == 0 for r in rows) and (10 * D) % (2 * chips * 48) == 0 and 10 * D // (2 * chips) <= 384


def solution(mesh):
    seq, tm = mesh.shape["seq"], mesh.shape["tm"]
    dims = (2, seq // 2, tm // 2)
    body = functools.partial(per_device, dims) if fits(mesh, dims) else plain_device
    placed = (
        P("seq", "tm", None),
        P("seq", "tm", None),
        P(("seq", "tm"), None),
        P(("seq", "tm"), None),
        P(("seq", "tm"), None),
        P(("seq", "tm"), None),
        P(("seq", "tm")),
    )
    return jax.shard_map(body, mesh=mesh, in_specs=placed, out_specs=placed, check_vma=False)
```

```python
import functools

import jax
import jax.numpy as jnp
from jax import lax
from jax.experimental import pallas as pl
from jax.experimental.pallas import tpu as pltpu
from jax.sharding import PartitionSpec as P

D = 768
HEADS = 12
FF = 3072

EPS = 1e-06
FAR = -1e30
MESH = pl.DeviceIdType.MESH
BF = jnp.bfloat16
F32 = jnp.float32
BLOCK = D // 2
ROWS = 48
LAG = 0.5
SLOTS = 18
EACH = 1.2
COPIES = 480


def extended(cells, sides, width):
    for axis, dim in sides:
        count = lax.axis_size(axis)
        ends = count - 1
        head = lax.slice_in_dim(cells, 0, width, axis=dim)
        tail = lax.slice_in_dim(cells, cells.shape[dim] - width, cells.shape[dim], axis=dim)
        cells = jnp.concatenate(
            [
                lax.ppermute(tail, axis, [(i, (i + 1) % count) for i in range(ends)]),
                cells,
                lax.ppermute(head, axis, [((i + 1) % count, i) for i in range(ends)]),
            ],
            axis=dim,
        )
    return cells


def from_behind(block, axis, distance):
    devices = range(lax.axis_size(axis))
    route = [(i - distance, i) for i in devices if i - distance in devices]
    return lax.ppermute(block, axis, route)


def norm_rows(x, gain):
    mean = jnp.mean(x, axis=-1, keepdims=True)
    centered = x - mean
    spread = jnp.mean(centered * centered, axis=-1, keepdims=True)
    return centered * lax.rsqrt(spread + EPS) * gain


def norm_back(x, gain, grad):
    unused, pull = jax.vjp(norm_rows, x, gain)
    return pull(grad)


def gelu_back(hidden_pre, grad):
    unused, pull = jax.vjp(lambda value: jax.nn.gelu(value, approximate=False), hidden_pre)
    return pull(grad)[0]


def lowered(value):
    return value.astype(jnp.bfloat16)


def product(left, right):
    return jnp.dot(left, right, preferred_element_type=jnp.float32)


def product_tn(left, right):
    return lax.dot_general(
        left, right, (((0,), (0,)), ((), ())), preferred_element_type=jnp.float32
    )


def product_nt(left, right):
    return lax.dot_general(
        left, right, (((1,), (1,)), ((), ())), preferred_element_type=jnp.float32
    )


def unstack(parts):
    qkv_flat, out_flat, up_flat, down_flat, gain_flat = parts
    return (
        qkv_flat.reshape(5, 3, D, D),
        out_flat.reshape(5, D, D),
        up_flat.reshape(3, D, FF),
        down_flat.reshape(3, FF, D),
        gain_flat.reshape(5, 2, D),
    )


def attend(query, keys, values, bias):
    rows, width = query.shape
    depth = width // HEADS
    qh = query.reshape(rows, HEADS, depth)
    kh = keys.reshape(keys.shape[0], HEADS, depth)
    vh = values.reshape(values.shape[0], HEADS, depth)
    scores = (
        jnp.einsum("qhd,khd->hqk", qh, kh, preferred_element_type=jnp.float32) * depth ** (-0.5)
        + bias
    )
    top = jnp.max(scores, axis=-1, keepdims=True)
    expo = jnp.exp(scores - top)
    probs = expo / jnp.sum(expo, axis=-1, keepdims=True)
    mixed = jnp.einsum("hqk,khd->qhd", lowered(probs), vh, preferred_element_type=jnp.float32)
    return (lowered(mixed.reshape(rows, width)), probs)


def attend_back(query, keys, values, probs, grad_mixed):
    rows, width = query.shape
    depth = width // HEADS
    qh = query.reshape(rows, HEADS, depth)
    kh = keys.reshape(keys.shape[0], HEADS, depth)
    vh = values.reshape(values.shape[0], HEADS, depth)
    gh = grad_mixed.reshape(rows, HEADS, depth)
    dprobs = jnp.einsum("qhd,khd->hqk", gh, vh, preferred_element_type=jnp.float32)
    dvalues = jnp.einsum("hqk,qhd->khd", lowered(probs), gh, preferred_element_type=jnp.float32)
    inner = jnp.sum(dprobs * probs, axis=-1, keepdims=True)
    dscores = lowered(probs * (dprobs - inner))
    scale = depth ** (-0.5)
    dquery = jnp.einsum("hqk,khd->qhd", dscores, kh, preferred_element_type=jnp.float32) * scale
    dkeys = jnp.einsum("hqk,qhd->khd", dscores, qh, preferred_element_type=jnp.float32) * scale
    return (dquery.reshape(rows, width), dkeys.reshape(-1, width), dvalues.reshape(-1, width))


class Place:
    def __init__(self, dims):
        self.dims = dims
        s = lax.axis_index("seq")
        t = lax.axis_index("tm")
        self.at = (s // dims[1], s % dims[1], t // 2)
        self.core = t % 2
        self.slab = t

    def device(self, at, core):
        return (at[0] * self.dims[1] + at[1], at[2] * 2 + core)

    def along(self, dim, value):
        at = list(self.at)
        at[dim] = value
        return self.device(at, self.core)

    def sibling(self):
        return self.device(self.at, 1 - self.core)


def meet(place):
    barrier = pltpu.get_barrier_semaphore()
    count = 1
    pl.semaphore_signal(barrier, inc=1, device_id=place.sibling(), device_id_type=MESH)
    for dim, n in enumerate(place.dims):
        me = place.at[dim]
        for step in (1, -1):
            ok = (me + step >= 0) & (me + step < n)

            @pl.when(ok)
            def _():
                pl.semaphore_signal(barrier, inc=1, device_id=place.along(dim, me + step), device_id_type=MESH)

            count = count + jnp.where(ok, 1, 0)
    step = 2 * place.core - 1
    ok = (place.at[2] + step >= 0) & (place.at[2] + step < place.dims[2])

    @pl.when(ok)
    def _():
        beside = (place.at[0], place.at[1], place.at[2] + step)
        pl.semaphore_signal(barrier, inc=1, device_id=place.device(beside, 1 - place.core), device_id_type=MESH)

    count = count + jnp.where(ok, 1, 0)
    pl.semaphore_wait(barrier, count)


class Copies:
    def __init__(self, send, recv):
        self.send, self.recv = send, recv
        self.used = 0
        self.sent = []

    def start(self, src, dst, device, ok=None):
        copy = pltpu.make_async_remote_copy(
            src_ref=src,
            dst_ref=dst,
            send_sem=self.send.at[self.used],
            recv_sem=self.recv.at[self.used],
            device_id=device,
            device_id_type=MESH,
        )
        self.used += 1
        when(ok, copy.start)
        self.sent.append((copy, ok))
        return copy

    def drain(self):
        for copy, ok in self.sent:
            when(ok, copy.wait_send)
        self.sent = []


def when(ok, action):
    if ok is None:
        action()
    else:

        @pl.when(ok)
        def _():
            action()


def gather_line(copies, place, dim, pick):
    n = place.dims[dim]
    me = place.at[dim]
    if n == 2:
        part = pick(me)
        copy = copies.start(part, part, place.along(dim, 1 - me))
        yield
        copy.wait_recv()
        return
    before = {}
    for hop in range(1, n):
        for step in (1, -1):
            origin = me - step * (hop - 1)
            held = (origin >= 0) & (origin < n)
            if hop > 1:
                when(held, before[step].wait_recv)
            ok = held & (me + step >= 0) & (me + step < n)
            part = pick(jnp.clip(origin, 0, n - 1))
            before[step] = copies.start(part, part, place.along(dim, jnp.clip(me + step, 0, n - 1)), ok)
        yield
    for step in (1, -1):
        origin = me - step * (n - 1)
        when((origin >= 0) & (origin < n), before[step].wait_recv)


def gather_piece(copies, place, full, rows, cols, order, pair):
    done = set()
    for dim in order:

        def pick(value):
            index = [slice(None) if d in done else place.at[d] for d in range(3)]
            index[dim] = value
            return full.at[(*index, pl.ds(*rows), cols)]

        yield from gather_line(copies, place, dim, pick)
        done.add(dim)
    if pair is not None:
        part = full.at[:, :, :, pl.ds(*rows), cols]
        pair.append(copies.start(part, part, place.sibling()))


ZXY, ZYX, XZY, YZX = (2, 1, 0), (2, 0, 1), (1, 2, 0), (0, 2, 1)
CYCLE = (XZY, YZX, ZXY, XZY, YZX, ZYX)


def pieces_of(slabs, arrays):
    flat = []
    for array in arrays:
        rows, width = slabs[array]
        for block in range(width // 2 // BLOCK):
            for row in range(0, rows, ROWS):
                flat.append((array, row, block, CYCLE[len(flat) % 6]))
    return [flat[i : i + 3] for i in range(0, len(flat), 3)]


def march(sets, begin, extra=()):
    waiting = list(sets)
    active = list(extra)
    step = 0
    while active or waiting:
        while waiting and step >= LAG * (len(sets) - len(waiting)):
            for piece in waiting.pop(0):
                active.append(begin(piece))
        still = []
        for one in active:
            try:
                yield next(one)
                still.append(one)
            except StopIteration:
                pass
        active = still
        step += 1


def weave(comm, work, each):
    live = [True, True]
    gate = [None, None]
    sources = (comm, work)

    def advance(k):
        if not live[k]:
            return None
        if gate[k] is not None:
            if not gate[k]():
                return None
            gate[k] = None
        try:
            item = next(sources[k])
        except StopIteration:
            live[k] = False
            return None
        if callable(item):
            gate[k] = item
            return 0.0
        return item or 0.0

    credit = 0.0
    while live[0] or live[1]:
        moved = advance(0)
        if moved is not None:
            credit = min(credit + each, 4.0)
        stuck = moved is None
        while live[1] and (credit > 0 or stuck):
            cost = advance(1)
            if cost is None:
                break
            credit = max(credit - cost, -8.0)
            if stuck and live[0] and (gate[0] is None or gate[0]()):
                break


def matmul(left, right):
    return jnp.dot(left, right, preferred_element_type=F32)


def matmul_nt(left, right):
    return lax.dot_general(left, right, (((1,), (1,)), ((), ())), preferred_element_type=F32)


def matmul_tn(left, right):
    return lax.dot_general(left, right, (((0,), (0,)), ((), ())), preferred_element_type=F32)


def halves_of(pair):
    low = lax.broadcasted_iota(jnp.int32, pair.shape, 1) < pair.shape[1] // 2
    zero = jnp.zeros_like(pair)
    return jnp.where(low, pair, zero), jnp.where(low, zero, pair)


def softmax_rows(scores):
    expo = jnp.exp(scores - jnp.max(scores, axis=-1, keepdims=True))
    return expo * (1.0 / jnp.sum(expo, axis=-1, keepdims=True))


def attend_pair(query, keys, values, bias):
    outs = []
    for part in halves_of(query):
        scores = matmul_nt(part, keys) * 0.125
        if bias is not None:
            scores = scores + bias
        outs.append(matmul(softmax_rows(scores).astype(BF), values))
    low = lax.broadcasted_iota(jnp.int32, outs[0].shape, 1) < outs[0].shape[1] // 2
    return jnp.where(low, outs[0], outs[1]).astype(BF)


def gain_table(tiles, own):
    rows = tiles.shape[0]
    filled = own // 48
    r = lax.broadcasted_iota(jnp.int32, (rows, D), 0)
    c = lax.broadcasted_iota(jnp.int32, (rows, D), 1)
    spread = (lax.broadcasted_iota(jnp.int32, (128, D), 0) == lax.broadcasted_iota(jnp.int32, (128, D), 1) % 48)
    wide = matmul(tiles.astype(BF), spread.astype(BF))
    flat = (r // 8) * filled + r % 8
    wide = jnp.where((r % 8 < filled) & (c // 48 == flat % 16), wide, 0.0).astype(BF)
    rr = lax.broadcasted_iota(jnp.int32, (16, rows), 1)
    vv = lax.broadcasted_iota(jnp.int32, (16, rows), 0)
    pick = (rr % 8 < filled) & (((rr // 8) * filled + rr % 8) // 16 == vv)
    return matmul(pick.astype(BF), wide)


class Weights:
    def __init__(self, dims, slabs, wholes, ring, sems, blocks):
        self.dims, self.slabs, self.wholes, self.ring, self.sems, self.blocks = dims, slabs, wholes, ring, sems, blocks
        self.depth = ring.shape[0]
        self.loading = {}
        self.next_load = 0
        self.next_use = 0
        self.ready = set()

    def fetch(self):
        while self.next_load < min(len(self.blocks), self.next_use + self.depth):
            i = self.next_load
            a, row, block = self.blocks[i]
            if a not in self.ready:
                return
            slot = i % self.depth
            copies = []
            at, end = row, row + D
            slab = self.slabs[a][0]
            while at < end:
                chip, off = at // slab, at % slab
                n = min(end - at, slab - off)
                p, q, z = chip // (self.dims[1] * self.dims[2]), chip // self.dims[2] % self.dims[1], chip % self.dims[2]
                copies.append(
                    pltpu.make_async_copy(
                        self.wholes[a].at[p, q, z, pl.ds(off, n), pl.ds(block * D, D)],
                        self.ring.at[slot, pl.ds(at - row, n)],
                        self.sems.at[slot, len(copies)],
                    )
                )
                at += n
            for one in copies:
                one.start()
            self.loading[i] = copies
            self.next_load += 1

    def take(self, expected):
        i = self.next_use
        assert self.blocks[i] == expected, (self.blocks[i], expected)
        self.fetch()
        for one in self.loading.pop(i):
            one.wait()
        return self.ring.at[i % self.depth]

    def give_back(self):
        self.next_use += 1
        self.fetch()


def forward_blocks():
    blocks = [(0, (9 + i) * D, 0) for i in range(6)]
    blocks += [(1, 3 * D, 0), (1, 4 * D, 0)]
    blocks += [(0, i * D, 0) for i in range(9)]
    blocks += [(1, i * D, 0) for i in range(3)]
    blocks += [(2, v * D, j) for v in range(3) for j in range(FF // D)]
    blocks += [(3, v * FF + j * D, 0) for v in range(3) for j in range(FF // D)]
    return blocks


KEPT = ("first", "second", "cq", "ck", "cv", "cmixed", "joined", "normed", "q", "kx", "vx", "mixed", "middle", "normed_two", "hidden", "active")


def forward_shapes(rows):
    u = rows // 7
    sizes = dict(
        first=(6 * u, D), second=(3 * u, D), cq=(6 * u, D), ck=(3 * u, D), cv=(3 * u, D), cmixed=(6 * u, D),
        joined=(rows, D), normed=(rows, D), q=(rows, D), kx=(rows + 6 * u, D), vx=(rows + 6 * u, D),
        mixed=(rows, D), middle=(rows, D), normed_two=(rows, D), hidden=(rows, FF), active=(rows, FF),
    )
    return {k: (sizes[k], F32 if k in ("joined", "middle", "hidden") else BF) for k in KEPT}


def halo_device(place, count, step):
    t = jnp.clip(place.slab + step, 0, count - 1)
    return (place.at[0] * place.dims[1] + place.at[1], t)


def slab_bias(place, count, width, spatial):
    col = lax.broadcasted_iota(jnp.int32, (1, width), 1)
    below = (col < spatial) & (place.slab == 0)
    above = (col >= width - spatial) & (place.slab == count - 1)
    return jnp.where(below | above, FAR, 0.0).astype(F32)


def forward_work(place, copies, weights, need, gain, x, layer, v, save):
    u = x.shape[0] // 7
    count = 2 * place.dims[2]
    spans = ((0, 4 * u), (4 * u, 2 * u), (6 * u, u))
    bases = (0, 6 * u, 10 * u)
    yield need("gain")
    for c in range(2):
        r0, n = spans[c]
        k0, m = spans[c + 1]
        rows, keys = pl.ds(r0, n), pl.ds(k0 - 4 * u, m)
        g = lambda j: gain[pl.ds(2 * (3 + c) + j, 1), :]
        v["first"][rows] = norm_rows(x[rows], g(0)).astype(BF)
        v["second"][keys] = norm_rows(x[pl.ds(k0, m)], g(1)).astype(BF)
        yield 0.5
    save("first")
    save("second")
    yield need(0)
    for c in range(2):
        r0, n = spans[c]
        k0, m = spans[c + 1]
        rows, keys = pl.ds(r0, n), pl.ds(k0 - 4 * u, m)
        for j, (src, dst, part) in enumerate((("first", "cq", rows), ("second", "ck", keys), ("second", "cv", keys))):
            w = weights.take((0, (9 + 3 * c + j) * D, 0))
            v[dst][part] = matmul(v[src][part], w[...]).astype(BF)
            weights.give_back()
            yield 0.8
        for h in range(HEADS // 2):
            cols = pl.ds(h * 128, 128)
            v["cmixed"][rows, cols] = attend_pair(v["cq"][rows, cols], v["ck"][keys, cols], v["cv"][keys, cols], None)
            yield 0.8 if c == 0 else 0.3
    for name in ("cq", "ck", "cv", "cmixed"):
        save(name)
    yield need(1)
    for c in range(2):
        rows = pl.ds(*spans[c])
        w = weights.take((1, (3 + c) * D, 0))
        v["joined"][rows] = x[rows] + matmul(v["cmixed"][rows], w[...])
        weights.give_back()
        yield 0.8
    v["joined"][pl.ds(*spans[2])] = x[pl.ds(*spans[2])]
    save("joined")
    for name in ("kx", "vx"):
        for view in range(3):
            base, n = bases[view], spans[view][1]

            @pl.when(place.slab == 0)
            def _():
                v[name][pl.ds(base, u)] = jnp.zeros((u, D), BF)

            @pl.when(place.slab == count - 1)
            def _():
                v[name][pl.ds(base + u + n, u)] = jnp.zeros((u, D), BF)

    halo = {0: [], 1: [], 2: []}
    for view in range(3):
        r0, n = spans[view]
        rows = pl.ds(r0, n)
        base = bases[view]
        v["normed"][rows] = norm_rows(v["joined"][rows], gain[pl.ds(2 * view, 1), :]).astype(BF)
        for j, (dst, part) in enumerate((("q", rows), ("kx", pl.ds(base + u, n)), ("vx", pl.ds(base + u, n)))):
            w = weights.take((0, (3 * view + j) * D, 0))
            v[dst][part] = matmul(v["normed"][rows], w[...]).astype(BF)
            weights.give_back()
            if j > 0:
                ref = v[dst]
                up, down = place.slab < count - 1, place.slab > 0
                halo[view].append(
                    (copies.start(ref.at[pl.ds(base + n, u)], ref.at[pl.ds(base, u)], halo_device(place, count, 1), up), down)
                )
                halo[view].append(
                    (
                        copies.start(
                            ref.at[pl.ds(base + u, u)], ref.at[pl.ds(base + u + n, u)], halo_device(place, count, -1), down
                        ),
                        up,
                    )
                )
            yield 0.8
    save("normed")
    save("q")
    for view in range(3):
        r0, n = spans[view]
        rows, keys = pl.ds(r0, n), pl.ds(bases[view], n + 2 * u)
        for one, ok in halo[view]:
            when(ok, one.wait_recv)
        bias = slab_bias(place, count, n + 2 * u, u)
        for h in range(HEADS // 2):
            cols = pl.ds(h * 128, 128)
            v["mixed"][rows, cols] = attend_pair(v["q"][rows, cols], v["kx"][keys, cols], v["vx"][keys, cols], bias)
            yield (1.4, 0.6, 0.3)[view]
        w = weights_later = None
    save("kx")
    save("vx")
    save("mixed")
    for view in range(3):
        rows = pl.ds(*spans[view])
        w = weights.take((1, view * D, 0))
        v["middle"][rows] = v["joined"][rows] + matmul(v["mixed"][rows], w[...])
        weights.give_back()
        v["normed_two"][rows] = norm_rows(v["middle"][rows], gain[pl.ds(2 * view + 1, 1), :]).astype(BF)
        yield 1.0
    save("middle")
    save("normed_two")
    yield need(2)
    for view in range(3):
        rows = pl.ds(*spans[view])
        for j in range(FF // D):
            cols = pl.ds(j * D, D)
            w = weights.take((2, view * D, j))
            pre = matmul(v["normed_two"][rows], w[...])
            weights.give_back()
            v["hidden"][rows, cols] = pre
            v["active"][rows, cols] = (0.5 * pre * (1.0 + lax.erf(pre * (0.5**0.5)))).astype(BF)
            yield 1.2
    save("hidden")
    save("active")
    yield need(3)
    for view in range(3):
        rows = pl.ds(*spans[view])
        for j in range(FF // D):
            w = weights.take((3, view * FF + j * D, 0))
            term = matmul(v["active"][rows, pl.ds(j * D, D)], w[...])
            weights.give_back()
            layer[rows] = (v["middle"][rows] if j == 0 else layer[rows]) + term
            yield 0.8
    save("layer")


def gather_kernel(dims, own_gains, *refs):
    refs = list(refs)
    take = lambda n: [refs.pop(0) for _ in range(n)]
    shards = take(4)
    gain_tile, x = take(2)
    fulls = take(4)
    gain_out, layer_out = take(2)
    kept_out = dict(zip(KEPT, take(len(KEPT))))
    theirs, merged = take(4), take(4)
    gain_all, gain, layer = take(3)
    v = dict(zip(KEPT, take(len(KEPT))))
    ring, send, recv, local, ring_sem, save_sem = take(6)
    place = Place(dims)
    copies = Copies(send, recv)
    core = place.core
    at = place.at
    meet(place)
    width = [s.shape[1] // 2 for s in shards]
    mine = [pl.ds(pl.multiple_of(core * w, 128), w) for w in width]
    other = [pl.ds(pl.multiple_of((1 - core) * w, 128), w) for w in width]
    swaps = []
    for a in range(4):
        swaps.append(copies.start(shards[a].at[:, other[a]], theirs[a], place.sibling()))
    own_tile = gain_all.at[at[0], at[1], at[2], core]
    own_tile[...] = gain_tile[...]
    swap_gain = copies.start(own_tile, own_tile, place.sibling())
    slabs = [(m.shape[0], 2 * m.shape[1]) for m in merged]
    sets = pieces_of(slabs, range(4))
    left = {a: sum(1 for s in sets for piece in s if piece[0] == a) for a in range(4)}
    pair = {a: [] for a in range(4)}
    ready = set()
    state = {"gain": False}

    def prepare(a):
        swaps[a].wait_recv()
        w = width[a]
        own = jnp.where(core == 0, shards[a][:, :w].astype(F32), shards[a][:, w:].astype(F32))
        got = theirs[a][...].astype(F32)
        upper = jnp.where(core == 0, own, got)
        lower = jnp.where(core == 0, got, own)
        merged[a][...] = jnp.concatenate([upper, lower], axis=0).astype(BF)
        copy = pltpu.make_async_copy(merged[a], fulls[a].at[at[0], at[1], at[2], :, mine[a]], local.at[a])
        copy.start()
        copy.wait()

    def begin(piece):
        a, row, block, order = piece
        if a not in ready:
            prepare(a)
            ready.add(a)
        cols = pl.ds(pl.multiple_of(core * width[a] + block * BLOCK, 128), BLOCK)
        yield from gather_piece(copies, place, fulls[a], (row, ROWS), cols, order, pair[a])
        left[a] -= 1

    def gains():
        swap_gain.wait_recv()
        done = set()
        for dim in ZXY:

            def pick(value):
                index = [slice(None) if d in done else at[d] for d in range(3)]
                index[dim] = value
                return gain_all.at[tuple(index)]

            yield from gather_line(copies, place, dim, pick)
            done.add(dim)
        gain[...] = gain_table(gain_all[...].reshape(-1, 128), own_gains)
        copy = pltpu.make_async_copy(gain, gain_out, local.at[4])
        copy.start()
        copy.wait()
        state["gain"] = True

    weights = Weights(dims, slabs, fulls, ring, ring_sem, forward_blocks())

    def need(what):
        def gate():
            if what == "gain":
                return state["gain"]
            if left[what]:
                return False
            if what not in weights.ready:
                for copy in pair[what]:
                    copy.wait_recv()
                weights.ready.add(what)
                weights.fetch()
            return True

        return gate

    saves = []

    def save(name):
        src, dst = (layer, layer_out) if name == "layer" else (v[name], kept_out[name])
        copy = pltpu.make_async_copy(src, dst, save_sem.at[len(saves)])
        copy.start()
        saves.append(copy)

    work = forward_work(place, copies, weights, need, gain, x, layer, v, save)
    weave(march(sets, begin, (gains(),)), work, 0.8)
    for copy in saves:
        copy.wait()
    copies.drain()


def gather_all(dims, own_gains, shards, tile, x):
    slabs = [(2 * s.shape[0], s.shape[1]) for s in shards]
    anywhere = pl.BlockSpec(memory_space=pl.ANY)
    vmem = pl.BlockSpec(memory_space=pltpu.VMEM)
    kept = forward_shapes(x.shape[0])
    segments = max(D // s[0] + 2 for s in slabs)
    outs = pl.pallas_call(
        functools.partial(gather_kernel, dims, own_gains),
        out_shape=[jax.ShapeDtypeStruct((*dims, *s), BF) for s in slabs]
        + [jax.ShapeDtypeStruct((16, D), F32), jax.ShapeDtypeStruct(x.shape, F32)]
        + [jax.ShapeDtypeStruct(*kept[k]) for k in KEPT],
        in_specs=[vmem] * 6,
        out_specs=[anywhere] * (6 + len(KEPT)),
        scratch_shapes=[pltpu.VMEM((r // 2, w // 2), BF) for r, w in slabs]
        + [pltpu.VMEM((r, w // 2), BF) for r, w in slabs]
        + [pltpu.VMEM((*dims, 2, 8, 128), F32), pltpu.VMEM((16, D), F32), pltpu.VMEM(x.shape, F32)]
        + [pltpu.VMEM(*kept[k]) for k in KEPT]
        + [
            pltpu.VMEM((4, D, D), BF),
            pltpu.SemaphoreType.DMA((COPIES,)),
            pltpu.SemaphoreType.DMA((COPIES,)),
            pltpu.SemaphoreType.DMA((5,)),
            pltpu.SemaphoreType.DMA((4, segments)),
            pltpu.SemaphoreType.DMA((1 + len(KEPT),)),
        ],
        compiler_params=pltpu.CompilerParams(collective_id=0, has_side_effects=True, vmem_limit_bytes=60 << 20),
    )(*shards, tile, x)
    return outs[:4], outs[4], outs[5], dict(zip(KEPT, outs[6:]))


class Stream:
    def __init__(self, depth, sems, makers):
        self.depth, self.sems, self.makers = depth, sems, makers
        self.loading = {}
        self.next_load = 0
        self.next_use = 0
        self.fetch()

    def fetch(self):
        while self.next_load < min(len(self.makers), self.next_use + self.depth):
            slot = self.next_load % self.depth
            copies = [
                pltpu.make_async_copy(src, dst, self.sems.at[slot, j])
                for j, (src, dst) in enumerate(self.makers[self.next_load](slot))
            ]
            for one in copies:
                one.start()
            self.loading[self.next_load] = copies
            self.next_load += 1

    def take(self):
        for one in self.loading.pop(self.next_use):
            one.wait()
        return self.next_use % self.depth

    def give_back(self):
        self.next_use += 1
        self.fetch()


def row_runs(dims, slab, row, count):
    at, end = row, row + count
    while at < end:
        chip, off = at // slab, at % slab
        n = min(end - at, slab - off)
        yield chip // (dims[1] * dims[2]), chip // dims[2] % dims[1], chip % dims[2], off, n, at - row
        at += n


def add_to(total, term):
    total[...] = (total[...].astype(F32) + term[...].astype(F32)).astype(total.dtype)


class Credits:
    def __init__(self, sems, waits, gives):
        self.sems, self.waits, self.gives = sems, waits, gives

    def wait(self, index, ok=None):
        if self.waits:
            when(ok, lambda: pl.semaphore_wait(self.sems.at[index], 1))

    def give(self, index, device):
        if self.gives:
            pl.semaphore_signal(self.sems.at[index], inc=1, device_id=device, device_id_type=MESH)


def reduce_line(copies, place, pick, slots, credits):
    n = place.dims[2]
    z = place.at[2]
    before = {}
    for turn in range(n):
        for step in (1, -1):
            far = z if step == 1 else n - 1 - z
            goal = far + n - 1 - turn
            goal = jnp.minimum(goal if step == 1 else n - 1 - goal, n - 1)
            goal = jnp.maximum(goal, 0)
            if turn > 0:

                def take(step=step, turn=turn, goal=goal):
                    before[step].wait_recv()
                    add_to(pick(goal), slots(turn - 1, step))
                    credits.give(2 + 2 * (turn - 1) + (1 - step) // 2, place.along(2, jnp.clip(z - step, 0, n - 1)))

                when((far >= 1) & (far <= turn), take)
            if turn < n - 1:
                credits.wait(2 + 2 * turn + (1 - step) // 2, far <= turn)
                before[step] = copies.start(
                    pick(goal), slots(turn, step), place.along(2, jnp.clip(z + step, 0, n - 1)), far <= turn
                )
        if turn < n - 1:
            yield


def reduce_piece(copies, place, source, order, acc, first, turns, last, local, credits, finish):
    lead = order[0]
    rest = 1 - lead
    me, mine = place.at[lead], place.at[rest]
    z = place.at[2]
    beside, across = place.along(lead, 1 - me), place.along(rest, 1 - mine)
    credits.wait(0)
    copy = copies.start(source(lead, 1 - me), first, beside)
    load = pltpu.make_async_copy(source(lead, me), acc, local)
    load.start()
    yield
    load.wait()
    copy.wait_recv()
    add_to(acc, first)
    credits.give(0, beside)
    slots = lambda turn, step: turns.at[turn, (1 - step) // 2]
    if order[1] == 2:
        yield from reduce_line(copies, place, lambda v: acc.at[:, v], slots, credits)
        credits.wait(1)
        copy = copies.start(acc.at[1 - mine, z], last, across)
        yield
        copy.wait_recv()
        finish(acc[mine, z].astype(F32) + last[...].astype(F32))
        credits.give(1, across)
    else:
        credits.wait(1)
        copy = copies.start(acc.at[1 - mine], last, across)
        yield
        copy.wait_recv()
        add_to(acc.at[mine], last)
        credits.give(1, across)
        yield from reduce_line(copies, place, lambda v: acc.at[mine, v], slots, credits)
        finish(acc[mine, z].astype(F32))


def march_ready(sets, begin, ready, limit):
    waiting = list(sets)
    active = []
    step = 0
    started = 0
    while active or waiting:
        while (
            waiting
            and step >= LAG * started
            and len(active) + len(waiting[0]) <= limit
            and ready(waiting[0])
        ):
            for piece in waiting.pop(0):
                active.append(begin(piece))
            started += 1
        if not active:
            if step < LAG * started:
                step += 1
            else:
                yield lambda: ready(waiting[0])
            continue
        still = []
        for one in active:
            try:
                yield next(one)
                still.append(one)
            except StopIteration:
                pass
        active = still
        step += 1


LEFTS = ("active", "normed_two", "mixed", "normed", "first", "second", "cmixed")
RIGHTS = ("d_out", "d_pre", "d_attn", "dq", "dk", "dv", "d_cross", "dcq", "dck", "dcv")
HELD = ("q", "kx", "vx", "cq", "ck", "cv")


def right_shapes(rows):
    u = rows // 7
    tall = dict(d_cross=6 * u, dcq=6 * u, dck=3 * u, dcv=3 * u)
    return [(tall.get(k, rows), FF if k == "d_pre" else D) for k in RIGHTS]


def job_batches(u):
    rows = ((0, 4 * u), (4 * u, 2 * u), (6 * u, u))
    late = ((0, 2 * u), (2 * u, u))
    batches = {"down": [], "up": [], "out": [], "qkv": [], "cout": [], "cqkv": []}
    for view in range(3):
        for block in range(FF // D):
            batches["down"].append((3, view * FF + block * D, 0, "active", block, rows[view], "d_out", rows[view]))
        for block in range(FF // 2 // BLOCK):
            batches["up"].append((2, view * D, block, "normed_two", 0, rows[view], "d_pre", rows[view]))
        batches["out"].append((1, view * D, 0, "mixed", 0, rows[view], "d_attn", rows[view]))
        for j, name in enumerate(("dq", "dk", "dv")):
            batches["qkv"].append((0, (3 * view + j) * D, 0, "normed", 0, rows[view], name, rows[view]))
    for c in range(2):
        batches["cout"].append((1, (3 + c) * D, 0, "cmixed", 0, rows[c], "d_cross", rows[c]))
        batches["cqkv"].append((0, (9 + 3 * c) * D, 0, "first", 0, rows[c], "dcq", rows[c]))
        for j, name in enumerate(("dck", "dcv")):
            batches["cqkv"].append((0, (10 + 3 * c + j) * D, 0, "second", 0, late[c], name, late[c]))
    return batches


def backward_blocks():
    blocks = []
    for view in range(3):
        for j in range(FF // D):
            blocks += [(3, view * FF + j * D, 0), (2, view * D, j)]
    blocks += [(1, view * D, 0) for view in range(3)]
    blocks += [(0, i * D, 0) for i in range(9)]
    for c in range(2):
        blocks += [(1, (3 + c) * D, 0)] + [(0, (9 + 3 * c + j) * D, 0) for j in range(3)]
    return blocks


def norm_pull(x, gain, grad):
    centered = x - jnp.mean(x, axis=-1, keepdims=True)
    scale = lax.rsqrt(jnp.mean(centered * centered, axis=-1, keepdims=True) + EPS)
    unit = centered * scale
    inner = grad * gain
    pulled = scale * (
        inner - jnp.mean(inner, axis=-1, keepdims=True) - unit * jnp.mean(inner * unit, axis=-1, keepdims=True)
    )
    return pulled, jnp.sum(grad * unit, axis=0, keepdims=True)


def gelu_slope(pre):
    return 0.5 * (1.0 + lax.erf(pre * (0.5**0.5))) + pre * jnp.exp(-0.5 * pre * pre) * 0.3989422804014327


def attend_pair_back(query, keys, values, grad, bias):
    dq, dk, dv = [], None, None
    for part, g in zip(halves_of(query), halves_of(grad)):
        scores = matmul_nt(part, keys) * 0.125
        if bias is not None:
            scores = scores + bias
        probs = softmax_rows(scores)
        dprobs = matmul_nt(g, values)
        inner = jnp.sum(dprobs * probs, axis=-1, keepdims=True)
        dscores = (probs * (dprobs - inner) * 0.125).astype(BF)
        dq.append(matmul(dscores, keys))
        k_term = matmul_tn(dscores, part)
        v_term = matmul_tn(probs.astype(BF), g)
        dk = k_term if dk is None else dk + k_term
        dv = v_term if dv is None else dv + v_term
    low = lax.broadcasted_iota(jnp.int32, dq[0].shape, 1) < dq[0].shape[1] // 2
    return jnp.where(low, dq[0], dq[1]), dk, dv


def gain_tiles(table, rows, own):
    filled = own // 48
    r = lax.broadcasted_iota(jnp.int32, (rows, D), 0)
    c = lax.broadcasted_iota(jnp.int32, (rows, D), 1)
    flat = (r // 8) * filled + r % 8
    rr = lax.broadcasted_iota(jnp.int32, (rows, 16), 0)
    vv = lax.broadcasted_iota(jnp.int32, (rows, 16), 1)
    pick = (rr % 8 < filled) & (((rr // 8) * filled + rr % 8) // 16 == vv)
    wide = jnp.dot(pick.astype(F32), table, precision=lax.Precision.HIGHEST, preferred_element_type=F32)
    wide = jnp.where((r % 8 < filled) & (c // 48 == flat % 16), wide, 0.0)
    j = lax.broadcasted_iota(jnp.int32, (D, 128), 1)
    fold = (j < 48) & (j == lax.broadcasted_iota(jnp.int32, (D, 128), 0) % 48)
    return jnp.dot(wide, fold.astype(F32), precision=lax.Precision.HIGHEST, preferred_element_type=F32)


def reduce_kernel(dims, slabs, sets, own_gains, *refs):
    refs = list(refs)
    take = lambda n: [refs.pop(0) for _ in range(n)]
    wholes = take(4)
    (cot, gain, x, joined, middle, hidden) = take(6)
    lefts = dict(zip(LEFTS, take(7)))
    held_in = dict(zip(HELD, take(6)))
    token_out = take(1)[0]
    results = take(4)
    (gain_out,) = take(1)
    parts = take(4)
    far_lefts, far_rights = dict(zip(LEFTS, take(7))), dict(zip(RIGHTS, take(10)))
    rights = dict(zip(RIGHTS, take(10)))
    held = dict(zip(HELD, take(6)))
    acc, first, turns_a, turns_b, last_a, last_b = take(6)
    finals = take(4)
    xs, ys, made = take(3)
    g_far, g_own, g_acc, g_first, g_turns, g_last, g_sum = take(7)
    ring, rowring, preing, flow, total, dmixed, dkf, dvf, halo_out, halo_in = take(10)
    send, recv, local, load_sem, store_sem, final_sem, ring_sem, row_sem, pre_sem, held_sem, credit = take(11)
    place = Place(dims)
    core = place.core
    copies = Copies(send, recv)
    meet(place)
    rows_all = cot.shape[0]
    u = rows_all // 7
    spans = ((0, 4 * u), (4 * u, 2 * u), (6 * u, u))
    bases = (0, 6 * u, 10 * u)
    count = 2 * dims[2]
    half_of = lambda ref, c: pl.ds(pl.multiple_of(c * (ref.shape[1] // 2), 128), ref.shape[1] // 2)
    coming = {}

    def swap(name):
        if name in lefts:
            coming[name] = copies.start(lefts[name], far_lefts[name], place.sibling())
        else:
            ref = rights[name]
            coming[name] = copies.start(ref.at[:, half_of(ref, 1 - core)], far_rights[name], place.sibling())

    arrived = set()

    def arrive(name):
        if name not in arrived:
            coming[name].wait_recv()
            arrived.add(name)

    def weight_maker(block):
        a, row, col = block
        return lambda slot: [
            (wholes[a].at[p, q, z, pl.ds(off, n), pl.ds(col * D, D)], ring.at[slot, pl.ds(at, n)])
            for p, q, z, off, n, at in row_runs(dims, slabs[a][0], row, D)
        ]

    def row_maker(ref, r0, n):
        return lambda slot: [(ref.at[pl.ds(r0, n)], rowring.at[slot, pl.ds(0, n)])]

    def pre_maker(view, j):
        r0, n = spans[view]
        return lambda slot: [(hidden.at[pl.ds(r0, n), pl.ds(j * D, D)], preing.at[slot, pl.ds(0, n)])]

    swap("active")
    rights["d_out"][...] = cot[...].astype(BF)
    swap("d_out")
    blocks = backward_blocks()
    weights = Stream(ring.shape[0], ring_sem, [weight_maker(b) for b in blocks])
    pres = Stream(2, pre_sem, [pre_maker(view, j) for view in range(3) for j in range(FF // D)])
    row_list = [(middle, *spans[view]) for view in range(3)] + [(joined, *spans[view]) for view in range(3)]
    for c in range(2):
        row_list += [(x, *spans[c]), (x, *spans[c + 1])]
    rowed = Stream(2, row_sem, [row_maker(*one) for one in row_list])
    used_blocks = []

    def weight(expected):
        assert blocks[len(used_blocks)] == expected
        used_blocks.append(expected)
        return ring.at[weights.take()][...]

    holding = {}
    for i, name in enumerate(HELD):
        holding[name] = pltpu.make_async_copy(held_in[name], held[name], held_sem.at[i])
        holding[name].start()
    for name in LEFTS[1:]:
        swap(name)

    state = {"jobs": 0, "gain": False}
    ready = set()
    storing = {}

    def finish_stores(i):
        for one in storing.pop(i, ()):
            one.wait()

    def load(job, i):
        a, row, block, left, lcol, lrows, right, rrows = job
        arrive(left)
        arrive(right)
        slot = i % 2
        n = lrows[1]
        ref = rights[right]
        own = pl.ds(pl.multiple_of(core * (ref.shape[1] // 2) + block * BLOCK, 128), BLOCK)
        pairs = [
            (lefts[left].at[pl.ds(*lrows), pl.ds(lcol * D, D)], xs.at[slot, pl.ds(0, n)]),
            (far_lefts[left].at[pl.ds(*lrows), pl.ds(lcol * D, D)], xs.at[slot, pl.ds(n, n)]),
            (ref.at[pl.ds(*rrows), own], ys.at[slot, pl.ds(0, n)]),
            (far_rights[right].at[pl.ds(*rrows), pl.ds(block * BLOCK, BLOCK)], ys.at[slot, pl.ds(n, n)]),
        ]
        loads = [pltpu.make_async_copy(s, d, load_sem.at[slot, j]) for j, (s, d) in enumerate(pairs)]
        for one in loads:
            one.start()
        return loads

    batches = job_batches(u)

    def multiply(name, cost):
        batch = batches[name]
        loading = load(batch[0], state["jobs"])
        for index, job in enumerate(batch):
            i = state["jobs"]
            slot = i % 2
            for one in loading:
                one.wait()
            if index + 1 < len(batch):
                loading = load(batch[index + 1], i + 1)
            finish_stores(i - 2)
            n = 2 * job[5][1]
            made[slot] = matmul_tn(xs[slot, :n], ys[slot, :n]).astype(BF)
            a, row, block = job[:3]
            storing[i] = [
                pltpu.make_async_copy(
                    made.at[slot, pl.ds(at, n)],
                    parts[a].at[p, q, z, pl.ds(off, n), pl.ds(block * BLOCK, BLOCK)],
                    store_sem.at[slot, k],
                )
                for k, (p, q, z, off, n, at) in enumerate(row_runs(dims, slabs[a][0], row, D))
            ]
            for one in storing[i]:
                one.start()
            state["jobs"] += 1
            yield cost
        for i in list(storing):
            finish_stores(i)

    g = lambda e, j: gain[pl.ds(2 * e + j, 1), :]

    def work():
        for view in range(3):
            r0, n = spans[view]
            rows = pl.ds(r0, n)
            cost = (2.0, 1.2, 0.9)[view]
            for j in range(FF // D):
                cols = pl.ds(j * D, D)
                dactive = matmul_nt(rights["d_out"][rows], weight((3, view * FF + j * D, 0)))
                weights.give_back()
                slot = pres.take()
                rights["d_pre"][rows, cols] = (dactive * gelu_slope(preing[slot, :n])).astype(BF)
                pres.give_back()
                term = matmul_nt(rights["d_pre"][rows, cols], weight((2, view * D, j)))
                weights.give_back()
                total[:n] = term if j == 0 else total[:n] + term
                yield cost
            slot = rowed.take()
            pulled, g_sum[pl.ds(2 * view + 1, 1), :] = norm_pull(rowring[slot, :n], g(view, 1), total[:n])
            rowed.give_back()
            flow[rows] = cot[rows] + pulled
            rights["d_attn"][rows] = flow[rows].astype(BF)
            yield 0.8
            if view == 0:
                yield from multiply("down", 0.8)
                ready.add(3)
        swap("d_pre")
        swap("d_attn")
        for view in range(3):
            rows = pl.ds(*spans[view])
            dmixed[rows] = matmul_nt(rights["d_attn"][rows], weight((1, view * D, 0))).astype(BF)
            weights.give_back()
            yield 0.7
        yield from multiply("up", 0.8)
        ready.add(2)
        for name in ("q", "kx", "vx"):
            holding[name].wait()
        halo = {}
        up, down = place.slab < count - 1, place.slab > 0
        for view in range(3):
            r0, n = spans[view]
            rows, keys = pl.ds(r0, n), pl.ds(bases[view], n + 2 * u)
            bias = slab_bias(place, count, n + 2 * u, u)
            for h in range(HEADS // 2):
                cols = pl.ds(h * 128, 128)
                dq, dk, dv = attend_pair_back(
                    held["q"][rows, cols], held["kx"][keys, cols], held["vx"][keys, cols], dmixed[rows, cols], bias
                )
                rights["dq"][rows, cols] = dq.astype(BF)
                for k, (whole, own) in enumerate(((dk, dkf), (dv, dvf))):
                    halo_out[k, view, 0, :, cols] = whole[:u].astype(BF)
                    own[rows, cols] = whole[u : u + n]
                    halo_out[k, view, 1, :, cols] = whole[u + n :].astype(BF)
                yield (3.0, 1.3, 0.7)[view]
            for k in range(2):
                for side, step, ok in ((0, -1, down), (1, 1, up)):
                    halo[k, view, side] = copies.start(
                        halo_out.at[k, view, side], halo_in.at[k, view, side], halo_device(place, count, step), ok
                    )
        swap("dq")
        yield from multiply("out", 0.8)
        for view in range(3):
            r0, n = spans[view]
            rows = pl.ds(r0, n)
            for k, (own, name) in enumerate(((dkf, "dk"), (dvf, "dv"))):
                for side, edge, ok in ((0, r0 + n - u, up), (1, r0, down)):

                    def join(k=k, side=side, edge=edge, own=own):
                        halo[k, view, side].wait_recv()
                        own[pl.ds(edge, u)] = own[pl.ds(edge, u)] + halo_in[k, view, side].astype(F32)

                    when(ok, join)
                rights[name][rows] = own[rows].astype(BF)
            for j, name in enumerate(("dq", "dk", "dv")):
                term = matmul_nt(rights[name][rows], weight((0, (3 * view + j) * D, 0)))
                weights.give_back()
                total[:n] = term if j == 0 else total[:n] + term
                yield 0.7
            slot = rowed.take()
            pulled, g_sum[pl.ds(2 * view, 1), :] = norm_pull(rowring[slot, :n], g(view, 0), total[:n])
            rowed.give_back()
            flow[rows] = flow[rows] + pulled
            yield 0.6
        swap("dk")
        swap("dv")
        rights["d_cross"][...] = flow[pl.ds(0, 6 * u)].astype(BF)
        swap("d_cross")
        for name in ("cq", "ck", "cv"):
            holding[name].wait()
        yield from multiply("qkv", 0.8)
        for c in range(2):
            r0, n = spans[c]
            k0, m = spans[c + 1]
            rows, keys = pl.ds(r0, n), pl.ds(k0 - 4 * u, m)
            dmixed[rows] = matmul_nt(rights["d_cross"][rows], weight((1, (3 + c) * D, 0))).astype(BF)
            weights.give_back()
            yield 0.7
            for h in range(HEADS // 2):
                cols = pl.ds(h * 128, 128)
                dq, dk, dv = attend_pair_back(
                    held["cq"][rows, cols], held["ck"][keys, cols], held["cv"][keys, cols], dmixed[rows, cols], None
                )
                rights["dcq"][rows, cols] = dq.astype(BF)
                rights["dck"][keys, cols] = dk.astype(BF)
                rights["dcv"][keys, cols] = dv.astype(BF)
                yield (1.5, 0.6)[c]
            term = matmul_nt(rights["dcq"][rows], weight((0, (9 + 3 * c) * D, 0)))
            weights.give_back()
            slot = rowed.take()
            pulled, g_sum[pl.ds(2 * (3 + c), 1), :] = norm_pull(rowring[slot, :n], g(3 + c, 0), term)
            rowed.give_back()
            flow[rows] = flow[rows] + pulled
            yield 1.0
            term = matmul_nt(rights["dck"][keys], weight((0, (10 + 3 * c) * D, 0)))
            weights.give_back()
            term = term + matmul_nt(rights["dcv"][keys], weight((0, (11 + 3 * c) * D, 0)))
            weights.give_back()
            slot = rowed.take()
            pulled, g_sum[pl.ds(2 * (3 + c) + 1, 1), :] = norm_pull(rowring[slot, :m], g(3 + c, 1), term)
            rowed.give_back()
            late = pl.ds(k0, m)
            flow[late] = flow[late] + pulled
            yield 1.0
        for name in ("dcq", "dck", "dcv"):
            swap(name)
        yield from multiply("cout", 0.8)
        ready.add(1)
        token = pltpu.make_async_copy(flow, token_out, final_sem.at[4])
        token.start()
        g_sum[pl.ds(10, 6), :] = jnp.zeros((6, D), F32)
        g_own[...] = gain_tiles(g_sum[...], 2 * dims[0] * dims[1] * dims[2] * 8, own_gains).reshape(g_own.shape)
        coming["gain"] = copies.start(g_own, g_far, place.sibling())
        yield 1.0
        yield from multiply("cqkv", 0.8)
        ready.add(0)
        state["gain"] = True
        token.wait()

    flat = [piece for group in sets for piece in group if piece != "gain"]
    owners = {}
    kinds = [0 if piece[3][1] == 2 else 1 for piece in flat[:SLOTS]]
    left_in = {a: sum(1 for piece in flat if piece[0] == a) for a in range(4)}
    ending = []
    begun = {"n": 0}

    def gains():
        coming["gain"].wait_recv()
        add_to(g_far, g_own)
        source = lambda dim, value: g_far.at[(*[value if d == dim else slice(None) for d in range(3)], core)]

        def finish(value):
            g_first[0, 0] = value
            copy = pltpu.make_async_copy(g_first.at[0, 0], gain_out, final_sem.at[5])
            copy.start()
            copy.wait()

        yield from reduce_piece(
            copies, place, source, (0, 1, 2), g_acc, g_first, g_turns, g_last, local.at[SLOTS], Credits(None, False, False), finish
        )

    def begin(piece):
        if piece == "gain":
            return gains()
        a, row, block, order = piece
        i = begun["n"]
        begun["n"] += 1
        slot = i % SLOTS
        if i >= SLOTS:
            owners[i - SLOTS].drain()
        mine = Copies(send, recv)
        mine.used = COPIES - 9 * (len(flat) - i)
        owners[i] = mine
        cols = pl.ds(block * BLOCK, BLOCK)
        kind = kinds[slot]
        k = kinds[:slot].count(kind)
        turns, last = ((turns_a, last_a), (turns_b, last_b))[kind]

        def source(dim, value):
            index = [slice(None)] * 3
            index[dim] = value
            return parts[a].at[(*index, pl.ds(row, ROWS), cols)]

        def finish(value):
            finals[a][pl.ds(row, ROWS), cols] = value
            left_in[a] -= 1
            if left_in[a] == 0:
                deliver(a)

        credits = Credits(credit.at[slot], i >= SLOTS, i + SLOTS < len(flat))
        return reduce_piece(
            mine, place, source, order[::-1], acc.at[slot], first.at[slot], turns.at[k], last.at[k], local.at[slot], credits, finish
        )

    def deliver(a):
        rows, width = slabs[a][0] // 2, slabs[a][1] // 2
        cols = pl.ds(pl.multiple_of(core * width, 128), width)
        ending.append(
            copies.start(
                finals[a].at[pl.ds(pl.multiple_of((1 - core) * rows, 8), rows)], results[a].at[:, cols], place.sibling()
            )
        )
        keep = pltpu.make_async_copy(
            finals[a].at[pl.ds(pl.multiple_of(core * rows, 8), rows)], results[a].at[:, cols], final_sem.at[a]
        )
        keep.start()
        keep.wait()

    def set_ready(group):
        return state["gain"] if group[0] == "gain" else all(piece[0] in ready for piece in group)

    weave(march_ready(sets, begin, set_ready, SLOTS), work(), EACH)
    for one in ending:
        one.wait_recv()
    copies.drain()
    for one in owners.values():
        one.drain()
    assert copies.used <= COPIES - 9 * len(flat)


def reduce_all(dims, slabs, own_gains, wholes, cot, gain, x, kept):
    anywhere = pl.BlockSpec(memory_space=pl.ANY)
    vmem = pl.BlockSpec(memory_space=pltpu.VMEM)
    sets = pieces_of(slabs, (3, 2, 1, 0))
    flat = [piece for group in sets for piece in group]
    sets.insert(len(sets) - 3, ["gain"])
    kinds = [0 if piece[3][1] == 2 else 1 for piece in flat[:SLOTS]]
    bundled, single = kinds.count(0), kinds.count(1)
    z = dims[2]
    rows = cot.shape[0]
    u = rows // 7
    tile = (ROWS, BLOCK)
    segments = max(D // slab[0] + 2 for slab in slabs)
    lefts = [kept[k] for k in LEFTS]
    held = [kept[k] for k in HELD]
    rights = right_shapes(rows)
    outs = pl.pallas_call(
        functools.partial(reduce_kernel, dims, slabs, sets, own_gains),
        out_shape=[jax.ShapeDtypeStruct((rows, D), F32)]
        + [jax.ShapeDtypeStruct((s[0] // 2, s[1]), F32) for s in slabs]
        + [jax.ShapeDtypeStruct((8, 128), F32)]
        + [jax.ShapeDtypeStruct((*dims, s[0], s[1] // 2), BF) for s in slabs]
        + [jax.ShapeDtypeStruct(one.shape, BF) for one in lefts]
        + [jax.ShapeDtypeStruct((r, w // 2), BF) for r, w in rights],
        in_specs=[anywhere] * 4 + [vmem] * 2 + [anywhere] * 17,
        out_specs=[anywhere] * 27,
        scratch_shapes=[pltpu.VMEM(s, BF) for s in rights]
        + [pltpu.VMEM(one.shape, BF) for one in held]
        + [
            pltpu.VMEM((SLOTS, 2, z, *tile), BF),
            pltpu.VMEM((SLOTS, 2, z, *tile), BF),
            pltpu.VMEM((bundled, z - 1, 2, 2, *tile), BF),
            pltpu.VMEM((single, z - 1, 2, *tile), BF),
            pltpu.VMEM((bundled, *tile), BF),
            pltpu.VMEM((single, z, *tile), BF),
        ]
        + [pltpu.VMEM((s[0], s[1] // 2), F32) for s in slabs]
        + [
            pltpu.VMEM((2, 8 * u, D), BF),
            pltpu.VMEM((2, 8 * u, BLOCK), BF),
            pltpu.VMEM((2, D, BLOCK), BF),
            pltpu.VMEM((*dims, 2, 8, 128), F32),
            pltpu.VMEM((*dims, 2, 8, 128), F32),
            pltpu.VMEM((2, z, 8, 128), F32),
            pltpu.VMEM((2, z, 8, 128), F32),
            pltpu.VMEM((z - 1, 2, 8, 128), F32),
            pltpu.VMEM((z, 8, 128), F32),
            pltpu.VMEM((16, D), F32),
            pltpu.VMEM((4, D, D), BF),
            pltpu.VMEM((2, 4 * u, D), F32),
            pltpu.VMEM((2, 4 * u, D), F32),
            pltpu.VMEM((rows, D), F32),
            pltpu.VMEM((4 * u, D), F32),
            pltpu.VMEM((rows, D), BF),
            pltpu.VMEM((rows, D), F32),
            pltpu.VMEM((rows, D), F32),
            pltpu.VMEM((2, 3, 2, u, D), BF),
            pltpu.VMEM((2, 3, 2, u, D), BF),
            pltpu.SemaphoreType.DMA((COPIES,)),
            pltpu.SemaphoreType.DMA((COPIES,)),
            pltpu.SemaphoreType.DMA((SLOTS + 1,)),
            pltpu.SemaphoreType.DMA((2, 4)),
            pltpu.SemaphoreType.DMA((2, segments)),
            pltpu.SemaphoreType.DMA((6,)),
            pltpu.SemaphoreType.DMA((4, segments)),
            pltpu.SemaphoreType.DMA((2, 1)),
            pltpu.SemaphoreType.DMA((2, 1)),
            pltpu.SemaphoreType.DMA((6,)),
            pltpu.SemaphoreType.REGULAR((SLOTS, 2 + 2 * (z - 1))),
        ],
        compiler_params=pltpu.CompilerParams(collective_id=1, has_side_effects=True, vmem_limit_bytes=62 << 20),
    )(*wholes, cot, gain, x, kept["joined"], kept["middle"], kept["hidden"], *lefts, *held)
    return outs[:6]


def plain_device(tokens, cotangent, qkv_weights, out_weights, up_weights, down_weights, gains):
    rows = tokens[0]
    incoming = cotangent[0]
    spatial = rows.shape[0] // 7
    bounds = ((0, 4 * spatial), (4 * spatial, 6 * spatial), (6 * spatial, 7 * spatial))
    qkv, outw, upw, downw, gain_low = unstack(
        (
            lax.all_gather(qkv_weights, ("seq", "tm"), axis=0, tiled=True),
            lax.all_gather(out_weights, ("seq", "tm"), axis=0, tiled=True),
            lax.all_gather(up_weights, ("seq", "tm"), axis=0, tiled=True),
            lax.all_gather(down_weights, ("seq", "tm"), axis=0, tiled=True),
            lax.all_gather(gains, ("seq", "tm"), axis=0, tiled=True),
        )
    )
    gain = gain_low.astype(jnp.float32)
    place = lax.axis_index("tm")
    count = lax.axis_size("tm")
    below_bias = jnp.where(place > 0, 0.0, FAR).astype(jnp.float32)
    above_bias = jnp.where(place < count - 1, 0.0, FAR).astype(jnp.float32)
    views = [rows[start:stop] for start, stop in bounds]
    cross_keep = []
    joined = []
    for view in range(2):
        first = lowered(norm_rows(views[view], gain[3 + view, 0]))
        second = lowered(norm_rows(views[view + 1], gain[3 + view, 1]))
        query = lowered(product(first, qkv[3 + view, 0]))
        keys = lowered(product(second, qkv[3 + view, 1]))
        values = lowered(product(second, qkv[3 + view, 2]))
        mixed, probs = attend(query, keys, values, 0.0)
        joined.append(views[view] + product(mixed, outw[3 + view]))
        cross_keep.append((first, second, query, keys, values, mixed, probs))
    joined.append(views[2])
    local_keep = []
    edges = []
    for view in range(3):
        normed = lowered(norm_rows(joined[view], gain[view, 0]))
        query = lowered(product(normed, qkv[view, 0]))
        keys = lowered(product(normed, qkv[view, 1]))
        values = lowered(product(normed, qkv[view, 2]))
        local_keep.append((normed, query, keys, values))
        paired = jnp.stack([keys, values])
        edges.append(jnp.concatenate([paired[:, :spatial], paired[:, -spatial:]], axis=1))
    rim = extended(jnp.stack(edges, axis=1), (("tm", 2),), spatial)
    self_keep = []
    outputs = []
    for view in range(3):
        normed, query, keys, values = local_keep[view]
        length = keys.shape[0]
        keys_all = jnp.concatenate(
            [rim[0, view, :spatial], keys, rim[0, view, 3 * spatial :]], axis=0
        )
        values_all = jnp.concatenate(
            [rim[1, view, :spatial], values, rim[1, view, 3 * spatial :]], axis=0
        )
        bias = jnp.concatenate(
            [
                jnp.broadcast_to(below_bias, (spatial,)),
                jnp.zeros((length,), jnp.float32),
                jnp.broadcast_to(above_bias, (spatial,)),
            ]
        )
        mixed, probs = attend(query, keys_all, values_all, bias)
        middle = joined[view] + product(mixed, outw[view])
        normed_two = lowered(norm_rows(middle, gain[view, 1]))
        hidden_pre = product(normed_two, upw[view])
        active = lowered(jax.nn.gelu(hidden_pre, approximate=False))
        outputs.append(middle + product(active, downw[view]))
        self_keep.append(
            (
                normed,
                query,
                keys_all,
                values_all,
                mixed,
                probs,
                middle,
                normed_two,
                hidden_pre,
                active,
            )
        )
    layer_out = jnp.concatenate(outputs, axis=0)[None]
    qkv, outw, upw, downw, gain_low = unstack(
        (
            lax.all_gather(qkv_weights, ("seq", "tm"), axis=0, tiled=True),
            lax.all_gather(out_weights, ("seq", "tm"), axis=0, tiled=True),
            lax.all_gather(up_weights, ("seq", "tm"), axis=0, tiled=True),
            lax.all_gather(down_weights, ("seq", "tm"), axis=0, tiled=True),
            lax.all_gather(gains, ("seq", "tm"), axis=0, tiled=True),
        )
    )
    grad_qkv = [[None, None, None] for index in range(5)]
    grad_out = [None] * 5
    grad_up = [None] * 3
    grad_down = [None] * 3
    grad_gain = [[None, None] for index in range(5)]
    halves = []
    for view in range(3):
        (
            normed,
            query,
            keys_all,
            values_all,
            mixed,
            probs,
            middle,
            normed_two,
            hidden_pre,
            active,
        ) = self_keep[view]
        start, stop = bounds[view]
        dfinal = incoming[start:stop]
        dbranch = lowered(dfinal)
        grad_down[view] = product_tn(active, dbranch)
        dactive = product_nt(dbranch, downw[view])
        dpre_low = lowered(gelu_back(hidden_pre, dactive))
        grad_up[view] = product_tn(normed_two, dpre_low)
        dnormed_two = product_nt(dpre_low, upw[view])
        dmid_norm, grad_gain[view][1] = norm_back(middle, gain[view, 1], dnormed_two)
        dmiddle = dfinal + dmid_norm
        dattn = lowered(dmiddle)
        grad_out[view] = product_tn(mixed, dattn)
        dmixed = lowered(product_nt(dattn, outw[view]))
        dquery, dkeys, dvalues = attend_back(query, keys_all, values_all, probs, dmixed)
        halves.append((dmiddle, dquery, dkeys, dvalues))
    lower_part = jnp.stack(
        [jnp.stack([half[2][:spatial], half[3][:spatial]]) for half in halves], axis=1
    )
    upper_part = jnp.stack(
        [jnp.stack([half[2][-spatial:], half[3][-spatial:]]) for half in halves], axis=1
    )
    from_above = from_behind(lower_part.astype(jnp.bfloat16), "tm", -1).astype(lower_part.dtype)
    from_below = from_behind(upper_part.astype(jnp.bfloat16), "tm", 1).astype(upper_part.dtype)
    dfused = []
    for view in range(3):
        dmiddle, dquery, dkeys, dvalues = halves[view]
        normed = self_keep[view][0]
        length = dquery.shape[0]
        own_keys = dkeys[spatial : spatial + length]
        own_values = dvalues[spatial : spatial + length]
        own_keys = (
            own_keys.at[:spatial]
            .add(from_below[0, view])
            .at[length - spatial :]
            .add(from_above[0, view])
        )
        own_values = (
            own_values.at[:spatial]
            .add(from_below[1, view])
            .at[length - spatial :]
            .add(from_above[1, view])
        )
        dq_low = lowered(dquery)
        dk_low = lowered(own_keys)
        dv_low = lowered(own_values)
        grad_qkv[view] = [
            product_tn(normed, dq_low),
            product_tn(normed, dk_low),
            product_tn(normed, dv_low),
        ]
        dnormed = (
            product_nt(dq_low, qkv[view, 0])
            + product_nt(dk_low, qkv[view, 1])
            + product_nt(dv_low, qkv[view, 2])
        )
        dfused_norm, grad_gain[view][0] = norm_back(joined[view], gain[view, 0], dnormed)
        dfused.append(dmiddle + dfused_norm)
    dviews = list(dfused)
    for view in range(2):
        first, second, query, keys, values, mixed, probs = cross_keep[view]
        dbranch = lowered(dfused[view])
        grad_out[3 + view] = product_tn(mixed, dbranch)
        dmixed = lowered(product_nt(dbranch, outw[3 + view]))
        dquery, dkeys, dvalues = attend_back(query, keys, values, probs, dmixed)
        dq_low = lowered(dquery)
        dk_low = lowered(dkeys)
        dv_low = lowered(dvalues)
        grad_qkv[3 + view] = [
            product_tn(first, dq_low),
            product_tn(second, dk_low),
            product_tn(second, dv_low),
        ]
        dfirst = product_nt(dq_low, qkv[3 + view, 0])
        dsecond = product_nt(dk_low, qkv[3 + view, 1]) + product_nt(dv_low, qkv[3 + view, 2])
        dx_first, grad_gain[3 + view][0] = norm_back(views[view], gain[3 + view, 0], dfirst)
        dx_second, grad_gain[3 + view][1] = norm_back(views[view + 1], gain[3 + view, 1], dsecond)
        dviews[view] = dviews[view] + dx_first
        dviews[view + 1] = dviews[view + 1] + dx_second
    token_grad = jnp.concatenate(dviews, axis=0)[None]
    qkv_total = jnp.stack([jnp.stack(entry) for entry in grad_qkv]).reshape(15 * D, D)
    out_total = jnp.stack(grad_out).reshape(5 * D, D)
    gain_total = jnp.stack([jnp.stack(entry) for entry in grad_gain]).reshape(10 * D)
    totals = (
        qkv_total,
        out_total,
        jnp.stack(grad_up).reshape(3 * D, FF),
        jnp.stack(grad_down).reshape(3 * FF, D),
        gain_total,
    )
    shares = (
        lax.psum_scatter(totals[0], ("seq", "tm"), scatter_dimension=0, tiled=True),
        lax.psum_scatter(totals[1], ("seq", "tm"), scatter_dimension=0, tiled=True),
        lax.psum_scatter(totals[2], ("seq", "tm"), scatter_dimension=0, tiled=True),
        lax.psum_scatter(totals[3], ("seq", "tm"), scatter_dimension=0, tiled=True),
        lax.psum_scatter(totals[4], ("seq", "tm"), scatter_dimension=0, tiled=True),
    )
    return (layer_out, token_grad, shares[0], shares[1], shares[2], shares[3], shares[4])


def per_device(dims, tokens, cotangent, qkv_weights, out_weights, up_weights, down_weights, gains):
    rows = tokens[0]
    own_gains = gains.shape[0]
    tile = jnp.pad(gains.astype(F32).reshape(-1, 48), ((0, 8 - own_gains // 48), (0, 80)))
    shards = (qkv_weights, out_weights, up_weights, down_weights)
    slabs = tuple((2 * w.shape[0], w.shape[1]) for w in shards)
    wholes, gain, layer_out, kept = gather_all(dims, own_gains, shards, tile, rows)
    shares = reduce_all(dims, slabs, own_gains, wholes, cotangent[0], gain, rows, kept)
    gain_share = shares[5][: own_gains // 48, :48].reshape(own_gains)
    return (layer_out[None], shares[0][None], *shares[1:5], gain_share)


def fits(mesh, dims):
    chips = dims[0] * dims[1] * dims[2]
    rows = (15 * D, 5 * D, 3 * D, 3 * FF)
    return dims[:2] == (2, 2) and all(r % (chips * ROWS) == 0 for r in rows) and (10 * D) % (2 * chips * 48) == 0 and 10 * D // (2 * chips) <= 384


def solution(mesh):
    seq, tm = mesh.shape["seq"], mesh.shape["tm"]
    dims = (2, seq // 2, tm // 2)
    body = functools.partial(per_device, dims) if fits(mesh, dims) else plain_device
    placed = (
        P("seq", "tm", None),
        P("seq", "tm", None),
        P(("seq", "tm"), None),
        P(("seq", "tm"), None),
        P(("seq", "tm"), None),
        P(("seq", "tm"), None),
        P(("seq", "tm")),
    )
    return jax.shard_map(body, mesh=mesh, in_specs=placed, out_specs=placed, check_vma=False)
```

```python
import functools

import jax
import jax.numpy as jnp
from jax import lax
from jax.experimental import pallas as pl
from jax.experimental.pallas import tpu as pltpu
from jax.sharding import PartitionSpec as P

D = 768
HEADS = 12
FF = 3072

EPS = 1e-06
FAR = -1e30
MESH = pl.DeviceIdType.MESH
BF = jnp.bfloat16
F32 = jnp.float32
BLOCK = D // 2
ROWS = 48
LAG = 0.5
SLOTS = 18
EACH = 1.0
EACH_FORWARD = 0.5
COPIES = 480


def extended(cells, sides, width):
    for axis, dim in sides:
        count = lax.axis_size(axis)
        ends = count - 1
        head = lax.slice_in_dim(cells, 0, width, axis=dim)
        tail = lax.slice_in_dim(cells, cells.shape[dim] - width, cells.shape[dim], axis=dim)
        cells = jnp.concatenate(
            [
                lax.ppermute(tail, axis, [(i, (i + 1) % count) for i in range(ends)]),
                cells,
                lax.ppermute(head, axis, [((i + 1) % count, i) for i in range(ends)]),
            ],
            axis=dim,
        )
    return cells


def from_behind(block, axis, distance):
    devices = range(lax.axis_size(axis))
    route = [(i - distance, i) for i in devices if i - distance in devices]
    return lax.ppermute(block, axis, route)


def norm_rows(x, gain):
    mean = jnp.mean(x, axis=-1, keepdims=True)
    centered = x - mean
    spread = jnp.mean(centered * centered, axis=-1, keepdims=True)
    return centered * lax.rsqrt(spread + EPS) * gain


def norm_back(x, gain, grad):
    unused, pull = jax.vjp(norm_rows, x, gain)
    return pull(grad)


def gelu_back(hidden_pre, grad):
    unused, pull = jax.vjp(lambda value: jax.nn.gelu(value, approximate=False), hidden_pre)
    return pull(grad)[0]


def lowered(value):
    return value.astype(jnp.bfloat16)


def product(left, right):
    return jnp.dot(left, right, preferred_element_type=jnp.float32)


def product_tn(left, right):
    return lax.dot_general(
        left, right, (((0,), (0,)), ((), ())), preferred_element_type=jnp.float32
    )


def product_nt(left, right):
    return lax.dot_general(
        left, right, (((1,), (1,)), ((), ())), preferred_element_type=jnp.float32
    )


def unstack(parts):
    qkv_flat, out_flat, up_flat, down_flat, gain_flat = parts
    return (
        qkv_flat.reshape(5, 3, D, D),
        out_flat.reshape(5, D, D),
        up_flat.reshape(3, D, FF),
        down_flat.reshape(3, FF, D),
        gain_flat.reshape(5, 2, D),
    )


def attend(query, keys, values, bias):
    rows, width = query.shape
    depth = width // HEADS
    qh = query.reshape(rows, HEADS, depth)
    kh = keys.reshape(keys.shape[0], HEADS, depth)
    vh = values.reshape(values.shape[0], HEADS, depth)
    scores = (
        jnp.einsum("qhd,khd->hqk", qh, kh, preferred_element_type=jnp.float32) * depth ** (-0.5)
        + bias
    )
    top = jnp.max(scores, axis=-1, keepdims=True)
    expo = jnp.exp(scores - top)
    probs = expo / jnp.sum(expo, axis=-1, keepdims=True)
    mixed = jnp.einsum("hqk,khd->qhd", lowered(probs), vh, preferred_element_type=jnp.float32)
    return (lowered(mixed.reshape(rows, width)), probs)


def attend_back(query, keys, values, probs, grad_mixed):
    rows, width = query.shape
    depth = width // HEADS
    qh = query.reshape(rows, HEADS, depth)
    kh = keys.reshape(keys.shape[0], HEADS, depth)
    vh = values.reshape(values.shape[0], HEADS, depth)
    gh = grad_mixed.reshape(rows, HEADS, depth)
    dprobs = jnp.einsum("qhd,khd->hqk", gh, vh, preferred_element_type=jnp.float32)
    dvalues = jnp.einsum("hqk,qhd->khd", lowered(probs), gh, preferred_element_type=jnp.float32)
    inner = jnp.sum(dprobs * probs, axis=-1, keepdims=True)
    dscores = lowered(probs * (dprobs - inner))
    scale = depth ** (-0.5)
    dquery = jnp.einsum("hqk,khd->qhd", dscores, kh, preferred_element_type=jnp.float32) * scale
    dkeys = jnp.einsum("hqk,qhd->khd", dscores, qh, preferred_element_type=jnp.float32) * scale
    return (dquery.reshape(rows, width), dkeys.reshape(-1, width), dvalues.reshape(-1, width))


class Place:
    def __init__(self, dims):
        self.dims = dims
        s = lax.axis_index("seq")
        t = lax.axis_index("tm")
        self.at = (s // dims[1], s % dims[1], t // 2)
        self.core = t % 2
        self.slab = t

    def device(self, at, core):
        return (at[0] * self.dims[1] + at[1], at[2] * 2 + core)

    def along(self, dim, value):
        at = list(self.at)
        at[dim] = value
        return self.device(at, self.core)

    def sibling(self):
        return self.device(self.at, 1 - self.core)


def meet(place):
    barrier = pltpu.get_barrier_semaphore()
    count = 1
    pl.semaphore_signal(barrier, inc=1, device_id=place.sibling(), device_id_type=MESH)
    for dim, n in enumerate(place.dims):
        me = place.at[dim]
        for step in (1, -1):
            ok = (me + step >= 0) & (me + step < n)

            @pl.when(ok)
            def _():
                pl.semaphore_signal(barrier, inc=1, device_id=place.along(dim, me + step), device_id_type=MESH)

            count = count + jnp.where(ok, 1, 0)
    step = 2 * place.core - 1
    ok = (place.at[2] + step >= 0) & (place.at[2] + step < place.dims[2])

    @pl.when(ok)
    def _():
        beside = (place.at[0], place.at[1], place.at[2] + step)
        pl.semaphore_signal(barrier, inc=1, device_id=place.device(beside, 1 - place.core), device_id_type=MESH)

    count = count + jnp.where(ok, 1, 0)
    pl.semaphore_wait(barrier, count)


class Copies:
    def __init__(self, send, recv):
        self.send, self.recv = send, recv
        self.used = 0
        self.sent = []

    def start(self, src, dst, device, ok=None):
        copy = pltpu.make_async_remote_copy(
            src_ref=src,
            dst_ref=dst,
            send_sem=self.send.at[self.used],
            recv_sem=self.recv.at[self.used],
            device_id=device,
            device_id_type=MESH,
        )
        self.used += 1
        when(ok, copy.start)
        self.sent.append((copy, ok))
        return copy

    def drain(self):
        for copy, ok in self.sent:
            when(ok, copy.wait_send)
        self.sent = []


def when(ok, action):
    if ok is None:
        action()
    else:

        @pl.when(ok)
        def _():
            action()


def gather_line(copies, place, dim, pick):
    n = place.dims[dim]
    me = place.at[dim]
    if n == 2:
        part = pick(me)
        copy = copies.start(part, part, place.along(dim, 1 - me))
        yield
        copy.wait_recv()
        return
    before = {}
    for hop in range(1, n):
        for step in (1, -1):
            origin = me - step * (hop - 1)
            held = (origin >= 0) & (origin < n)
            if hop > 1:
                when(held, before[step].wait_recv)
            ok = held & (me + step >= 0) & (me + step < n)
            part = pick(jnp.clip(origin, 0, n - 1))
            before[step] = copies.start(part, part, place.along(dim, jnp.clip(me + step, 0, n - 1)), ok)
        yield
    for step in (1, -1):
        origin = me - step * (n - 1)
        when((origin >= 0) & (origin < n), before[step].wait_recv)


def gather_piece(copies, place, full, rows, cols, order, pair):
    done = set()
    for dim in order:

        def pick(value):
            index = [slice(None) if d in done else place.at[d] for d in range(3)]
            index[dim] = value
            return full.at[(*index, pl.ds(*rows), cols)]

        yield from gather_line(copies, place, dim, pick)
        done.add(dim)
    if pair is not None:
        part = full.at[:, :, :, pl.ds(*rows), cols]
        pair.append(copies.start(part, part, place.sibling()))


ZXY, ZYX, XZY, YZX = (2, 1, 0), (2, 0, 1), (1, 2, 0), (0, 2, 1)
CYCLE = (XZY, YZX, ZXY, XZY, YZX, ZYX)


def pieces_of(slabs, arrays):
    flat = []
    for array in arrays:
        rows, width = slabs[array]
        for block in range(width // 2 // BLOCK):
            for row in range(0, rows, ROWS):
                flat.append((array, row, block, CYCLE[len(flat) % 6]))
    return [flat[i : i + 3] for i in range(0, len(flat), 3)]


def march(sets, begin, extra=()):
    waiting = list(sets)
    active = list(extra)
    step = 0
    while active or waiting:
        while waiting and step >= LAG * (len(sets) - len(waiting)):
            for piece in waiting.pop(0):
                active.append(begin(piece))
        still = []
        for one in active:
            try:
                yield next(one)
                still.append(one)
            except StopIteration:
                pass
        active = still
        step += 1


def weave(comm, work, each):
    live = [True, True]
    gate = [None, None]
    sources = (comm, work)

    def advance(k):
        if not live[k]:
            return None
        if gate[k] is not None:
            if not gate[k]():
                return None
            gate[k] = None
        try:
            item = next(sources[k])
        except StopIteration:
            live[k] = False
            return None
        if callable(item):
            gate[k] = item
            return 0.0
        return item or 0.0

    credit = 0.0
    while live[0] or live[1]:
        moved = advance(0)
        if moved is not None:
            credit = min(credit + each, 4.0)
        stuck = moved is None
        while live[1] and (credit > 0 or stuck):
            cost = advance(1)
            if cost is None:
                break
            credit = max(credit - cost, -8.0)
            if stuck and live[0] and (gate[0] is None or gate[0]()):
                break


def matmul(left, right):
    return jnp.dot(left, right, preferred_element_type=F32)


def matmul_nt(left, right):
    return lax.dot_general(left, right, (((1,), (1,)), ((), ())), preferred_element_type=F32)


def matmul_tn(left, right):
    return lax.dot_general(left, right, (((0,), (0,)), ((), ())), preferred_element_type=F32)


def halves_of(pair):
    low = lax.broadcasted_iota(jnp.int32, pair.shape, 1) < pair.shape[1] // 2
    zero = jnp.zeros_like(pair)
    return jnp.where(low, pair, zero), jnp.where(low, zero, pair)


def softmax_rows(scores):
    expo = jnp.exp(scores - jnp.max(scores, axis=-1, keepdims=True))
    return expo * (1.0 / jnp.sum(expo, axis=-1, keepdims=True))


def attend_pair(query, keys, values, bias):
    outs = []
    for part in halves_of(query):
        scores = matmul_nt(part, keys) * 0.125
        if bias is not None:
            scores = scores + bias
        outs.append(matmul(softmax_rows(scores).astype(BF), values))
    low = lax.broadcasted_iota(jnp.int32, outs[0].shape, 1) < outs[0].shape[1] // 2
    return jnp.where(low, outs[0], outs[1]).astype(BF)


def gain_table(tiles, own):
    rows = tiles.shape[0]
    filled = own // 48
    r = lax.broadcasted_iota(jnp.int32, (rows, D), 0)
    c = lax.broadcasted_iota(jnp.int32, (rows, D), 1)
    spread = (lax.broadcasted_iota(jnp.int32, (128, D), 0) == lax.broadcasted_iota(jnp.int32, (128, D), 1) % 48)
    wide = matmul(tiles.astype(BF), spread.astype(BF))
    flat = (r // 8) * filled + r % 8
    wide = jnp.where((r % 8 < filled) & (c // 48 == flat % 16), wide, 0.0).astype(BF)
    rr = lax.broadcasted_iota(jnp.int32, (16, rows), 1)
    vv = lax.broadcasted_iota(jnp.int32, (16, rows), 0)
    pick = (rr % 8 < filled) & (((rr // 8) * filled + rr % 8) // 16 == vv)
    return matmul(pick.astype(BF), wide)


def row_runs(dims, slab, row, count):
    at, end = row, row + count
    while at < end:
        chip, off = at // slab, at % slab
        n = min(end - at, slab - off)
        yield chip // (dims[1] * dims[2]), chip // dims[2] % dims[1], chip % dims[2], off, n, at - row
        at += n


class Weights:
    def __init__(self, dims, slabs, wholes, ring, sems, blocks):
        self.dims, self.slabs, self.wholes, self.ring, self.sems, self.blocks = dims, slabs, wholes, ring, sems, blocks
        self.depth = ring.shape[0]
        self.loading = {}
        self.next_load = 0
        self.next_use = 0
        self.ready = set()

    def fetch(self):
        while self.next_load < min(len(self.blocks), self.next_use + self.depth):
            i = self.next_load
            a, row, block = self.blocks[i]
            if a not in self.ready:
                return
            slot = i % self.depth
            copies = []
            at, end = row, row + D
            slab = self.slabs[a][0]
            while at < end:
                chip, off = at // slab, at % slab
                n = min(end - at, slab - off)
                p, q, z = chip // (self.dims[1] * self.dims[2]), chip // self.dims[2] % self.dims[1], chip % self.dims[2]
                copies.append(
                    pltpu.make_async_copy(
                        self.wholes[a].at[p, q, z, pl.ds(off, n), pl.ds(block * D, D)],
                        self.ring.at[slot, pl.ds(at - row, n)],
                        self.sems.at[slot, len(copies)],
                    )
                )
                at += n
            for one in copies:
                one.start()
            self.loading[i] = copies
            self.next_load += 1

    def take(self, expected):
        i = self.next_use
        assert self.blocks[i] == expected, (self.blocks[i], expected)
        self.fetch()
        for one in self.loading.pop(i):
            one.wait()
        return self.ring.at[i % self.depth]

    def give_back(self):
        self.next_use += 1
        self.fetch()


def forward_blocks():
    blocks = [(0, (9 + i) * D, 0) for i in range(6)]
    blocks += [(1, 3 * D, 0), (1, 4 * D, 0)]
    blocks += [(0, i * D, 0) for i in range(9)]
    blocks += [(1, i * D, 0) for i in range(3)]
    blocks += [(2, v * D, j) for v in range(3) for j in range(FF // D)]
    return blocks


KEPT = ("first", "second", "cq", "ck", "cv", "cmixed", "joined", "normed", "q", "kx", "vx", "mixed", "middle", "normed_two", "slope", "active")


def forward_shapes(rows):
    u = rows // 7
    sizes = dict(
        first=(6 * u, D), second=(3 * u, D), cq=(6 * u, D), ck=(3 * u, D), cv=(3 * u, D), cmixed=(6 * u, D),
        joined=(rows, D), normed=(rows, D), q=(rows, D), kx=(rows + 6 * u, D), vx=(rows + 6 * u, D),
        mixed=(rows, D), middle=(rows, D), normed_two=(rows, D), slope=(rows, FF), active=(rows, FF),
    )
    return {k: (sizes[k], F32 if k in ("joined", "middle", "slope") else BF) for k in KEPT}


def halo_device(place, count, step):
    t = jnp.clip(place.slab + step, 0, count - 1)
    return (place.at[0] * place.dims[1] + place.at[1], t)


def slab_bias(place, count, width, spatial):
    col = lax.broadcasted_iota(jnp.int32, (1, width), 1)
    below = (col < spatial) & (place.slab == 0)
    above = (col >= width - spatial) & (place.slab == count - 1)
    return jnp.where(below | above, FAR, 0.0).astype(F32)


def forward_work(place, copies, weights, need, gain, x, v, save, swap, products):
    u = x.shape[0] // 7
    count = 2 * place.dims[2]
    spans = ((0, 4 * u), (4 * u, 2 * u), (6 * u, u))
    bases = (0, 6 * u, 10 * u)
    yield need("gain")
    for c in range(2):
        r0, n = spans[c]
        k0, m = spans[c + 1]
        rows, keys = pl.ds(r0, n), pl.ds(k0 - 4 * u, m)
        g = lambda j: gain[pl.ds(2 * (3 + c) + j, 1), :]
        v["first"][rows] = norm_rows(x[rows], g(0)).astype(BF)
        v["second"][keys] = norm_rows(x[pl.ds(k0, m)], g(1)).astype(BF)
        yield 0.5
    save("first")
    save("second")
    yield need(0)
    for c in range(2):
        r0, n = spans[c]
        k0, m = spans[c + 1]
        rows, keys = pl.ds(r0, n), pl.ds(k0 - 4 * u, m)
        for j, (src, dst, part) in enumerate((("first", "cq", rows), ("second", "ck", keys), ("second", "cv", keys))):
            w = weights.take((0, (9 + 3 * c + j) * D, 0))
            v[dst][part] = matmul(v[src][part], w[...]).astype(BF)
            weights.give_back()
            yield 0.8
        for h in range(HEADS // 2):
            cols = pl.ds(h * 128, 128)
            v["cmixed"][rows, cols] = attend_pair(v["cq"][rows, cols], v["ck"][keys, cols], v["cv"][keys, cols], None)
            yield 0.8 if c == 0 else 0.3
    for name in ("cq", "ck", "cv", "cmixed"):
        save(name)
    yield need(1)
    for c in range(2):
        rows = pl.ds(*spans[c])
        w = weights.take((1, (3 + c) * D, 0))
        v["joined"][rows] = x[rows] + matmul(v["cmixed"][rows], w[...])
        weights.give_back()
        yield 0.8
    v["joined"][pl.ds(*spans[2])] = x[pl.ds(*spans[2])]
    save("joined")
    for name in ("kx", "vx"):
        for view in range(3):
            base, n = bases[view], spans[view][1]

            @pl.when(place.slab == 0)
            def _():
                v[name][pl.ds(base, u)] = jnp.zeros((u, D), BF)

            @pl.when(place.slab == count - 1)
            def _():
                v[name][pl.ds(base + u + n, u)] = jnp.zeros((u, D), BF)

    halo = {0: [], 1: [], 2: []}
    for view in range(3):
        r0, n = spans[view]
        rows = pl.ds(r0, n)
        base = bases[view]
        v["normed"][rows] = norm_rows(v["joined"][rows], gain[pl.ds(2 * view, 1), :]).astype(BF)
        for j, (dst, part) in enumerate((("q", rows), ("kx", pl.ds(base + u, n)), ("vx", pl.ds(base + u, n)))):
            w = weights.take((0, (3 * view + j) * D, 0))
            v[dst][part] = matmul(v["normed"][rows], w[...]).astype(BF)
            weights.give_back()
            if j > 0:
                ref = v[dst]
                up, down = place.slab < count - 1, place.slab > 0
                halo[view].append(
                    (copies.start(ref.at[pl.ds(base + n, u)], ref.at[pl.ds(base, u)], halo_device(place, count, 1), up), down)
                )
                halo[view].append(
                    (
                        copies.start(
                            ref.at[pl.ds(base + u, u)], ref.at[pl.ds(base + u + n, u)], halo_device(place, count, -1), down
                        ),
                        up,
                    )
                )
            yield 0.8
    save("normed")
    save("q")
    for view in range(3):
        r0, n = spans[view]
        rows, keys = pl.ds(r0, n), pl.ds(bases[view], n + 2 * u)
        for one, ok in halo[view]:
            when(ok, one.wait_recv)
        bias = slab_bias(place, count, n + 2 * u, u)
        for h in range(HEADS // 2):
            cols = pl.ds(h * 128, 128)
            v["mixed"][rows, cols] = attend_pair(v["q"][rows, cols], v["kx"][keys, cols], v["vx"][keys, cols], bias)
            yield (1.4, 0.6, 0.3)[view]
    save("kx")
    save("vx")
    save("mixed")
    for view in range(3):
        rows = pl.ds(*spans[view])
        w = weights.take((1, view * D, 0))
        v["middle"][rows] = v["joined"][rows] + matmul(v["mixed"][rows], w[...])
        weights.give_back()
        v["normed_two"][rows] = norm_rows(v["middle"][rows], gain[pl.ds(2 * view + 1, 1), :]).astype(BF)
        yield 1.0
    save("middle")
    save("normed_two")
    yield need(2)
    for view in range(3):
        rows = pl.ds(*spans[view])
        for j in range(FF // D):
            cols = pl.ds(j * D, D)
            w = weights.take((2, view * D, j))
            pre = matmul(v["normed_two"][rows], w[...])
            weights.give_back()
            area = 0.5 * (1.0 + lax.erf(pre * (0.5**0.5)))
            v["active"][rows, cols] = (pre * area).astype(BF)
            v["slope"][rows, cols] = area + pre * jnp.exp(-0.5 * pre * pre) * 0.3989422804014327
            yield 1.4
        swap(view)
    save("slope")
    save("active")
    yield from products()


def gather_kernel(dims, own_gains, *refs):
    refs = list(refs)
    take = lambda n: [refs.pop(0) for _ in range(n)]
    shards = take(4)
    gain_tile, x, cot = take(3)
    fulls = take(4)
    gain_out, down_part = take(2)
    kept_out = dict(zip(KEPT, take(len(KEPT))))
    theirs, merged = take(4), take(4)
    gain_all, gain, d_out, far_d_out, far_active, made = take(6)
    v = dict(zip(KEPT, take(len(KEPT))))
    ring, send, recv, local, ring_sem, save_sem, store_sem = take(7)
    place = Place(dims)
    copies = Copies(send, recv)
    core = place.core
    at = place.at
    meet(place)
    width = [s.shape[1] // 2 for s in shards]
    mine = [pl.ds(pl.multiple_of(core * w, 128), w) for w in width]
    other = [pl.ds(pl.multiple_of((1 - core) * w, 128), w) for w in width]
    swaps = []
    for a in range(4):
        swaps.append(copies.start(shards[a].at[:, other[a]], theirs[a], place.sibling()))
    own_tile = gain_all.at[at[0], at[1], at[2], core]
    own_tile[...] = gain_tile[...]
    swap_gain = copies.start(own_tile, own_tile, place.sibling())
    slabs = [(m.shape[0], 2 * m.shape[1]) for m in merged]
    sets = pieces_of(slabs, range(4))
    left = {a: sum(1 for s in sets for piece in s if piece[0] == a) for a in range(4)}
    pair = {a: [] for a in range(4)}
    ready = set()
    state = {"gain": False}

    def prepare(a):
        swaps[a].wait_recv()
        w = width[a]
        own = jnp.where(core == 0, shards[a][:, :w].astype(F32), shards[a][:, w:].astype(F32))
        got = theirs[a][...].astype(F32)
        upper = jnp.where(core == 0, own, got)
        lower = jnp.where(core == 0, got, own)
        merged[a][...] = jnp.concatenate([upper, lower], axis=0).astype(BF)
        copy = pltpu.make_async_copy(merged[a], fulls[a].at[at[0], at[1], at[2], :, mine[a]], local.at[a])
        copy.start()
        copy.wait()

    def begin(piece):
        a, row, block, order = piece
        if a not in ready:
            prepare(a)
            ready.add(a)
        cols = pl.ds(pl.multiple_of(core * width[a] + block * BLOCK, 128), BLOCK)
        yield from gather_piece(copies, place, fulls[a], (row, ROWS), cols, order, pair[a])
        left[a] -= 1

    def gains():
        swap_gain.wait_recv()
        done = set()
        for dim in ZXY:

            def pick(value):
                index = [slice(None) if d in done else at[d] for d in range(3)]
                index[dim] = value
                return gain_all.at[tuple(index)]

            yield from gather_line(copies, place, dim, pick)
            done.add(dim)
        gain[...] = gain_table(gain_all[...].reshape(-1, 128), own_gains)
        copy = pltpu.make_async_copy(gain, gain_out, local.at[4])
        copy.start()
        copy.wait()
        state["gain"] = True

    weights = Weights(dims, slabs, fulls, ring, ring_sem, forward_blocks())

    def need(what):
        def gate():
            if what == "gain":
                return state["gain"]
            if left[what]:
                return False
            if what not in weights.ready:
                for copy in pair[what]:
                    copy.wait_recv()
                weights.ready.add(what)
                weights.fetch()
            return True

        return gate

    saves = []

    def save(name):
        copy = pltpu.make_async_copy(v[name], kept_out[name], save_sem.at[len(saves)])
        copy.start()
        saves.append(copy)

    u = x.shape[0] // 7
    spans = ((0, 4 * u), (4 * u, 2 * u), (6 * u, u))
    d_out[...] = cot[...].astype(BF)
    swap_out = copies.start(d_out.at[:, other[0]], far_d_out, place.sibling())
    swapped = {}

    def swap(view):
        rows = pl.ds(*spans[view])
        swapped[view] = copies.start(v["active"].at[rows], far_active.at[rows], place.sibling())

    def products():
        storing = {}
        swap_out.wait_recv()
        own_right = [jnp.where(core == 0, d_out[pl.ds(*s), :BLOCK], d_out[pl.ds(*s), BLOCK:]) for s in spans]
        for view in range(3):
            swapped[view].wait_recv()
            rows = pl.ds(*spans[view])
            right = jnp.concatenate([own_right[view], far_d_out[rows]], axis=0)
            for j in range(FF // D):
                i = view * (FF // D) + j
                slot = i % 2
                for one in storing.pop(i - 2, ()):
                    one.wait()
                cols = pl.ds(j * D, D)
                left = jnp.concatenate([v["active"][rows, cols], far_active[rows, cols]], axis=0)
                made[slot] = matmul_tn(left, right).astype(BF)
                storing[i] = [
                    pltpu.make_async_copy(
                        made.at[slot, pl.ds(at_, n)], down_part.at[p, q, z, pl.ds(off, n)], store_sem.at[slot, k]
                    )
                    for k, (p, q, z, off, n, at_) in enumerate(row_runs(dims, slabs[3][0], view * FF + j * D, D))
                ]
                for one in storing[i]:
                    one.start()
                yield 0.8
        for i in list(storing):
            for one in storing.pop(i):
                one.wait()

    work = forward_work(place, copies, weights, need, gain, x, v, save, swap, products)
    weave(march(sets, begin, (gains(),)), work, EACH_FORWARD)
    for copy in pair[3]:
        copy.wait_recv()
    for copy in saves:
        copy.wait()
    copies.drain()


def gather_all(dims, own_gains, shards, tile, x, cot):
    slabs = [(2 * s.shape[0], s.shape[1]) for s in shards]
    anywhere = pl.BlockSpec(memory_space=pl.ANY)
    vmem = pl.BlockSpec(memory_space=pltpu.VMEM)
    kept = forward_shapes(x.shape[0])
    segments = max(D // s[0] + 2 for s in slabs)
    outs = pl.pallas_call(
        functools.partial(gather_kernel, dims, own_gains),
        out_shape=[jax.ShapeDtypeStruct((*dims, *s), BF) for s in slabs]
        + [jax.ShapeDtypeStruct((16, D), F32), jax.ShapeDtypeStruct((*dims, slabs[3][0], D // 2), BF)]
        + [jax.ShapeDtypeStruct(*kept[k]) for k in KEPT],
        in_specs=[vmem] * 7,
        out_specs=[anywhere] * (6 + len(KEPT)),
        scratch_shapes=[pltpu.VMEM((r // 2, w // 2), BF) for r, w in slabs]
        + [pltpu.VMEM((r, w // 2), BF) for r, w in slabs]
        + [pltpu.VMEM((*dims, 2, 8, 128), F32), pltpu.VMEM((16, D), F32)]
        + [
            pltpu.VMEM(x.shape, BF),
            pltpu.VMEM((x.shape[0], D // 2), BF),
            pltpu.VMEM((x.shape[0], FF), BF),
            pltpu.VMEM((2, D, BLOCK), BF),
        ]
        + [pltpu.VMEM(*kept[k]) for k in KEPT]
        + [
            pltpu.VMEM((4, D, D), BF),
            pltpu.SemaphoreType.DMA((COPIES,)),
            pltpu.SemaphoreType.DMA((COPIES,)),
            pltpu.SemaphoreType.DMA((5,)),
            pltpu.SemaphoreType.DMA((4, segments)),
            pltpu.SemaphoreType.DMA((len(KEPT),)),
            pltpu.SemaphoreType.DMA((2, segments)),
        ],
        compiler_params=pltpu.CompilerParams(collective_id=0, has_side_effects=True, vmem_limit_bytes=60 << 20),
    )(*shards, tile, x, cot)
    return outs[:4], outs[4], outs[5], dict(zip(KEPT, outs[6:]))


class Stream:
    def __init__(self, depth, sems, makers):
        self.depth, self.sems, self.makers = depth, sems, makers
        self.loading = {}
        self.next_load = 0
        self.next_use = 0
        self.fetch()

    def fetch(self):
        while self.next_load < min(len(self.makers), self.next_use + self.depth):
            slot = self.next_load % self.depth
            copies = [
                pltpu.make_async_copy(src, dst, self.sems.at[slot, j])
                for j, (src, dst) in enumerate(self.makers[self.next_load](slot))
            ]
            for one in copies:
                one.start()
            self.loading[self.next_load] = copies
            self.next_load += 1

    def take(self):
        for one in self.loading.pop(self.next_use):
            one.wait()
        return self.next_use % self.depth

    def give_back(self):
        self.next_use += 1
        self.fetch()


def add_to(total, term):
    total[...] = (total[...].astype(F32) + term[...].astype(F32)).astype(total.dtype)


class Credits:
    def __init__(self, sems, waits, gives):
        self.sems, self.waits, self.gives = sems, waits, gives

    def wait(self, index, ok=None):
        if self.waits:
            when(ok, lambda: pl.semaphore_wait(self.sems.at[index], 1))

    def give(self, index, device):
        if self.gives:
            pl.semaphore_signal(self.sems.at[index], inc=1, device_id=device, device_id_type=MESH)


def reduce_line(copies, place, pick, slots, credits):
    n = place.dims[2]
    z = place.at[2]
    before = {}
    for turn in range(n):
        for step in (1, -1):
            far = z if step == 1 else n - 1 - z
            goal = far + n - 1 - turn
            goal = jnp.minimum(goal if step == 1 else n - 1 - goal, n - 1)
            goal = jnp.maximum(goal, 0)
            if turn > 0:

                def take(step=step, turn=turn, goal=goal):
                    before[step].wait_recv()
                    add_to(pick(goal), slots(turn - 1, step))
                    credits.give(2 + 2 * (turn - 1) + (1 - step) // 2, place.along(2, jnp.clip(z - step, 0, n - 1)))

                when((far >= 1) & (far <= turn), take)
            if turn < n - 1:
                credits.wait(2 + 2 * turn + (1 - step) // 2, far <= turn)
                before[step] = copies.start(
                    pick(goal), slots(turn, step), place.along(2, jnp.clip(z + step, 0, n - 1)), far <= turn
                )
        if turn < n - 1:
            yield


def reduce_piece(copies, place, source, order, acc, first, turns, last, local, credits, finish):
    lead = order[0]
    rest = 1 - lead
    me, mine = place.at[lead], place.at[rest]
    z = place.at[2]
    beside, across = place.along(lead, 1 - me), place.along(rest, 1 - mine)
    credits.wait(0)
    copy = copies.start(source(lead, 1 - me), first, beside)
    load = pltpu.make_async_copy(source(lead, me), acc, local)
    load.start()
    yield
    load.wait()
    copy.wait_recv()
    add_to(acc, first)
    credits.give(0, beside)
    slots = lambda turn, step: turns.at[turn, (1 - step) // 2]
    if order[1] == 2:
        yield from reduce_line(copies, place, lambda v: acc.at[:, v], slots, credits)
        credits.wait(1)
        copy = copies.start(acc.at[1 - mine, z], last, across)
        yield
        copy.wait_recv()
        finish(acc[mine, z].astype(F32) + last[...].astype(F32))
        credits.give(1, across)
    else:
        credits.wait(1)
        copy = copies.start(acc.at[1 - mine], last, across)
        yield
        copy.wait_recv()
        add_to(acc.at[mine], last)
        credits.give(1, across)
        yield from reduce_line(copies, place, lambda v: acc.at[mine, v], slots, credits)
        finish(acc[mine, z].astype(F32))


def march_ready(sets, begin, ready, limit):
    waiting = list(sets)
    active = []
    step = 0
    started = 0
    while active or waiting:
        while (
            waiting
            and step >= LAG * started
            and len(active) + len(waiting[0]) <= limit
            and ready(waiting[0])
        ):
            for piece in waiting.pop(0):
                active.append(begin(piece))
            started += 1
        if not active:
            if step < LAG * started:
                step += 1
            else:
                yield lambda: ready(waiting[0])
            continue
        still = []
        for one in active:
            try:
                yield next(one)
                still.append(one)
            except StopIteration:
                pass
        active = still
        step += 1


LEFTS = ("normed_two", "mixed", "normed", "first", "second", "cmixed")
RIGHTS = ("d_out", "d_pre", "d_attn", "dq", "dk", "dv", "d_cross", "dcq", "dck", "dcv")
HELD = ("q", "kx", "vx", "cq", "ck", "cv")


def right_shapes(rows):
    u = rows // 7
    tall = dict(d_cross=6 * u, dcq=6 * u, dck=3 * u, dcv=3 * u)
    return [(tall.get(k, rows), FF if k == "d_pre" else D) for k in RIGHTS]


def job_batches(u):
    rows = ((0, 4 * u), (4 * u, 2 * u), (6 * u, u))
    late = ((0, 2 * u), (2 * u, u))
    batches = {"up": [], "out": [], "qkv": [], "cout": [], "cqkv": []}
    for view in range(3):
        for block in range(FF // 2 // BLOCK):
            batches["up"].append((2, view * D, block, "normed_two", 0, rows[view], "d_pre", rows[view]))
        batches["out"].append((1, view * D, 0, "mixed", 0, rows[view], "d_attn", rows[view]))
        for j, name in enumerate(("dq", "dk", "dv")):
            batches["qkv"].append((0, (3 * view + j) * D, 0, "normed", 0, rows[view], name, rows[view]))
    for c in range(2):
        batches["cout"].append((1, (3 + c) * D, 0, "cmixed", 0, rows[c], "d_cross", rows[c]))
        batches["cqkv"].append((0, (9 + 3 * c) * D, 0, "first", 0, rows[c], "dcq", rows[c]))
        for j, name in enumerate(("dck", "dcv")):
            batches["cqkv"].append((0, (10 + 3 * c + j) * D, 0, "second", 0, late[c], name, late[c]))
    return batches


def backward_blocks():
    blocks = []
    for view in range(3):
        for j in range(FF // D):
            blocks += [(3, view * FF + j * D, 0), (2, view * D, j)]
    blocks += [(1, view * D, 0) for view in range(3)]
    blocks += [(0, i * D, 0) for i in range(9)]
    for c in range(2):
        blocks += [(1, (3 + c) * D, 0)] + [(0, (9 + 3 * c + j) * D, 0) for j in range(3)]
    return blocks


def norm_pull(x, gain, grad):
    centered = x - jnp.mean(x, axis=-1, keepdims=True)
    scale = lax.rsqrt(jnp.mean(centered * centered, axis=-1, keepdims=True) + EPS)
    unit = centered * scale
    inner = grad * gain
    pulled = scale * (
        inner - jnp.mean(inner, axis=-1, keepdims=True) - unit * jnp.mean(inner * unit, axis=-1, keepdims=True)
    )
    return pulled, jnp.sum(grad * unit, axis=0, keepdims=True)


def attend_pair_back(query, keys, values, grad, bias):
    dq, dk, dv = [], None, None
    for part, g in zip(halves_of(query), halves_of(grad)):
        scores = matmul_nt(part, keys) * 0.125
        if bias is not None:
            scores = scores + bias
        probs = softmax_rows(scores)
        dprobs = matmul_nt(g, values)
        inner = jnp.sum(dprobs * probs, axis=-1, keepdims=True)
        dscores = (probs * (dprobs - inner) * 0.125).astype(BF)
        dq.append(matmul(dscores, keys))
        k_term = matmul_tn(dscores, part)
        v_term = matmul_tn(probs.astype(BF), g)
        dk = k_term if dk is None else dk + k_term
        dv = v_term if dv is None else dv + v_term
    low = lax.broadcasted_iota(jnp.int32, dq[0].shape, 1) < dq[0].shape[1] // 2
    return jnp.where(low, dq[0], dq[1]), dk, dv


def gain_tiles(table, rows, own):
    filled = own // 48
    r = lax.broadcasted_iota(jnp.int32, (rows, D), 0)
    c = lax.broadcasted_iota(jnp.int32, (rows, D), 1)
    flat = (r // 8) * filled + r % 8
    rr = lax.broadcasted_iota(jnp.int32, (rows, 16), 0)
    vv = lax.broadcasted_iota(jnp.int32, (rows, 16), 1)
    pick = (rr % 8 < filled) & (((rr // 8) * filled + rr % 8) // 16 == vv)
    wide = jnp.dot(pick.astype(F32), table, precision=lax.Precision.HIGHEST, preferred_element_type=F32)
    wide = jnp.where((r % 8 < filled) & (c // 48 == flat % 16), wide, 0.0)
    j = lax.broadcasted_iota(jnp.int32, (D, 128), 1)
    fold = (j < 48) & (j == lax.broadcasted_iota(jnp.int32, (D, 128), 0) % 48)
    return jnp.dot(wide, fold.astype(F32), precision=lax.Precision.HIGHEST, preferred_element_type=F32)


def reduce_kernel(dims, slabs, sets, own_gains, *refs):
    refs = list(refs)
    take = lambda n: [refs.pop(0) for _ in range(n)]
    wholes = take(4)
    (cot, gain, x, joined, middle, slope, active, down_part) = take(8)
    lefts = dict(zip(LEFTS, take(6)))
    held_in = dict(zip(HELD, take(6)))
    token_out, layer_out = take(2)
    results = take(4)
    (gain_out,) = take(1)
    parts = take(3) + [down_part]
    far_lefts, far_rights = dict(zip(LEFTS, take(6))), dict(zip(RIGHTS, take(10)))
    rights = dict(zip(RIGHTS, take(10)))
    held = dict(zip(HELD, take(6)))
    acc, first, turns_a, turns_b, last_a, last_b = take(6)
    finals = take(4)
    xs, ys, made = take(3)
    g_far, g_own, g_acc, g_first, g_turns, g_last, g_sum = take(7)
    ring, rowring, preing, acting, layer, flow, total, dmixed, dkf, dvf, halo_out, halo_in = take(12)
    send, recv, local, load_sem, store_sem, final_sem, ring_sem, row_sem, pre_sem, held_sem, layer_sem, credit = take(12)
    place = Place(dims)
    core = place.core
    copies = Copies(send, recv)
    meet(place)
    rows_all = cot.shape[0]
    u = rows_all // 7
    spans = ((0, 4 * u), (4 * u, 2 * u), (6 * u, u))
    bases = (0, 6 * u, 10 * u)
    count = 2 * dims[2]
    half_of = lambda ref, c: pl.ds(pl.multiple_of(c * (ref.shape[1] // 2), 128), ref.shape[1] // 2)
    coming = {}

    def swap(name):
        if name in lefts:
            coming[name] = copies.start(lefts[name], far_lefts[name], place.sibling())
        else:
            ref = rights[name]
            coming[name] = copies.start(ref.at[:, half_of(ref, 1 - core)], far_rights[name], place.sibling())

    arrived = set()

    def arrive(name):
        if name not in arrived:
            coming[name].wait_recv()
            arrived.add(name)

    def weight_maker(block):
        a, row, col = block
        return lambda slot: [
            (wholes[a].at[p, q, z, pl.ds(off, n), pl.ds(col * D, D)], ring.at[slot, pl.ds(at, n)])
            for p, q, z, off, n, at in row_runs(dims, slabs[a][0], row, D)
        ]

    def row_maker(ref, r0, n):
        return lambda slot: [(ref.at[pl.ds(r0, n)], rowring.at[slot, pl.ds(0, n)])]

    def pre_maker(view, j):
        r0, n = spans[view]
        block = (pl.ds(r0, n), pl.ds(j * D, D))
        return lambda slot: [
            (slope.at[block], preing.at[slot, pl.ds(0, n)]),
            (active.at[block], acting.at[slot, pl.ds(0, n)]),
        ]

    rights["d_out"][...] = cot[...].astype(BF)
    blocks = backward_blocks()
    weights = Stream(ring.shape[0], ring_sem, [weight_maker(b) for b in blocks])
    pres = Stream(2, pre_sem, [pre_maker(view, j) for view in range(3) for j in range(FF // D)])
    row_list = [(middle, *spans[view]) for view in range(3)] + [(joined, *spans[view]) for view in range(3)]
    for c in range(2):
        row_list += [(x, *spans[c]), (x, *spans[c + 1])]
    rowed = Stream(2, row_sem, [row_maker(*one) for one in row_list])
    used_blocks = []

    def weight(expected):
        assert blocks[len(used_blocks)] == expected
        used_blocks.append(expected)
        return ring.at[weights.take()][...]

    holding = {}
    for i, name in enumerate(HELD):
        holding[name] = pltpu.make_async_copy(held_in[name], held[name], held_sem.at[i])
        holding[name].start()
    for name in LEFTS:
        swap(name)

    state = {"jobs": 0, "gain": False}
    ready = {3}
    storing = {}

    def finish_stores(i):
        for one in storing.pop(i, ()):
            one.wait()

    def load(job, i):
        a, row, block, left, lcol, lrows, right, rrows = job
        arrive(left)
        arrive(right)
        slot = i % 2
        n = lrows[1]
        ref = rights[right]
        own = pl.ds(pl.multiple_of(core * (ref.shape[1] // 2) + block * BLOCK, 128), BLOCK)
        pairs = [
            (lefts[left].at[pl.ds(*lrows), pl.ds(lcol * D, D)], xs.at[slot, pl.ds(0, n)]),
            (far_lefts[left].at[pl.ds(*lrows), pl.ds(lcol * D, D)], xs.at[slot, pl.ds(n, n)]),
            (ref.at[pl.ds(*rrows), own], ys.at[slot, pl.ds(0, n)]),
            (far_rights[right].at[pl.ds(*rrows), pl.ds(block * BLOCK, BLOCK)], ys.at[slot, pl.ds(n, n)]),
        ]
        loads = [pltpu.make_async_copy(s, d, load_sem.at[slot, j]) for j, (s, d) in enumerate(pairs)]
        for one in loads:
            one.start()
        return loads

    batches = job_batches(u)

    def multiply(name, cost):
        batch = batches[name]
        loading = load(batch[0], state["jobs"])
        for index, job in enumerate(batch):
            i = state["jobs"]
            slot = i % 2
            for one in loading:
                one.wait()
            if index + 1 < len(batch):
                loading = load(batch[index + 1], i + 1)
            finish_stores(i - 2)
            n = 2 * job[5][1]
            made[slot] = matmul_tn(xs[slot, :n], ys[slot, :n]).astype(BF)
            a, row, block = job[:3]
            storing[i] = [
                pltpu.make_async_copy(
                    made.at[slot, pl.ds(at, n)],
                    parts[a].at[p, q, z, pl.ds(off, n), pl.ds(block * BLOCK, BLOCK)],
                    store_sem.at[slot, k],
                )
                for k, (p, q, z, off, n, at) in enumerate(row_runs(dims, slabs[a][0], row, D))
            ]
            for one in storing[i]:
                one.start()
            state["jobs"] += 1
            yield cost
        for i in list(storing):
            finish_stores(i)

    g = lambda e, j: gain[pl.ds(2 * e + j, 1), :]

    def work():
        for view in range(3):
            r0, n = spans[view]
            rows = pl.ds(r0, n)
            cost = (2.0, 1.2, 0.9)[view]
            for j in range(FF // D):
                cols = pl.ds(j * D, D)
                down_block = weight((3, view * FF + j * D, 0))
                dactive = matmul_nt(rights["d_out"][rows], down_block)
                slot = pres.take()
                rights["d_pre"][rows, cols] = (dactive * preing[slot, :n]).astype(BF)
                term = matmul(acting[slot, :n], down_block)
                layer[rows] = term if j == 0 else layer[rows] + term
                weights.give_back()
                pres.give_back()
                term = matmul_nt(rights["d_pre"][rows, cols], weight((2, view * D, j)))
                weights.give_back()
                total[:n] = term if j == 0 else total[:n] + term
                yield cost
            slot = rowed.take()
            mid = rowring[slot, :n]
            layer[rows] = layer[rows] + mid
            pulled, g_sum[pl.ds(2 * view + 1, 1), :] = norm_pull(mid, g(view, 1), total[:n])
            rowed.give_back()
            flow[rows] = cot[rows] + pulled
            rights["d_attn"][rows] = flow[rows].astype(BF)
            yield 0.8
        swap("d_pre")
        swap("d_attn")
        layered = pltpu.make_async_copy(layer, layer_out, layer_sem)
        layered.start()
        for view in range(3):
            rows = pl.ds(*spans[view])
            dmixed[rows] = matmul_nt(rights["d_attn"][rows], weight((1, view * D, 0))).astype(BF)
            weights.give_back()
            yield 0.7
        yield from multiply("up", 0.8)
        ready.add(2)
        for name in ("q", "kx", "vx"):
            holding[name].wait()
        halo = {}
        up, down = place.slab < count - 1, place.slab > 0
        for view in range(3):
            r0, n = spans[view]
            rows, keys = pl.ds(r0, n), pl.ds(bases[view], n + 2 * u)
            bias = slab_bias(place, count, n + 2 * u, u)
            for h in range(HEADS // 2):
                cols = pl.ds(h * 128, 128)
                dq, dk, dv = attend_pair_back(
                    held["q"][rows, cols], held["kx"][keys, cols], held["vx"][keys, cols], dmixed[rows, cols], bias
                )
                rights["dq"][rows, cols] = dq.astype(BF)
                for k, (whole, own) in enumerate(((dk, dkf), (dv, dvf))):
                    halo_out[k, view, 0, :, cols] = whole[:u].astype(BF)
                    own[rows, cols] = whole[u : u + n]
                    halo_out[k, view, 1, :, cols] = whole[u + n :].astype(BF)
                yield (3.0, 1.3, 0.7)[view]
            for k in range(2):
                for side, step, ok in ((0, -1, down), (1, 1, up)):
                    halo[k, view, side] = copies.start(
                        halo_out.at[k, view, side], halo_in.at[k, view, side], halo_device(place, count, step), ok
                    )
        swap("dq")
        yield from multiply("out", 0.8)
        for view in range(3):
            r0, n = spans[view]
            rows = pl.ds(r0, n)
            for k, (own, name) in enumerate(((dkf, "dk"), (dvf, "dv"))):
                for side, edge, ok in ((0, r0 + n - u, up), (1, r0, down)):

                    def join(k=k, side=side, edge=edge, own=own):
                        halo[k, view, side].wait_recv()
                        own[pl.ds(edge, u)] = own[pl.ds(edge, u)] + halo_in[k, view, side].astype(F32)

                    when(ok, join)
                rights[name][rows] = own[rows].astype(BF)
            for j, name in enumerate(("dq", "dk", "dv")):
                term = matmul_nt(rights[name][rows], weight((0, (3 * view + j) * D, 0)))
                weights.give_back()
                total[:n] = term if j == 0 else total[:n] + term
                yield 0.7
            slot = rowed.take()
            pulled, g_sum[pl.ds(2 * view, 1), :] = norm_pull(rowring[slot, :n], g(view, 0), total[:n])
            rowed.give_back()
            flow[rows] = flow[rows] + pulled
            yield 0.6
        swap("dk")
        swap("dv")
        rights["d_cross"][...] = flow[pl.ds(0, 6 * u)].astype(BF)
        swap("d_cross")
        for name in ("cq", "ck", "cv"):
            holding[name].wait()
        yield from multiply("qkv", 0.8)
        for c in range(2):
            r0, n = spans[c]
            k0, m = spans[c + 1]
            rows, keys = pl.ds(r0, n), pl.ds(k0 - 4 * u, m)
            dmixed[rows] = matmul_nt(rights["d_cross"][rows], weight((1, (3 + c) * D, 0))).astype(BF)
            weights.give_back()
            yield 0.7
            for h in range(HEADS // 2):
                cols = pl.ds(h * 128, 128)
                dq, dk, dv = attend_pair_back(
                    held["cq"][rows, cols], held["ck"][keys, cols], held["cv"][keys, cols], dmixed[rows, cols], None
                )
                rights["dcq"][rows, cols] = dq.astype(BF)
                rights["dck"][keys, cols] = dk.astype(BF)
                rights["dcv"][keys, cols] = dv.astype(BF)
                yield (1.5, 0.6)[c]
            term = matmul_nt(rights["dcq"][rows], weight((0, (9 + 3 * c) * D, 0)))
            weights.give_back()
            slot = rowed.take()
            pulled, g_sum[pl.ds(2 * (3 + c), 1), :] = norm_pull(rowring[slot, :n], g(3 + c, 0), term)
            rowed.give_back()
            flow[rows] = flow[rows] + pulled
            yield 1.0
            term = matmul_nt(rights["dck"][keys], weight((0, (10 + 3 * c) * D, 0)))
            weights.give_back()
            term = term + matmul_nt(rights["dcv"][keys], weight((0, (11 + 3 * c) * D, 0)))
            weights.give_back()
            slot = rowed.take()
            pulled, g_sum[pl.ds(2 * (3 + c) + 1, 1), :] = norm_pull(rowring[slot, :m], g(3 + c, 1), term)
            rowed.give_back()
            late = pl.ds(k0, m)
            flow[late] = flow[late] + pulled
            yield 1.0
        for name in ("dcq", "dck", "dcv"):
            swap(name)
        yield from multiply("cout", 0.8)
        ready.add(1)
        token = pltpu.make_async_copy(flow, token_out, final_sem.at[4])
        token.start()
        g_sum[pl.ds(10, 6), :] = jnp.zeros((6, D), F32)
        g_own[...] = gain_tiles(g_sum[...], 2 * dims[0] * dims[1] * dims[2] * 8, own_gains).reshape(g_own.shape)
        coming["gain"] = copies.start(g_own, g_far, place.sibling())
        yield 1.0
        yield from multiply("cqkv", 0.8)
        ready.add(0)
        state["gain"] = True
        token.wait()
        layered.wait()

    flat = [piece for group in sets for piece in group if piece != "gain"]
    owners = {}
    kinds = [0 if piece[3][1] == 2 else 1 for piece in flat[:SLOTS]]
    left_in = {a: sum(1 for piece in flat if piece[0] == a) for a in range(4)}
    ending = []
    begun = {"n": 0}

    def gains():
        coming["gain"].wait_recv()
        add_to(g_far, g_own)
        source = lambda dim, value: g_far.at[(*[value if d == dim else slice(None) for d in range(3)], core)]

        def finish(value):
            g_first[0, 0] = value
            copy = pltpu.make_async_copy(g_first.at[0, 0], gain_out, final_sem.at[5])
            copy.start()
            copy.wait()

        yield from reduce_piece(
            copies, place, source, (0, 1, 2), g_acc, g_first, g_turns, g_last, local.at[SLOTS], Credits(None, False, False), finish
        )

    def begin(piece):
        if piece == "gain":
            return gains()
        a, row, block, order = piece
        i = begun["n"]
        begun["n"] += 1
        slot = i % SLOTS
        if i >= SLOTS:
            owners[i - SLOTS].drain()
        mine = Copies(send, recv)
        mine.used = COPIES - 9 * (len(flat) - i)
        owners[i] = mine
        cols = pl.ds(block * BLOCK, BLOCK)
        kind = kinds[slot]
        k = kinds[:slot].count(kind)
        turns, last = ((turns_a, last_a), (turns_b, last_b))[kind]

        def source(dim, value):
            index = [slice(None)] * 3
            index[dim] = value
            return parts[a].at[(*index, pl.ds(row, ROWS), cols)]

        def finish(value):
            finals[a][pl.ds(row, ROWS), cols] = value
            left_in[a] -= 1
            if left_in[a] == 0:
                deliver(a)

        credits = Credits(credit.at[slot], i >= SLOTS, i + SLOTS < len(flat))
        return reduce_piece(
            mine, place, source, order[::-1], acc.at[slot], first.at[slot], turns.at[k], last.at[k], local.at[slot], credits, finish
        )

    def deliver(a):
        rows, width = slabs[a][0] // 2, slabs[a][1] // 2
        cols = pl.ds(pl.multiple_of(core * width, 128), width)
        ending.append(
            copies.start(
                finals[a].at[pl.ds(pl.multiple_of((1 - core) * rows, 8), rows)], results[a].at[:, cols], place.sibling()
            )
        )
        keep = pltpu.make_async_copy(
            finals[a].at[pl.ds(pl.multiple_of(core * rows, 8), rows)], results[a].at[:, cols], final_sem.at[a]
        )
        keep.start()
        keep.wait()

    def set_ready(group):
        return state["gain"] if group[0] == "gain" else all(piece[0] in ready for piece in group)

    weave(march_ready(sets, begin, set_ready, SLOTS), work(), EACH)
    for one in ending:
        one.wait_recv()
    copies.drain()
    for one in owners.values():
        one.drain()
    assert copies.used <= COPIES - 9 * len(flat)


def reduce_all(dims, slabs, own_gains, wholes, down_part, cot, gain, x, kept):
    anywhere = pl.BlockSpec(memory_space=pl.ANY)
    vmem = pl.BlockSpec(memory_space=pltpu.VMEM)
    sets = pieces_of(slabs, (3, 2, 1, 0))
    flat = [piece for group in sets for piece in group]
    sets.insert(len(sets) - 3, ["gain"])
    kinds = [0 if piece[3][1] == 2 else 1 for piece in flat[:SLOTS]]
    bundled, single = kinds.count(0), kinds.count(1)
    z = dims[2]
    rows = cot.shape[0]
    u = rows // 7
    tile = (ROWS, BLOCK)
    segments = max(D // slab[0] + 2 for slab in slabs)
    lefts = [kept[k] for k in LEFTS]
    held = [kept[k] for k in HELD]
    rights = right_shapes(rows)
    outs = pl.pallas_call(
        functools.partial(reduce_kernel, dims, slabs, sets, own_gains),
        out_shape=[jax.ShapeDtypeStruct((rows, D), F32)] * 2
        + [jax.ShapeDtypeStruct((s[0] // 2, s[1]), F32) for s in slabs]
        + [jax.ShapeDtypeStruct((8, 128), F32)]
        + [jax.ShapeDtypeStruct((*dims, s[0], s[1] // 2), BF) for s in slabs[:3]]
        + [jax.ShapeDtypeStruct(one.shape, BF) for one in lefts]
        + [jax.ShapeDtypeStruct((r, w // 2), BF) for r, w in rights],
        in_specs=[anywhere] * 4 + [vmem] * 2 + [anywhere] * 18,
        out_specs=[anywhere] * 26,
        scratch_shapes=[pltpu.VMEM(s, BF) for s in rights]
        + [pltpu.VMEM(one.shape, BF) for one in held]
        + [
            pltpu.VMEM((SLOTS, 2, z, *tile), BF),
            pltpu.VMEM((SLOTS, 2, z, *tile), BF),
            pltpu.VMEM((bundled, z - 1, 2, 2, *tile), BF),
            pltpu.VMEM((single, z - 1, 2, *tile), BF),
            pltpu.VMEM((bundled, *tile), BF),
            pltpu.VMEM((single, z, *tile), BF),
        ]
        + [pltpu.VMEM((s[0], s[1] // 2), F32) for s in slabs]
        + [
            pltpu.VMEM((2, 8 * u, D), BF),
            pltpu.VMEM((2, 8 * u, BLOCK), BF),
            pltpu.VMEM((2, D, BLOCK), BF),
            pltpu.VMEM((*dims, 2, 8, 128), F32),
            pltpu.VMEM((*dims, 2, 8, 128), F32),
            pltpu.VMEM((2, z, 8, 128), F32),
            pltpu.VMEM((2, z, 8, 128), F32),
            pltpu.VMEM((z - 1, 2, 8, 128), F32),
            pltpu.VMEM((z, 8, 128), F32),
            pltpu.VMEM((16, D), F32),
            pltpu.VMEM((4, D, D), BF),
            pltpu.VMEM((2, 4 * u, D), F32),
            pltpu.VMEM((2, 4 * u, D), F32),
            pltpu.VMEM((2, 4 * u, D), BF),
            pltpu.VMEM((rows, D), F32),
            pltpu.VMEM((rows, D), F32),
            pltpu.VMEM((4 * u, D), F32),
            pltpu.VMEM((rows, D), BF),
            pltpu.VMEM((rows, D), F32),
            pltpu.VMEM((rows, D), F32),
            pltpu.VMEM((2, 3, 2, u, D), BF),
            pltpu.VMEM((2, 3, 2, u, D), BF),
            pltpu.SemaphoreType.DMA((COPIES,)),
            pltpu.SemaphoreType.DMA((COPIES,)),
            pltpu.SemaphoreType.DMA((SLOTS + 1,)),
            pltpu.SemaphoreType.DMA((2, 4)),
            pltpu.SemaphoreType.DMA((2, segments)),
            pltpu.SemaphoreType.DMA((6,)),
            pltpu.SemaphoreType.DMA((4, segments)),
            pltpu.SemaphoreType.DMA((2, 1)),
            pltpu.SemaphoreType.DMA((2, 2)),
            pltpu.SemaphoreType.DMA((6,)),
            pltpu.SemaphoreType.DMA,
            pltpu.SemaphoreType.REGULAR((SLOTS, 2 + 2 * (z - 1))),
        ],
        compiler_params=pltpu.CompilerParams(collective_id=1, has_side_effects=True, vmem_limit_bytes=62 << 20),
    )(*wholes, cot, gain, x, kept["joined"], kept["middle"], kept["slope"], kept["active"], down_part, *lefts, *held)
    return outs[:7]


def plain_device(tokens, cotangent, qkv_weights, out_weights, up_weights, down_weights, gains):
    rows = tokens[0]
    incoming = cotangent[0]
    spatial = rows.shape[0] // 7
    bounds = ((0, 4 * spatial), (4 * spatial, 6 * spatial), (6 * spatial, 7 * spatial))
    qkv, outw, upw, downw, gain_low = unstack(
        (
            lax.all_gather(qkv_weights, ("seq", "tm"), axis=0, tiled=True),
            lax.all_gather(out_weights, ("seq", "tm"), axis=0, tiled=True),
            lax.all_gather(up_weights, ("seq", "tm"), axis=0, tiled=True),
            lax.all_gather(down_weights, ("seq", "tm"), axis=0, tiled=True),
            lax.all_gather(gains, ("seq", "tm"), axis=0, tiled=True),
        )
    )
    gain = gain_low.astype(jnp.float32)
    place = lax.axis_index("tm")
    count = lax.axis_size("tm")
    below_bias = jnp.where(place > 0, 0.0, FAR).astype(jnp.float32)
    above_bias = jnp.where(place < count - 1, 0.0, FAR).astype(jnp.float32)
    views = [rows[start:stop] for start, stop in bounds]
    cross_keep = []
    joined = []
    for view in range(2):
        first = lowered(norm_rows(views[view], gain[3 + view, 0]))
        second = lowered(norm_rows(views[view + 1], gain[3 + view, 1]))
        query = lowered(product(first, qkv[3 + view, 0]))
        keys = lowered(product(second, qkv[3 + view, 1]))
        values = lowered(product(second, qkv[3 + view, 2]))
        mixed, probs = attend(query, keys, values, 0.0)
        joined.append(views[view] + product(mixed, outw[3 + view]))
        cross_keep.append((first, second, query, keys, values, mixed, probs))
    joined.append(views[2])
    local_keep = []
    edges = []
    for view in range(3):
        normed = lowered(norm_rows(joined[view], gain[view, 0]))
        query = lowered(product(normed, qkv[view, 0]))
        keys = lowered(product(normed, qkv[view, 1]))
        values = lowered(product(normed, qkv[view, 2]))
        local_keep.append((normed, query, keys, values))
        paired = jnp.stack([keys, values])
        edges.append(jnp.concatenate([paired[:, :spatial], paired[:, -spatial:]], axis=1))
    rim = extended(jnp.stack(edges, axis=1), (("tm", 2),), spatial)
    self_keep = []
    outputs = []
    for view in range(3):
        normed, query, keys, values = local_keep[view]
        length = keys.shape[0]
        keys_all = jnp.concatenate(
            [rim[0, view, :spatial], keys, rim[0, view, 3 * spatial :]], axis=0
        )
        values_all = jnp.concatenate(
            [rim[1, view, :spatial], values, rim[1, view, 3 * spatial :]], axis=0
        )
        bias = jnp.concatenate(
            [
                jnp.broadcast_to(below_bias, (spatial,)),
                jnp.zeros((length,), jnp.float32),
                jnp.broadcast_to(above_bias, (spatial,)),
            ]
        )
        mixed, probs = attend(query, keys_all, values_all, bias)
        middle = joined[view] + product(mixed, outw[view])
        normed_two = lowered(norm_rows(middle, gain[view, 1]))
        hidden_pre = product(normed_two, upw[view])
        active = lowered(jax.nn.gelu(hidden_pre, approximate=False))
        outputs.append(middle + product(active, downw[view]))
        self_keep.append(
            (
                normed,
                query,
                keys_all,
                values_all,
                mixed,
                probs,
                middle,
                normed_two,
                hidden_pre,
                active,
            )
        )
    layer_out = jnp.concatenate(outputs, axis=0)[None]
    qkv, outw, upw, downw, gain_low = unstack(
        (
            lax.all_gather(qkv_weights, ("seq", "tm"), axis=0, tiled=True),
            lax.all_gather(out_weights, ("seq", "tm"), axis=0, tiled=True),
            lax.all_gather(up_weights, ("seq", "tm"), axis=0, tiled=True),
            lax.all_gather(down_weights, ("seq", "tm"), axis=0, tiled=True),
            lax.all_gather(gains, ("seq", "tm"), axis=0, tiled=True),
        )
    )
    grad_qkv = [[None, None, None] for index in range(5)]
    grad_out = [None] * 5
    grad_up = [None] * 3
    grad_down = [None] * 3
    grad_gain = [[None, None] for index in range(5)]
    halves = []
    for view in range(3):
        (
            normed,
            query,
            keys_all,
            values_all,
            mixed,
            probs,
            middle,
            normed_two,
            hidden_pre,
            active,
        ) = self_keep[view]
        start, stop = bounds[view]
        dfinal = incoming[start:stop]
        dbranch = lowered(dfinal)
        grad_down[view] = product_tn(active, dbranch)
        dactive = product_nt(dbranch, downw[view])
        dpre_low = lowered(gelu_back(hidden_pre, dactive))
        grad_up[view] = product_tn(normed_two, dpre_low)
        dnormed_two = product_nt(dpre_low, upw[view])
        dmid_norm, grad_gain[view][1] = norm_back(middle, gain[view, 1], dnormed_two)
        dmiddle = dfinal + dmid_norm
        dattn = lowered(dmiddle)
        grad_out[view] = product_tn(mixed, dattn)
        dmixed = lowered(product_nt(dattn, outw[view]))
        dquery, dkeys, dvalues = attend_back(query, keys_all, values_all, probs, dmixed)
        halves.append((dmiddle, dquery, dkeys, dvalues))
    lower_part = jnp.stack(
        [jnp.stack([half[2][:spatial], half[3][:spatial]]) for half in halves], axis=1
    )
    upper_part = jnp.stack(
        [jnp.stack([half[2][-spatial:], half[3][-spatial:]]) for half in halves], axis=1
    )
    from_above = from_behind(lower_part.astype(jnp.bfloat16), "tm", -1).astype(lower_part.dtype)
    from_below = from_behind(upper_part.astype(jnp.bfloat16), "tm", 1).astype(upper_part.dtype)
    dfused = []
    for view in range(3):
        dmiddle, dquery, dkeys, dvalues = halves[view]
        normed = self_keep[view][0]
        length = dquery.shape[0]
        own_keys = dkeys[spatial : spatial + length]
        own_values = dvalues[spatial : spatial + length]
        own_keys = (
            own_keys.at[:spatial]
            .add(from_below[0, view])
            .at[length - spatial :]
            .add(from_above[0, view])
        )
        own_values = (
            own_values.at[:spatial]
            .add(from_below[1, view])
            .at[length - spatial :]
            .add(from_above[1, view])
        )
        dq_low = lowered(dquery)
        dk_low = lowered(own_keys)
        dv_low = lowered(own_values)
        grad_qkv[view] = [
            product_tn(normed, dq_low),
            product_tn(normed, dk_low),
            product_tn(normed, dv_low),
        ]
        dnormed = (
            product_nt(dq_low, qkv[view, 0])
            + product_nt(dk_low, qkv[view, 1])
            + product_nt(dv_low, qkv[view, 2])
        )
        dfused_norm, grad_gain[view][0] = norm_back(joined[view], gain[view, 0], dnormed)
        dfused.append(dmiddle + dfused_norm)
    dviews = list(dfused)
    for view in range(2):
        first, second, query, keys, values, mixed, probs = cross_keep[view]
        dbranch = lowered(dfused[view])
        grad_out[3 + view] = product_tn(mixed, dbranch)
        dmixed = lowered(product_nt(dbranch, outw[3 + view]))
        dquery, dkeys, dvalues = attend_back(query, keys, values, probs, dmixed)
        dq_low = lowered(dquery)
        dk_low = lowered(dkeys)
        dv_low = lowered(dvalues)
        grad_qkv[3 + view] = [
            product_tn(first, dq_low),
            product_tn(second, dk_low),
            product_tn(second, dv_low),
        ]
        dfirst = product_nt(dq_low, qkv[3 + view, 0])
        dsecond = product_nt(dk_low, qkv[3 + view, 1]) + product_nt(dv_low, qkv[3 + view, 2])
        dx_first, grad_gain[3 + view][0] = norm_back(views[view], gain[3 + view, 0], dfirst)
        dx_second, grad_gain[3 + view][1] = norm_back(views[view + 1], gain[3 + view, 1], dsecond)
        dviews[view] = dviews[view] + dx_first
        dviews[view + 1] = dviews[view + 1] + dx_second
    token_grad = jnp.concatenate(dviews, axis=0)[None]
    qkv_total = jnp.stack([jnp.stack(entry) for entry in grad_qkv]).reshape(15 * D, D)
    out_total = jnp.stack(grad_out).reshape(5 * D, D)
    gain_total = jnp.stack([jnp.stack(entry) for entry in grad_gain]).reshape(10 * D)
    totals = (
        qkv_total,
        out_total,
        jnp.stack(grad_up).reshape(3 * D, FF),
        jnp.stack(grad_down).reshape(3 * FF, D),
        gain_total,
    )
    shares = (
        lax.psum_scatter(totals[0], ("seq", "tm"), scatter_dimension=0, tiled=True),
        lax.psum_scatter(totals[1], ("seq", "tm"), scatter_dimension=0, tiled=True),
        lax.psum_scatter(totals[2], ("seq", "tm"), scatter_dimension=0, tiled=True),
        lax.psum_scatter(totals[3], ("seq", "tm"), scatter_dimension=0, tiled=True),
        lax.psum_scatter(totals[4], ("seq", "tm"), scatter_dimension=0, tiled=True),
    )
    return (layer_out, token_grad, shares[0], shares[1], shares[2], shares[3], shares[4])


def per_device(dims, tokens, cotangent, qkv_weights, out_weights, up_weights, down_weights, gains):
    rows = tokens[0]
    own_gains = gains.shape[0]
    tile = jnp.pad(gains.astype(F32).reshape(-1, 48), ((0, 8 - own_gains // 48), (0, 80)))
    shards = (qkv_weights, out_weights, up_weights, down_weights)
    slabs = tuple((2 * w.shape[0], w.shape[1]) for w in shards)
    wholes, gain, down_part, kept = gather_all(dims, own_gains, shards, tile, rows, cotangent[0])
    shares = reduce_all(dims, slabs, own_gains, wholes, down_part, cotangent[0], gain, rows, kept)
    gain_share = shares[6][: own_gains // 48, :48].reshape(own_gains)
    return (shares[1][None], shares[0][None], *shares[2:6], gain_share)


def fits(mesh, dims):
    chips = dims[0] * dims[1] * dims[2]
    rows = (15 * D, 5 * D, 3 * D, 3 * FF)
    return dims[:2] == (2, 2) and all(r % (chips * ROWS) == 0 for r in rows) and (10 * D) % (2 * chips * 48) == 0 and 10 * D // (2 * chips) <= 384


def solution(mesh):
    seq, tm = mesh.shape["seq"], mesh.shape["tm"]
    dims = (2, seq // 2, tm // 2)
    body = functools.partial(per_device, dims) if fits(mesh, dims) else plain_device
    placed = (
        P("seq", "tm", None),
        P("seq", "tm", None),
        P(("seq", "tm"), None),
        P(("seq", "tm"), None),
        P(("seq", "tm"), None),
        P(("seq", "tm"), None),
        P(("seq", "tm")),
    )
    return jax.shard_map(body, mesh=mesh, in_specs=placed, out_specs=placed, check_vma=False)
```

```python
import functools

import jax
import jax.numpy as jnp
from jax import lax
from jax.experimental import pallas as pl
from jax.experimental.pallas import tpu as pltpu
from jax.sharding import PartitionSpec as P

D = 768
HEADS = 12
FF = 3072

EPS = 1e-06
FAR = -1e30
MESH = pl.DeviceIdType.MESH
BF = jnp.bfloat16
F32 = jnp.float32
BLOCK = D // 2
ROWS = 48
POOLS = (0, 0, 8, 8, 4, 4)
SLOTS = sum(POOLS)
EACH = (6.48, 0.8, 12.38)
EACH_FORWARD = 1.07
COPIES = 480


def extended(cells, sides, width):
    for axis, dim in sides:
        count = lax.axis_size(axis)
        ends = count - 1
        head = lax.slice_in_dim(cells, 0, width, axis=dim)
        tail = lax.slice_in_dim(cells, cells.shape[dim] - width, cells.shape[dim], axis=dim)
        cells = jnp.concatenate(
            [
                lax.ppermute(tail, axis, [(i, (i + 1) % count) for i in range(ends)]),
                cells,
                lax.ppermute(head, axis, [((i + 1) % count, i) for i in range(ends)]),
            ],
            axis=dim,
        )
    return cells


def from_behind(block, axis, distance):
    devices = range(lax.axis_size(axis))
    route = [(i - distance, i) for i in devices if i - distance in devices]
    return lax.ppermute(block, axis, route)


def norm_rows(x, gain):
    mean = jnp.mean(x, axis=-1, keepdims=True)
    centered = x - mean
    spread = jnp.mean(centered * centered, axis=-1, keepdims=True)
    return centered * lax.rsqrt(spread + EPS) * gain


def norm_back(x, gain, grad):
    unused, pull = jax.vjp(norm_rows, x, gain)
    return pull(grad)


def gelu_back(hidden_pre, grad):
    unused, pull = jax.vjp(lambda value: jax.nn.gelu(value, approximate=False), hidden_pre)
    return pull(grad)[0]


def lowered(value):
    return value.astype(jnp.bfloat16)


def product(left, right):
    return jnp.dot(left, right, preferred_element_type=jnp.float32)


def product_tn(left, right):
    return lax.dot_general(
        left, right, (((0,), (0,)), ((), ())), preferred_element_type=jnp.float32
    )


def product_nt(left, right):
    return lax.dot_general(
        left, right, (((1,), (1,)), ((), ())), preferred_element_type=jnp.float32
    )


def unstack(parts):
    qkv_flat, out_flat, up_flat, down_flat, gain_flat = parts
    return (
        qkv_flat.reshape(5, 3, D, D),
        out_flat.reshape(5, D, D),
        up_flat.reshape(3, D, FF),
        down_flat.reshape(3, FF, D),
        gain_flat.reshape(5, 2, D),
    )


def attend(query, keys, values, bias):
    rows, width = query.shape
    depth = width // HEADS
    qh = query.reshape(rows, HEADS, depth)
    kh = keys.reshape(keys.shape[0], HEADS, depth)
    vh = values.reshape(values.shape[0], HEADS, depth)
    scores = (
        jnp.einsum("qhd,khd->hqk", qh, kh, preferred_element_type=jnp.float32) * depth ** (-0.5)
        + bias
    )
    top = jnp.max(scores, axis=-1, keepdims=True)
    expo = jnp.exp(scores - top)
    probs = expo / jnp.sum(expo, axis=-1, keepdims=True)
    mixed = jnp.einsum("hqk,khd->qhd", lowered(probs), vh, preferred_element_type=jnp.float32)
    return (lowered(mixed.reshape(rows, width)), probs)


def attend_back(query, keys, values, probs, grad_mixed):
    rows, width = query.shape
    depth = width // HEADS
    qh = query.reshape(rows, HEADS, depth)
    kh = keys.reshape(keys.shape[0], HEADS, depth)
    vh = values.reshape(values.shape[0], HEADS, depth)
    gh = grad_mixed.reshape(rows, HEADS, depth)
    dprobs = jnp.einsum("qhd,khd->hqk", gh, vh, preferred_element_type=jnp.float32)
    dvalues = jnp.einsum("hqk,qhd->khd", lowered(probs), gh, preferred_element_type=jnp.float32)
    inner = jnp.sum(dprobs * probs, axis=-1, keepdims=True)
    dscores = lowered(probs * (dprobs - inner))
    scale = depth ** (-0.5)
    dquery = jnp.einsum("hqk,khd->qhd", dscores, kh, preferred_element_type=jnp.float32) * scale
    dkeys = jnp.einsum("hqk,qhd->khd", dscores, qh, preferred_element_type=jnp.float32) * scale
    return (dquery.reshape(rows, width), dkeys.reshape(-1, width), dvalues.reshape(-1, width))


class Place:
    def __init__(self, dims):
        self.dims = dims
        s = lax.axis_index("seq")
        t = lax.axis_index("tm")
        self.at = (s // dims[1], s % dims[1], t // 2)
        self.core = t % 2
        self.slab = t

    def device(self, at, core):
        return (at[0] * self.dims[1] + at[1], at[2] * 2 + core)

    def along(self, dim, value):
        at = list(self.at)
        at[dim] = value
        return self.device(at, self.core)

    def sibling(self):
        return self.device(self.at, 1 - self.core)


def meet(place):
    barrier = pltpu.get_barrier_semaphore()
    count = 1
    pl.semaphore_signal(barrier, inc=1, device_id=place.sibling(), device_id_type=MESH)
    for dim, n in enumerate(place.dims):
        me = place.at[dim]
        for step in (1, -1):
            ok = (me + step >= 0) & (me + step < n)

            @pl.when(ok)
            def _():
                pl.semaphore_signal(barrier, inc=1, device_id=place.along(dim, me + step), device_id_type=MESH)

            count = count + jnp.where(ok, 1, 0)
    step = 2 * place.core - 1
    ok = (place.at[2] + step >= 0) & (place.at[2] + step < place.dims[2])

    @pl.when(ok)
    def _():
        beside = (place.at[0], place.at[1], place.at[2] + step)
        pl.semaphore_signal(barrier, inc=1, device_id=place.device(beside, 1 - place.core), device_id_type=MESH)

    count = count + jnp.where(ok, 1, 0)
    pl.semaphore_wait(barrier, count)


class Copies:
    def __init__(self, send, recv):
        self.send, self.recv = send, recv
        self.used = 0
        self.sent = []

    def start(self, src, dst, device, ok=None):
        copy = pltpu.make_async_remote_copy(
            src_ref=src,
            dst_ref=dst,
            send_sem=self.send.at[self.used],
            recv_sem=self.recv.at[self.used],
            device_id=device,
            device_id_type=MESH,
        )
        self.used += 1
        when(ok, copy.start)
        self.sent.append((copy, ok))
        return copy

    def drain(self):
        for copy, ok in self.sent:
            when(ok, copy.wait_send)
        self.sent = []


def when(ok, action):
    if ok is None:
        action()
    else:

        @pl.when(ok)
        def _():
            action()


def gather_line(copies, place, dim, pick):
    n = place.dims[dim]
    me = place.at[dim]
    if n == 2:
        part = pick(me)
        copy = copies.start(part, part, place.along(dim, 1 - me))
        yield
        copy.wait_recv()
        return
    before = {}
    for hop in range(1, n):
        for step in (1, -1):
            origin = me - step * (hop - 1)
            held = (origin >= 0) & (origin < n)
            if hop > 1:
                when(held, before[step].wait_recv)
            ok = held & (me + step >= 0) & (me + step < n)
            part = pick(jnp.clip(origin, 0, n - 1))
            before[step] = copies.start(part, part, place.along(dim, jnp.clip(me + step, 0, n - 1)), ok)
        yield
    for step in (1, -1):
        origin = me - step * (n - 1)
        when((origin >= 0) & (origin < n), before[step].wait_recv)


def gather_piece(copies, place, full, rows, cols, order, pair):
    done = set()
    for dim in order:

        def pick(value):
            index = [slice(None) if d in done else place.at[d] for d in range(3)]
            index[dim] = value
            return full.at[(*index, pl.ds(*rows), cols)]

        yield from gather_line(copies, place, dim, pick)
        done.add(dim)
    if pair is not None:
        part = full.at[:, :, :, pl.ds(*rows), cols]
        pair.append(copies.start(part, part, place.sibling()))


XYZ, YXZ, XZY, YZX, ZXY, ZYX = (1, 0, 2), (0, 1, 2), (1, 2, 0), (0, 2, 1), (2, 1, 0), (2, 0, 1)
ORDERS = (XYZ, YXZ, XZY, YZX, ZXY, ZYX)
CYCLE = (2, 3, 4, 2, 3, 5)
GATHER_PLAN = (
    (5, 0), (5, 0), (4, 0), (5, 1), (2, 2), (5, 2), (4, 2), (5, 3), (2, 3), (1, 3), (3, 3),
    (4, 3), (5, 3), (5, 3), (4, 3), (2, 4), (5, 4), (4, 4), (4, 4), (5, 4), (4, 5), (3, 5),
    (2, 5), (3, 5), (3, 5), (1, 5), (2, 5), (4, 5), (3, 5), (4, 5), (0, 5), (5, 5), (2, 6),
    (5, 6), (4, 6), (5, 6), (5, 7), (1, 7), (2, 7), (1, 7), (4, 7), (0, 7), (0, 7), (5, 7),
)
REDUCE_PLAN = (
    (2, 0), (3, 0), (3, 0), (2, 0), (5, 0), (4, 0), (2, 0), (3, 0), (2, 0), (3, 1), (2, 1),
    (3, 1), (5, 2), (2, 2), (5, 2), (4, 2), (3, 3), (4, 3), (4, 4), (5, 4), (3, 4), (2, 4),
    (2, 4), (3, 4), (3, 5), (4, 6), (2, 6), (2, 6), (3, 6), (5, 6), (2, 6), (3, 6), (5, 7),
    (2, 7), (4, 7), (5, 7), (2, 7), (3, 7), (3, 7), (2, 8), (5, 9), (2, 10), (4, 10), (3, 10),
)


def pieces_of(slabs, arrays, plan):
    flat = []
    for array in arrays:
        rows, width = slabs[array]
        for block in range(width // 2 // BLOCK):
            for row in range(0, rows, ROWS):
                i = len(flat)
                order, start = plan[i] if i < len(plan) else (CYCLE[i % 6], plan[-1][1] + (i - len(plan)) // 6)
                flat.append((array, row, block, ORDERS[order], start))
    return flat


def march(pieces, begin, extra=()):
    waiting = list(pieces)
    active = list(extra)
    step = 0
    while active or waiting:
        while waiting and step >= waiting[0][4]:
            active.append(begin(waiting.pop(0)))
        still = []
        for one in active:
            try:
                yield next(one)
                still.append(one)
            except StopIteration:
                pass
        active = still
        step += 1


def weave(comm, work, each):
    live = [True, True]
    gate = [None, None]
    sources = (comm, work)

    def advance(k):
        if not live[k]:
            return None
        if gate[k] is not None:
            if not gate[k]():
                return None
            gate[k] = None
        try:
            item = next(sources[k])
        except StopIteration:
            live[k] = False
            return None
        if callable(item):
            gate[k] = item
            return 0.0
        return item or 0.0

    credit = 0.0
    while live[0] or live[1]:
        moved = advance(0)
        if moved is not None:
            credit = min(credit + each(), 4.0)
        stuck = moved is None
        while live[1] and (credit > 0 or stuck):
            cost = advance(1)
            if cost is None:
                break
            credit = max(credit - cost, -8.0)
            if stuck and live[0] and (gate[0] is None or gate[0]()):
                break


def matmul(left, right):
    return jnp.dot(left, right, preferred_element_type=F32)


def matmul_nt(left, right):
    return lax.dot_general(left, right, (((1,), (1,)), ((), ())), preferred_element_type=F32)


def matmul_tn(left, right):
    return lax.dot_general(left, right, (((0,), (0,)), ((), ())), preferred_element_type=F32)


def halves_of(pair):
    low = lax.broadcasted_iota(jnp.int32, pair.shape, 1) < pair.shape[1] // 2
    zero = jnp.zeros_like(pair)
    return jnp.where(low, pair, zero), jnp.where(low, zero, pair)


def softmax_rows(scores):
    expo = jnp.exp(scores - jnp.max(scores, axis=-1, keepdims=True))
    return expo * (1.0 / jnp.sum(expo, axis=-1, keepdims=True))


def attend_pair(query, keys, values, bias):
    outs = []
    for part in halves_of(query):
        scores = matmul_nt(part, keys) * 0.125
        if bias is not None:
            scores = scores + bias
        outs.append(matmul(softmax_rows(scores).astype(BF), values))
    low = lax.broadcasted_iota(jnp.int32, outs[0].shape, 1) < outs[0].shape[1] // 2
    return jnp.where(low, outs[0], outs[1]).astype(BF)


def gain_table(tiles, own):
    rows = tiles.shape[0]
    filled = own // 48
    r = lax.broadcasted_iota(jnp.int32, (rows, D), 0)
    c = lax.broadcasted_iota(jnp.int32, (rows, D), 1)
    spread = (lax.broadcasted_iota(jnp.int32, (128, D), 0) == lax.broadcasted_iota(jnp.int32, (128, D), 1) % 48)
    wide = matmul(tiles.astype(BF), spread.astype(BF))
    flat = (r // 8) * filled + r % 8
    wide = jnp.where((r % 8 < filled) & (c // 48 == flat % 16), wide, 0.0).astype(BF)
    rr = lax.broadcasted_iota(jnp.int32, (16, rows), 1)
    vv = lax.broadcasted_iota(jnp.int32, (16, rows), 0)
    pick = (rr % 8 < filled) & (((rr // 8) * filled + rr % 8) // 16 == vv)
    return matmul(pick.astype(BF), wide)


def row_runs(dims, slab, row, count):
    at, end = row, row + count
    while at < end:
        chip, off = at // slab, at % slab
        n = min(end - at, slab - off)
        yield chip // (dims[1] * dims[2]), chip // dims[2] % dims[1], chip % dims[2], off, n, at - row
        at += n


class Weights:
    def __init__(self, dims, slabs, wholes, ring, sems, blocks):
        self.dims, self.slabs, self.wholes, self.ring, self.sems, self.blocks = dims, slabs, wholes, ring, sems, blocks
        self.depth = ring.shape[0]
        self.loading = {}
        self.next_load = 0
        self.next_use = 0
        self.ready = set()

    def fetch(self):
        while self.next_load < min(len(self.blocks), self.next_use + self.depth):
            i = self.next_load
            a, row, block = self.blocks[i]
            if a not in self.ready:
                return
            slot = i % self.depth
            copies = []
            at, end = row, row + D
            slab = self.slabs[a][0]
            while at < end:
                chip, off = at // slab, at % slab
                n = min(end - at, slab - off)
                p, q, z = chip // (self.dims[1] * self.dims[2]), chip // self.dims[2] % self.dims[1], chip % self.dims[2]
                copies.append(
                    pltpu.make_async_copy(
                        self.wholes[a].at[p, q, z, pl.ds(off, n), pl.ds(block * D, D)],
                        self.ring.at[slot, pl.ds(at - row, n)],
                        self.sems.at[slot, len(copies)],
                    )
                )
                at += n
            for one in copies:
                one.start()
            self.loading[i] = copies
            self.next_load += 1

    def take(self, expected):
        i = self.next_use
        assert self.blocks[i] == expected, (self.blocks[i], expected)
        self.fetch()
        for one in self.loading.pop(i):
            one.wait()
        return self.ring.at[i % self.depth]

    def give_back(self):
        self.next_use += 1
        self.fetch()


def forward_blocks():
    blocks = [(0, (9 + i) * D, 0) for i in range(6)]
    blocks += [(1, 3 * D, 0), (1, 4 * D, 0)]
    blocks += [(0, i * D, 0) for i in range(9)]
    blocks += [(1, i * D, 0) for i in range(3)]
    blocks += [(2, v * D, j) for v in range(3) for j in range(FF // D)]
    return blocks


KEPT = ("first", "second", "cq", "ck", "cv", "cmixed", "joined", "normed", "q", "kx", "vx", "mixed", "middle", "normed_two", "slope", "active")


def forward_shapes(rows):
    u = rows // 7
    sizes = dict(
        first=(6 * u, D), second=(3 * u, D), cq=(6 * u, D), ck=(3 * u, D), cv=(3 * u, D), cmixed=(6 * u, D),
        joined=(rows, D), normed=(rows, D), q=(rows, D), kx=(rows + 6 * u, D), vx=(rows + 6 * u, D),
        mixed=(rows, D), middle=(rows, D), normed_two=(rows, D), slope=(rows, FF), active=(rows, FF),
    )
    return {k: (sizes[k], F32 if k in ("joined", "middle", "slope") else BF) for k in KEPT}


def halo_device(place, count, step):
    t = jnp.clip(place.slab + step, 0, count - 1)
    return (place.at[0] * place.dims[1] + place.at[1], t)


def slab_bias(place, count, width, spatial, axis=1):
    col = lax.broadcasted_iota(jnp.int32, (1, width) if axis else (width, 1), axis)
    below = (col < spatial) & (place.slab == 0)
    above = (col >= width - spatial) & (place.slab == count - 1)
    return jnp.where(below | above, FAR, 0.0).astype(F32)


def forward_work(place, copies, weights, need, gain, x, v, save, swap, products):
    u = x.shape[0] // 7
    count = 2 * place.dims[2]
    spans = ((0, 4 * u), (4 * u, 2 * u), (6 * u, u))
    bases = (0, 6 * u, 10 * u)
    yield need("gain")
    for c in range(2):
        r0, n = spans[c]
        k0, m = spans[c + 1]
        rows, keys = pl.ds(r0, n), pl.ds(k0 - 4 * u, m)
        g = lambda j: gain[pl.ds(2 * (3 + c) + j, 1), :]
        v["first"][rows] = norm_rows(x[rows], g(0)).astype(BF)
        v["second"][keys] = norm_rows(x[pl.ds(k0, m)], g(1)).astype(BF)
        yield 0.5
    save("first")
    save("second")
    yield need(0)
    for c in range(2):
        r0, n = spans[c]
        k0, m = spans[c + 1]
        rows, keys = pl.ds(r0, n), pl.ds(k0 - 4 * u, m)
        for j, (src, dst, part) in enumerate((("first", "cq", rows), ("second", "ck", keys), ("second", "cv", keys))):
            w = weights.take((0, (9 + 3 * c + j) * D, 0))
            v[dst][part] = matmul(v[src][part], w[...]).astype(BF)
            weights.give_back()
            yield 0.8
        for h in range(HEADS // 2):
            cols = pl.ds(h * 128, 128)
            v["cmixed"][rows, cols] = attend_pair(v["cq"][rows, cols], v["ck"][keys, cols], v["cv"][keys, cols], None)
            yield 0.8 if c == 0 else 0.3
    for name in ("cq", "ck", "cv", "cmixed"):
        save(name)
    yield need(1)
    for c in range(2):
        rows = pl.ds(*spans[c])
        w = weights.take((1, (3 + c) * D, 0))
        v["joined"][rows] = x[rows] + matmul(v["cmixed"][rows], w[...])
        weights.give_back()
        yield 0.8
    v["joined"][pl.ds(*spans[2])] = x[pl.ds(*spans[2])]
    save("joined")
    for name in ("kx", "vx"):
        for view in range(3):
            base, n = bases[view], spans[view][1]

            @pl.when(place.slab == 0)
            def _():
                v[name][pl.ds(base, u)] = jnp.zeros((u, D), BF)

            @pl.when(place.slab == count - 1)
            def _():
                v[name][pl.ds(base + u + n, u)] = jnp.zeros((u, D), BF)

    halo = {0: [], 1: [], 2: []}
    for view in range(3):
        r0, n = spans[view]
        rows = pl.ds(r0, n)
        base = bases[view]
        v["normed"][rows] = norm_rows(v["joined"][rows], gain[pl.ds(2 * view, 1), :]).astype(BF)
        for j, (dst, part) in enumerate((("q", rows), ("kx", pl.ds(base + u, n)), ("vx", pl.ds(base + u, n)))):
            w = weights.take((0, (3 * view + j) * D, 0))
            v[dst][part] = matmul(v["normed"][rows], w[...]).astype(BF)
            weights.give_back()
            if j > 0:
                ref = v[dst]
                up, down = place.slab < count - 1, place.slab > 0
                halo[view].append(
                    (copies.start(ref.at[pl.ds(base + n, u)], ref.at[pl.ds(base, u)], halo_device(place, count, 1), up), down)
                )
                halo[view].append(
                    (
                        copies.start(
                            ref.at[pl.ds(base + u, u)], ref.at[pl.ds(base + u + n, u)], halo_device(place, count, -1), down
                        ),
                        up,
                    )
                )
            yield 0.8
    save("normed")
    save("q")
    for view in range(3):
        r0, n = spans[view]
        rows, keys = pl.ds(r0, n), pl.ds(bases[view], n + 2 * u)
        for one, ok in halo[view]:
            when(ok, one.wait_recv)
        bias = slab_bias(place, count, n + 2 * u, u)
        for h in range(HEADS // 2):
            cols = pl.ds(h * 128, 128)
            v["mixed"][rows, cols] = attend_pair(v["q"][rows, cols], v["kx"][keys, cols], v["vx"][keys, cols], bias)
            yield (1.4, 0.6, 0.3)[view]
    save("kx")
    save("vx")
    save("mixed")
    for view in range(3):
        rows = pl.ds(*spans[view])
        w = weights.take((1, view * D, 0))
        v["middle"][rows] = v["joined"][rows] + matmul(v["mixed"][rows], w[...])
        weights.give_back()
        v["normed_two"][rows] = norm_rows(v["middle"][rows], gain[pl.ds(2 * view + 1, 1), :]).astype(BF)
        yield 1.0
    save("middle")
    save("normed_two")
    yield need(2)
    for view in range(3):
        rows = pl.ds(*spans[view])
        for j in range(FF // D):
            cols = pl.ds(j * D, D)
            w = weights.take((2, view * D, j))
            pre = matmul(v["normed_two"][rows], w[...])
            weights.give_back()
            area = 0.5 * (1.0 + lax.erf(pre * (0.5**0.5)))
            v["active"][rows, cols] = (pre * area).astype(BF)
            v["slope"][rows, cols] = area + pre * jnp.exp(-0.5 * pre * pre) * 0.3989422804014327
            yield 1.4
        swap(view)
    save("slope")
    save("active")
    yield from products()


def gather_kernel(dims, own_gains, *refs):
    refs = list(refs)
    take = lambda n: [refs.pop(0) for _ in range(n)]
    shards = take(4)
    gain_tile, x, cot = take(3)
    fulls = take(4)
    gain_out, down_part = take(2)
    kept_out = dict(zip(KEPT, take(len(KEPT))))
    theirs, merged = take(4), take(4)
    gain_all, gain, d_out, far_d_out, far_active, made = take(6)
    v = dict(zip(KEPT, take(len(KEPT))))
    ring, send, recv, local, ring_sem, save_sem, store_sem = take(7)
    place = Place(dims)
    copies = Copies(send, recv)
    core = place.core
    at = place.at
    meet(place)
    width = [s.shape[1] // 2 for s in shards]
    mine = [pl.ds(pl.multiple_of(core * w, 128), w) for w in width]
    other = [pl.ds(pl.multiple_of((1 - core) * w, 128), w) for w in width]
    swaps = []
    for a in range(4):
        swaps.append(copies.start(shards[a].at[:, other[a]], theirs[a], place.sibling()))
    own_tile = gain_all.at[at[0], at[1], at[2], core]
    own_tile[...] = gain_tile[...]
    swap_gain = copies.start(own_tile, own_tile, place.sibling())
    slabs = [(m.shape[0], 2 * m.shape[1]) for m in merged]
    pieces = pieces_of(slabs, range(4), GATHER_PLAN)
    left = {a: sum(1 for piece in pieces if piece[0] == a) for a in range(4)}
    pair = {a: [] for a in range(4)}
    ready = set()
    state = {"gain": False}

    def prepare(a):
        swaps[a].wait_recv()
        w = width[a]
        own = jnp.where(core == 0, shards[a][:, :w].astype(F32), shards[a][:, w:].astype(F32))
        got = theirs[a][...].astype(F32)
        upper = jnp.where(core == 0, own, got)
        lower = jnp.where(core == 0, got, own)
        merged[a][...] = jnp.concatenate([upper, lower], axis=0).astype(BF)
        copy = pltpu.make_async_copy(merged[a], fulls[a].at[at[0], at[1], at[2], :, mine[a]], local.at[a])
        copy.start()
        copy.wait()

    def begin(piece):
        a, row, block, order, _ = piece
        if a not in ready:
            prepare(a)
            ready.add(a)
        cols = pl.ds(pl.multiple_of(core * width[a] + block * BLOCK, 128), BLOCK)
        yield from gather_piece(copies, place, fulls[a], (row, ROWS), cols, order, pair[a])
        left[a] -= 1

    def gains():
        swap_gain.wait_recv()
        done = set()
        for dim in ZXY:

            def pick(value):
                index = [slice(None) if d in done else at[d] for d in range(3)]
                index[dim] = value
                return gain_all.at[tuple(index)]

            yield from gather_line(copies, place, dim, pick)
            done.add(dim)
        gain[...] = gain_table(gain_all[...].reshape(-1, 128), own_gains)
        copy = pltpu.make_async_copy(gain, gain_out, local.at[4])
        copy.start()
        copy.wait()
        state["gain"] = True

    weights = Weights(dims, slabs, fulls, ring, ring_sem, forward_blocks())

    def need(what):
        def gate():
            if what == "gain":
                return state["gain"]
            if left[what]:
                return False
            if what not in weights.ready:
                for copy in pair[what]:
                    copy.wait_recv()
                weights.ready.add(what)
                weights.fetch()
            return True

        return gate

    saves = []

    def save(name):
        copy = pltpu.make_async_copy(v[name], kept_out[name], save_sem.at[len(saves)])
        copy.start()
        saves.append(copy)

    u = x.shape[0] // 7
    spans = ((0, 4 * u), (4 * u, 2 * u), (6 * u, u))
    d_out[...] = cot[...].astype(BF)
    swap_out = copies.start(d_out.at[:, other[0]], far_d_out, place.sibling())
    swapped = {}

    def swap(view):
        rows = pl.ds(*spans[view])
        swapped[view] = copies.start(v["active"].at[rows], far_active.at[rows], place.sibling())

    def products():
        storing = {}
        swap_out.wait_recv()
        own_right = [jnp.where(core == 0, d_out[pl.ds(*s), :BLOCK], d_out[pl.ds(*s), BLOCK:]) for s in spans]
        for view in range(3):
            swapped[view].wait_recv()
            rows = pl.ds(*spans[view])
            right = jnp.concatenate([own_right[view], far_d_out[rows]], axis=0)
            for j in range(FF // D):
                i = view * (FF // D) + j
                slot = i % 2
                for one in storing.pop(i - 2, ()):
                    one.wait()
                cols = pl.ds(j * D, D)
                left = jnp.concatenate([v["active"][rows, cols], far_active[rows, cols]], axis=0)
                made[slot] = matmul_tn(left, right).astype(BF)
                storing[i] = [
                    pltpu.make_async_copy(
                        made.at[slot, pl.ds(at_, n)], down_part.at[p, q, z, pl.ds(off, n)], store_sem.at[slot, k]
                    )
                    for k, (p, q, z, off, n, at_) in enumerate(row_runs(dims, slabs[3][0], view * FF + j * D, D))
                ]
                for one in storing[i]:
                    one.start()
                yield 0.8
        for i in list(storing):
            for one in storing.pop(i):
                one.wait()

    work = forward_work(place, copies, weights, need, gain, x, v, save, swap, products)
    weave(march(pieces, begin, (gains(),)), work, lambda: EACH_FORWARD)
    for copy in pair[3]:
        copy.wait_recv()
    for copy in saves:
        copy.wait()
    copies.drain()


def gather_all(dims, own_gains, shards, tile, x, cot):
    slabs = [(2 * s.shape[0], s.shape[1]) for s in shards]
    anywhere = pl.BlockSpec(memory_space=pl.ANY)
    vmem = pl.BlockSpec(memory_space=pltpu.VMEM)
    kept = forward_shapes(x.shape[0])
    segments = max(D // s[0] + 2 for s in slabs)
    outs = pl.pallas_call(
        functools.partial(gather_kernel, dims, own_gains),
        out_shape=[jax.ShapeDtypeStruct((*dims, *s), BF) for s in slabs]
        + [jax.ShapeDtypeStruct((16, D), F32), jax.ShapeDtypeStruct((*dims, slabs[3][0], D // 2), BF)]
        + [jax.ShapeDtypeStruct(*kept[k]) for k in KEPT],
        in_specs=[vmem] * 7,
        out_specs=[anywhere] * (6 + len(KEPT)),
        scratch_shapes=[pltpu.VMEM((r // 2, w // 2), BF) for r, w in slabs]
        + [pltpu.VMEM((r, w // 2), BF) for r, w in slabs]
        + [pltpu.VMEM((*dims, 2, 8, 128), F32), pltpu.VMEM((16, D), F32)]
        + [
            pltpu.VMEM(x.shape, BF),
            pltpu.VMEM((x.shape[0], D // 2), BF),
            pltpu.VMEM((x.shape[0], FF), BF),
            pltpu.VMEM((2, D, BLOCK), BF),
        ]
        + [pltpu.VMEM(*kept[k]) for k in KEPT]
        + [
            pltpu.VMEM((4, D, D), BF),
            pltpu.SemaphoreType.DMA((COPIES,)),
            pltpu.SemaphoreType.DMA((COPIES,)),
            pltpu.SemaphoreType.DMA((5,)),
            pltpu.SemaphoreType.DMA((4, segments)),
            pltpu.SemaphoreType.DMA((len(KEPT),)),
            pltpu.SemaphoreType.DMA((2, segments)),
        ],
        compiler_params=pltpu.CompilerParams(collective_id=0, has_side_effects=True, vmem_limit_bytes=60 << 20),
    )(*shards, tile, x, cot)
    return outs[:4], outs[4], outs[5], dict(zip(KEPT, outs[6:]))


class Stream:
    def __init__(self, depth, sems, makers):
        self.depth, self.sems, self.makers = depth, sems, makers
        self.loading = {}
        self.next_load = 0
        self.next_use = 0
        self.fetch()

    def fetch(self):
        while self.next_load < min(len(self.makers), self.next_use + self.depth):
            slot = self.next_load % self.depth
            copies = [
                pltpu.make_async_copy(src, dst, self.sems.at[slot, j])
                for j, (src, dst) in enumerate(self.makers[self.next_load](slot))
            ]
            for one in copies:
                one.start()
            self.loading[self.next_load] = copies
            self.next_load += 1

    def take(self):
        for one in self.loading.pop(self.next_use):
            one.wait()
        return self.next_use % self.depth

    def give_back(self):
        self.next_use += 1
        self.fetch()


def add_to(total, term):
    total[...] = (total[...].astype(F32) + term[...].astype(F32)).astype(total.dtype)


class Credits:
    def __init__(self, sems, waits):
        self.sems, self.waits = sems, waits

    def wait(self, index, ok=None):
        if self.waits:
            when(ok, lambda: pl.semaphore_wait(self.sems.at[index], 1))

    def give(self, index, device):
        if self.sems is not None:
            pl.semaphore_signal(self.sems.at[index], inc=1, device_id=device, device_id_type=MESH)

    def settle(self, place):
        self.waits = True
        n, z = place.dims[2], place.at[2]
        self.wait(0)
        self.wait(1)
        for turn in range(n - 1):
            for step in (1, -1):
                far = z if step == 1 else n - 1 - z
                self.wait(2 + 2 * turn + (1 - step) // 2, far <= turn)


def reduce_line(copies, place, pick, slots, credits):
    n = place.dims[2]
    z = place.at[2]
    before = {}
    for turn in range(n):
        for step in (1, -1):
            far = z if step == 1 else n - 1 - z
            goal = far + n - 1 - turn
            goal = jnp.minimum(goal if step == 1 else n - 1 - goal, n - 1)
            goal = jnp.maximum(goal, 0)
            if turn > 0:

                def take(step=step, turn=turn, goal=goal):
                    before[step].wait_recv()
                    add_to(pick(goal), slots(turn - 1, step))
                    credits.give(2 + 2 * (turn - 1) + (1 - step) // 2, place.along(2, jnp.clip(z - step, 0, n - 1)))

                when((far >= 1) & (far <= turn), take)
            if turn < n - 1:
                credits.wait(2 + 2 * turn + (1 - step) // 2, far <= turn)
                before[step] = copies.start(
                    pick(goal), slots(turn, step), place.along(2, jnp.clip(z + step, 0, n - 1)), far <= turn
                )
        if turn < n - 1:
            yield


def reduce_piece(copies, place, source, order, acc, first, turns, last, local, credits, finish):
    lead = order[0]
    rest = 1 - lead
    me, mine = place.at[lead], place.at[rest]
    z = place.at[2]
    beside, across = place.along(lead, 1 - me), place.along(rest, 1 - mine)
    credits.wait(0)
    copy = copies.start(source(lead, 1 - me), first, beside)
    load = pltpu.make_async_copy(source(lead, me), acc, local)
    load.start()
    yield
    load.wait()
    copy.wait_recv()
    add_to(acc, first)
    credits.give(0, beside)
    slots = lambda turn, step: turns.at[turn, (1 - step) // 2]
    if order[1] == 2:
        yield from reduce_line(copies, place, lambda v: acc.at[:, v], slots, credits)
        credits.wait(1)
        copy = copies.start(acc.at[1 - mine, z], last, across)
        yield
        copy.wait_recv()
        finish(acc[mine, z].astype(F32) + last[...].astype(F32))
        credits.give(1, across)
    else:
        credits.wait(1)
        copy = copies.start(acc.at[1 - mine], last, across)
        yield
        copy.wait_recv()
        add_to(acc.at[mine], last)
        credits.give(1, across)
        yield from reduce_line(copies, place, lambda v: acc.at[mine, v], slots, credits)
        finish(acc[mine, z].astype(F32))


def march_ready(pieces, begin, ready):
    waiting = list(pieces)
    active = []
    step = 0
    while active or waiting:
        while waiting and step >= waiting[0][4] and ready(waiting[0]):
            active.append(begin(waiting.pop(0)))
        if not active:
            if step < waiting[0][4]:
                step += 1
            else:
                yield lambda: ready(waiting[0])
            continue
        still = []
        for one in active:
            try:
                yield next(one)
                still.append(one)
            except StopIteration:
                pass
        active = still
        step += 1


LEFTS = ("normed_two", "mixed", "normed", "first", "second", "cmixed")
RIGHTS = ("d_out", "d_pre", "d_attn", "dq", "dk", "dv", "d_cross", "dcq", "dck", "dcv")
HELD = ("q", "kx", "vx", "cq", "ck", "cv")


def right_shapes(rows):
    u = rows // 7
    tall = dict(d_cross=6 * u, dcq=6 * u, dck=3 * u, dcv=3 * u)
    return [(tall.get(k, rows), FF if k == "d_pre" else D) for k in RIGHTS]


def job_batches(u):
    rows = ((0, 4 * u), (4 * u, 2 * u), (6 * u, u))
    late = ((0, 2 * u), (2 * u, u))
    batches = {"up": [], "out": [], "qkv": [], "cout": [], "cqkv": []}
    for view in range(3):
        for block in range(FF // 2 // BLOCK):
            batches["up"].append((2, view * D, block, "normed_two", 0, rows[view], "d_pre", rows[view]))
        batches["out"].append((1, view * D, 0, "mixed", 0, rows[view], "d_attn", rows[view]))
        for j, name in enumerate(("dq", "dk", "dv")):
            batches["qkv"].append((0, (3 * view + j) * D, 0, "normed", 0, rows[view], name, rows[view]))
    for c in range(2):
        batches["cout"].append((1, (3 + c) * D, 0, "cmixed", 0, rows[c], "d_cross", rows[c]))
        batches["cqkv"].append((0, (9 + 3 * c) * D, 0, "first", 0, rows[c], "dcq", rows[c]))
        for j, name in enumerate(("dck", "dcv")):
            batches["cqkv"].append((0, (10 + 3 * c + j) * D, 0, "second", 0, late[c], name, late[c]))
    return batches


def backward_blocks():
    blocks = []
    for view in range(3):
        for j in range(FF // D):
            blocks += [(3, view * FF + j * D, 0), (2, view * D, j)]
    blocks += [(1, view * D, 0) for view in range(3)]
    blocks += [(0, i * D, 0) for i in range(9)]
    for c in range(2):
        blocks += [(1, (3 + c) * D, 0)] + [(0, (9 + 3 * c + j) * D, 0) for j in range(3)]
    return blocks


def norm_pull(x, gain, grad):
    centered = x - jnp.mean(x, axis=-1, keepdims=True)
    scale = lax.rsqrt(jnp.mean(centered * centered, axis=-1, keepdims=True) + EPS)
    unit = centered * scale
    inner = grad * gain
    pulled = scale * (
        inner - jnp.mean(inner, axis=-1, keepdims=True) - unit * jnp.mean(inner * unit, axis=-1, keepdims=True)
    )
    return pulled, jnp.sum(grad * unit, axis=0, keepdims=True)


def attend_pair_back(query, keys, values, grad, bias):
    dq, dk, dv = [], None, None
    for part, g in zip(halves_of(query), halves_of(grad)):
        scores = matmul_nt(keys, part) * 0.125
        if bias is not None:
            scores = scores + bias
        expo = jnp.exp(scores - jnp.max(scores, axis=0, keepdims=True))
        probs = expo * (1.0 / jnp.sum(expo, axis=0, keepdims=True))
        dprobs = matmul_nt(values, g)
        inner = jnp.sum(dprobs * probs, axis=0, keepdims=True)
        dscores = (probs * (dprobs - inner) * 0.125).astype(BF)
        dq.append(matmul_tn(dscores, keys))
        k_term = matmul(dscores, part)
        v_term = matmul(probs.astype(BF), g)
        dk = k_term if dk is None else dk + k_term
        dv = v_term if dv is None else dv + v_term
    low = lax.broadcasted_iota(jnp.int32, dq[0].shape, 1) < dq[0].shape[1] // 2
    return jnp.where(low, dq[0], dq[1]), dk, dv


def gain_tiles(table, rows, own):
    filled = own // 48
    r = lax.broadcasted_iota(jnp.int32, (rows, D), 0)
    c = lax.broadcasted_iota(jnp.int32, (rows, D), 1)
    flat = (r // 8) * filled + r % 8
    rr = lax.broadcasted_iota(jnp.int32, (rows, 16), 0)
    vv = lax.broadcasted_iota(jnp.int32, (rows, 16), 1)
    pick = (rr % 8 < filled) & (((rr // 8) * filled + rr % 8) // 16 == vv)
    wide = jnp.dot(pick.astype(F32), table, precision=lax.Precision.HIGHEST, preferred_element_type=F32)
    wide = jnp.where((r % 8 < filled) & (c // 48 == flat % 16), wide, 0.0)
    j = lax.broadcasted_iota(jnp.int32, (D, 128), 1)
    fold = (j < 48) & (j == lax.broadcasted_iota(jnp.int32, (D, 128), 0) % 48)
    return jnp.dot(wide, fold.astype(F32), precision=lax.Precision.HIGHEST, preferred_element_type=F32)


def reduce_kernel(dims, slabs, pieces, own_gains, *refs):
    refs = list(refs)
    take = lambda n: [refs.pop(0) for _ in range(n)]
    wholes = take(4)
    (cot, gain, x, joined, middle, slope, active, down_part) = take(8)
    lefts = dict(zip(LEFTS, take(6)))
    held_in = dict(zip(HELD, take(6)))
    token_out, layer_out = take(2)
    results = take(4)
    (gain_out,) = take(1)
    parts = take(3) + [down_part]
    far_lefts, far_rights = dict(zip(LEFTS, take(6))), dict(zip(RIGHTS, take(10)))
    rights = dict(zip(RIGHTS, take(10)))
    held = dict(zip(HELD, take(6)))
    acc, first, turns_a, turns_b, last_a, last_b = take(6)
    finals = take(4)
    xs, ys, made = take(3)
    g_far, g_own, g_acc, g_first, g_turns, g_last, g_sum = take(7)
    ring, rowring, preing, acting, layer, flow, total, dvf, halo_out, halo_in = take(10)
    send, recv, local, left_sem, right_sem, store_sem, final_sem, ring_sem, row_sem, pre_sem, held_sem, layer_sem, credit = take(13)
    place = Place(dims)
    core = place.core
    copies = Copies(send, recv)
    meet(place)
    rows_all = cot.shape[0]
    u = rows_all // 7
    spans = ((0, 4 * u), (4 * u, 2 * u), (6 * u, u))
    bases = (0, 6 * u, 10 * u)
    count = 2 * dims[2]
    half_of = lambda ref, c: pl.ds(pl.multiple_of(c * (ref.shape[1] // 2), 128), ref.shape[1] // 2)
    coming = {}

    def swap(name):
        if name in lefts:
            coming[name] = copies.start(lefts[name], far_lefts[name], place.sibling())
        else:
            ref = rights[name]
            coming[name] = copies.start(ref.at[:, half_of(ref, 1 - core)], far_rights[name], place.sibling())

    arrived = set()

    def arrive(name):
        if name not in arrived:
            coming[name].wait_recv()
            arrived.add(name)

    def weight_maker(block):
        a, row, col = block
        return lambda slot: [
            (wholes[a].at[p, q, z, pl.ds(off, n), pl.ds(col * D, D)], ring.at[slot, pl.ds(at, n)])
            for p, q, z, off, n, at in row_runs(dims, slabs[a][0], row, D)
        ]

    def row_maker(ref, r0, n):
        return lambda slot: [(ref.at[pl.ds(r0, n)], rowring.at[slot, pl.ds(0, n)])]

    def pre_maker(view, j):
        r0, n = spans[view]
        block = (pl.ds(r0, n), pl.ds(j * D, D))
        return lambda slot: [
            (slope.at[block], preing.at[slot, pl.ds(0, n)]),
            (active.at[block], acting.at[slot, pl.ds(0, n)]),
        ]

    rights["d_out"][...] = cot[...].astype(BF)
    blocks = backward_blocks()
    weights = Stream(ring.shape[0], ring_sem, [weight_maker(b) for b in blocks])
    pres = Stream(2, pre_sem, [pre_maker(view, j) for view in range(3) for j in range(FF // D)])
    row_list = [(middle, *spans[view]) for view in range(3)] + [(joined, *spans[view]) for view in range(3)]
    for c in range(2):
        row_list += [(x, *spans[c]), (x, *spans[c + 1])]
    rowed = Stream(2, row_sem, [row_maker(*one) for one in row_list])
    used_blocks = []

    def weight(expected):
        assert blocks[len(used_blocks)] == expected
        used_blocks.append(expected)
        return ring.at[weights.take()][...]

    holding = {}
    for i, name in enumerate(HELD):
        holding[name] = pltpu.make_async_copy(held_in[name], held[name], held_sem.at[i])
        holding[name].start()
    for name in LEFTS:
        swap(name)

    state = {"jobs": 0, "lefts": 0, "gain": False}
    ready = {3}
    storing = {}

    def finish_stores(i):
        for one in storing.pop(i, ()):
            one.wait()

    def load_left(group, slot):
        left, lcol, lrows = group
        arrive(left)
        n = lrows[1]
        block = (pl.ds(*lrows), pl.ds(lcol * D, D))
        loads = [
            pltpu.make_async_copy(lefts[left].at[block], xs.at[slot, pl.ds(0, n)], left_sem.at[slot, 0]),
            pltpu.make_async_copy(far_lefts[left].at[block], xs.at[slot, pl.ds(n, n)], left_sem.at[slot, 1]),
        ]
        for one in loads:
            one.start()
        return loads

    def load_right(job, slot):
        block, right, rrows = job[2], job[6], job[7]
        arrive(right)
        n = rrows[1]
        ref = rights[right]
        own = pl.ds(pl.multiple_of(core * (ref.shape[1] // 2) + block * BLOCK, 128), BLOCK)
        far = (pl.ds(*rrows), pl.ds(block * BLOCK, BLOCK))
        loads = [
            pltpu.make_async_copy(ref.at[pl.ds(*rrows), own], ys.at[slot, pl.ds(0, n)], right_sem.at[slot, 0]),
            pltpu.make_async_copy(far_rights[right].at[far], ys.at[slot, pl.ds(n, n)], right_sem.at[slot, 1]),
        ]
        for one in loads:
            one.start()
        return loads

    batches = job_batches(u)

    def multiply(name, cost):
        batch = batches[name]
        groups, member = [], []
        for job in batch:
            if not groups or groups[-1] != job[3:6]:
                groups.append(job[3:6])
            member.append(len(groups) - 1)
        x0, i0 = state["lefts"], state["jobs"]
        left_loads = {k: load_left(groups[k], (x0 + k) % 2) for k in range(min(2, len(groups)))}
        right_loads = {k: load_right(batch[k], (i0 + k) % 3) for k in range(min(2, len(batch)))}
        for index, job in enumerate(batch):
            i, k = i0 + index, member[index]
            if k in left_loads:
                for one in left_loads.pop(k):
                    one.wait()
                if 0 < k < len(groups) - 1:
                    left_loads[k + 1] = load_left(groups[k + 1], (x0 + k + 1) % 2)
            for one in right_loads.pop(index):
                one.wait()
            if index + 2 < len(batch):
                right_loads[index + 2] = load_right(batch[index + 2], (i + 2) % 3)
            finish_stores(i - 2)
            n = 2 * job[5][1]
            slot = i % 2
            made[slot] = matmul_tn(xs[(x0 + k) % 2, :n], ys[i % 3, :n]).astype(BF)
            a, row, block = job[:3]
            storing[i] = [
                pltpu.make_async_copy(
                    made.at[slot, pl.ds(at, n)],
                    parts[a].at[p, q, z, pl.ds(off, n), pl.ds(block * BLOCK, BLOCK)],
                    store_sem.at[slot, j],
                )
                for j, (p, q, z, off, n, at) in enumerate(row_runs(dims, slabs[a][0], row, D))
            ]
            for one in storing[i]:
                one.start()
            yield cost
        state["lefts"] += len(groups)
        state["jobs"] += len(batch)
        for i in list(storing):
            finish_stores(i)

    g = lambda e, j: gain[pl.ds(2 * e + j, 1), :]

    def work():
        for view in range(3):
            r0, n = spans[view]
            rows = pl.ds(r0, n)
            cost = (2.0, 1.2, 0.9)[view]
            for j in range(FF // D):
                cols = pl.ds(j * D, D)
                down_block = weight((3, view * FF + j * D, 0))
                dactive = matmul_nt(rights["d_out"][rows], down_block)
                slot = pres.take()
                rights["d_pre"][rows, cols] = (dactive * preing[slot, :n]).astype(BF)
                term = matmul(acting[slot, :n], down_block)
                layer[rows] = term if j == 0 else layer[rows] + term
                weights.give_back()
                pres.give_back()
                term = matmul_nt(rights["d_pre"][rows, cols], weight((2, view * D, j)))
                weights.give_back()
                total[:n] = term if j == 0 else total[:n] + term
                yield cost
            slot = rowed.take()
            mid = rowring[slot, :n]
            layer[rows] = layer[rows] + mid
            pulled, g_sum[pl.ds(2 * view + 1, 1), :] = norm_pull(mid, g(view, 1), total[:n])
            rowed.give_back()
            flow[rows] = cot[rows] + pulled
            rights["d_attn"][rows] = flow[rows].astype(BF)
            yield 0.8
        swap("d_pre")
        swap("d_attn")
        layered = pltpu.make_async_copy(layer, layer_out, layer_sem)
        layered.start()
        dmixed = rights["d_out"]
        for view in range(3):
            rows = pl.ds(*spans[view])
            dmixed[rows] = matmul_nt(rights["d_attn"][rows], weight((1, view * D, 0))).astype(BF)
            weights.give_back()
            yield 0.7
        yield from multiply("up", 0.6)
        ready.add(2)
        for name in ("q", "kx", "vx"):
            holding[name].wait()
        layered.wait()
        dkf = layer
        halo = {}
        up, down = place.slab < count - 1, place.slab > 0
        for view in range(3):
            r0, n = spans[view]
            rows, keys = pl.ds(r0, n), pl.ds(bases[view], n + 2 * u)
            bias = slab_bias(place, count, n + 2 * u, u, 0)
            for h in range(HEADS // 2):
                cols = pl.ds(h * 128, 128)
                dq, dk, dv = attend_pair_back(
                    held["q"][rows, cols], held["kx"][keys, cols], held["vx"][keys, cols], dmixed[rows, cols], bias
                )
                rights["dq"][rows, cols] = dq.astype(BF)
                for k, (whole, own) in enumerate(((dk, dkf), (dv, dvf))):
                    halo_out[k, view, 0, :, cols] = whole[:u].astype(BF)
                    own[rows, cols] = whole[u : u + n]
                    halo_out[k, view, 1, :, cols] = whole[u + n :].astype(BF)
                yield (3.0, 1.3, 0.7)[view]
            for k in range(2):
                for side, step, ok in ((0, -1, down), (1, 1, up)):
                    halo[k, view, side] = copies.start(
                        halo_out.at[k, view, side], halo_in.at[k, view, side], halo_device(place, count, step), ok
                    )
        swap("dq")
        yield from multiply("out", 0.6)
        for view in range(3):
            r0, n = spans[view]
            rows = pl.ds(r0, n)
            for k, (own, name) in enumerate(((dkf, "dk"), (dvf, "dv"))):
                for side, edge, ok in ((0, r0 + n - u, up), (1, r0, down)):

                    def join(k=k, side=side, edge=edge, own=own):
                        halo[k, view, side].wait_recv()
                        own[pl.ds(edge, u)] = own[pl.ds(edge, u)] + halo_in[k, view, side].astype(F32)

                    when(ok, join)
                rights[name][rows] = own[rows].astype(BF)
            for j, name in enumerate(("dq", "dk", "dv")):
                term = matmul_nt(rights[name][rows], weight((0, (3 * view + j) * D, 0)))
                weights.give_back()
                total[:n] = term if j == 0 else total[:n] + term
                yield 0.7
            slot = rowed.take()
            pulled, g_sum[pl.ds(2 * view, 1), :] = norm_pull(rowring[slot, :n], g(view, 0), total[:n])
            rowed.give_back()
            flow[rows] = flow[rows] + pulled
            yield 0.6
        swap("dk")
        swap("dv")
        rights["d_cross"][...] = flow[pl.ds(0, 6 * u)].astype(BF)
        swap("d_cross")
        for name in ("cq", "ck", "cv"):
            holding[name].wait()
        yield from multiply("qkv", 0.6)
        for c in range(2):
            r0, n = spans[c]
            k0, m = spans[c + 1]
            rows, keys = pl.ds(r0, n), pl.ds(k0 - 4 * u, m)
            dmixed[rows] = matmul_nt(rights["d_cross"][rows], weight((1, (3 + c) * D, 0))).astype(BF)
            weights.give_back()
            yield 0.7
            for h in range(HEADS // 2):
                cols = pl.ds(h * 128, 128)
                dq, dk, dv = attend_pair_back(
                    held["cq"][rows, cols], held["ck"][keys, cols], held["cv"][keys, cols], dmixed[rows, cols], None
                )
                rights["dcq"][rows, cols] = dq.astype(BF)
                rights["dck"][keys, cols] = dk.astype(BF)
                rights["dcv"][keys, cols] = dv.astype(BF)
                yield (1.5, 0.6)[c]
            term = matmul_nt(rights["dcq"][rows], weight((0, (9 + 3 * c) * D, 0)))
            weights.give_back()
            slot = rowed.take()
            pulled, g_sum[pl.ds(2 * (3 + c), 1), :] = norm_pull(rowring[slot, :n], g(3 + c, 0), term)
            rowed.give_back()
            flow[rows] = flow[rows] + pulled
            yield 1.0
            term = matmul_nt(rights["dck"][keys], weight((0, (10 + 3 * c) * D, 0)))
            weights.give_back()
            term = term + matmul_nt(rights["dcv"][keys], weight((0, (11 + 3 * c) * D, 0)))
            weights.give_back()
            slot = rowed.take()
            pulled, g_sum[pl.ds(2 * (3 + c) + 1, 1), :] = norm_pull(rowring[slot, :m], g(3 + c, 1), term)
            rowed.give_back()
            late = pl.ds(k0, m)
            flow[late] = flow[late] + pulled
            yield 1.0
        for name in ("dcq", "dck", "dcv"):
            swap(name)
        yield from multiply("cout", 0.6)
        ready.add(1)
        token = pltpu.make_async_copy(flow, token_out, final_sem.at[4])
        token.start()
        g_sum[pl.ds(10, 6), :] = jnp.zeros((6, D), F32)
        g_own[...] = gain_tiles(g_sum[...], 2 * dims[0] * dims[1] * dims[2] * 8, own_gains).reshape(g_own.shape)
        coming["gain"] = copies.start(g_own, g_far, place.sibling())
        yield 1.0
        yield from multiply("cqkv", 0.6)
        ready.add(0)
        state["gain"] = True
        token.wait()

    left_in = {a: sum(1 for piece in pieces if piece[0] == a) for a in range(4)}
    count_pieces = sum(left_in.values())
    bases_of = [sum(POOLS[:k]) for k in range(len(POOLS))]
    free = {k: [[bases_of[k] + j, None, None] for j in range(POOLS[k])] for k in range(len(POOLS))}
    owners = []
    ending = []

    def gains():
        coming["gain"].wait_recv()
        add_to(g_far, g_own)
        source = lambda dim, value: g_far.at[(*[value if d == dim else slice(None) for d in range(3)], core)]

        def finish(value):
            g_first[0, 0] = value
            copy = pltpu.make_async_copy(g_first.at[0, 0], gain_out, final_sem.at[5])
            copy.start()
            copy.wait()

        yield from reduce_piece(
            copies, place, source, (0, 1, 2), g_acc, g_first, g_turns, g_last, local.at[SLOTS], Credits(None, False), finish
        )

    def begin(piece):
        if piece[0] == "gain":
            return gains()
        a, row, block, order, _ = piece
        kind = ORDERS.index(order)
        buffer = free[kind].pop(0)
        slot, before, _ = buffer
        if before is not None:
            before.drain()
        mine = Copies(send, recv)
        mine.used = COPIES - 9 * (count_pieces - len(owners))
        owners.append(mine)
        buffer[1] = mine
        cols = pl.ds(block * BLOCK, BLOCK)
        single = order[1] != 2
        k = slot - sum(POOLS[:4]) if single else slot
        turns, last = ((turns_a, last_a), (turns_b, last_b))[single]

        def source(dim, value):
            index = [slice(None)] * 3
            index[dim] = value
            return parts[a].at[(*index, pl.ds(row, ROWS), cols)]

        def finish(value):
            finals[a][pl.ds(row, ROWS), cols] = value
            left_in[a] -= 1
            free[kind].append(buffer)
            if left_in[a] == 0:
                deliver(a)

        credits = Credits(credit.at[slot], before is not None)
        buffer[2] = credits
        return reduce_piece(
            mine, place, source, order[::-1], acc.at[slot], first.at[slot], turns.at[k], last.at[k], local.at[slot], credits, finish
        )

    def deliver(a):
        rows, width = slabs[a][0] // 2, slabs[a][1] // 2
        cols = pl.ds(pl.multiple_of(core * width, 128), width)
        ending.append(
            copies.start(
                finals[a].at[pl.ds(pl.multiple_of((1 - core) * rows, 8), rows)], results[a].at[:, cols], place.sibling()
            )
        )
        keep = pltpu.make_async_copy(
            finals[a].at[pl.ds(pl.multiple_of(core * rows, 8), rows)], results[a].at[:, cols], final_sem.at[a]
        )
        keep.start()
        keep.wait()

    def piece_ready(piece):
        if piece[0] == "gain":
            return state["gain"]
        return piece[0] in ready and bool(free[ORDERS.index(piece[3])])

    weave(march_ready(pieces, begin, piece_ready), work(), lambda: EACH[min(len(ready) - 1, 2)])
    for buffers in free.values():
        for slot, user, credits in buffers:
            if user is not None:
                credits.settle(place)
    for one in ending:
        one.wait_recv()
    copies.drain()
    for one in owners:
        one.drain()
    assert copies.used <= COPIES - 9 * count_pieces


def reduce_all(dims, slabs, own_gains, wholes, down_part, cot, gain, x, kept):
    anywhere = pl.BlockSpec(memory_space=pl.ANY)
    vmem = pl.BlockSpec(memory_space=pltpu.VMEM)
    pieces = pieces_of(slabs, (3, 2, 1, 0), REDUCE_PLAN)
    pieces.insert(len(pieces) - 8, ("gain", 0, 0, None, pieces[-9][4]))
    bundled, single = sum(POOLS[:4]), sum(POOLS[4:])
    z = dims[2]
    rows = cot.shape[0]
    u = rows // 7
    tile = (ROWS, BLOCK)
    segments = max(D // slab[0] + 2 for slab in slabs)
    lefts = [kept[k] for k in LEFTS]
    held = [kept[k] for k in HELD]
    rights = right_shapes(rows)
    outs = pl.pallas_call(
        functools.partial(reduce_kernel, dims, slabs, pieces, own_gains),
        out_shape=[jax.ShapeDtypeStruct((rows, D), F32)] * 2
        + [jax.ShapeDtypeStruct((s[0] // 2, s[1]), F32) for s in slabs]
        + [jax.ShapeDtypeStruct((8, 128), F32)]
        + [jax.ShapeDtypeStruct((*dims, s[0], s[1] // 2), BF) for s in slabs[:3]]
        + [jax.ShapeDtypeStruct(one.shape, BF) for one in lefts]
        + [jax.ShapeDtypeStruct((r, w // 2), BF) for r, w in rights],
        in_specs=[anywhere] * 4 + [vmem] * 2 + [anywhere] * 18,
        out_specs=[anywhere] * 26,
        scratch_shapes=[pltpu.VMEM(s, BF) for s in rights]
        + [pltpu.VMEM(one.shape, BF) for one in held]
        + [
            pltpu.VMEM((SLOTS, 2, z, *tile), BF),
            pltpu.VMEM((SLOTS, 2, z, *tile), BF),
            pltpu.VMEM((bundled, z - 1, 2, 2, *tile), BF),
            pltpu.VMEM((single, z - 1, 2, *tile), BF),
            pltpu.VMEM((bundled, *tile), BF),
            pltpu.VMEM((single, z, *tile), BF),
        ]
        + [pltpu.VMEM((s[0], s[1] // 2), F32) for s in slabs]
        + [
            pltpu.VMEM((2, 8 * u, D), BF),
            pltpu.VMEM((3, 8 * u, BLOCK), BF),
            pltpu.VMEM((2, D, BLOCK), BF),
            pltpu.VMEM((*dims, 2, 8, 128), F32),
            pltpu.VMEM((*dims, 2, 8, 128), F32),
            pltpu.VMEM((2, z, 8, 128), F32),
            pltpu.VMEM((2, z, 8, 128), F32),
            pltpu.VMEM((z - 1, 2, 8, 128), F32),
            pltpu.VMEM((z, 8, 128), F32),
            pltpu.VMEM((16, D), F32),
            pltpu.VMEM((4, D, D), BF),
            pltpu.VMEM((2, 4 * u, D), F32),
            pltpu.VMEM((2, 4 * u, D), F32),
            pltpu.VMEM((2, 4 * u, D), BF),
            pltpu.VMEM((rows, D), F32),
            pltpu.VMEM((rows, D), F32),
            pltpu.VMEM((4 * u, D), F32),
            pltpu.VMEM((rows, D), F32),
            pltpu.VMEM((2, 3, 2, u, D), BF),
            pltpu.VMEM((2, 3, 2, u, D), BF),
            pltpu.SemaphoreType.DMA((COPIES,)),
            pltpu.SemaphoreType.DMA((COPIES,)),
            pltpu.SemaphoreType.DMA((SLOTS + 1,)),
            pltpu.SemaphoreType.DMA((2, 2)),
            pltpu.SemaphoreType.DMA((3, 2)),
            pltpu.SemaphoreType.DMA((2, segments)),
            pltpu.SemaphoreType.DMA((6,)),
            pltpu.SemaphoreType.DMA((4, segments)),
            pltpu.SemaphoreType.DMA((2, 1)),
            pltpu.SemaphoreType.DMA((2, 2)),
            pltpu.SemaphoreType.DMA((6,)),
            pltpu.SemaphoreType.DMA,
            pltpu.SemaphoreType.REGULAR((SLOTS, 2 + 2 * (z - 1))),
        ],
        compiler_params=pltpu.CompilerParams(collective_id=1, has_side_effects=True, vmem_limit_bytes=63 << 20),
    )(*wholes, cot, gain, x, kept["joined"], kept["middle"], kept["slope"], kept["active"], down_part, *lefts, *held)
    return outs[:7]


def plain_device(tokens, cotangent, qkv_weights, out_weights, up_weights, down_weights, gains):
    rows = tokens[0]
    incoming = cotangent[0]
    spatial = rows.shape[0] // 7
    bounds = ((0, 4 * spatial), (4 * spatial, 6 * spatial), (6 * spatial, 7 * spatial))
    qkv, outw, upw, downw, gain_low = unstack(
        (
            lax.all_gather(qkv_weights, ("seq", "tm"), axis=0, tiled=True),
            lax.all_gather(out_weights, ("seq", "tm"), axis=0, tiled=True),
            lax.all_gather(up_weights, ("seq", "tm"), axis=0, tiled=True),
            lax.all_gather(down_weights, ("seq", "tm"), axis=0, tiled=True),
            lax.all_gather(gains, ("seq", "tm"), axis=0, tiled=True),
        )
    )
    gain = gain_low.astype(jnp.float32)
    place = lax.axis_index("tm")
    count = lax.axis_size("tm")
    below_bias = jnp.where(place > 0, 0.0, FAR).astype(jnp.float32)
    above_bias = jnp.where(place < count - 1, 0.0, FAR).astype(jnp.float32)
    views = [rows[start:stop] for start, stop in bounds]
    cross_keep = []
    joined = []
    for view in range(2):
        first = lowered(norm_rows(views[view], gain[3 + view, 0]))
        second = lowered(norm_rows(views[view + 1], gain[3 + view, 1]))
        query = lowered(product(first, qkv[3 + view, 0]))
        keys = lowered(product(second, qkv[3 + view, 1]))
        values = lowered(product(second, qkv[3 + view, 2]))
        mixed, probs = attend(query, keys, values, 0.0)
        joined.append(views[view] + product(mixed, outw[3 + view]))
        cross_keep.append((first, second, query, keys, values, mixed, probs))
    joined.append(views[2])
    local_keep = []
    edges = []
    for view in range(3):
        normed = lowered(norm_rows(joined[view], gain[view, 0]))
        query = lowered(product(normed, qkv[view, 0]))
        keys = lowered(product(normed, qkv[view, 1]))
        values = lowered(product(normed, qkv[view, 2]))
        local_keep.append((normed, query, keys, values))
        paired = jnp.stack([keys, values])
        edges.append(jnp.concatenate([paired[:, :spatial], paired[:, -spatial:]], axis=1))
    rim = extended(jnp.stack(edges, axis=1), (("tm", 2),), spatial)
    self_keep = []
    outputs = []
    for view in range(3):
        normed, query, keys, values = local_keep[view]
        length = keys.shape[0]
        keys_all = jnp.concatenate(
            [rim[0, view, :spatial], keys, rim[0, view, 3 * spatial :]], axis=0
        )
        values_all = jnp.concatenate(
            [rim[1, view, :spatial], values, rim[1, view, 3 * spatial :]], axis=0
        )
        bias = jnp.concatenate(
            [
                jnp.broadcast_to(below_bias, (spatial,)),
                jnp.zeros((length,), jnp.float32),
                jnp.broadcast_to(above_bias, (spatial,)),
            ]
        )
        mixed, probs = attend(query, keys_all, values_all, bias)
        middle = joined[view] + product(mixed, outw[view])
        normed_two = lowered(norm_rows(middle, gain[view, 1]))
        hidden_pre = product(normed_two, upw[view])
        active = lowered(jax.nn.gelu(hidden_pre, approximate=False))
        outputs.append(middle + product(active, downw[view]))
        self_keep.append(
            (
                normed,
                query,
                keys_all,
                values_all,
                mixed,
                probs,
                middle,
                normed_two,
                hidden_pre,
                active,
            )
        )
    layer_out = jnp.concatenate(outputs, axis=0)[None]
    qkv, outw, upw, downw, gain_low = unstack(
        (
            lax.all_gather(qkv_weights, ("seq", "tm"), axis=0, tiled=True),
            lax.all_gather(out_weights, ("seq", "tm"), axis=0, tiled=True),
            lax.all_gather(up_weights, ("seq", "tm"), axis=0, tiled=True),
            lax.all_gather(down_weights, ("seq", "tm"), axis=0, tiled=True),
            lax.all_gather(gains, ("seq", "tm"), axis=0, tiled=True),
        )
    )
    grad_qkv = [[None, None, None] for index in range(5)]
    grad_out = [None] * 5
    grad_up = [None] * 3
    grad_down = [None] * 3
    grad_gain = [[None, None] for index in range(5)]
    halves = []
    for view in range(3):
        (
            normed,
            query,
            keys_all,
            values_all,
            mixed,
            probs,
            middle,
            normed_two,
            hidden_pre,
            active,
        ) = self_keep[view]
        start, stop = bounds[view]
        dfinal = incoming[start:stop]
        dbranch = lowered(dfinal)
        grad_down[view] = product_tn(active, dbranch)
        dactive = product_nt(dbranch, downw[view])
        dpre_low = lowered(gelu_back(hidden_pre, dactive))
        grad_up[view] = product_tn(normed_two, dpre_low)
        dnormed_two = product_nt(dpre_low, upw[view])
        dmid_norm, grad_gain[view][1] = norm_back(middle, gain[view, 1], dnormed_two)
        dmiddle = dfinal + dmid_norm
        dattn = lowered(dmiddle)
        grad_out[view] = product_tn(mixed, dattn)
        dmixed = lowered(product_nt(dattn, outw[view]))
        dquery, dkeys, dvalues = attend_back(query, keys_all, values_all, probs, dmixed)
        halves.append((dmiddle, dquery, dkeys, dvalues))
    lower_part = jnp.stack(
        [jnp.stack([half[2][:spatial], half[3][:spatial]]) for half in halves], axis=1
    )
    upper_part = jnp.stack(
        [jnp.stack([half[2][-spatial:], half[3][-spatial:]]) for half in halves], axis=1
    )
    from_above = from_behind(lower_part.astype(jnp.bfloat16), "tm", -1).astype(lower_part.dtype)
    from_below = from_behind(upper_part.astype(jnp.bfloat16), "tm", 1).astype(upper_part.dtype)
    dfused = []
    for view in range(3):
        dmiddle, dquery, dkeys, dvalues = halves[view]
        normed = self_keep[view][0]
        length = dquery.shape[0]
        own_keys = dkeys[spatial : spatial + length]
        own_values = dvalues[spatial : spatial + length]
        own_keys = (
            own_keys.at[:spatial]
            .add(from_below[0, view])
            .at[length - spatial :]
            .add(from_above[0, view])
        )
        own_values = (
            own_values.at[:spatial]
            .add(from_below[1, view])
            .at[length - spatial :]
            .add(from_above[1, view])
        )
        dq_low = lowered(dquery)
        dk_low = lowered(own_keys)
        dv_low = lowered(own_values)
        grad_qkv[view] = [
            product_tn(normed, dq_low),
            product_tn(normed, dk_low),
            product_tn(normed, dv_low),
        ]
        dnormed = (
            product_nt(dq_low, qkv[view, 0])
            + product_nt(dk_low, qkv[view, 1])
            + product_nt(dv_low, qkv[view, 2])
        )
        dfused_norm, grad_gain[view][0] = norm_back(joined[view], gain[view, 0], dnormed)
        dfused.append(dmiddle + dfused_norm)
    dviews = list(dfused)
    for view in range(2):
        first, second, query, keys, values, mixed, probs = cross_keep[view]
        dbranch = lowered(dfused[view])
        grad_out[3 + view] = product_tn(mixed, dbranch)
        dmixed = lowered(product_nt(dbranch, outw[3 + view]))
        dquery, dkeys, dvalues = attend_back(query, keys, values, probs, dmixed)
        dq_low = lowered(dquery)
        dk_low = lowered(dkeys)
        dv_low = lowered(dvalues)
        grad_qkv[3 + view] = [
            product_tn(first, dq_low),
            product_tn(second, dk_low),
            product_tn(second, dv_low),
        ]
        dfirst = product_nt(dq_low, qkv[3 + view, 0])
        dsecond = product_nt(dk_low, qkv[3 + view, 1]) + product_nt(dv_low, qkv[3 + view, 2])
        dx_first, grad_gain[3 + view][0] = norm_back(views[view], gain[3 + view, 0], dfirst)
        dx_second, grad_gain[3 + view][1] = norm_back(views[view + 1], gain[3 + view, 1], dsecond)
        dviews[view] = dviews[view] + dx_first
        dviews[view + 1] = dviews[view + 1] + dx_second
    token_grad = jnp.concatenate(dviews, axis=0)[None]
    qkv_total = jnp.stack([jnp.stack(entry) for entry in grad_qkv]).reshape(15 * D, D)
    out_total = jnp.stack(grad_out).reshape(5 * D, D)
    gain_total = jnp.stack([jnp.stack(entry) for entry in grad_gain]).reshape(10 * D)
    totals = (
        qkv_total,
        out_total,
        jnp.stack(grad_up).reshape(3 * D, FF),
        jnp.stack(grad_down).reshape(3 * FF, D),
        gain_total,
    )
    shares = (
        lax.psum_scatter(totals[0], ("seq", "tm"), scatter_dimension=0, tiled=True),
        lax.psum_scatter(totals[1], ("seq", "tm"), scatter_dimension=0, tiled=True),
        lax.psum_scatter(totals[2], ("seq", "tm"), scatter_dimension=0, tiled=True),
        lax.psum_scatter(totals[3], ("seq", "tm"), scatter_dimension=0, tiled=True),
        lax.psum_scatter(totals[4], ("seq", "tm"), scatter_dimension=0, tiled=True),
    )
    return (layer_out, token_grad, shares[0], shares[1], shares[2], shares[3], shares[4])


def per_device(dims, tokens, cotangent, qkv_weights, out_weights, up_weights, down_weights, gains):
    rows = tokens[0]
    own_gains = gains.shape[0]
    tile = jnp.pad(gains.astype(F32).reshape(-1, 48), ((0, 8 - own_gains // 48), (0, 80)))
    shards = (qkv_weights, out_weights, up_weights, down_weights)
    slabs = tuple((2 * w.shape[0], w.shape[1]) for w in shards)
    wholes, gain, down_part, kept = gather_all(dims, own_gains, shards, tile, rows, cotangent[0])
    shares = reduce_all(dims, slabs, own_gains, wholes, down_part, cotangent[0], gain, rows, kept)
    gain_share = shares[6][: own_gains // 48, :48].reshape(own_gains)
    return (shares[1][None], shares[0][None], *shares[2:6], gain_share)


def fits(mesh, dims):
    chips = dims[0] * dims[1] * dims[2]
    rows = (15 * D, 5 * D, 3 * D, 3 * FF)
    return dims[:2] == (2, 2) and all(r % (chips * ROWS) == 0 for r in rows) and (10 * D) % (2 * chips * 48) == 0 and 10 * D // (2 * chips) <= 384


def solution(mesh):
    seq, tm = mesh.shape["seq"], mesh.shape["tm"]
    dims = (2, seq // 2, tm // 2)
    body = functools.partial(per_device, dims) if fits(mesh, dims) else plain_device
    placed = (
        P("seq", "tm", None),
        P("seq", "tm", None),
        P(("seq", "tm"), None),
        P(("seq", "tm"), None),
        P(("seq", "tm"), None),
        P(("seq", "tm"), None),
        P(("seq", "tm")),
    )
    return jax.shard_map(body, mesh=mesh, in_specs=placed, out_specs=placed, check_vma=False)
```

```python
import functools

import jax
import jax.numpy as jnp
from jax import lax
from jax.experimental import pallas as pl
from jax.experimental.pallas import tpu as pltpu
from jax.sharding import PartitionSpec as P

D = 768
HEADS = 12
FF = 3072

EPS = 1e-06
FAR = -1e30
MESH = pl.DeviceIdType.MESH
BF = jnp.bfloat16
F32 = jnp.float32
BLOCK = D // 2
ROWS = 48
POOLS = (0, 0, 8, 8, 4, 4)
SLOTS = sum(POOLS)
EACH = (1.51, 0.49, 0.68, 0.42)
EACH_FORWARD = 1.07
COPIES = 480


def extended(cells, sides, width):
    for axis, dim in sides:
        count = lax.axis_size(axis)
        ends = count - 1
        head = lax.slice_in_dim(cells, 0, width, axis=dim)
        tail = lax.slice_in_dim(cells, cells.shape[dim] - width, cells.shape[dim], axis=dim)
        cells = jnp.concatenate(
            [
                lax.ppermute(tail, axis, [(i, (i + 1) % count) for i in range(ends)]),
                cells,
                lax.ppermute(head, axis, [((i + 1) % count, i) for i in range(ends)]),
            ],
            axis=dim,
        )
    return cells


def from_behind(block, axis, distance):
    devices = range(lax.axis_size(axis))
    route = [(i - distance, i) for i in devices if i - distance in devices]
    return lax.ppermute(block, axis, route)


def norm_rows(x, gain):
    mean = jnp.mean(x, axis=-1, keepdims=True)
    centered = x - mean
    spread = jnp.mean(centered * centered, axis=-1, keepdims=True)
    return centered * lax.rsqrt(spread + EPS) * gain


def norm_back(x, gain, grad):
    unused, pull = jax.vjp(norm_rows, x, gain)
    return pull(grad)


def gelu_back(hidden_pre, grad):
    unused, pull = jax.vjp(lambda value: jax.nn.gelu(value, approximate=False), hidden_pre)
    return pull(grad)[0]


def lowered(value):
    return value.astype(jnp.bfloat16)


def product(left, right):
    return jnp.dot(left, right, preferred_element_type=jnp.float32)


def product_tn(left, right):
    return lax.dot_general(
        left, right, (((0,), (0,)), ((), ())), preferred_element_type=jnp.float32
    )


def product_nt(left, right):
    return lax.dot_general(
        left, right, (((1,), (1,)), ((), ())), preferred_element_type=jnp.float32
    )


def unstack(parts):
    qkv_flat, out_flat, up_flat, down_flat, gain_flat = parts
    return (
        qkv_flat.reshape(5, 3, D, D),
        out_flat.reshape(5, D, D),
        up_flat.reshape(3, D, FF),
        down_flat.reshape(3, FF, D),
        gain_flat.reshape(5, 2, D),
    )


def attend(query, keys, values, bias):
    rows, width = query.shape
    depth = width // HEADS
    qh = query.reshape(rows, HEADS, depth)
    kh = keys.reshape(keys.shape[0], HEADS, depth)
    vh = values.reshape(values.shape[0], HEADS, depth)
    scores = (
        jnp.einsum("qhd,khd->hqk", qh, kh, preferred_element_type=jnp.float32) * depth ** (-0.5)
        + bias
    )
    top = jnp.max(scores, axis=-1, keepdims=True)
    expo = jnp.exp(scores - top)
    probs = expo / jnp.sum(expo, axis=-1, keepdims=True)
    mixed = jnp.einsum("hqk,khd->qhd", lowered(probs), vh, preferred_element_type=jnp.float32)
    return (lowered(mixed.reshape(rows, width)), probs)


def attend_back(query, keys, values, probs, grad_mixed):
    rows, width = query.shape
    depth = width // HEADS
    qh = query.reshape(rows, HEADS, depth)
    kh = keys.reshape(keys.shape[0], HEADS, depth)
    vh = values.reshape(values.shape[0], HEADS, depth)
    gh = grad_mixed.reshape(rows, HEADS, depth)
    dprobs = jnp.einsum("qhd,khd->hqk", gh, vh, preferred_element_type=jnp.float32)
    dvalues = jnp.einsum("hqk,qhd->khd", lowered(probs), gh, preferred_element_type=jnp.float32)
    inner = jnp.sum(dprobs * probs, axis=-1, keepdims=True)
    dscores = lowered(probs * (dprobs - inner))
    scale = depth ** (-0.5)
    dquery = jnp.einsum("hqk,khd->qhd", dscores, kh, preferred_element_type=jnp.float32) * scale
    dkeys = jnp.einsum("hqk,qhd->khd", dscores, qh, preferred_element_type=jnp.float32) * scale
    return (dquery.reshape(rows, width), dkeys.reshape(-1, width), dvalues.reshape(-1, width))


class Place:
    def __init__(self, dims):
        self.dims = dims
        s = lax.axis_index("seq")
        t = lax.axis_index("tm")
        self.at = (s // dims[1], s % dims[1], t // 2)
        self.core = t % 2
        self.slab = t

    def device(self, at, core):
        return (at[0] * self.dims[1] + at[1], at[2] * 2 + core)

    def along(self, dim, value):
        at = list(self.at)
        at[dim] = value
        return self.device(at, self.core)

    def sibling(self):
        return self.device(self.at, 1 - self.core)


def meet(place):
    barrier = pltpu.get_barrier_semaphore()
    count = 1
    pl.semaphore_signal(barrier, inc=1, device_id=place.sibling(), device_id_type=MESH)
    for dim, n in enumerate(place.dims):
        me = place.at[dim]
        for step in (1, -1):
            ok = (me + step >= 0) & (me + step < n)

            @pl.when(ok)
            def _():
                pl.semaphore_signal(barrier, inc=1, device_id=place.along(dim, me + step), device_id_type=MESH)

            count = count + jnp.where(ok, 1, 0)
    step = 2 * place.core - 1
    ok = (place.at[2] + step >= 0) & (place.at[2] + step < place.dims[2])

    @pl.when(ok)
    def _():
        beside = (place.at[0], place.at[1], place.at[2] + step)
        pl.semaphore_signal(barrier, inc=1, device_id=place.device(beside, 1 - place.core), device_id_type=MESH)

    count = count + jnp.where(ok, 1, 0)
    pl.semaphore_wait(barrier, count)


class Copies:
    def __init__(self, send, recv):
        self.send, self.recv = send, recv
        self.used = 0
        self.sent = []

    def start(self, src, dst, device, ok=None):
        copy = pltpu.make_async_remote_copy(
            src_ref=src,
            dst_ref=dst,
            send_sem=self.send.at[self.used],
            recv_sem=self.recv.at[self.used],
            device_id=device,
            device_id_type=MESH,
        )
        self.used += 1
        when(ok, copy.start)
        self.sent.append((copy, ok))
        return copy

    def drain(self):
        for copy, ok in self.sent:
            when(ok, copy.wait_send)
        self.sent = []


def when(ok, action):
    if ok is None:
        action()
    else:

        @pl.when(ok)
        def _():
            action()


def gather_line(copies, place, dim, pick):
    n = place.dims[dim]
    me = place.at[dim]
    if n == 2:
        part = pick(me)
        copy = copies.start(part, part, place.along(dim, 1 - me))
        yield
        copy.wait_recv()
        return
    before = {}
    for hop in range(1, n):
        for step in (1, -1):
            origin = me - step * (hop - 1)
            held = (origin >= 0) & (origin < n)
            if hop > 1:
                when(held, before[step].wait_recv)
            ok = held & (me + step >= 0) & (me + step < n)
            part = pick(jnp.clip(origin, 0, n - 1))
            before[step] = copies.start(part, part, place.along(dim, jnp.clip(me + step, 0, n - 1)), ok)
        yield
    for step in (1, -1):
        origin = me - step * (n - 1)
        when((origin >= 0) & (origin < n), before[step].wait_recv)


def gather_piece(copies, place, full, rows, cols, order, pair):
    done = set()
    for dim in order:

        def pick(value):
            index = [slice(None) if d in done else place.at[d] for d in range(3)]
            index[dim] = value
            return full.at[(*index, pl.ds(*rows), cols)]

        yield from gather_line(copies, place, dim, pick)
        done.add(dim)
    if pair is not None:
        part = full.at[:, :, :, pl.ds(*rows), cols]
        pair.append(copies.start(part, part, place.sibling()))


XYZ, YXZ, XZY, YZX, ZXY, ZYX = (1, 0, 2), (0, 1, 2), (1, 2, 0), (0, 2, 1), (2, 1, 0), (2, 0, 1)
ORDERS = (XYZ, YXZ, XZY, YZX, ZXY, ZYX)
CYCLE = (2, 3, 4, 2, 3, 5)
GATHER_PLAN = (
    (5, 0), (5, 0), (4, 0), (5, 1), (2, 2), (5, 2), (4, 2), (5, 3), (2, 3), (1, 3), (3, 3),
    (4, 3), (5, 3), (5, 3), (4, 3), (2, 4), (5, 4), (4, 4), (4, 4), (5, 4), (4, 5), (3, 5),
    (2, 5), (3, 5), (3, 5), (1, 5), (2, 5), (4, 5), (3, 5), (4, 5), (0, 5), (5, 5), (2, 6),
    (5, 6), (4, 6), (5, 6), (5, 7), (1, 7), (2, 7), (1, 7), (4, 7), (0, 7), (0, 7), (5, 7),
)
REDUCE_PLAN = (
    (3, 0), (2, 0), (3, 0), (3, 0), (2, 0), (2, 0), (3, 0), (2, 0), (2, 1), (5, 1), (3, 2),
    (3, 2), (2, 2), (3, 2), (2, 2), (4, 2), (5, 2), (3, 4), (5, 4), (4, 4), (4, 4), (5, 4),
    (2, 4), (2, 4), (3, 4), (3, 4), (2, 4), (2, 4), (3, 5), (2, 6), (3, 6), (2, 6), (2, 6),
    (4, 6), (5, 6), (3, 6), (3, 6), (4, 6), (5, 6), (2, 6), (5, 6), (4, 6), (4, 6), (5, 6),
)


def pieces_of(slabs, arrays, plan):
    flat = []
    for array in arrays:
        rows, width = slabs[array]
        for block in range(width // 2 // BLOCK):
            for row in range(0, rows, ROWS):
                i = len(flat)
                order, start = plan[i] if i < len(plan) else (CYCLE[i % 6], plan[-1][1] + (i - len(plan)) // 6)
                flat.append((array, row, block, ORDERS[order], start))
    return flat


def march(pieces, begin, extra=()):
    waiting = list(pieces)
    active = list(extra)
    step = 0
    while active or waiting:
        while waiting and step >= waiting[0][4]:
            active.append(begin(waiting.pop(0)))
        still = []
        for one in active:
            try:
                yield next(one)
                still.append(one)
            except StopIteration:
                pass
        active = still
        step += 1


def weave(comm, work, each):
    live = [True, True]
    gate = [None, None]
    sources = (comm, work)

    def advance(k):
        if not live[k]:
            return None
        if gate[k] is not None:
            if not gate[k]():
                return None
            gate[k] = None
        try:
            item = next(sources[k])
        except StopIteration:
            live[k] = False
            return None
        if callable(item):
            gate[k] = item
            return 0.0
        return item or 0.0

    credit = 0.0
    while live[0] or live[1]:
        moved = advance(0)
        if moved is not None:
            credit = min(credit + each(), 4.0)
        stuck = moved is None
        while live[1] and (credit > 0 or stuck):
            cost = advance(1)
            if cost is None:
                break
            credit = max(credit - cost, -8.0)
            if stuck and live[0] and (gate[0] is None or gate[0]()):
                break


def matmul(left, right):
    return jnp.dot(left, right, preferred_element_type=F32)


def matmul_nt(left, right):
    return lax.dot_general(left, right, (((1,), (1,)), ((), ())), preferred_element_type=F32)


def matmul_tn(left, right):
    return lax.dot_general(left, right, (((0,), (0,)), ((), ())), preferred_element_type=F32)


def halves_of(pair):
    low = lax.broadcasted_iota(jnp.int32, pair.shape, 1) < pair.shape[1] // 2
    zero = jnp.zeros_like(pair)
    return jnp.where(low, pair, zero), jnp.where(low, zero, pair)


def softmax_rows(scores):
    expo = jnp.exp(scores - jnp.max(scores, axis=-1, keepdims=True))
    return expo * (1.0 / jnp.sum(expo, axis=-1, keepdims=True))


def attend_pair(query, keys, values, bias):
    outs = []
    for part in halves_of(query):
        scores = matmul_nt(part, keys) * 0.125
        if bias is not None:
            scores = scores + bias
        outs.append(matmul(softmax_rows(scores).astype(BF), values))
    low = lax.broadcasted_iota(jnp.int32, outs[0].shape, 1) < outs[0].shape[1] // 2
    return jnp.where(low, outs[0], outs[1]).astype(BF)


def gain_table(tiles, own):
    rows = tiles.shape[0]
    filled = own // 48
    r = lax.broadcasted_iota(jnp.int32, (rows, D), 0)
    c = lax.broadcasted_iota(jnp.int32, (rows, D), 1)
    spread = (lax.broadcasted_iota(jnp.int32, (128, D), 0) == lax.broadcasted_iota(jnp.int32, (128, D), 1) % 48)
    wide = matmul(tiles.astype(BF), spread.astype(BF))
    flat = (r // 8) * filled + r % 8
    wide = jnp.where((r % 8 < filled) & (c // 48 == flat % 16), wide, 0.0).astype(BF)
    rr = lax.broadcasted_iota(jnp.int32, (16, rows), 1)
    vv = lax.broadcasted_iota(jnp.int32, (16, rows), 0)
    pick = (rr % 8 < filled) & (((rr // 8) * filled + rr % 8) // 16 == vv)
    return matmul(pick.astype(BF), wide)


def row_runs(dims, slab, row, count):
    at, end = row, row + count
    while at < end:
        chip, off = at // slab, at % slab
        n = min(end - at, slab - off)
        yield chip // (dims[1] * dims[2]), chip // dims[2] % dims[1], chip % dims[2], off, n, at - row
        at += n


class Weights:
    def __init__(self, dims, slabs, wholes, ring, sems, blocks):
        self.dims, self.slabs, self.wholes, self.ring, self.sems, self.blocks = dims, slabs, wholes, ring, sems, blocks
        self.depth = ring.shape[0]
        self.loading = {}
        self.next_load = 0
        self.next_use = 0
        self.ready = set()

    def fetch(self):
        while self.next_load < min(len(self.blocks), self.next_use + self.depth):
            i = self.next_load
            a, row, block = self.blocks[i]
            if a not in self.ready:
                return
            slot = i % self.depth
            copies = []
            at, end = row, row + D
            slab = self.slabs[a][0]
            while at < end:
                chip, off = at // slab, at % slab
                n = min(end - at, slab - off)
                p, q, z = chip // (self.dims[1] * self.dims[2]), chip // self.dims[2] % self.dims[1], chip % self.dims[2]
                copies.append(
                    pltpu.make_async_copy(
                        self.wholes[a].at[p, q, z, pl.ds(off, n), pl.ds(block * D, D)],
                        self.ring.at[slot, pl.ds(at - row, n)],
                        self.sems.at[slot, len(copies)],
                    )
                )
                at += n
            for one in copies:
                one.start()
            self.loading[i] = copies
            self.next_load += 1

    def take(self, expected):
        i = self.next_use
        assert self.blocks[i] == expected, (self.blocks[i], expected)
        self.fetch()
        for one in self.loading.pop(i):
            one.wait()
        return self.ring.at[i % self.depth]

    def give_back(self):
        self.next_use += 1
        self.fetch()


def forward_blocks():
    blocks = [(0, (9 + i) * D, 0) for i in range(6)]
    blocks += [(1, 3 * D, 0), (1, 4 * D, 0)]
    blocks += [(0, i * D, 0) for i in range(9)]
    blocks += [(1, i * D, 0) for i in range(3)]
    blocks += [(2, v * D, j) for v in range(3) for j in range(FF // D)]
    return blocks


KEPT = ("first", "second", "cq", "ck", "cv", "cmixed", "joined", "normed", "q", "kx", "vx", "mixed", "middle", "normed_two", "slope", "active")


def forward_shapes(rows):
    u = rows // 7
    sizes = dict(
        first=(6 * u, D), second=(3 * u, D), cq=(6 * u, D), ck=(3 * u, D), cv=(3 * u, D), cmixed=(6 * u, D),
        joined=(rows, D), normed=(rows, D), q=(rows, D), kx=(rows + 6 * u, D), vx=(rows + 6 * u, D),
        mixed=(rows, D), middle=(rows, D), normed_two=(rows, D), slope=(rows, FF), active=(rows, FF),
    )
    return {k: (sizes[k], F32 if k in ("joined", "middle", "slope") else BF) for k in KEPT}


def halo_device(place, count, step):
    t = jnp.clip(place.slab + step, 0, count - 1)
    return (place.at[0] * place.dims[1] + place.at[1], t)


def slab_bias(place, count, width, spatial, axis=1):
    col = lax.broadcasted_iota(jnp.int32, (1, width) if axis else (width, 1), axis)
    below = (col < spatial) & (place.slab == 0)
    above = (col >= width - spatial) & (place.slab == count - 1)
    return jnp.where(below | above, FAR, 0.0).astype(F32)


def forward_work(place, copies, weights, need, gain, x, v, save, swap, products):
    u = x.shape[0] // 7
    count = 2 * place.dims[2]
    spans = ((0, 4 * u), (4 * u, 2 * u), (6 * u, u))
    bases = (0, 6 * u, 10 * u)
    yield need("gain")
    for c in range(2):
        r0, n = spans[c]
        k0, m = spans[c + 1]
        rows, keys = pl.ds(r0, n), pl.ds(k0 - 4 * u, m)
        g = lambda j: gain[pl.ds(2 * (3 + c) + j, 1), :]
        v["first"][rows] = norm_rows(x[rows], g(0)).astype(BF)
        v["second"][keys] = norm_rows(x[pl.ds(k0, m)], g(1)).astype(BF)
        yield 0.5
    save("first")
    save("second")
    yield need(0)
    for c in range(2):
        r0, n = spans[c]
        k0, m = spans[c + 1]
        rows, keys = pl.ds(r0, n), pl.ds(k0 - 4 * u, m)
        for j, (src, dst, part) in enumerate((("first", "cq", rows), ("second", "ck", keys), ("second", "cv", keys))):
            w = weights.take((0, (9 + 3 * c + j) * D, 0))
            v[dst][part] = matmul(v[src][part], w[...]).astype(BF)
            weights.give_back()
            yield 0.8
        for h in range(HEADS // 2):
            cols = pl.ds(h * 128, 128)
            v["cmixed"][rows, cols] = attend_pair(v["cq"][rows, cols], v["ck"][keys, cols], v["cv"][keys, cols], None)
            yield 0.8 if c == 0 else 0.3
    for name in ("cq", "ck", "cv", "cmixed"):
        save(name)
    yield need(1)
    for c in range(2):
        rows = pl.ds(*spans[c])
        w = weights.take((1, (3 + c) * D, 0))
        v["joined"][rows] = x[rows] + matmul(v["cmixed"][rows], w[...])
        weights.give_back()
        yield 0.8
    v["joined"][pl.ds(*spans[2])] = x[pl.ds(*spans[2])]
    save("joined")
    for name in ("kx", "vx"):
        for view in range(3):
            base, n = bases[view], spans[view][1]

            @pl.when(place.slab == 0)
            def _():
                v[name][pl.ds(base, u)] = jnp.zeros((u, D), BF)

            @pl.when(place.slab == count - 1)
            def _():
                v[name][pl.ds(base + u + n, u)] = jnp.zeros((u, D), BF)

    halo = {0: [], 1: [], 2: []}
    for view in range(3):
        r0, n = spans[view]
        rows = pl.ds(r0, n)
        base = bases[view]
        v["normed"][rows] = norm_rows(v["joined"][rows], gain[pl.ds(2 * view, 1), :]).astype(BF)
        for j, (dst, part) in enumerate((("q", rows), ("kx", pl.ds(base + u, n)), ("vx", pl.ds(base + u, n)))):
            w = weights.take((0, (3 * view + j) * D, 0))
            v[dst][part] = matmul(v["normed"][rows], w[...]).astype(BF)
            weights.give_back()
            if j > 0:
                ref = v[dst]
                up, down = place.slab < count - 1, place.slab > 0
                halo[view].append(
                    (copies.start(ref.at[pl.ds(base + n, u)], ref.at[pl.ds(base, u)], halo_device(place, count, 1), up), down)
                )
                halo[view].append(
                    (
                        copies.start(
                            ref.at[pl.ds(base + u, u)], ref.at[pl.ds(base + u + n, u)], halo_device(place, count, -1), down
                        ),
                        up,
                    )
                )
            yield 0.8
    save("normed")
    save("q")
    for view in range(3):
        r0, n = spans[view]
        rows, keys = pl.ds(r0, n), pl.ds(bases[view], n + 2 * u)
        for one, ok in halo[view]:
            when(ok, one.wait_recv)
        bias = slab_bias(place, count, n + 2 * u, u)
        for h in range(HEADS // 2):
            cols = pl.ds(h * 128, 128)
            v["mixed"][rows, cols] = attend_pair(v["q"][rows, cols], v["kx"][keys, cols], v["vx"][keys, cols], bias)
            yield (1.4, 0.6, 0.3)[view]
    save("kx")
    save("vx")
    save("mixed")
    for view in range(3):
        rows = pl.ds(*spans[view])
        w = weights.take((1, view * D, 0))
        v["middle"][rows] = v["joined"][rows] + matmul(v["mixed"][rows], w[...])
        weights.give_back()
        v["normed_two"][rows] = norm_rows(v["middle"][rows], gain[pl.ds(2 * view + 1, 1), :]).astype(BF)
        yield 1.0
    save("middle")
    save("normed_two")
    yield need(2)
    for view in range(3):
        rows = pl.ds(*spans[view])
        for j in range(FF // D):
            cols = pl.ds(j * D, D)
            w = weights.take((2, view * D, j))
            pre = matmul(v["normed_two"][rows], w[...])
            weights.give_back()
            area = 0.5 * (1.0 + lax.erf(pre * (0.5**0.5)))
            v["active"][rows, cols] = (pre * area).astype(BF)
            v["slope"][rows, cols] = area + pre * jnp.exp(-0.5 * pre * pre) * 0.3989422804014327
            yield 1.4
        swap(view)
    save("slope")
    save("active")
    yield from products()


def gather_kernel(dims, own_gains, *refs):
    refs = list(refs)
    take = lambda n: [refs.pop(0) for _ in range(n)]
    shards = take(4)
    gain_tile, x, cot = take(3)
    fulls = take(4)
    gain_out, down_part = take(2)
    kept_out = dict(zip(KEPT, take(len(KEPT))))
    theirs, merged = take(4), take(4)
    gain_all, gain, d_out, far_d_out, far_active, made = take(6)
    v = dict(zip(KEPT, take(len(KEPT))))
    ring, send, recv, local, ring_sem, save_sem, store_sem = take(7)
    place = Place(dims)
    copies = Copies(send, recv)
    core = place.core
    at = place.at
    meet(place)
    width = [s.shape[1] // 2 for s in shards]
    mine = [pl.ds(pl.multiple_of(core * w, 128), w) for w in width]
    other = [pl.ds(pl.multiple_of((1 - core) * w, 128), w) for w in width]
    swaps = []
    for a in range(4):
        swaps.append(copies.start(shards[a].at[:, other[a]], theirs[a], place.sibling()))
    own_tile = gain_all.at[at[0], at[1], at[2], core]
    own_tile[...] = gain_tile[...]
    swap_gain = copies.start(own_tile, own_tile, place.sibling())
    slabs = [(m.shape[0], 2 * m.shape[1]) for m in merged]
    pieces = pieces_of(slabs, range(4), GATHER_PLAN)
    left = {a: sum(1 for piece in pieces if piece[0] == a) for a in range(4)}
    pair = {a: [] for a in range(4)}
    ready = set()
    state = {"gain": False}

    def prepare(a):
        swaps[a].wait_recv()
        w = width[a]
        own = jnp.where(core == 0, shards[a][:, :w].astype(F32), shards[a][:, w:].astype(F32))
        got = theirs[a][...].astype(F32)
        upper = jnp.where(core == 0, own, got)
        lower = jnp.where(core == 0, got, own)
        merged[a][...] = jnp.concatenate([upper, lower], axis=0).astype(BF)
        copy = pltpu.make_async_copy(merged[a], fulls[a].at[at[0], at[1], at[2], :, mine[a]], local.at[a])
        copy.start()
        copy.wait()

    def begin(piece):
        a, row, block, order, _ = piece
        if a not in ready:
            prepare(a)
            ready.add(a)
        cols = pl.ds(pl.multiple_of(core * width[a] + block * BLOCK, 128), BLOCK)
        yield from gather_piece(copies, place, fulls[a], (row, ROWS), cols, order, pair[a])
        left[a] -= 1

    def gains():
        swap_gain.wait_recv()
        done = set()
        for dim in ZXY:

            def pick(value):
                index = [slice(None) if d in done else at[d] for d in range(3)]
                index[dim] = value
                return gain_all.at[tuple(index)]

            yield from gather_line(copies, place, dim, pick)
            done.add(dim)
        gain[...] = gain_table(gain_all[...].reshape(-1, 128), own_gains)
        copy = pltpu.make_async_copy(gain, gain_out, local.at[4])
        copy.start()
        copy.wait()
        state["gain"] = True

    weights = Weights(dims, slabs, fulls, ring, ring_sem, forward_blocks())

    def need(what):
        def gate():
            if what == "gain":
                return state["gain"]
            if left[what]:
                return False
            if what not in weights.ready:
                for copy in pair[what]:
                    copy.wait_recv()
                weights.ready.add(what)
                weights.fetch()
            return True

        return gate

    saves = []

    def save(name):
        copy = pltpu.make_async_copy(v[name], kept_out[name], save_sem.at[len(saves)])
        copy.start()
        saves.append(copy)

    u = x.shape[0] // 7
    spans = ((0, 4 * u), (4 * u, 2 * u), (6 * u, u))
    d_out[...] = cot[...].astype(BF)
    swap_out = copies.start(d_out.at[:, other[0]], far_d_out, place.sibling())
    swapped = {}

    def swap(view):
        rows = pl.ds(*spans[view])
        swapped[view] = copies.start(v["active"].at[rows], far_active.at[rows], place.sibling())

    def products():
        storing = {}
        swap_out.wait_recv()
        own_right = [jnp.where(core == 0, d_out[pl.ds(*s), :BLOCK], d_out[pl.ds(*s), BLOCK:]) for s in spans]
        for view in range(3):
            swapped[view].wait_recv()
            rows = pl.ds(*spans[view])
            right = jnp.concatenate([own_right[view], far_d_out[rows]], axis=0)
            for j in range(FF // D):
                i = view * (FF // D) + j
                slot = i % 2
                for one in storing.pop(i - 2, ()):
                    one.wait()
                cols = pl.ds(j * D, D)
                left = jnp.concatenate([v["active"][rows, cols], far_active[rows, cols]], axis=0)
                made[slot] = matmul_tn(left, right).astype(BF)
                storing[i] = [
                    pltpu.make_async_copy(
                        made.at[slot, pl.ds(at_, n)], down_part.at[p, q, z, pl.ds(off, n)], store_sem.at[slot, k]
                    )
                    for k, (p, q, z, off, n, at_) in enumerate(row_runs(dims, slabs[3][0], view * FF + j * D, D))
                ]
                for one in storing[i]:
                    one.start()
                yield 0.8
        for i in list(storing):
            for one in storing.pop(i):
                one.wait()

    work = forward_work(place, copies, weights, need, gain, x, v, save, swap, products)
    weave(march(pieces, begin, (gains(),)), work, lambda: EACH_FORWARD)
    for copy in pair[3]:
        copy.wait_recv()
    for copy in saves:
        copy.wait()
    copies.drain()


def gather_all(dims, own_gains, shards, tile, x, cot):
    slabs = [(2 * s.shape[0], s.shape[1]) for s in shards]
    anywhere = pl.BlockSpec(memory_space=pl.ANY)
    vmem = pl.BlockSpec(memory_space=pltpu.VMEM)
    kept = forward_shapes(x.shape[0])
    segments = max(D // s[0] + 2 for s in slabs)
    outs = pl.pallas_call(
        functools.partial(gather_kernel, dims, own_gains),
        out_shape=[jax.ShapeDtypeStruct((*dims, *s), BF) for s in slabs]
        + [jax.ShapeDtypeStruct((16, D), F32), jax.ShapeDtypeStruct((*dims, slabs[3][0], D // 2), BF)]
        + [jax.ShapeDtypeStruct(*kept[k]) for k in KEPT],
        in_specs=[vmem] * 7,
        out_specs=[anywhere] * (6 + len(KEPT)),
        scratch_shapes=[pltpu.VMEM((r // 2, w // 2), BF) for r, w in slabs]
        + [pltpu.VMEM((r, w // 2), BF) for r, w in slabs]
        + [pltpu.VMEM((*dims, 2, 8, 128), F32), pltpu.VMEM((16, D), F32)]
        + [
            pltpu.VMEM(x.shape, BF),
            pltpu.VMEM((x.shape[0], D // 2), BF),
            pltpu.VMEM((x.shape[0], FF), BF),
            pltpu.VMEM((2, D, BLOCK), BF),
        ]
        + [pltpu.VMEM(*kept[k]) for k in KEPT]
        + [
            pltpu.VMEM((4, D, D), BF),
            pltpu.SemaphoreType.DMA((COPIES,)),
            pltpu.SemaphoreType.DMA((COPIES,)),
            pltpu.SemaphoreType.DMA((5,)),
            pltpu.SemaphoreType.DMA((4, segments)),
            pltpu.SemaphoreType.DMA((len(KEPT),)),
            pltpu.SemaphoreType.DMA((2, segments)),
        ],
        compiler_params=pltpu.CompilerParams(collective_id=0, has_side_effects=True, vmem_limit_bytes=60 << 20),
    )(*shards, tile, x, cot)
    return outs[:4], outs[4], outs[5], dict(zip(KEPT, outs[6:]))


class Stream:
    def __init__(self, depth, sems, makers):
        self.depth, self.sems, self.makers = depth, sems, makers
        self.loading = {}
        self.next_load = 0
        self.next_use = 0
        self.fetch()

    def fetch(self):
        while self.next_load < min(len(self.makers), self.next_use + self.depth):
            slot = self.next_load % self.depth
            copies = [
                pltpu.make_async_copy(src, dst, self.sems.at[slot, j])
                for j, (src, dst) in enumerate(self.makers[self.next_load](slot))
            ]
            for one in copies:
                one.start()
            self.loading[self.next_load] = copies
            self.next_load += 1

    def take(self):
        for one in self.loading.pop(self.next_use):
            one.wait()
        return self.next_use % self.depth

    def give_back(self):
        self.next_use += 1
        self.fetch()


def add_to(total, term):
    total[...] = (total[...].astype(F32) + term[...].astype(F32)).astype(total.dtype)


class Credits:
    def __init__(self, sems, waits):
        self.sems, self.waits = sems, waits

    def wait(self, index, ok=None):
        if self.waits:
            when(ok, lambda: pl.semaphore_wait(self.sems.at[index], 1))

    def give(self, index, device):
        if self.sems is not None:
            pl.semaphore_signal(self.sems.at[index], inc=1, device_id=device, device_id_type=MESH)

    def settle(self, place):
        self.waits = True
        n, z = place.dims[2], place.at[2]
        self.wait(0)
        self.wait(1)
        for turn in range(n - 1):
            for step in (1, -1):
                far = z if step == 1 else n - 1 - z
                self.wait(2 + 2 * turn + (1 - step) // 2, far <= turn)


def reduce_line(copies, place, pick, slots, credits):
    n = place.dims[2]
    z = place.at[2]
    before = {}
    for turn in range(n):
        for step in (1, -1):
            far = z if step == 1 else n - 1 - z
            goal = far + n - 1 - turn
            goal = jnp.minimum(goal if step == 1 else n - 1 - goal, n - 1)
            goal = jnp.maximum(goal, 0)
            if turn > 0:

                def take(step=step, turn=turn, goal=goal):
                    before[step].wait_recv()
                    add_to(pick(goal), slots(turn - 1, step))
                    credits.give(2 + 2 * (turn - 1) + (1 - step) // 2, place.along(2, jnp.clip(z - step, 0, n - 1)))

                when((far >= 1) & (far <= turn), take)
            if turn < n - 1:
                credits.wait(2 + 2 * turn + (1 - step) // 2, far <= turn)
                before[step] = copies.start(
                    pick(goal), slots(turn, step), place.along(2, jnp.clip(z + step, 0, n - 1)), far <= turn
                )
        if turn < n - 1:
            yield


def reduce_piece(copies, place, source, order, acc, first, turns, last, local, credits, finish):
    lead = order[0]
    rest = 1 - lead
    me, mine = place.at[lead], place.at[rest]
    z = place.at[2]
    beside, across = place.along(lead, 1 - me), place.along(rest, 1 - mine)
    credits.wait(0)
    copy = copies.start(source(lead, 1 - me), first, beside)
    load = pltpu.make_async_copy(source(lead, me), acc, local)
    load.start()
    yield
    load.wait()
    copy.wait_recv()
    add_to(acc, first)
    credits.give(0, beside)
    slots = lambda turn, step: turns.at[turn, (1 - step) // 2]
    if order[1] == 2:
        yield from reduce_line(copies, place, lambda v: acc.at[:, v], slots, credits)
        credits.wait(1)
        copy = copies.start(acc.at[1 - mine, z], last, across)
        yield
        copy.wait_recv()
        finish(acc[mine, z].astype(F32) + last[...].astype(F32))
        credits.give(1, across)
    else:
        credits.wait(1)
        copy = copies.start(acc.at[1 - mine], last, across)
        yield
        copy.wait_recv()
        add_to(acc.at[mine], last)
        credits.give(1, across)
        yield from reduce_line(copies, place, lambda v: acc.at[mine, v], slots, credits)
        finish(acc[mine, z].astype(F32))


def march_ready(pieces, begin, ready):
    waiting = list(pieces)
    active = []
    step = 0
    while active or waiting:
        while waiting and step >= waiting[0][4] and ready(waiting[0]):
            active.append(begin(waiting.pop(0)))
        if not active:
            if step < waiting[0][4]:
                step += 1
            else:
                yield lambda: ready(waiting[0])
            continue
        still = []
        for one in active:
            try:
                yield next(one)
                still.append(one)
            except StopIteration:
                pass
        active = still
        step += 1


LEFTS = ("normed_two", "mixed", "normed", "first", "second", "cmixed")
RIGHTS = ("d_out", "d_pre", "d_attn", "dq", "dk", "dv", "d_cross", "dcq", "dck", "dcv")
HELD = ("q", "kx", "vx", "cq", "ck", "cv")


def right_shapes(rows):
    u = rows // 7
    tall = dict(d_cross=6 * u, dcq=6 * u, dck=3 * u, dcv=3 * u)
    return [(tall.get(k, rows), FF if k == "d_pre" else D) for k in RIGHTS]


def job_batches(u):
    rows = ((0, 4 * u), (4 * u, 2 * u), (6 * u, u))
    late = ((0, 2 * u), (2 * u, u))
    batches = {"up": [], "out": [], "qkv": [], "cout": [], "cqkv": []}
    for view in range(3):
        for block in range(FF // 2 // BLOCK):
            batches["up"].append((2, view * D, block, "normed_two", 0, rows[view], "d_pre", rows[view]))
        batches["out"].append((1, view * D, 0, "mixed", 0, rows[view], "d_attn", rows[view]))
        for j, name in enumerate(("dq", "dk", "dv")):
            batches["qkv"].append((0, (3 * view + j) * D, 0, "normed", 0, rows[view], name, rows[view]))
    for c in range(2):
        batches["cout"].append((1, (3 + c) * D, 0, "cmixed", 0, rows[c], "d_cross", rows[c]))
        batches["cqkv"].append((0, (9 + 3 * c) * D, 0, "first", 0, rows[c], "dcq", rows[c]))
        for j, name in enumerate(("dck", "dcv")):
            batches["cqkv"].append((0, (10 + 3 * c + j) * D, 0, "second", 0, late[c], name, late[c]))
    return batches


def backward_blocks():
    blocks = []
    for view in range(3):
        for j in range(FF // D):
            blocks += [(3, view * FF + j * D, 0), (2, view * D, j)]
    blocks += [(1, view * D, 0) for view in range(3)]
    blocks += [(0, i * D, 0) for i in range(9)]
    blocks += [(1, (3 + c) * D, 0) for c in range(2)]
    blocks += [(0, (9 + j) * D, 0) for j in range(6)]
    blocks += [(3, view * FF + j * D, 0) for view in range(3) for j in range(FF // D)]
    return blocks


def norm_pull(x, gain, grad):
    centered = x - jnp.mean(x, axis=-1, keepdims=True)
    scale = lax.rsqrt(jnp.mean(centered * centered, axis=-1, keepdims=True) + EPS)
    unit = centered * scale
    inner = grad * gain
    pulled = scale * (
        inner - jnp.mean(inner, axis=-1, keepdims=True) - unit * jnp.mean(inner * unit, axis=-1, keepdims=True)
    )
    return pulled, jnp.sum(grad * unit, axis=0, keepdims=True)


def attend_pair_back(query, keys, values, grad, bias):
    dq, dk, dv = [], None, None
    for part, g in zip(halves_of(query), halves_of(grad)):
        scores = matmul_nt(keys, part) * 0.125
        if bias is not None:
            scores = scores + bias
        expo = jnp.exp(scores - jnp.max(scores, axis=0, keepdims=True))
        probs = expo * (1.0 / jnp.sum(expo, axis=0, keepdims=True))
        dprobs = matmul_nt(values, g)
        inner = jnp.sum(dprobs * probs, axis=0, keepdims=True)
        dscores = (probs * (dprobs - inner) * 0.125).astype(BF)
        dq.append(matmul_tn(dscores, keys))
        k_term = matmul(dscores, part)
        v_term = matmul(probs.astype(BF), g)
        dk = k_term if dk is None else dk + k_term
        dv = v_term if dv is None else dv + v_term
    low = lax.broadcasted_iota(jnp.int32, dq[0].shape, 1) < dq[0].shape[1] // 2
    return jnp.where(low, dq[0], dq[1]), dk, dv


def gain_tiles(table, rows, own):
    filled = own // 48
    r = lax.broadcasted_iota(jnp.int32, (rows, D), 0)
    c = lax.broadcasted_iota(jnp.int32, (rows, D), 1)
    flat = (r // 8) * filled + r % 8
    rr = lax.broadcasted_iota(jnp.int32, (rows, 16), 0)
    vv = lax.broadcasted_iota(jnp.int32, (rows, 16), 1)
    pick = (rr % 8 < filled) & (((rr // 8) * filled + rr % 8) // 16 == vv)
    wide = jnp.dot(pick.astype(F32), table, precision=lax.Precision.HIGHEST, preferred_element_type=F32)
    wide = jnp.where((r % 8 < filled) & (c // 48 == flat % 16), wide, 0.0)
    j = lax.broadcasted_iota(jnp.int32, (D, 128), 1)
    fold = (j < 48) & (j == lax.broadcasted_iota(jnp.int32, (D, 128), 0) % 48)
    return jnp.dot(wide, fold.astype(F32), precision=lax.Precision.HIGHEST, preferred_element_type=F32)


def reduce_kernel(dims, slabs, pieces, own_gains, *refs):
    refs = list(refs)
    take = lambda n: [refs.pop(0) for _ in range(n)]
    wholes = take(4)
    (cot, gain, x, joined, middle, slope, active, down_part) = take(8)
    lefts = dict(zip(LEFTS, take(6)))
    held_in = dict(zip(HELD, take(6)))
    token_out, layer_out = take(2)
    results = take(4)
    (gain_out,) = take(1)
    parts = take(3) + [down_part]
    far_lefts, far_rights = dict(zip(LEFTS, take(6))), dict(zip(RIGHTS, take(10)))
    rights = dict(zip(RIGHTS, take(10)))
    held = dict(zip(HELD, take(6)))
    acc, first, turns_a, turns_b, last_a, last_b = take(6)
    finals = take(4)
    xs, ys, made = take(3)
    g_far, g_own, g_acc, g_first, g_turns, g_last, g_sum = take(7)
    ring, rowring, preing, acting, layer, flow, total, dvf, halo_out, halo_in = take(10)
    send, recv, local, left_sem, right_sem, store_sem, final_sem, ring_sem, row_sem, pre_sem, act_sem, held_sem, layer_sem, credit = take(14)
    place = Place(dims)
    core = place.core
    copies = Copies(send, recv)
    meet(place)
    rows_all = cot.shape[0]
    u = rows_all // 7
    spans = ((0, 4 * u), (4 * u, 2 * u), (6 * u, u))
    bases = (0, 6 * u, 10 * u)
    count = 2 * dims[2]
    half_of = lambda ref, c: pl.ds(pl.multiple_of(c * (ref.shape[1] // 2), 128), ref.shape[1] // 2)
    coming = {}

    def swap(name):
        if name in lefts:
            coming[name] = copies.start(lefts[name], far_lefts[name], place.sibling())
        else:
            ref = rights[name]
            coming[name] = copies.start(ref.at[:, half_of(ref, 1 - core)], far_rights[name], place.sibling())

    arrived = set()

    def arrive(name):
        if name not in arrived:
            coming[name].wait_recv()
            arrived.add(name)

    def weight_maker(block):
        a, row, col = block
        return lambda slot: [
            (wholes[a].at[p, q, z, pl.ds(off, n), pl.ds(col * D, D)], ring.at[slot, pl.ds(at, n)])
            for p, q, z, off, n, at in row_runs(dims, slabs[a][0], row, D)
        ]

    def row_maker(ref, r0, n):
        return lambda slot: [(ref.at[pl.ds(r0, n)], rowring.at[slot, pl.ds(0, n)])]

    def pre_maker(view, j):
        r0, n = spans[view]
        block = (pl.ds(r0, n), pl.ds(j * D, D))
        return lambda slot: [(slope.at[block], preing.at[slot, pl.ds(0, n)])]

    def act_maker(view, j):
        r0, n = spans[view]
        block = (pl.ds(r0, n), pl.ds(j * D, D))
        return lambda slot: [(active.at[block], acting.at[slot, pl.ds(0, n)])]

    rights["d_out"][...] = cot[...].astype(BF)
    blocks = backward_blocks()
    weights = Stream(ring.shape[0], ring_sem, [weight_maker(b) for b in blocks])
    pres = Stream(2, pre_sem, [pre_maker(view, j) for view in range(3) for j in range(FF // D)])
    acts = Stream(2, act_sem, [act_maker(view, j) for view in range(3) for j in range(FF // D)])
    row_list = [(middle, *spans[view]) for view in range(3)] + [(joined, *spans[view]) for view in range(3)]
    for c in range(2):
        row_list += [(x, *spans[c]), (x, *spans[c + 1])]
    row_list += [(middle, *spans[view]) for view in range(3)]
    rowed = Stream(2, row_sem, [row_maker(*one) for one in row_list])
    used_blocks = []

    def weight(expected):
        assert blocks[len(used_blocks)] == expected
        used_blocks.append(expected)
        return ring.at[weights.take()][...]

    holding = {}
    for i, name in enumerate(HELD):
        holding[name] = pltpu.make_async_copy(held_in[name], held[name], held_sem.at[i])
        holding[name].start()
    for name in LEFTS:
        swap(name)

    state = {"jobs": 0, "lefts": 0, "gain": False}
    ready = {3}
    storing = {}

    def finish_stores(i):
        for one in storing.pop(i, ()):
            one.wait()

    def load_left(group, slot):
        left, lcol, lrows = group
        arrive(left)
        n = lrows[1]
        block = (pl.ds(*lrows), pl.ds(lcol * D, D))
        loads = [
            pltpu.make_async_copy(lefts[left].at[block], xs.at[slot, pl.ds(0, n)], left_sem.at[slot, 0]),
            pltpu.make_async_copy(far_lefts[left].at[block], xs.at[slot, pl.ds(n, n)], left_sem.at[slot, 1]),
        ]
        for one in loads:
            one.start()
        return loads

    def load_right(job, slot):
        block, right, rrows = job[2], job[6], job[7]
        arrive(right)
        n = rrows[1]
        ref = rights[right]
        own = pl.ds(pl.multiple_of(core * (ref.shape[1] // 2) + block * BLOCK, 128), BLOCK)
        far = (pl.ds(*rrows), pl.ds(block * BLOCK, BLOCK))
        loads = [
            pltpu.make_async_copy(ref.at[pl.ds(*rrows), own], ys.at[slot, pl.ds(0, n)], right_sem.at[slot, 0]),
            pltpu.make_async_copy(far_rights[right].at[far], ys.at[slot, pl.ds(n, n)], right_sem.at[slot, 1]),
        ]
        for one in loads:
            one.start()
        return loads

    batches = job_batches(u)

    def multiply(name, cost):
        batch = batches[name]
        groups, member = [], []
        for job in batch:
            if not groups or groups[-1] != job[3:6]:
                groups.append(job[3:6])
            member.append(len(groups) - 1)
        x0, i0 = state["lefts"], state["jobs"]
        left_loads = {k: load_left(groups[k], (x0 + k) % 2) for k in range(min(2, len(groups)))}
        right_loads = {k: load_right(batch[k], (i0 + k) % 3) for k in range(min(2, len(batch)))}
        for index, job in enumerate(batch):
            i, k = i0 + index, member[index]
            if k in left_loads:
                for one in left_loads.pop(k):
                    one.wait()
                if 0 < k < len(groups) - 1:
                    left_loads[k + 1] = load_left(groups[k + 1], (x0 + k + 1) % 2)
            for one in right_loads.pop(index):
                one.wait()
            if index + 2 < len(batch):
                right_loads[index + 2] = load_right(batch[index + 2], (i + 2) % 3)
            finish_stores(i - 2)
            n = 2 * job[5][1]
            slot = i % 2
            made[slot] = matmul_tn(xs[(x0 + k) % 2, :n], ys[i % 3, :n]).astype(BF)
            a, row, block = job[:3]
            storing[i] = [
                pltpu.make_async_copy(
                    made.at[slot, pl.ds(at, n)],
                    parts[a].at[p, q, z, pl.ds(off, n), pl.ds(block * BLOCK, BLOCK)],
                    store_sem.at[slot, j],
                )
                for j, (p, q, z, off, n, at) in enumerate(row_runs(dims, slabs[a][0], row, D))
            ]
            for one in storing[i]:
                one.start()
            yield cost
        state["lefts"] += len(groups)
        state["jobs"] += len(batch)
        for i in list(storing):
            finish_stores(i)

    g = lambda e, j: gain[pl.ds(2 * e + j, 1), :]

    def work():
        for view in range(3):
            r0, n = spans[view]
            rows = pl.ds(r0, n)
            cost = (1.5, 0.9, 0.7)[view]
            for j in range(FF // D):
                cols = pl.ds(j * D, D)
                dactive = matmul_nt(rights["d_out"][rows], weight((3, view * FF + j * D, 0)))
                weights.give_back()
                slot = pres.take()
                rights["d_pre"][rows, cols] = (dactive * preing[slot, :n]).astype(BF)
                pres.give_back()
                term = matmul_nt(rights["d_pre"][rows, cols], weight((2, view * D, j)))
                weights.give_back()
                total[:n] = term if j == 0 else total[:n] + term
                yield cost
            slot = rowed.take()
            pulled, g_sum[pl.ds(2 * view + 1, 1), :] = norm_pull(rowring[slot, :n], g(view, 1), total[:n])
            rowed.give_back()
            flow[rows] = cot[rows] + pulled
            rights["d_attn"][rows] = flow[rows].astype(BF)
            yield 0.8
        swap("d_pre")
        swap("d_attn")
        dmixed = rights["d_out"]
        for view in range(3):
            rows = pl.ds(*spans[view])
            dmixed[rows] = matmul_nt(rights["d_attn"][rows], weight((1, view * D, 0))).astype(BF)
            weights.give_back()
            yield 0.7
        yield from multiply("up", 0.6)
        ready.add(2)
        for name in ("q", "kx", "vx"):
            holding[name].wait()
        dkf = layer
        halo = {}
        up, down = place.slab < count - 1, place.slab > 0
        for view in range(3):
            r0, n = spans[view]
            rows, keys = pl.ds(r0, n), pl.ds(bases[view], n + 2 * u)
            bias = slab_bias(place, count, n + 2 * u, u, 0)
            for h in range(HEADS // 2):
                cols = pl.ds(h * 128, 128)
                dq, dk, dv = attend_pair_back(
                    held["q"][rows, cols], held["kx"][keys, cols], held["vx"][keys, cols], dmixed[rows, cols], bias
                )
                rights["dq"][rows, cols] = dq.astype(BF)
                for k, (whole, own) in enumerate(((dk, dkf), (dv, dvf))):
                    halo_out[k, view, 0, :, cols] = whole[:u].astype(BF)
                    own[rows, cols] = whole[u : u + n]
                    halo_out[k, view, 1, :, cols] = whole[u + n :].astype(BF)
                yield (2.0, 0.9, 0.5)[view]
            for k in range(2):
                for side, step, ok in ((0, -1, down), (1, 1, up)):
                    halo[k, view, side] = copies.start(
                        halo_out.at[k, view, side], halo_in.at[k, view, side], halo_device(place, count, step), ok
                    )
        swap("dq")
        yield from multiply("out", 0.6)
        for view in range(3):
            r0, n = spans[view]
            rows = pl.ds(r0, n)
            for k, (own, name) in enumerate(((dkf, "dk"), (dvf, "dv"))):
                for side, edge, ok in ((0, r0 + n - u, up), (1, r0, down)):

                    def join(k=k, side=side, edge=edge, own=own):
                        halo[k, view, side].wait_recv()
                        own[pl.ds(edge, u)] = own[pl.ds(edge, u)] + halo_in[k, view, side].astype(F32)

                    when(ok, join)
                rights[name][rows] = own[rows].astype(BF)
            for j, name in enumerate(("dq", "dk", "dv")):
                term = matmul_nt(rights[name][rows], weight((0, (3 * view + j) * D, 0)))
                weights.give_back()
                total[:n] = term if j == 0 else total[:n] + term
                yield 0.7
            slot = rowed.take()
            pulled, g_sum[pl.ds(2 * view, 1), :] = norm_pull(rowring[slot, :n], g(view, 0), total[:n])
            rowed.give_back()
            flow[rows] = flow[rows] + pulled
            yield 0.6
        swap("dk")
        swap("dv")
        rights["d_cross"][...] = flow[pl.ds(0, 6 * u)].astype(BF)
        swap("d_cross")
        for name in ("cq", "ck", "cv"):
            holding[name].wait()
        yield from multiply("cout", 0.6)
        ready.add(1)
        for c in range(2):
            rows = pl.ds(*spans[c])
            dmixed[rows] = matmul_nt(rights["d_cross"][rows], weight((1, (3 + c) * D, 0))).astype(BF)
            weights.give_back()
            yield 0.7
        for c in range(2):
            rows, keys = pl.ds(*spans[c]), pl.ds(spans[c + 1][0] - 4 * u, spans[c + 1][1])
            for h in range(HEADS // 2):
                cols = pl.ds(h * 128, 128)
                dq, dk, dv = attend_pair_back(
                    held["cq"][rows, cols], held["ck"][keys, cols], held["cv"][keys, cols], dmixed[rows, cols], None
                )
                rights["dcq"][rows, cols] = dq.astype(BF)
                rights["dck"][keys, cols] = dk.astype(BF)
                rights["dcv"][keys, cols] = dv.astype(BF)
                yield (1.0, 0.45)[c]
        for name in ("dcq", "dck", "dcv"):
            swap(name)
        yield from multiply("qkv", 0.6)
        yield from multiply("cqkv", 0.6)
        ready.add(0)
        for c in range(2):
            r0, n = spans[c]
            k0, m = spans[c + 1]
            rows, keys, late = pl.ds(r0, n), pl.ds(k0 - 4 * u, m), pl.ds(k0, m)
            term = matmul_nt(rights["dcq"][rows], weight((0, (9 + 3 * c) * D, 0)))
            weights.give_back()
            slot = rowed.take()
            pulled, g_sum[pl.ds(2 * (3 + c), 1), :] = norm_pull(rowring[slot, :n], g(3 + c, 0), term)
            rowed.give_back()
            flow[rows] = flow[rows] + pulled
            yield 1.0
            term = matmul_nt(rights["dck"][keys], weight((0, (10 + 3 * c) * D, 0)))
            weights.give_back()
            term = term + matmul_nt(rights["dcv"][keys], weight((0, (11 + 3 * c) * D, 0)))
            weights.give_back()
            slot = rowed.take()
            pulled, g_sum[pl.ds(2 * (3 + c) + 1, 1), :] = norm_pull(rowring[slot, :m], g(3 + c, 1), term)
            rowed.give_back()
            flow[late] = flow[late] + pulled
            yield 1.0
        token = pltpu.make_async_copy(flow, token_out, final_sem.at[4])
        token.start()
        g_sum[pl.ds(10, 6), :] = jnp.zeros((6, D), F32)
        g_own[...] = gain_tiles(g_sum[...], 2 * dims[0] * dims[1] * dims[2] * 8, own_gains).reshape(g_own.shape)
        coming["gain"] = copies.start(g_own, g_far, place.sibling())
        state["gain"] = True
        yield 1.0
        for view in range(3):
            r0, n = spans[view]
            rows = pl.ds(r0, n)
            for j in range(FF // D):
                slot = acts.take()
                term = matmul(acting[slot, :n], weight((3, view * FF + j * D, 0)))
                acts.give_back()
                weights.give_back()
                layer[rows] = term if j == 0 else layer[rows] + term
                yield 0.6
            slot = rowed.take()
            layer[rows] = layer[rows] + rowring[slot, :n]
            rowed.give_back()
        layered = pltpu.make_async_copy(layer, layer_out, layer_sem)
        layered.start()
        token.wait()
        layered.wait()

    left_in = {a: sum(1 for piece in pieces if piece[0] == a) for a in range(4)}
    count_pieces = sum(left_in.values())
    bases_of = [sum(POOLS[:k]) for k in range(len(POOLS))]
    free = {k: [[bases_of[k] + j, None, None] for j in range(POOLS[k])] for k in range(len(POOLS))}
    owners = []
    ending = []

    def gains():
        coming["gain"].wait_recv()
        add_to(g_far, g_own)
        source = lambda dim, value: g_far.at[(*[value if d == dim else slice(None) for d in range(3)], core)]

        def finish(value):
            g_first[0, 0] = value
            copy = pltpu.make_async_copy(g_first.at[0, 0], gain_out, final_sem.at[5])
            copy.start()
            copy.wait()

        yield from reduce_piece(
            copies, place, source, (0, 1, 2), g_acc, g_first, g_turns, g_last, local.at[SLOTS], Credits(None, False), finish
        )

    def begin(piece):
        if piece[0] == "gain":
            return gains()
        a, row, block, order, _ = piece
        kind = ORDERS.index(order)
        buffer = free[kind].pop(0)
        slot, before, _ = buffer
        if before is not None:
            before.drain()
        mine = Copies(send, recv)
        mine.used = COPIES - 9 * (count_pieces - len(owners))
        owners.append(mine)
        buffer[1] = mine
        cols = pl.ds(block * BLOCK, BLOCK)
        single = order[1] != 2
        k = slot - sum(POOLS[:4]) if single else slot
        turns, last = ((turns_a, last_a), (turns_b, last_b))[single]

        def source(dim, value):
            index = [slice(None)] * 3
            index[dim] = value
            return parts[a].at[(*index, pl.ds(row, ROWS), cols)]

        def finish(value):
            finals[a][pl.ds(row, ROWS), cols] = value
            left_in[a] -= 1
            free[kind].append(buffer)
            if left_in[a] == 0:
                deliver(a)

        credits = Credits(credit.at[slot], before is not None)
        buffer[2] = credits
        return reduce_piece(
            mine, place, source, order[::-1], acc.at[slot], first.at[slot], turns.at[k], last.at[k], local.at[slot], credits, finish
        )

    def deliver(a):
        rows, width = slabs[a][0] // 2, slabs[a][1] // 2
        cols = pl.ds(pl.multiple_of(core * width, 128), width)
        ending.append(
            copies.start(
                finals[a].at[pl.ds(pl.multiple_of((1 - core) * rows, 8), rows)], results[a].at[:, cols], place.sibling()
            )
        )
        keep = pltpu.make_async_copy(
            finals[a].at[pl.ds(pl.multiple_of(core * rows, 8), rows)], results[a].at[:, cols], final_sem.at[a]
        )
        keep.start()
        keep.wait()

    def piece_ready(piece):
        if piece[0] == "gain":
            return state["gain"]
        return piece[0] in ready and bool(free[ORDERS.index(piece[3])])

    weave(march_ready(pieces, begin, piece_ready), work(), lambda: EACH[len(ready) - 1])
    for buffers in free.values():
        for slot, user, credits in buffers:
            if user is not None:
                credits.settle(place)
    for one in ending:
        one.wait_recv()
    copies.drain()
    for one in owners:
        one.drain()
    assert copies.used <= COPIES - 9 * count_pieces


def reduce_all(dims, slabs, own_gains, wholes, down_part, cot, gain, x, kept):
    anywhere = pl.BlockSpec(memory_space=pl.ANY)
    vmem = pl.BlockSpec(memory_space=pltpu.VMEM)
    pieces = pieces_of(slabs, (3, 2, 1, 0), REDUCE_PLAN)
    pieces.append(("gain", 0, 0, None, pieces[-1][4]))
    bundled, single = sum(POOLS[:4]), sum(POOLS[4:])
    z = dims[2]
    rows = cot.shape[0]
    u = rows // 7
    tile = (ROWS, BLOCK)
    segments = max(D // slab[0] + 2 for slab in slabs)
    lefts = [kept[k] for k in LEFTS]
    held = [kept[k] for k in HELD]
    rights = right_shapes(rows)
    outs = pl.pallas_call(
        functools.partial(reduce_kernel, dims, slabs, pieces, own_gains),
        out_shape=[jax.ShapeDtypeStruct((rows, D), F32)] * 2
        + [jax.ShapeDtypeStruct((s[0] // 2, s[1]), F32) for s in slabs]
        + [jax.ShapeDtypeStruct((8, 128), F32)]
        + [jax.ShapeDtypeStruct((*dims, s[0], s[1] // 2), BF) for s in slabs[:3]]
        + [jax.ShapeDtypeStruct(one.shape, BF) for one in lefts]
        + [jax.ShapeDtypeStruct((r, w // 2), BF) for r, w in rights],
        in_specs=[anywhere] * 4 + [vmem] * 2 + [anywhere] * 18,
        out_specs=[anywhere] * 26,
        scratch_shapes=[pltpu.VMEM(s, BF) for s in rights]
        + [pltpu.VMEM(one.shape, BF) for one in held]
        + [
            pltpu.VMEM((SLOTS, 2, z, *tile), BF),
            pltpu.VMEM((SLOTS, 2, z, *tile), BF),
            pltpu.VMEM((bundled, z - 1, 2, 2, *tile), BF),
            pltpu.VMEM((single, z - 1, 2, *tile), BF),
            pltpu.VMEM((bundled, *tile), BF),
            pltpu.VMEM((single, z, *tile), BF),
        ]
        + [pltpu.VMEM((s[0], s[1] // 2), F32) for s in slabs]
        + [
            pltpu.VMEM((2, 8 * u, D), BF),
            pltpu.VMEM((3, 8 * u, BLOCK), BF),
            pltpu.VMEM((2, D, BLOCK), BF),
            pltpu.VMEM((*dims, 2, 8, 128), F32),
            pltpu.VMEM((*dims, 2, 8, 128), F32),
            pltpu.VMEM((2, z, 8, 128), F32),
            pltpu.VMEM((2, z, 8, 128), F32),
            pltpu.VMEM((z - 1, 2, 8, 128), F32),
            pltpu.VMEM((z, 8, 128), F32),
            pltpu.VMEM((16, D), F32),
            pltpu.VMEM((4, D, D), BF),
            pltpu.VMEM((2, 4 * u, D), F32),
            pltpu.VMEM((2, 4 * u, D), F32),
            pltpu.VMEM((2, 4 * u, D), BF),
            pltpu.VMEM((rows, D), F32),
            pltpu.VMEM((rows, D), F32),
            pltpu.VMEM((4 * u, D), F32),
            pltpu.VMEM((rows, D), F32),
            pltpu.VMEM((2, 3, 2, u, D), BF),
            pltpu.VMEM((2, 3, 2, u, D), BF),
            pltpu.SemaphoreType.DMA((COPIES,)),
            pltpu.SemaphoreType.DMA((COPIES,)),
            pltpu.SemaphoreType.DMA((SLOTS + 1,)),
            pltpu.SemaphoreType.DMA((2, 2)),
            pltpu.SemaphoreType.DMA((3, 2)),
            pltpu.SemaphoreType.DMA((2, segments)),
            pltpu.SemaphoreType.DMA((6,)),
            pltpu.SemaphoreType.DMA((4, segments)),
            pltpu.SemaphoreType.DMA((2, 1)),
            pltpu.SemaphoreType.DMA((2, 1)),
            pltpu.SemaphoreType.DMA((2, 1)),
            pltpu.SemaphoreType.DMA((6,)),
            pltpu.SemaphoreType.DMA,
            pltpu.SemaphoreType.REGULAR((SLOTS, 2 + 2 * (z - 1))),
        ],
        compiler_params=pltpu.CompilerParams(collective_id=1, has_side_effects=True, vmem_limit_bytes=63 << 20),
    )(*wholes, cot, gain, x, kept["joined"], kept["middle"], kept["slope"], kept["active"], down_part, *lefts, *held)
    return outs[:7]


def plain_device(tokens, cotangent, qkv_weights, out_weights, up_weights, down_weights, gains):
    rows = tokens[0]
    incoming = cotangent[0]
    spatial = rows.shape[0] // 7
    bounds = ((0, 4 * spatial), (4 * spatial, 6 * spatial), (6 * spatial, 7 * spatial))
    qkv, outw, upw, downw, gain_low = unstack(
        (
            lax.all_gather(qkv_weights, ("seq", "tm"), axis=0, tiled=True),
            lax.all_gather(out_weights, ("seq", "tm"), axis=0, tiled=True),
            lax.all_gather(up_weights, ("seq", "tm"), axis=0, tiled=True),
            lax.all_gather(down_weights, ("seq", "tm"), axis=0, tiled=True),
            lax.all_gather(gains, ("seq", "tm"), axis=0, tiled=True),
        )
    )
    gain = gain_low.astype(jnp.float32)
    place = lax.axis_index("tm")
    count = lax.axis_size("tm")
    below_bias = jnp.where(place > 0, 0.0, FAR).astype(jnp.float32)
    above_bias = jnp.where(place < count - 1, 0.0, FAR).astype(jnp.float32)
    views = [rows[start:stop] for start, stop in bounds]
    cross_keep = []
    joined = []
    for view in range(2):
        first = lowered(norm_rows(views[view], gain[3 + view, 0]))
        second = lowered(norm_rows(views[view + 1], gain[3 + view, 1]))
        query = lowered(product(first, qkv[3 + view, 0]))
        keys = lowered(product(second, qkv[3 + view, 1]))
        values = lowered(product(second, qkv[3 + view, 2]))
        mixed, probs = attend(query, keys, values, 0.0)
        joined.append(views[view] + product(mixed, outw[3 + view]))
        cross_keep.append((first, second, query, keys, values, mixed, probs))
    joined.append(views[2])
    local_keep = []
    edges = []
    for view in range(3):
        normed = lowered(norm_rows(joined[view], gain[view, 0]))
        query = lowered(product(normed, qkv[view, 0]))
        keys = lowered(product(normed, qkv[view, 1]))
        values = lowered(product(normed, qkv[view, 2]))
        local_keep.append((normed, query, keys, values))
        paired = jnp.stack([keys, values])
        edges.append(jnp.concatenate([paired[:, :spatial], paired[:, -spatial:]], axis=1))
    rim = extended(jnp.stack(edges, axis=1), (("tm", 2),), spatial)
    self_keep = []
    outputs = []
    for view in range(3):
        normed, query, keys, values = local_keep[view]
        length = keys.shape[0]
        keys_all = jnp.concatenate(
            [rim[0, view, :spatial], keys, rim[0, view, 3 * spatial :]], axis=0
        )
        values_all = jnp.concatenate(
            [rim[1, view, :spatial], values, rim[1, view, 3 * spatial :]], axis=0
        )
        bias = jnp.concatenate(
            [
                jnp.broadcast_to(below_bias, (spatial,)),
                jnp.zeros((length,), jnp.float32),
                jnp.broadcast_to(above_bias, (spatial,)),
            ]
        )
        mixed, probs = attend(query, keys_all, values_all, bias)
        middle = joined[view] + product(mixed, outw[view])
        normed_two = lowered(norm_rows(middle, gain[view, 1]))
        hidden_pre = product(normed_two, upw[view])
        active = lowered(jax.nn.gelu(hidden_pre, approximate=False))
        outputs.append(middle + product(active, downw[view]))
        self_keep.append(
            (
                normed,
                query,
                keys_all,
                values_all,
                mixed,
                probs,
                middle,
                normed_two,
                hidden_pre,
                active,
            )
        )
    layer_out = jnp.concatenate(outputs, axis=0)[None]
    qkv, outw, upw, downw, gain_low = unstack(
        (
            lax.all_gather(qkv_weights, ("seq", "tm"), axis=0, tiled=True),
            lax.all_gather(out_weights, ("seq", "tm"), axis=0, tiled=True),
            lax.all_gather(up_weights, ("seq", "tm"), axis=0, tiled=True),
            lax.all_gather(down_weights, ("seq", "tm"), axis=0, tiled=True),
            lax.all_gather(gains, ("seq", "tm"), axis=0, tiled=True),
        )
    )
    grad_qkv = [[None, None, None] for index in range(5)]
    grad_out = [None] * 5
    grad_up = [None] * 3
    grad_down = [None] * 3
    grad_gain = [[None, None] for index in range(5)]
    halves = []
    for view in range(3):
        (
            normed,
            query,
            keys_all,
            values_all,
            mixed,
            probs,
            middle,
            normed_two,
            hidden_pre,
            active,
        ) = self_keep[view]
        start, stop = bounds[view]
        dfinal = incoming[start:stop]
        dbranch = lowered(dfinal)
        grad_down[view] = product_tn(active, dbranch)
        dactive = product_nt(dbranch, downw[view])
        dpre_low = lowered(gelu_back(hidden_pre, dactive))
        grad_up[view] = product_tn(normed_two, dpre_low)
        dnormed_two = product_nt(dpre_low, upw[view])
        dmid_norm, grad_gain[view][1] = norm_back(middle, gain[view, 1], dnormed_two)
        dmiddle = dfinal + dmid_norm
        dattn = lowered(dmiddle)
        grad_out[view] = product_tn(mixed, dattn)
        dmixed = lowered(product_nt(dattn, outw[view]))
        dquery, dkeys, dvalues = attend_back(query, keys_all, values_all, probs, dmixed)
        halves.append((dmiddle, dquery, dkeys, dvalues))
    lower_part = jnp.stack(
        [jnp.stack([half[2][:spatial], half[3][:spatial]]) for half in halves], axis=1
    )
    upper_part = jnp.stack(
        [jnp.stack([half[2][-spatial:], half[3][-spatial:]]) for half in halves], axis=1
    )
    from_above = from_behind(lower_part.astype(jnp.bfloat16), "tm", -1).astype(lower_part.dtype)
    from_below = from_behind(upper_part.astype(jnp.bfloat16), "tm", 1).astype(upper_part.dtype)
    dfused = []
    for view in range(3):
        dmiddle, dquery, dkeys, dvalues = halves[view]
        normed = self_keep[view][0]
        length = dquery.shape[0]
        own_keys = dkeys[spatial : spatial + length]
        own_values = dvalues[spatial : spatial + length]
        own_keys = (
            own_keys.at[:spatial]
            .add(from_below[0, view])
            .at[length - spatial :]
            .add(from_above[0, view])
        )
        own_values = (
            own_values.at[:spatial]
            .add(from_below[1, view])
            .at[length - spatial :]
            .add(from_above[1, view])
        )
        dq_low = lowered(dquery)
        dk_low = lowered(own_keys)
        dv_low = lowered(own_values)
        grad_qkv[view] = [
            product_tn(normed, dq_low),
            product_tn(normed, dk_low),
            product_tn(normed, dv_low),
        ]
        dnormed = (
            product_nt(dq_low, qkv[view, 0])
            + product_nt(dk_low, qkv[view, 1])
            + product_nt(dv_low, qkv[view, 2])
        )
        dfused_norm, grad_gain[view][0] = norm_back(joined[view], gain[view, 0], dnormed)
        dfused.append(dmiddle + dfused_norm)
    dviews = list(dfused)
    for view in range(2):
        first, second, query, keys, values, mixed, probs = cross_keep[view]
        dbranch = lowered(dfused[view])
        grad_out[3 + view] = product_tn(mixed, dbranch)
        dmixed = lowered(product_nt(dbranch, outw[3 + view]))
        dquery, dkeys, dvalues = attend_back(query, keys, values, probs, dmixed)
        dq_low = lowered(dquery)
        dk_low = lowered(dkeys)
        dv_low = lowered(dvalues)
        grad_qkv[3 + view] = [
            product_tn(first, dq_low),
            product_tn(second, dk_low),
            product_tn(second, dv_low),
        ]
        dfirst = product_nt(dq_low, qkv[3 + view, 0])
        dsecond = product_nt(dk_low, qkv[3 + view, 1]) + product_nt(dv_low, qkv[3 + view, 2])
        dx_first, grad_gain[3 + view][0] = norm_back(views[view], gain[3 + view, 0], dfirst)
        dx_second, grad_gain[3 + view][1] = norm_back(views[view + 1], gain[3 + view, 1], dsecond)
        dviews[view] = dviews[view] + dx_first
        dviews[view + 1] = dviews[view + 1] + dx_second
    token_grad = jnp.concatenate(dviews, axis=0)[None]
    qkv_total = jnp.stack([jnp.stack(entry) for entry in grad_qkv]).reshape(15 * D, D)
    out_total = jnp.stack(grad_out).reshape(5 * D, D)
    gain_total = jnp.stack([jnp.stack(entry) for entry in grad_gain]).reshape(10 * D)
    totals = (
        qkv_total,
        out_total,
        jnp.stack(grad_up).reshape(3 * D, FF),
        jnp.stack(grad_down).reshape(3 * FF, D),
        gain_total,
    )
    shares = (
        lax.psum_scatter(totals[0], ("seq", "tm"), scatter_dimension=0, tiled=True),
        lax.psum_scatter(totals[1], ("seq", "tm"), scatter_dimension=0, tiled=True),
        lax.psum_scatter(totals[2], ("seq", "tm"), scatter_dimension=0, tiled=True),
        lax.psum_scatter(totals[3], ("seq", "tm"), scatter_dimension=0, tiled=True),
        lax.psum_scatter(totals[4], ("seq", "tm"), scatter_dimension=0, tiled=True),
    )
    return (layer_out, token_grad, shares[0], shares[1], shares[2], shares[3], shares[4])


def per_device(dims, tokens, cotangent, qkv_weights, out_weights, up_weights, down_weights, gains):
    rows = tokens[0]
    own_gains = gains.shape[0]
    tile = jnp.pad(gains.astype(F32).reshape(-1, 48), ((0, 8 - own_gains // 48), (0, 80)))
    shards = (qkv_weights, out_weights, up_weights, down_weights)
    slabs = tuple((2 * w.shape[0], w.shape[1]) for w in shards)
    wholes, gain, down_part, kept = gather_all(dims, own_gains, shards, tile, rows, cotangent[0])
    shares = reduce_all(dims, slabs, own_gains, wholes, down_part, cotangent[0], gain, rows, kept)
    gain_share = shares[6][: own_gains // 48, :48].reshape(own_gains)
    return (shares[1][None], shares[0][None], *shares[2:6], gain_share)


def fits(mesh, dims):
    chips = dims[0] * dims[1] * dims[2]
    rows = (15 * D, 5 * D, 3 * D, 3 * FF)
    return dims[:2] == (2, 2) and all(r % (chips * ROWS) == 0 for r in rows) and (10 * D) % (2 * chips * 48) == 0 and 10 * D // (2 * chips) <= 384


def solution(mesh):
    seq, tm = mesh.shape["seq"], mesh.shape["tm"]
    dims = (2, seq // 2, tm // 2)
    body = functools.partial(per_device, dims) if fits(mesh, dims) else plain_device
    placed = (
        P("seq", "tm", None),
        P("seq", "tm", None),
        P(("seq", "tm"), None),
        P(("seq", "tm"), None),
        P(("seq", "tm"), None),
        P(("seq", "tm"), None),
        P(("seq", "tm")),
    )
    return jax.shard_map(body, mesh=mesh, in_specs=placed, out_specs=placed, check_vma=False)
```

```python
import functools

import jax
import jax.numpy as jnp
from jax import lax
from jax.experimental import pallas as pl
from jax.experimental.pallas import tpu as pltpu
from jax.sharding import PartitionSpec as P

D = 768
HEADS = 12
FF = 3072

EPS = 1e-06
FAR = -1e30
MESH = pl.DeviceIdType.MESH
BF = jnp.bfloat16
F32 = jnp.float32
BLOCK = D // 2
ROWS = 48
POOLS = (0, 0, 10, 10, 4, 4)
SLOTS = sum(POOLS)
EACH = (1.78, 0.49, 0.58, 0.14)
EACH_FORWARD = 1.07
COPIES = 480


def extended(cells, sides, width):
    for axis, dim in sides:
        count = lax.axis_size(axis)
        ends = count - 1
        head = lax.slice_in_dim(cells, 0, width, axis=dim)
        tail = lax.slice_in_dim(cells, cells.shape[dim] - width, cells.shape[dim], axis=dim)
        cells = jnp.concatenate(
            [
                lax.ppermute(tail, axis, [(i, (i + 1) % count) for i in range(ends)]),
                cells,
                lax.ppermute(head, axis, [((i + 1) % count, i) for i in range(ends)]),
            ],
            axis=dim,
        )
    return cells


def from_behind(block, axis, distance):
    devices = range(lax.axis_size(axis))
    route = [(i - distance, i) for i in devices if i - distance in devices]
    return lax.ppermute(block, axis, route)


def norm_rows(x, gain):
    mean = jnp.mean(x, axis=-1, keepdims=True)
    centered = x - mean
    spread = jnp.mean(centered * centered, axis=-1, keepdims=True)
    return centered * lax.rsqrt(spread + EPS) * gain


def norm_back(x, gain, grad):
    unused, pull = jax.vjp(norm_rows, x, gain)
    return pull(grad)


def gelu_back(hidden_pre, grad):
    unused, pull = jax.vjp(lambda value: jax.nn.gelu(value, approximate=False), hidden_pre)
    return pull(grad)[0]


def lowered(value):
    return value.astype(jnp.bfloat16)


def product(left, right):
    return jnp.dot(left, right, preferred_element_type=jnp.float32)


def product_tn(left, right):
    return lax.dot_general(
        left, right, (((0,), (0,)), ((), ())), preferred_element_type=jnp.float32
    )


def product_nt(left, right):
    return lax.dot_general(
        left, right, (((1,), (1,)), ((), ())), preferred_element_type=jnp.float32
    )


def unstack(parts):
    qkv_flat, out_flat, up_flat, down_flat, gain_flat = parts
    return (
        qkv_flat.reshape(5, 3, D, D),
        out_flat.reshape(5, D, D),
        up_flat.reshape(3, D, FF),
        down_flat.reshape(3, FF, D),
        gain_flat.reshape(5, 2, D),
    )


def attend(query, keys, values, bias):
    rows, width = query.shape
    depth = width // HEADS
    qh = query.reshape(rows, HEADS, depth)
    kh = keys.reshape(keys.shape[0], HEADS, depth)
    vh = values.reshape(values.shape[0], HEADS, depth)
    scores = (
        jnp.einsum("qhd,khd->hqk", qh, kh, preferred_element_type=jnp.float32) * depth ** (-0.5)
        + bias
    )
    top = jnp.max(scores, axis=-1, keepdims=True)
    expo = jnp.exp(scores - top)
    probs = expo / jnp.sum(expo, axis=-1, keepdims=True)
    mixed = jnp.einsum("hqk,khd->qhd", lowered(probs), vh, preferred_element_type=jnp.float32)
    return (lowered(mixed.reshape(rows, width)), probs)


def attend_back(query, keys, values, probs, grad_mixed):
    rows, width = query.shape
    depth = width // HEADS
    qh = query.reshape(rows, HEADS, depth)
    kh = keys.reshape(keys.shape[0], HEADS, depth)
    vh = values.reshape(values.shape[0], HEADS, depth)
    gh = grad_mixed.reshape(rows, HEADS, depth)
    dprobs = jnp.einsum("qhd,khd->hqk", gh, vh, preferred_element_type=jnp.float32)
    dvalues = jnp.einsum("hqk,qhd->khd", lowered(probs), gh, preferred_element_type=jnp.float32)
    inner = jnp.sum(dprobs * probs, axis=-1, keepdims=True)
    dscores = lowered(probs * (dprobs - inner))
    scale = depth ** (-0.5)
    dquery = jnp.einsum("hqk,khd->qhd", dscores, kh, preferred_element_type=jnp.float32) * scale
    dkeys = jnp.einsum("hqk,qhd->khd", dscores, qh, preferred_element_type=jnp.float32) * scale
    return (dquery.reshape(rows, width), dkeys.reshape(-1, width), dvalues.reshape(-1, width))


class Place:
    def __init__(self, dims):
        self.dims = dims
        s = lax.axis_index("seq")
        t = lax.axis_index("tm")
        self.at = (s // dims[1], s % dims[1], t // 2)
        self.core = t % 2
        self.slab = t

    def device(self, at, core):
        return (at[0] * self.dims[1] + at[1], at[2] * 2 + core)

    def along(self, dim, value):
        at = list(self.at)
        at[dim] = value
        return self.device(at, self.core)

    def sibling(self):
        return self.device(self.at, 1 - self.core)


def meet(place):
    barrier = pltpu.get_barrier_semaphore()
    count = 1
    pl.semaphore_signal(barrier, inc=1, device_id=place.sibling(), device_id_type=MESH)
    for dim, n in enumerate(place.dims):
        me = place.at[dim]
        for step in (1, -1):
            ok = (me + step >= 0) & (me + step < n)

            @pl.when(ok)
            def _():
                pl.semaphore_signal(barrier, inc=1, device_id=place.along(dim, me + step), device_id_type=MESH)

            count = count + jnp.where(ok, 1, 0)
    step = 2 * place.core - 1
    ok = (place.at[2] + step >= 0) & (place.at[2] + step < place.dims[2])

    @pl.when(ok)
    def _():
        beside = (place.at[0], place.at[1], place.at[2] + step)
        pl.semaphore_signal(barrier, inc=1, device_id=place.device(beside, 1 - place.core), device_id_type=MESH)

    count = count + jnp.where(ok, 1, 0)
    pl.semaphore_wait(barrier, count)


class Copies:
    def __init__(self, send, recv):
        self.send, self.recv = send, recv
        self.used = 0
        self.sent = []

    def start(self, src, dst, device, ok=None):
        copy = pltpu.make_async_remote_copy(
            src_ref=src,
            dst_ref=dst,
            send_sem=self.send.at[self.used],
            recv_sem=self.recv.at[self.used],
            device_id=device,
            device_id_type=MESH,
        )
        self.used += 1
        when(ok, copy.start)
        self.sent.append((copy, ok))
        return copy

    def drain(self):
        for copy, ok in self.sent:
            when(ok, copy.wait_send)
        self.sent = []


def when(ok, action):
    if ok is None:
        action()
    else:

        @pl.when(ok)
        def _():
            action()


def gather_line(copies, place, dim, pick):
    n = place.dims[dim]
    me = place.at[dim]
    if n == 2:
        part = pick(me)
        copy = copies.start(part, part, place.along(dim, 1 - me))
        yield
        copy.wait_recv()
        return
    before = {}
    for hop in range(1, n):
        for step in (1, -1):
            origin = me - step * (hop - 1)
            held = (origin >= 0) & (origin < n)
            if hop > 1:
                when(held, before[step].wait_recv)
            ok = held & (me + step >= 0) & (me + step < n)
            part = pick(jnp.clip(origin, 0, n - 1))
            before[step] = copies.start(part, part, place.along(dim, jnp.clip(me + step, 0, n - 1)), ok)
        yield
    for step in (1, -1):
        origin = me - step * (n - 1)
        when((origin >= 0) & (origin < n), before[step].wait_recv)


def gather_piece(copies, place, full, rows, cols, order, pair):
    done = set()
    for dim in order:

        def pick(value):
            index = [slice(None) if d in done else place.at[d] for d in range(3)]
            index[dim] = value
            return full.at[(*index, pl.ds(*rows), cols)]

        yield from gather_line(copies, place, dim, pick)
        done.add(dim)
    if pair is not None:
        part = full.at[:, :, :, pl.ds(*rows), cols]
        pair.append(copies.start(part, part, place.sibling()))


XYZ, YXZ, XZY, YZX, ZXY, ZYX = (1, 0, 2), (0, 1, 2), (1, 2, 0), (0, 2, 1), (2, 1, 0), (2, 0, 1)
ORDERS = (XYZ, YXZ, XZY, YZX, ZXY, ZYX)
CYCLE = (2, 3, 4, 2, 3, 5)
GATHER_PLAN = (
    (5, 0), (5, 0), (4, 0), (5, 1), (2, 2), (5, 2), (4, 2), (5, 3), (2, 3), (1, 3), (3, 3),
    (4, 3), (5, 3), (5, 3), (4, 3), (2, 4), (5, 4), (4, 4), (4, 4), (5, 4), (4, 5), (3, 5),
    (2, 5), (3, 5), (3, 5), (1, 5), (2, 5), (4, 5), (3, 5), (4, 5), (0, 5), (5, 5), (2, 6),
    (5, 6), (4, 6), (5, 6), (5, 7), (1, 7), (2, 7), (1, 7), (4, 7), (0, 7), (0, 7), (5, 7),
)
REDUCE_PLAN = (
    (5, 0), (2, 0), (3, 0), (2, 0), (4, 0), (3, 0), (5, 0), (2, 0), (3, 0), (3, 1), (2, 1),
    (5, 2), (2, 2), (3, 2), (2, 3), (3, 3), (3, 3), (2, 3), (4, 3), (5, 3), (3, 4), (2, 4),
    (3, 4), (4, 4), (2, 4), (3, 4), (2, 4), (3, 4), (2, 4), (2, 4), (3, 5), (4, 6), (5, 6),
    (3, 6), (2, 6), (2, 6), (3, 6), (2, 6), (5, 6), (4, 6), (3, 6), (4, 6), (5, 6), (5, 6),
)


def pieces_of(slabs, arrays, plan):
    flat = []
    for array in arrays:
        rows, width = slabs[array]
        for block in range(width // 2 // BLOCK):
            for row in range(0, rows, ROWS):
                i = len(flat)
                order, start = plan[i] if i < len(plan) else (CYCLE[i % 6], plan[-1][1] + (i - len(plan)) // 6)
                flat.append((array, row, block, ORDERS[order], start))
    return flat


def march(pieces, begin, extra=()):
    waiting = list(pieces)
    active = list(extra)
    step = 0
    while active or waiting:
        while waiting and step >= waiting[0][4]:
            active.append(begin(waiting.pop(0)))
        still = []
        for one in active:
            try:
                yield next(one)
                still.append(one)
            except StopIteration:
                pass
        active = still
        step += 1


def weave(comm, work, each):
    live = [True, True]
    gate = [None, None]
    sources = (comm, work)

    def advance(k):
        if not live[k]:
            return None
        if gate[k] is not None:
            if not gate[k]():
                return None
            gate[k] = None
        try:
            item = next(sources[k])
        except StopIteration:
            live[k] = False
            return None
        if callable(item):
            gate[k] = item
            return 0.0
        return item or 0.0

    credit = 0.0
    while live[0] or live[1]:
        moved = advance(0)
        if moved is not None:
            credit = min(credit + each(), 4.0)
        stuck = moved is None
        while live[1] and (credit > 0 or stuck):
            cost = advance(1)
            if cost is None:
                break
            credit = max(credit - cost, -8.0)
            if stuck and live[0] and (gate[0] is None or gate[0]()):
                break


def matmul(left, right):
    return jnp.dot(left, right, preferred_element_type=F32)


def matmul_nt(left, right):
    return lax.dot_general(left, right, (((1,), (1,)), ((), ())), preferred_element_type=F32)


def matmul_tn(left, right):
    return lax.dot_general(left, right, (((0,), (0,)), ((), ())), preferred_element_type=F32)


def halves_of(pair):
    low = lax.broadcasted_iota(jnp.int32, pair.shape, 1) < pair.shape[1] // 2
    zero = jnp.zeros_like(pair)
    return jnp.where(low, pair, zero), jnp.where(low, zero, pair)


def softmax_rows(scores):
    expo = jnp.exp(scores - jnp.max(scores, axis=-1, keepdims=True))
    return expo * (1.0 / jnp.sum(expo, axis=-1, keepdims=True))


def attend_pair(query, keys, values, bias):
    outs = []
    for part in halves_of(query):
        scores = matmul_nt(part, keys) * 0.125
        if bias is not None:
            scores = scores + bias
        outs.append(matmul(softmax_rows(scores).astype(BF), values))
    low = lax.broadcasted_iota(jnp.int32, outs[0].shape, 1) < outs[0].shape[1] // 2
    return jnp.where(low, outs[0], outs[1]).astype(BF)


def gain_table(tiles, own):
    rows = tiles.shape[0]
    filled = own // 48
    r = lax.broadcasted_iota(jnp.int32, (rows, D), 0)
    c = lax.broadcasted_iota(jnp.int32, (rows, D), 1)
    spread = (lax.broadcasted_iota(jnp.int32, (128, D), 0) == lax.broadcasted_iota(jnp.int32, (128, D), 1) % 48)
    wide = matmul(tiles.astype(BF), spread.astype(BF))
    flat = (r // 8) * filled + r % 8
    wide = jnp.where((r % 8 < filled) & (c // 48 == flat % 16), wide, 0.0).astype(BF)
    rr = lax.broadcasted_iota(jnp.int32, (16, rows), 1)
    vv = lax.broadcasted_iota(jnp.int32, (16, rows), 0)
    pick = (rr % 8 < filled) & (((rr // 8) * filled + rr % 8) // 16 == vv)
    return matmul(pick.astype(BF), wide)


def row_runs(dims, slab, row, count):
    at, end = row, row + count
    while at < end:
        chip, off = at // slab, at % slab
        n = min(end - at, slab - off)
        yield chip // (dims[1] * dims[2]), chip // dims[2] % dims[1], chip % dims[2], off, n, at - row
        at += n


class Weights:
    def __init__(self, dims, slabs, wholes, ring, sems, blocks):
        self.dims, self.slabs, self.wholes, self.ring, self.sems, self.blocks = dims, slabs, wholes, ring, sems, blocks
        self.depth = ring.shape[0]
        self.loading = {}
        self.next_load = 0
        self.next_use = 0
        self.ready = set()

    def fetch(self):
        while self.next_load < min(len(self.blocks), self.next_use + self.depth):
            i = self.next_load
            a, row, block = self.blocks[i]
            if a not in self.ready:
                return
            slot = i % self.depth
            copies = []
            at, end = row, row + D
            slab = self.slabs[a][0]
            while at < end:
                chip, off = at // slab, at % slab
                n = min(end - at, slab - off)
                p, q, z = chip // (self.dims[1] * self.dims[2]), chip // self.dims[2] % self.dims[1], chip % self.dims[2]
                copies.append(
                    pltpu.make_async_copy(
                        self.wholes[a].at[p, q, z, pl.ds(off, n), pl.ds(block * D, D)],
                        self.ring.at[slot, pl.ds(at - row, n)],
                        self.sems.at[slot, len(copies)],
                    )
                )
                at += n
            for one in copies:
                one.start()
            self.loading[i] = copies
            self.next_load += 1

    def take(self, expected):
        i = self.next_use
        assert self.blocks[i] == expected, (self.blocks[i], expected)
        self.fetch()
        for one in self.loading.pop(i):
            one.wait()
        return self.ring.at[i % self.depth]

    def give_back(self):
        self.next_use += 1
        self.fetch()


def forward_blocks():
    blocks = [(0, (9 + i) * D, 0) for i in range(6)]
    blocks += [(1, 3 * D, 0), (1, 4 * D, 0)]
    blocks += [(0, i * D, 0) for i in range(9)]
    blocks += [(1, i * D, 0) for i in range(3)]
    blocks += [(2, v * D, j) for v in range(3) for j in range(FF // D)]
    return blocks


KEPT = ("first", "second", "cq", "ck", "cv", "cmixed", "joined", "normed", "q", "kx", "vx", "mixed", "middle", "normed_two", "slope", "active")


def forward_shapes(rows):
    u = rows // 7
    sizes = dict(
        first=(6 * u, D), second=(3 * u, D), cq=(6 * u, D), ck=(3 * u, D), cv=(3 * u, D), cmixed=(6 * u, D),
        joined=(rows, D), normed=(rows, D), q=(rows, D), kx=(rows + 6 * u, D), vx=(rows + 6 * u, D),
        mixed=(rows, D), middle=(rows, D), normed_two=(rows, D), slope=(rows, FF), active=(rows, FF),
    )
    return {k: (sizes[k], F32 if k in ("joined", "middle", "slope") else BF) for k in KEPT}


def halo_device(place, count, step):
    t = jnp.clip(place.slab + step, 0, count - 1)
    return (place.at[0] * place.dims[1] + place.at[1], t)


def slab_bias(place, count, width, spatial, axis=1):
    col = lax.broadcasted_iota(jnp.int32, (1, width) if axis else (width, 1), axis)
    below = (col < spatial) & (place.slab == 0)
    above = (col >= width - spatial) & (place.slab == count - 1)
    return jnp.where(below | above, FAR, 0.0).astype(F32)


def forward_work(place, copies, weights, need, gain, x, v, save, swap, products):
    u = x.shape[0] // 7
    count = 2 * place.dims[2]
    spans = ((0, 4 * u), (4 * u, 2 * u), (6 * u, u))
    bases = (0, 6 * u, 10 * u)
    yield need("gain")
    for c in range(2):
        r0, n = spans[c]
        k0, m = spans[c + 1]
        rows, keys = pl.ds(r0, n), pl.ds(k0 - 4 * u, m)
        g = lambda j: gain[pl.ds(2 * (3 + c) + j, 1), :]
        v["first"][rows] = norm_rows(x[rows], g(0)).astype(BF)
        v["second"][keys] = norm_rows(x[pl.ds(k0, m)], g(1)).astype(BF)
        yield 0.5
    save("first")
    save("second")
    yield need(0)
    for c in range(2):
        r0, n = spans[c]
        k0, m = spans[c + 1]
        rows, keys = pl.ds(r0, n), pl.ds(k0 - 4 * u, m)
        for j, (src, dst, part) in enumerate((("first", "cq", rows), ("second", "ck", keys), ("second", "cv", keys))):
            w = weights.take((0, (9 + 3 * c + j) * D, 0))
            v[dst][part] = matmul(v[src][part], w[...]).astype(BF)
            weights.give_back()
            yield 0.8
        for h in range(HEADS // 2):
            cols = pl.ds(h * 128, 128)
            v["cmixed"][rows, cols] = attend_pair(v["cq"][rows, cols], v["ck"][keys, cols], v["cv"][keys, cols], None)
            yield 0.8 if c == 0 else 0.3
    for name in ("cq", "ck", "cv", "cmixed"):
        save(name)
    yield need(1)
    for c in range(2):
        rows = pl.ds(*spans[c])
        w = weights.take((1, (3 + c) * D, 0))
        v["joined"][rows] = x[rows] + matmul(v["cmixed"][rows], w[...])
        weights.give_back()
        yield 0.8
    v["joined"][pl.ds(*spans[2])] = x[pl.ds(*spans[2])]
    save("joined")
    for name in ("kx", "vx"):
        for view in range(3):
            base, n = bases[view], spans[view][1]

            @pl.when(place.slab == 0)
            def _():
                v[name][pl.ds(base, u)] = jnp.zeros((u, D), BF)

            @pl.when(place.slab == count - 1)
            def _():
                v[name][pl.ds(base + u + n, u)] = jnp.zeros((u, D), BF)

    halo = {0: [], 1: [], 2: []}
    for view in range(3):
        r0, n = spans[view]
        rows = pl.ds(r0, n)
        base = bases[view]
        v["normed"][rows] = norm_rows(v["joined"][rows], gain[pl.ds(2 * view, 1), :]).astype(BF)
        for j, (dst, part) in enumerate((("q", rows), ("kx", pl.ds(base + u, n)), ("vx", pl.ds(base + u, n)))):
            w = weights.take((0, (3 * view + j) * D, 0))
            v[dst][part] = matmul(v["normed"][rows], w[...]).astype(BF)
            weights.give_back()
            if j > 0:
                ref = v[dst]
                up, down = place.slab < count - 1, place.slab > 0
                halo[view].append(
                    (copies.start(ref.at[pl.ds(base + n, u)], ref.at[pl.ds(base, u)], halo_device(place, count, 1), up), down)
                )
                halo[view].append(
                    (
                        copies.start(
                            ref.at[pl.ds(base + u, u)], ref.at[pl.ds(base + u + n, u)], halo_device(place, count, -1), down
                        ),
                        up,
                    )
                )
            yield 0.8
    save("normed")
    save("q")
    for view in range(3):
        r0, n = spans[view]
        rows, keys = pl.ds(r0, n), pl.ds(bases[view], n + 2 * u)
        for one, ok in halo[view]:
            when(ok, one.wait_recv)
        bias = slab_bias(place, count, n + 2 * u, u)
        for h in range(HEADS // 2):
            cols = pl.ds(h * 128, 128)
            v["mixed"][rows, cols] = attend_pair(v["q"][rows, cols], v["kx"][keys, cols], v["vx"][keys, cols], bias)
            yield (1.4, 0.6, 0.3)[view]
    save("kx")
    save("vx")
    save("mixed")
    for view in range(3):
        rows = pl.ds(*spans[view])
        w = weights.take((1, view * D, 0))
        v["middle"][rows] = v["joined"][rows] + matmul(v["mixed"][rows], w[...])
        weights.give_back()
        v["normed_two"][rows] = norm_rows(v["middle"][rows], gain[pl.ds(2 * view + 1, 1), :]).astype(BF)
        yield 1.0
    save("middle")
    save("normed_two")
    yield need(2)
    for view in range(3):
        rows = pl.ds(*spans[view])
        for j in range(FF // D):
            cols = pl.ds(j * D, D)
            w = weights.take((2, view * D, j))
            pre = matmul(v["normed_two"][rows], w[...])
            weights.give_back()
            area = 0.5 * (1.0 + lax.erf(pre * (0.5**0.5)))
            v["active"][rows, cols] = (pre * area).astype(BF)
            v["slope"][rows, cols] = area + pre * jnp.exp(-0.5 * pre * pre) * 0.3989422804014327
            yield 1.4
        swap(view)
    save("slope")
    save("active")
    yield from products()


def gather_kernel(dims, own_gains, *refs):
    refs = list(refs)
    take = lambda n: [refs.pop(0) for _ in range(n)]
    shards = take(4)
    gain_tile, x, cot = take(3)
    fulls = take(4)
    gain_out, down_part = take(2)
    kept_out = dict(zip(KEPT, take(len(KEPT))))
    theirs, merged = take(4), take(4)
    gain_all, gain, d_out, far_d_out, far_active, made = take(6)
    v = dict(zip(KEPT, take(len(KEPT))))
    ring, send, recv, local, ring_sem, save_sem, store_sem = take(7)
    place = Place(dims)
    copies = Copies(send, recv)
    core = place.core
    at = place.at
    meet(place)
    width = [s.shape[1] // 2 for s in shards]
    mine = [pl.ds(pl.multiple_of(core * w, 128), w) for w in width]
    other = [pl.ds(pl.multiple_of((1 - core) * w, 128), w) for w in width]
    swaps = []
    for a in range(4):
        swaps.append(copies.start(shards[a].at[:, other[a]], theirs[a], place.sibling()))
    own_tile = gain_all.at[at[0], at[1], at[2], core]
    own_tile[...] = gain_tile[...]
    swap_gain = copies.start(own_tile, own_tile, place.sibling())
    slabs = [(m.shape[0], 2 * m.shape[1]) for m in merged]
    pieces = pieces_of(slabs, range(4), GATHER_PLAN)
    left = {a: sum(1 for piece in pieces if piece[0] == a) for a in range(4)}
    pair = {a: [] for a in range(4)}
    ready = set()
    state = {"gain": False}

    def prepare(a):
        swaps[a].wait_recv()
        w = width[a]
        own = jnp.where(core == 0, shards[a][:, :w].astype(F32), shards[a][:, w:].astype(F32))
        got = theirs[a][...].astype(F32)
        upper = jnp.where(core == 0, own, got)
        lower = jnp.where(core == 0, got, own)
        merged[a][...] = jnp.concatenate([upper, lower], axis=0).astype(BF)
        copy = pltpu.make_async_copy(merged[a], fulls[a].at[at[0], at[1], at[2], :, mine[a]], local.at[a])
        copy.start()
        copy.wait()

    def begin(piece):
        a, row, block, order, _ = piece
        if a not in ready:
            prepare(a)
            ready.add(a)
        cols = pl.ds(pl.multiple_of(core * width[a] + block * BLOCK, 128), BLOCK)
        yield from gather_piece(copies, place, fulls[a], (row, ROWS), cols, order, pair[a])
        left[a] -= 1

    def gains():
        swap_gain.wait_recv()
        done = set()
        for dim in ZXY:

            def pick(value):
                index = [slice(None) if d in done else at[d] for d in range(3)]
                index[dim] = value
                return gain_all.at[tuple(index)]

            yield from gather_line(copies, place, dim, pick)
            done.add(dim)
        gain[...] = gain_table(gain_all[...].reshape(-1, 128), own_gains)
        copy = pltpu.make_async_copy(gain, gain_out, local.at[4])
        copy.start()
        copy.wait()
        state["gain"] = True

    weights = Weights(dims, slabs, fulls, ring, ring_sem, forward_blocks())

    def need(what):
        def gate():
            if what == "gain":
                return state["gain"]
            if left[what]:
                return False
            if what not in weights.ready:
                for copy in pair[what]:
                    copy.wait_recv()
                weights.ready.add(what)
                weights.fetch()
            return True

        return gate

    saves = []

    def save(name):
        copy = pltpu.make_async_copy(v[name], kept_out[name], save_sem.at[len(saves)])
        copy.start()
        saves.append(copy)

    u = x.shape[0] // 7
    spans = ((0, 4 * u), (4 * u, 2 * u), (6 * u, u))
    d_out[...] = cot[...].astype(BF)
    swap_out = copies.start(d_out.at[:, other[0]], far_d_out, place.sibling())
    swapped = {}

    def swap(view):
        rows = pl.ds(*spans[view])
        swapped[view] = copies.start(v["active"].at[rows], far_active.at[rows], place.sibling())

    def products():
        storing = {}
        swap_out.wait_recv()
        own_right = [jnp.where(core == 0, d_out[pl.ds(*s), :BLOCK], d_out[pl.ds(*s), BLOCK:]) for s in spans]
        for view in range(3):
            swapped[view].wait_recv()
            rows = pl.ds(*spans[view])
            right = jnp.concatenate([own_right[view], far_d_out[rows]], axis=0)
            for j in range(FF // D):
                i = view * (FF // D) + j
                slot = i % 2
                for one in storing.pop(i - 2, ()):
                    one.wait()
                cols = pl.ds(j * D, D)
                left = jnp.concatenate([v["active"][rows, cols], far_active[rows, cols]], axis=0)
                made[slot] = matmul_tn(left, right).astype(BF)
                storing[i] = [
                    pltpu.make_async_copy(
                        made.at[slot, pl.ds(at_, n)], down_part.at[p, q, z, pl.ds(off, n)], store_sem.at[slot, k]
                    )
                    for k, (p, q, z, off, n, at_) in enumerate(row_runs(dims, slabs[3][0], view * FF + j * D, D))
                ]
                for one in storing[i]:
                    one.start()
                yield 0.8
        for i in list(storing):
            for one in storing.pop(i):
                one.wait()

    work = forward_work(place, copies, weights, need, gain, x, v, save, swap, products)
    weave(march(pieces, begin, (gains(),)), work, lambda: EACH_FORWARD)
    for copy in pair[3]:
        copy.wait_recv()
    for copy in saves:
        copy.wait()
    copies.drain()


def gather_all(dims, own_gains, shards, tile, x, cot):
    slabs = [(2 * s.shape[0], s.shape[1]) for s in shards]
    anywhere = pl.BlockSpec(memory_space=pl.ANY)
    vmem = pl.BlockSpec(memory_space=pltpu.VMEM)
    kept = forward_shapes(x.shape[0])
    segments = max(D // s[0] + 2 for s in slabs)
    outs = pl.pallas_call(
        functools.partial(gather_kernel, dims, own_gains),
        out_shape=[jax.ShapeDtypeStruct((*dims, *s), BF) for s in slabs]
        + [jax.ShapeDtypeStruct((16, D), F32), jax.ShapeDtypeStruct((*dims, slabs[3][0], D // 2), BF)]
        + [jax.ShapeDtypeStruct(*kept[k]) for k in KEPT],
        in_specs=[vmem] * 7,
        out_specs=[anywhere] * (6 + len(KEPT)),
        scratch_shapes=[pltpu.VMEM((r // 2, w // 2), BF) for r, w in slabs]
        + [pltpu.VMEM((r, w // 2), BF) for r, w in slabs]
        + [pltpu.VMEM((*dims, 2, 8, 128), F32), pltpu.VMEM((16, D), F32)]
        + [
            pltpu.VMEM(x.shape, BF),
            pltpu.VMEM((x.shape[0], D // 2), BF),
            pltpu.VMEM((x.shape[0], FF), BF),
            pltpu.VMEM((2, D, BLOCK), BF),
        ]
        + [pltpu.VMEM(*kept[k]) for k in KEPT]
        + [
            pltpu.VMEM((4, D, D), BF),
            pltpu.SemaphoreType.DMA((COPIES,)),
            pltpu.SemaphoreType.DMA((COPIES,)),
            pltpu.SemaphoreType.DMA((5,)),
            pltpu.SemaphoreType.DMA((4, segments)),
            pltpu.SemaphoreType.DMA((len(KEPT),)),
            pltpu.SemaphoreType.DMA((2, segments)),
        ],
        compiler_params=pltpu.CompilerParams(collective_id=0, has_side_effects=True, vmem_limit_bytes=60 << 20),
    )(*shards, tile, x, cot)
    return outs[:4], outs[4], outs[5], dict(zip(KEPT, outs[6:]))


class Stream:
    def __init__(self, depth, sems, makers):
        self.depth, self.sems, self.makers = depth, sems, makers
        self.loading = {}
        self.next_load = 0
        self.next_use = 0
        self.fetch()

    def fetch(self):
        while self.next_load < min(len(self.makers), self.next_use + self.depth):
            slot = self.next_load % self.depth
            copies = [
                pltpu.make_async_copy(src, dst, self.sems.at[slot, j])
                for j, (src, dst) in enumerate(self.makers[self.next_load](slot))
            ]
            for one in copies:
                one.start()
            self.loading[self.next_load] = copies
            self.next_load += 1

    def take(self):
        for one in self.loading.pop(self.next_use):
            one.wait()
        return self.next_use % self.depth

    def give_back(self):
        self.next_use += 1
        self.fetch()


def add_to(total, term):
    total[...] = (total[...].astype(F32) + term[...].astype(F32)).astype(total.dtype)


class Credits:
    def __init__(self, sems, waits):
        self.sems, self.waits = sems, waits

    def wait(self, index, ok=None):
        if self.waits:
            when(ok, lambda: pl.semaphore_wait(self.sems.at[index], 1))

    def give(self, index, device):
        if self.sems is not None:
            pl.semaphore_signal(self.sems.at[index], inc=1, device_id=device, device_id_type=MESH)

    def settle(self, place):
        self.waits = True
        n, z = place.dims[2], place.at[2]
        self.wait(0)
        self.wait(1)
        for turn in range(n - 1):
            for step in (1, -1):
                far = z if step == 1 else n - 1 - z
                self.wait(2 + 2 * turn + (1 - step) // 2, far <= turn)


def reduce_line(copies, place, pick, slots, credits):
    n = place.dims[2]
    z = place.at[2]
    before = {}
    for turn in range(n):
        for step in (1, -1):
            far = z if step == 1 else n - 1 - z
            goal = far + n - 1 - turn
            goal = jnp.minimum(goal if step == 1 else n - 1 - goal, n - 1)
            goal = jnp.maximum(goal, 0)
            if turn > 0:

                def take(step=step, turn=turn, goal=goal):
                    before[step].wait_recv()
                    add_to(pick(goal), slots(turn - 1, step))
                    credits.give(2 + 2 * (turn - 1) + (1 - step) // 2, place.along(2, jnp.clip(z - step, 0, n - 1)))

                when((far >= 1) & (far <= turn), take)
            if turn < n - 1:
                credits.wait(2 + 2 * turn + (1 - step) // 2, far <= turn)
                before[step] = copies.start(
                    pick(goal), slots(turn, step), place.along(2, jnp.clip(z + step, 0, n - 1)), far <= turn
                )
        if turn < n - 1:
            yield


def reduce_piece(copies, place, source, order, acc, first, turns, last, local, credits, finish):
    lead = order[0]
    rest = 1 - lead
    me, mine = place.at[lead], place.at[rest]
    z = place.at[2]
    z_last = place.dims[2] - 1
    beside, across = place.along(lead, 1 - me), place.along(rest, 1 - mine)
    credits.wait(0)
    copy = copies.start(source(lead, 1 - me), first, beside)
    load = pltpu.make_async_copy(source(lead, me), acc, local)
    load.start()
    yield
    load.wait()
    copy.wait_recv()
    add_to(acc, first)
    credits.give(0, beside)
    slots = lambda turn, step: turns.at[turn if step == 1 or turn == 0 else z_last + turn - 1]
    if order[1] == 2:
        yield from reduce_line(copies, place, lambda v: acc.at[:, v], slots, credits)
        credits.wait(1)
        copy = copies.start(acc.at[1 - mine, z], last, across)
        yield
        copy.wait_recv()
        finish(acc[mine, z].astype(F32) + last[...].astype(F32))
        credits.give(1, across)
    else:
        credits.wait(1)
        copy = copies.start(acc.at[1 - mine], last, across)
        yield
        copy.wait_recv()
        add_to(acc.at[mine], last)
        credits.give(1, across)
        yield from reduce_line(copies, place, lambda v: acc.at[mine, v], slots, credits)
        finish(acc[mine, z].astype(F32))


def march_ready(pieces, begin, ready):
    waiting = list(pieces)
    active = []
    step = 0
    while active or waiting:
        while waiting and step >= waiting[0][4] and ready(waiting[0]):
            active.append(begin(waiting.pop(0)))
        if not active:
            if step < waiting[0][4]:
                step += 1
            else:
                yield lambda: ready(waiting[0])
            continue
        still = []
        for one in active:
            try:
                yield next(one)
                still.append(one)
            except StopIteration:
                pass
        active = still
        step += 1


LEFTS = ("normed_two", "mixed", "normed", "first", "second", "cmixed")
RIGHTS = ("d_out", "d_pre", "d_attn", "dq", "dk", "dv", "d_cross", "dcq", "dck", "dcv")
HELD = ("q", "kx", "vx", "cq", "ck", "cv")


def right_shapes(rows):
    u = rows // 7
    tall = dict(d_cross=6 * u, dcq=6 * u, dck=3 * u, dcv=3 * u)
    return [(tall.get(k, rows), FF if k == "d_pre" else D) for k in RIGHTS]


def job_batches(u):
    rows = ((0, 4 * u), (4 * u, 2 * u), (6 * u, u))
    late = ((0, 2 * u), (2 * u, u))
    batches = {"up": [], "out": [], "qkv": [], "cout": [], "cqkv": []}
    for view in range(3):
        for block in range(FF // 2 // BLOCK):
            batches["up"].append((2, view * D, block, "normed_two", 0, rows[view], "d_pre", rows[view]))
        batches["out"].append((1, view * D, 0, "mixed", 0, rows[view], "d_attn", rows[view]))
        for j, name in enumerate(("dq", "dk", "dv")):
            batches["qkv"].append((0, (3 * view + j) * D, 0, "normed", 0, rows[view], name, rows[view]))
    for c in range(2):
        batches["cout"].append((1, (3 + c) * D, 0, "cmixed", 0, rows[c], "d_cross", rows[c]))
        batches["cqkv"].append((0, (9 + 3 * c) * D, 0, "first", 0, rows[c], "dcq", rows[c]))
        for j, name in enumerate(("dck", "dcv")):
            batches["cqkv"].append((0, (10 + 3 * c + j) * D, 0, "second", 0, late[c], name, late[c]))
    return batches


def backward_blocks():
    blocks = []
    for view in range(3):
        for j in range(FF // D):
            blocks += [(3, view * FF + j * D, 0), (2, view * D, j)]
    blocks += [(1, view * D, 0) for view in range(3)]
    blocks += [(0, i * D, 0) for i in range(9)]
    blocks += [(1, (3 + c) * D, 0) for c in range(2)]
    blocks += [(0, (9 + j) * D, 0) for j in range(6)]
    blocks += [(3, view * FF + j * D, 0) for view in range(3) for j in range(FF // D)]
    return blocks


def norm_pull(x, gain, grad):
    centered = x - jnp.mean(x, axis=-1, keepdims=True)
    scale = lax.rsqrt(jnp.mean(centered * centered, axis=-1, keepdims=True) + EPS)
    unit = centered * scale
    inner = grad * gain
    pulled = scale * (
        inner - jnp.mean(inner, axis=-1, keepdims=True) - unit * jnp.mean(inner * unit, axis=-1, keepdims=True)
    )
    return pulled, jnp.sum(grad * unit, axis=0, keepdims=True)


def attend_pair_back(query, keys, values, grad, bias):
    dq, dk, dv = [], None, None
    for part, g in zip(halves_of(query), halves_of(grad)):
        scores = matmul_nt(keys, part) * 0.125
        if bias is not None:
            scores = scores + bias
        expo = jnp.exp(scores - jnp.max(scores, axis=0, keepdims=True))
        probs = expo * (1.0 / jnp.sum(expo, axis=0, keepdims=True))
        dprobs = matmul_nt(values, g)
        inner = jnp.sum(dprobs * probs, axis=0, keepdims=True)
        dscores = (probs * (dprobs - inner) * 0.125).astype(BF)
        dq.append(matmul_tn(dscores, keys))
        k_term = matmul(dscores, part)
        v_term = matmul(probs.astype(BF), g)
        dk = k_term if dk is None else dk + k_term
        dv = v_term if dv is None else dv + v_term
    low = lax.broadcasted_iota(jnp.int32, dq[0].shape, 1) < dq[0].shape[1] // 2
    return jnp.where(low, dq[0], dq[1]), dk, dv


def gain_tiles(table, rows, own):
    filled = own // 48
    r = lax.broadcasted_iota(jnp.int32, (rows, D), 0)
    c = lax.broadcasted_iota(jnp.int32, (rows, D), 1)
    flat = (r // 8) * filled + r % 8
    rr = lax.broadcasted_iota(jnp.int32, (rows, 16), 0)
    vv = lax.broadcasted_iota(jnp.int32, (rows, 16), 1)
    pick = (rr % 8 < filled) & (((rr // 8) * filled + rr % 8) // 16 == vv)
    wide = jnp.dot(pick.astype(F32), table, precision=lax.Precision.HIGHEST, preferred_element_type=F32)
    wide = jnp.where((r % 8 < filled) & (c // 48 == flat % 16), wide, 0.0)
    j = lax.broadcasted_iota(jnp.int32, (D, 128), 1)
    fold = (j < 48) & (j == lax.broadcasted_iota(jnp.int32, (D, 128), 0) % 48)
    return jnp.dot(wide, fold.astype(F32), precision=lax.Precision.HIGHEST, preferred_element_type=F32)


def reduce_kernel(dims, slabs, pieces, own_gains, *refs):
    refs = list(refs)
    take = lambda n: [refs.pop(0) for _ in range(n)]
    wholes = take(4)
    (cot, gain, x, joined, middle, slope, active, down_part) = take(8)
    lefts = dict(zip(LEFTS, take(6)))
    held_in = dict(zip(HELD, take(6)))
    token_out, layer_out = take(2)
    results = take(4)
    (gain_out,) = take(1)
    parts = take(3) + [down_part]
    far_lefts, far_rights = dict(zip(LEFTS, take(6))), dict(zip(RIGHTS, take(10)))
    rights = dict(zip(RIGHTS, take(10)))
    held = dict(zip(HELD, take(6)))
    acc, first, turns_a, turns_b, last_a, last_b = take(6)
    finals = take(4)
    xs, ys, made = take(3)
    g_far, g_own, g_acc, g_first, g_turns, g_last, g_sum = take(7)
    ring, rowring, preing, acting, layer, flow, total, dvf, halo_out, halo_in = take(10)
    send, recv, local, left_sem, right_sem, store_sem, final_sem, ring_sem, row_sem, pre_sem, act_sem, held_sem, layer_sem, credit = take(14)
    place = Place(dims)
    core = place.core
    copies = Copies(send, recv)
    meet(place)
    rows_all = cot.shape[0]
    u = rows_all // 7
    spans = ((0, 4 * u), (4 * u, 2 * u), (6 * u, u))
    bases = (0, 6 * u, 10 * u)
    count = 2 * dims[2]
    half_of = lambda ref, c: pl.ds(pl.multiple_of(c * (ref.shape[1] // 2), 128), ref.shape[1] // 2)
    coming = {}

    def swap(name):
        if name in lefts:
            coming[name] = copies.start(lefts[name], far_lefts[name], place.sibling())
        else:
            ref = rights[name]
            coming[name] = copies.start(ref.at[:, half_of(ref, 1 - core)], far_rights[name], place.sibling())

    arrived = set()

    def arrive(name):
        if name not in arrived:
            coming[name].wait_recv()
            arrived.add(name)

    def weight_maker(block):
        a, row, col = block
        return lambda slot: [
            (wholes[a].at[p, q, z, pl.ds(off, n), pl.ds(col * D, D)], ring.at[slot, pl.ds(at, n)])
            for p, q, z, off, n, at in row_runs(dims, slabs[a][0], row, D)
        ]

    def row_maker(ref, r0, n):
        return lambda slot: [(ref.at[pl.ds(r0, n)], rowring.at[slot, pl.ds(0, n)])]

    def pre_maker(view, j):
        r0, n = spans[view]
        block = (pl.ds(r0, n), pl.ds(j * D, D))
        return lambda slot: [(slope.at[block], preing.at[slot, pl.ds(0, n)])]

    def act_maker(view, j):
        r0, n = spans[view]
        block = (pl.ds(r0, n), pl.ds(j * D, D))
        return lambda slot: [(active.at[block], acting.at[slot, pl.ds(0, n)])]

    incoming = pltpu.make_async_copy(cot, flow, final_sem.at[4])
    incoming.start()
    blocks = backward_blocks()
    weights = Stream(ring.shape[0], ring_sem, [weight_maker(b) for b in blocks])
    pres = Stream(2, pre_sem, [pre_maker(view, j) for view in range(3) for j in range(FF // D)])
    acts = Stream(2, act_sem, [act_maker(view, j) for view in range(3) for j in range(FF // D)])
    row_list = [(middle, *spans[view]) for view in range(3)] + [(joined, *spans[view]) for view in range(3)]
    for c in range(2):
        row_list += [(x, *spans[c]), (x, *spans[c + 1])]
    row_list += [(middle, *spans[view]) for view in range(3)]
    rowed = Stream(2, row_sem, [row_maker(*one) for one in row_list])
    used_blocks = []

    def weight(expected):
        assert blocks[len(used_blocks)] == expected
        used_blocks.append(expected)
        return ring.at[weights.take()][...]

    holding = {}
    for i, name in enumerate(HELD):
        holding[name] = pltpu.make_async_copy(held_in[name], held[name], held_sem.at[i])
        holding[name].start()
    for name in LEFTS:
        swap(name)

    state = {"jobs": 0, "lefts": 0, "gain": False}
    ready = {3}
    storing = {}

    def finish_stores(i):
        for one in storing.pop(i, ()):
            one.wait()

    def load_left(group, slot):
        left, lcol, lrows = group
        arrive(left)
        n = lrows[1]
        block = (pl.ds(*lrows), pl.ds(lcol * D, D))
        loads = [
            pltpu.make_async_copy(lefts[left].at[block], xs.at[slot, pl.ds(0, n)], left_sem.at[slot, 0]),
            pltpu.make_async_copy(far_lefts[left].at[block], xs.at[slot, pl.ds(n, n)], left_sem.at[slot, 1]),
        ]
        for one in loads:
            one.start()
        return loads

    def load_right(job, slot):
        block, right, rrows = job[2], job[6], job[7]
        arrive(right)
        n = rrows[1]
        ref = rights[right]
        own = pl.ds(pl.multiple_of(core * (ref.shape[1] // 2) + block * BLOCK, 128), BLOCK)
        far = (pl.ds(*rrows), pl.ds(block * BLOCK, BLOCK))
        loads = [
            pltpu.make_async_copy(ref.at[pl.ds(*rrows), own], ys.at[slot, pl.ds(0, n)], right_sem.at[slot, 0]),
            pltpu.make_async_copy(far_rights[right].at[far], ys.at[slot, pl.ds(n, n)], right_sem.at[slot, 1]),
        ]
        for one in loads:
            one.start()
        return loads

    batches = job_batches(u)

    def multiply(name, cost):
        batch = batches[name]
        groups, member = [], []
        for job in batch:
            if not groups or groups[-1] != job[3:6]:
                groups.append(job[3:6])
            member.append(len(groups) - 1)
        x0, i0 = state["lefts"], state["jobs"]
        left_loads = {k: load_left(groups[k], (x0 + k) % 2) for k in range(min(2, len(groups)))}
        right_loads = {k: load_right(batch[k], (i0 + k) % 3) for k in range(min(2, len(batch)))}
        for index, job in enumerate(batch):
            i, k = i0 + index, member[index]
            if k in left_loads:
                for one in left_loads.pop(k):
                    one.wait()
                if 0 < k < len(groups) - 1:
                    left_loads[k + 1] = load_left(groups[k + 1], (x0 + k + 1) % 2)
            for one in right_loads.pop(index):
                one.wait()
            if index + 2 < len(batch):
                right_loads[index + 2] = load_right(batch[index + 2], (i + 2) % 3)
            finish_stores(i - 2)
            n = 2 * job[5][1]
            slot = i % 2
            made[slot] = matmul_tn(xs[(x0 + k) % 2, :n], ys[i % 3, :n]).astype(BF)
            a, row, block = job[:3]
            storing[i] = [
                pltpu.make_async_copy(
                    made.at[slot, pl.ds(at, n)],
                    parts[a].at[p, q, z, pl.ds(off, n), pl.ds(block * BLOCK, BLOCK)],
                    store_sem.at[slot, j],
                )
                for j, (p, q, z, off, n, at) in enumerate(row_runs(dims, slabs[a][0], row, D))
            ]
            for one in storing[i]:
                one.start()
            yield cost
        state["lefts"] += len(groups)
        state["jobs"] += len(batch)
        for i in list(storing):
            finish_stores(i)

    g = lambda e, j: gain[pl.ds(2 * e + j, 1), :]

    def work():
        incoming.wait()
        rights["d_out"][...] = flow[...].astype(BF)
        for view in range(3):
            r0, n = spans[view]
            rows = pl.ds(r0, n)
            cost = (1.5, 0.9, 0.7)[view]
            for j in range(FF // D):
                cols = pl.ds(j * D, D)
                dactive = matmul_nt(rights["d_out"][rows], weight((3, view * FF + j * D, 0)))
                weights.give_back()
                slot = pres.take()
                rights["d_pre"][rows, cols] = (dactive * preing[slot, :n]).astype(BF)
                pres.give_back()
                term = matmul_nt(rights["d_pre"][rows, cols], weight((2, view * D, j)))
                weights.give_back()
                total[:n] = term if j == 0 else total[:n] + term
                yield cost
            slot = rowed.take()
            pulled, g_sum[pl.ds(2 * view + 1, 1), :] = norm_pull(rowring[slot, :n], g(view, 1), total[:n])
            rowed.give_back()
            flow[rows] = flow[rows] + pulled
            rights["d_attn"][rows] = flow[rows].astype(BF)
            yield 0.8
        swap("d_pre")
        swap("d_attn")
        dmixed = rights["d_out"]
        for view in range(3):
            rows = pl.ds(*spans[view])
            dmixed[rows] = matmul_nt(rights["d_attn"][rows], weight((1, view * D, 0))).astype(BF)
            weights.give_back()
            yield 0.7
        yield from multiply("up", 0.6)
        ready.add(2)
        for name in ("q", "kx", "vx"):
            holding[name].wait()
        dkf = layer
        halo = {}
        up, down = place.slab < count - 1, place.slab > 0
        for view in range(3):
            r0, n = spans[view]
            rows, keys = pl.ds(r0, n), pl.ds(bases[view], n + 2 * u)
            bias = slab_bias(place, count, n + 2 * u, u, 0)
            for h in range(HEADS // 2):
                cols = pl.ds(h * 128, 128)
                dq, dk, dv = attend_pair_back(
                    held["q"][rows, cols], held["kx"][keys, cols], held["vx"][keys, cols], dmixed[rows, cols], bias
                )
                rights["dq"][rows, cols] = dq.astype(BF)
                for k, (whole, own) in enumerate(((dk, dkf), (dv, dvf))):
                    halo_out[k, view, 0, :, cols] = whole[:u].astype(BF)
                    own[rows, cols] = whole[u : u + n]
                    halo_out[k, view, 1, :, cols] = whole[u + n :].astype(BF)
                yield (2.0, 0.9, 0.5)[view]
            for k in range(2):
                for side, step, ok in ((0, -1, down), (1, 1, up)):
                    halo[k, view, side] = copies.start(
                        halo_out.at[k, view, side], halo_in.at[k, view, side], halo_device(place, count, step), ok
                    )
        swap("dq")
        yield from multiply("out", 0.6)
        for view in range(3):
            r0, n = spans[view]
            rows = pl.ds(r0, n)
            for k, (own, name) in enumerate(((dkf, "dk"), (dvf, "dv"))):
                for side, edge, ok in ((0, r0 + n - u, up), (1, r0, down)):

                    def join(k=k, side=side, edge=edge, own=own):
                        halo[k, view, side].wait_recv()
                        own[pl.ds(edge, u)] = own[pl.ds(edge, u)] + halo_in[k, view, side].astype(F32)

                    when(ok, join)
                rights[name][rows] = own[rows].astype(BF)
            for j, name in enumerate(("dq", "dk", "dv")):
                term = matmul_nt(rights[name][rows], weight((0, (3 * view + j) * D, 0)))
                weights.give_back()
                total[:n] = term if j == 0 else total[:n] + term
                yield 0.7
            slot = rowed.take()
            pulled, g_sum[pl.ds(2 * view, 1), :] = norm_pull(rowring[slot, :n], g(view, 0), total[:n])
            rowed.give_back()
            flow[rows] = flow[rows] + pulled
            yield 0.6
        swap("dk")
        swap("dv")
        rights["d_cross"][...] = flow[pl.ds(0, 6 * u)].astype(BF)
        swap("d_cross")
        for name in ("cq", "ck", "cv"):
            holding[name].wait()
        yield from multiply("cout", 0.6)
        ready.add(1)
        for c in range(2):
            rows = pl.ds(*spans[c])
            dmixed[rows] = matmul_nt(rights["d_cross"][rows], weight((1, (3 + c) * D, 0))).astype(BF)
            weights.give_back()
            yield 0.7
        for c in range(2):
            rows, keys = pl.ds(*spans[c]), pl.ds(spans[c + 1][0] - 4 * u, spans[c + 1][1])
            for h in range(HEADS // 2):
                cols = pl.ds(h * 128, 128)
                dq, dk, dv = attend_pair_back(
                    held["cq"][rows, cols], held["ck"][keys, cols], held["cv"][keys, cols], dmixed[rows, cols], None
                )
                rights["dcq"][rows, cols] = dq.astype(BF)
                rights["dck"][keys, cols] = dk.astype(BF)
                rights["dcv"][keys, cols] = dv.astype(BF)
                yield (1.0, 0.45)[c]
        for name in ("dcq", "dck", "dcv"):
            swap(name)
        yield from multiply("qkv", 0.6)
        yield from multiply("cqkv", 0.6)
        ready.add(0)
        for c in range(2):
            r0, n = spans[c]
            k0, m = spans[c + 1]
            rows, keys, late = pl.ds(r0, n), pl.ds(k0 - 4 * u, m), pl.ds(k0, m)
            term = matmul_nt(rights["dcq"][rows], weight((0, (9 + 3 * c) * D, 0)))
            weights.give_back()
            slot = rowed.take()
            pulled, g_sum[pl.ds(2 * (3 + c), 1), :] = norm_pull(rowring[slot, :n], g(3 + c, 0), term)
            rowed.give_back()
            flow[rows] = flow[rows] + pulled
            yield 1.0
            term = matmul_nt(rights["dck"][keys], weight((0, (10 + 3 * c) * D, 0)))
            weights.give_back()
            term = term + matmul_nt(rights["dcv"][keys], weight((0, (11 + 3 * c) * D, 0)))
            weights.give_back()
            slot = rowed.take()
            pulled, g_sum[pl.ds(2 * (3 + c) + 1, 1), :] = norm_pull(rowring[slot, :m], g(3 + c, 1), term)
            rowed.give_back()
            flow[late] = flow[late] + pulled
            yield 1.0
        token = pltpu.make_async_copy(flow, token_out, final_sem.at[4])
        token.start()
        g_sum[pl.ds(10, 6), :] = jnp.zeros((6, D), F32)
        g_own[...] = gain_tiles(g_sum[...], 2 * dims[0] * dims[1] * dims[2] * 8, own_gains).reshape(g_own.shape)
        coming["gain"] = copies.start(g_own, g_far, place.sibling())
        state["gain"] = True
        yield 1.0
        for view in range(3):
            r0, n = spans[view]
            rows = pl.ds(r0, n)
            for j in range(FF // D):
                slot = acts.take()
                term = matmul(acting[slot, :n], weight((3, view * FF + j * D, 0)))
                acts.give_back()
                weights.give_back()
                layer[rows] = term if j == 0 else layer[rows] + term
                yield 0.6
            slot = rowed.take()
            layer[rows] = layer[rows] + rowring[slot, :n]
            rowed.give_back()
        layered = pltpu.make_async_copy(layer, layer_out, layer_sem)
        layered.start()
        token.wait()
        layered.wait()

    left_in = {a: sum(1 for piece in pieces if piece[0] == a) for a in range(4)}
    count_pieces = sum(left_in.values())
    bases_of = [sum(POOLS[:k]) for k in range(len(POOLS))]
    free = {k: [[bases_of[k] + j, None, None] for j in range(POOLS[k])] for k in range(len(POOLS))}
    owners = []
    ending = []

    def gains():
        coming["gain"].wait_recv()
        add_to(g_far, g_own)
        source = lambda dim, value: g_far.at[(*[value if d == dim else slice(None) for d in range(3)], core)]

        def finish(value):
            g_first[0, 0] = value
            copy = pltpu.make_async_copy(g_first.at[0, 0], gain_out, final_sem.at[5])
            copy.start()
            copy.wait()

        yield from reduce_piece(
            copies, place, source, (0, 1, 2), g_acc, g_first, g_turns, g_last, local.at[SLOTS], Credits(None, False), finish
        )

    def begin(piece):
        if piece[0] == "gain":
            return gains()
        a, row, block, order, _ = piece
        kind = ORDERS.index(order)
        buffer = free[kind].pop(0)
        slot, before, _ = buffer
        if before is not None:
            before.drain()
        mine = Copies(send, recv)
        mine.used = COPIES - 9 * (count_pieces - len(owners))
        owners.append(mine)
        buffer[1] = mine
        cols = pl.ds(block * BLOCK, BLOCK)
        single = order[1] != 2
        k = slot - sum(POOLS[:4]) if single else slot
        turns, last = ((turns_a, last_a), (turns_b, last_b))[single]

        def source(dim, value):
            index = [slice(None)] * 3
            index[dim] = value
            return parts[a].at[(*index, pl.ds(row, ROWS), cols)]

        def finish(value):
            finals[a][pl.ds(row, ROWS), cols] = value
            left_in[a] -= 1
            free[kind].append(buffer)
            if left_in[a] == 0:
                deliver(a)

        credits = Credits(credit.at[slot], before is not None)
        buffer[2] = credits
        return reduce_piece(
            mine, place, source, order[::-1], acc.at[slot], first.at[slot], turns.at[k], last.at[k], local.at[slot], credits, finish
        )

    def deliver(a):
        rows, width = slabs[a][0] // 2, slabs[a][1] // 2
        cols = pl.ds(pl.multiple_of(core * width, 128), width)
        ending.append(
            copies.start(
                finals[a].at[pl.ds(pl.multiple_of((1 - core) * rows, 8), rows)], results[a].at[:, cols], place.sibling()
            )
        )
        keep = pltpu.make_async_copy(
            finals[a].at[pl.ds(pl.multiple_of(core * rows, 8), rows)], results[a].at[:, cols], final_sem.at[a]
        )
        keep.start()
        keep.wait()

    def piece_ready(piece):
        if piece[0] == "gain":
            return state["gain"]
        return piece[0] in ready and bool(free[ORDERS.index(piece[3])])

    weave(march_ready(pieces, begin, piece_ready), work(), lambda: EACH[len(ready) - 1])
    for buffers in free.values():
        for slot, user, credits in buffers:
            if user is not None:
                credits.settle(place)
    for one in ending:
        one.wait_recv()
    copies.drain()
    for one in owners:
        one.drain()
    assert copies.used <= COPIES - 9 * count_pieces


def reduce_all(dims, slabs, own_gains, wholes, down_part, cot, gain, x, kept):
    anywhere = pl.BlockSpec(memory_space=pl.ANY)
    vmem = pl.BlockSpec(memory_space=pltpu.VMEM)
    pieces = pieces_of(slabs, (3, 2, 1, 0), REDUCE_PLAN)
    pieces.append(("gain", 0, 0, None, pieces[-1][4]))
    bundled, single = sum(POOLS[:4]), sum(POOLS[4:])
    z = dims[2]
    rows = cot.shape[0]
    u = rows // 7
    tile = (ROWS, BLOCK)
    segments = max(D // slab[0] + 2 for slab in slabs)
    lefts = [kept[k] for k in LEFTS]
    held = [kept[k] for k in HELD]
    rights = right_shapes(rows)
    outs = pl.pallas_call(
        functools.partial(reduce_kernel, dims, slabs, pieces, own_gains),
        out_shape=[jax.ShapeDtypeStruct((rows, D), F32)] * 2
        + [jax.ShapeDtypeStruct((s[0] // 2, s[1]), F32) for s in slabs]
        + [jax.ShapeDtypeStruct((8, 128), F32)]
        + [jax.ShapeDtypeStruct((*dims, s[0], s[1] // 2), BF) for s in slabs[:3]]
        + [jax.ShapeDtypeStruct(one.shape, BF) for one in lefts]
        + [jax.ShapeDtypeStruct((r, w // 2), BF) for r, w in rights],
        in_specs=[anywhere] * 5 + [vmem] + [anywhere] * 18,
        out_specs=[anywhere] * 26,
        scratch_shapes=[pltpu.VMEM(s, BF) for s in rights]
        + [pltpu.VMEM(one.shape, BF) for one in held]
        + [
            pltpu.VMEM((SLOTS, 2, z, *tile), BF),
            pltpu.VMEM((SLOTS, 2, z, *tile), BF),
            pltpu.VMEM((bundled, 2 * z - 3, 2, *tile), BF),
            pltpu.VMEM((single, 2 * z - 3, *tile), BF),
            pltpu.VMEM((bundled, *tile), BF),
            pltpu.VMEM((single, z, *tile), BF),
        ]
        + [pltpu.VMEM((s[0], s[1] // 2), F32) for s in slabs]
        + [
            pltpu.VMEM((2, 8 * u, D), BF),
            pltpu.VMEM((3, 8 * u, BLOCK), BF),
            pltpu.VMEM((2, D, BLOCK), BF),
            pltpu.VMEM((*dims, 2, 8, 128), F32),
            pltpu.VMEM((*dims, 2, 8, 128), F32),
            pltpu.VMEM((2, z, 8, 128), F32),
            pltpu.VMEM((2, z, 8, 128), F32),
            pltpu.VMEM((2 * z - 3, 8, 128), F32),
            pltpu.VMEM((z, 8, 128), F32),
            pltpu.VMEM((16, D), F32),
            pltpu.VMEM((3, D, D), BF),
            pltpu.VMEM((2, 4 * u, D), F32),
            pltpu.VMEM((2, 4 * u, D), F32),
            pltpu.VMEM((2, 4 * u, D), BF),
            pltpu.VMEM((rows, D), F32),
            pltpu.VMEM((rows, D), F32),
            pltpu.VMEM((4 * u, D), F32),
            pltpu.VMEM((rows, D), F32),
            pltpu.VMEM((2, 3, 2, u, D), BF),
            pltpu.VMEM((2, 3, 2, u, D), BF),
            pltpu.SemaphoreType.DMA((COPIES,)),
            pltpu.SemaphoreType.DMA((COPIES,)),
            pltpu.SemaphoreType.DMA((SLOTS + 1,)),
            pltpu.SemaphoreType.DMA((2, 2)),
            pltpu.SemaphoreType.DMA((3, 2)),
            pltpu.SemaphoreType.DMA((2, segments)),
            pltpu.SemaphoreType.DMA((6,)),
            pltpu.SemaphoreType.DMA((3, segments)),
            pltpu.SemaphoreType.DMA((2, 1)),
            pltpu.SemaphoreType.DMA((2, 1)),
            pltpu.SemaphoreType.DMA((2, 1)),
            pltpu.SemaphoreType.DMA((6,)),
            pltpu.SemaphoreType.DMA,
            pltpu.SemaphoreType.REGULAR((SLOTS, 2 + 2 * (z - 1))),
        ],
        compiler_params=pltpu.CompilerParams(collective_id=1, has_side_effects=True, vmem_limit_bytes=63 << 20),
    )(*wholes, cot, gain, x, kept["joined"], kept["middle"], kept["slope"], kept["active"], down_part, *lefts, *held)
    return outs[:7]


def plain_device(tokens, cotangent, qkv_weights, out_weights, up_weights, down_weights, gains):
    rows = tokens[0]
    incoming = cotangent[0]
    spatial = rows.shape[0] // 7
    bounds = ((0, 4 * spatial), (4 * spatial, 6 * spatial), (6 * spatial, 7 * spatial))
    qkv, outw, upw, downw, gain_low = unstack(
        (
            lax.all_gather(qkv_weights, ("seq", "tm"), axis=0, tiled=True),
            lax.all_gather(out_weights, ("seq", "tm"), axis=0, tiled=True),
            lax.all_gather(up_weights, ("seq", "tm"), axis=0, tiled=True),
            lax.all_gather(down_weights, ("seq", "tm"), axis=0, tiled=True),
            lax.all_gather(gains, ("seq", "tm"), axis=0, tiled=True),
        )
    )
    gain = gain_low.astype(jnp.float32)
    place = lax.axis_index("tm")
    count = lax.axis_size("tm")
    below_bias = jnp.where(place > 0, 0.0, FAR).astype(jnp.float32)
    above_bias = jnp.where(place < count - 1, 0.0, FAR).astype(jnp.float32)
    views = [rows[start:stop] for start, stop in bounds]
    cross_keep = []
    joined = []
    for view in range(2):
        first = lowered(norm_rows(views[view], gain[3 + view, 0]))
        second = lowered(norm_rows(views[view + 1], gain[3 + view, 1]))
        query = lowered(product(first, qkv[3 + view, 0]))
        keys = lowered(product(second, qkv[3 + view, 1]))
        values = lowered(product(second, qkv[3 + view, 2]))
        mixed, probs = attend(query, keys, values, 0.0)
        joined.append(views[view] + product(mixed, outw[3 + view]))
        cross_keep.append((first, second, query, keys, values, mixed, probs))
    joined.append(views[2])
    local_keep = []
    edges = []
    for view in range(3):
        normed = lowered(norm_rows(joined[view], gain[view, 0]))
        query = lowered(product(normed, qkv[view, 0]))
        keys = lowered(product(normed, qkv[view, 1]))
        values = lowered(product(normed, qkv[view, 2]))
        local_keep.append((normed, query, keys, values))
        paired = jnp.stack([keys, values])
        edges.append(jnp.concatenate([paired[:, :spatial], paired[:, -spatial:]], axis=1))
    rim = extended(jnp.stack(edges, axis=1), (("tm", 2),), spatial)
    self_keep = []
    outputs = []
    for view in range(3):
        normed, query, keys, values = local_keep[view]
        length = keys.shape[0]
        keys_all = jnp.concatenate(
            [rim[0, view, :spatial], keys, rim[0, view, 3 * spatial :]], axis=0
        )
        values_all = jnp.concatenate(
            [rim[1, view, :spatial], values, rim[1, view, 3 * spatial :]], axis=0
        )
        bias = jnp.concatenate(
            [
                jnp.broadcast_to(below_bias, (spatial,)),
                jnp.zeros((length,), jnp.float32),
                jnp.broadcast_to(above_bias, (spatial,)),
            ]
        )
        mixed, probs = attend(query, keys_all, values_all, bias)
        middle = joined[view] + product(mixed, outw[view])
        normed_two = lowered(norm_rows(middle, gain[view, 1]))
        hidden_pre = product(normed_two, upw[view])
        active = lowered(jax.nn.gelu(hidden_pre, approximate=False))
        outputs.append(middle + product(active, downw[view]))
        self_keep.append(
            (
                normed,
                query,
                keys_all,
                values_all,
                mixed,
                probs,
                middle,
                normed_two,
                hidden_pre,
                active,
            )
        )
    layer_out = jnp.concatenate(outputs, axis=0)[None]
    qkv, outw, upw, downw, gain_low = unstack(
        (
            lax.all_gather(qkv_weights, ("seq", "tm"), axis=0, tiled=True),
            lax.all_gather(out_weights, ("seq", "tm"), axis=0, tiled=True),
            lax.all_gather(up_weights, ("seq", "tm"), axis=0, tiled=True),
            lax.all_gather(down_weights, ("seq", "tm"), axis=0, tiled=True),
            lax.all_gather(gains, ("seq", "tm"), axis=0, tiled=True),
        )
    )
    grad_qkv = [[None, None, None] for index in range(5)]
    grad_out = [None] * 5
    grad_up = [None] * 3
    grad_down = [None] * 3
    grad_gain = [[None, None] for index in range(5)]
    halves = []
    for view in range(3):
        (
            normed,
            query,
            keys_all,
            values_all,
            mixed,
            probs,
            middle,
            normed_two,
            hidden_pre,
            active,
        ) = self_keep[view]
        start, stop = bounds[view]
        dfinal = incoming[start:stop]
        dbranch = lowered(dfinal)
        grad_down[view] = product_tn(active, dbranch)
        dactive = product_nt(dbranch, downw[view])
        dpre_low = lowered(gelu_back(hidden_pre, dactive))
        grad_up[view] = product_tn(normed_two, dpre_low)
        dnormed_two = product_nt(dpre_low, upw[view])
        dmid_norm, grad_gain[view][1] = norm_back(middle, gain[view, 1], dnormed_two)
        dmiddle = dfinal + dmid_norm
        dattn = lowered(dmiddle)
        grad_out[view] = product_tn(mixed, dattn)
        dmixed = lowered(product_nt(dattn, outw[view]))
        dquery, dkeys, dvalues = attend_back(query, keys_all, values_all, probs, dmixed)
        halves.append((dmiddle, dquery, dkeys, dvalues))
    lower_part = jnp.stack(
        [jnp.stack([half[2][:spatial], half[3][:spatial]]) for half in halves], axis=1
    )
    upper_part = jnp.stack(
        [jnp.stack([half[2][-spatial:], half[3][-spatial:]]) for half in halves], axis=1
    )
    from_above = from_behind(lower_part.astype(jnp.bfloat16), "tm", -1).astype(lower_part.dtype)
    from_below = from_behind(upper_part.astype(jnp.bfloat16), "tm", 1).astype(upper_part.dtype)
    dfused = []
    for view in range(3):
        dmiddle, dquery, dkeys, dvalues = halves[view]
        normed = self_keep[view][0]
        length = dquery.shape[0]
        own_keys = dkeys[spatial : spatial + length]
        own_values = dvalues[spatial : spatial + length]
        own_keys = (
            own_keys.at[:spatial]
            .add(from_below[0, view])
            .at[length - spatial :]
            .add(from_above[0, view])
        )
        own_values = (
            own_values.at[:spatial]
            .add(from_below[1, view])
            .at[length - spatial :]
            .add(from_above[1, view])
        )
        dq_low = lowered(dquery)
        dk_low = lowered(own_keys)
        dv_low = lowered(own_values)
        grad_qkv[view] = [
            product_tn(normed, dq_low),
            product_tn(normed, dk_low),
            product_tn(normed, dv_low),
        ]
        dnormed = (
            product_nt(dq_low, qkv[view, 0])
            + product_nt(dk_low, qkv[view, 1])
            + product_nt(dv_low, qkv[view, 2])
        )
        dfused_norm, grad_gain[view][0] = norm_back(joined[view], gain[view, 0], dnormed)
        dfused.append(dmiddle + dfused_norm)
    dviews = list(dfused)
    for view in range(2):
        first, second, query, keys, values, mixed, probs = cross_keep[view]
        dbranch = lowered(dfused[view])
        grad_out[3 + view] = product_tn(mixed, dbranch)
        dmixed = lowered(product_nt(dbranch, outw[3 + view]))
        dquery, dkeys, dvalues = attend_back(query, keys, values, probs, dmixed)
        dq_low = lowered(dquery)
        dk_low = lowered(dkeys)
        dv_low = lowered(dvalues)
        grad_qkv[3 + view] = [
            product_tn(first, dq_low),
            product_tn(second, dk_low),
            product_tn(second, dv_low),
        ]
        dfirst = product_nt(dq_low, qkv[3 + view, 0])
        dsecond = product_nt(dk_low, qkv[3 + view, 1]) + product_nt(dv_low, qkv[3 + view, 2])
        dx_first, grad_gain[3 + view][0] = norm_back(views[view], gain[3 + view, 0], dfirst)
        dx_second, grad_gain[3 + view][1] = norm_back(views[view + 1], gain[3 + view, 1], dsecond)
        dviews[view] = dviews[view] + dx_first
        dviews[view + 1] = dviews[view + 1] + dx_second
    token_grad = jnp.concatenate(dviews, axis=0)[None]
    qkv_total = jnp.stack([jnp.stack(entry) for entry in grad_qkv]).reshape(15 * D, D)
    out_total = jnp.stack(grad_out).reshape(5 * D, D)
    gain_total = jnp.stack([jnp.stack(entry) for entry in grad_gain]).reshape(10 * D)
    totals = (
        qkv_total,
        out_total,
        jnp.stack(grad_up).reshape(3 * D, FF),
        jnp.stack(grad_down).reshape(3 * FF, D),
        gain_total,
    )
    shares = (
        lax.psum_scatter(totals[0], ("seq", "tm"), scatter_dimension=0, tiled=True),
        lax.psum_scatter(totals[1], ("seq", "tm"), scatter_dimension=0, tiled=True),
        lax.psum_scatter(totals[2], ("seq", "tm"), scatter_dimension=0, tiled=True),
        lax.psum_scatter(totals[3], ("seq", "tm"), scatter_dimension=0, tiled=True),
        lax.psum_scatter(totals[4], ("seq", "tm"), scatter_dimension=0, tiled=True),
    )
    return (layer_out, token_grad, shares[0], shares[1], shares[2], shares[3], shares[4])


def per_device(dims, tokens, cotangent, qkv_weights, out_weights, up_weights, down_weights, gains):
    rows = tokens[0]
    own_gains = gains.shape[0]
    tile = jnp.pad(gains.astype(F32).reshape(-1, 48), ((0, 8 - own_gains // 48), (0, 80)))
    shards = (qkv_weights, out_weights, up_weights, down_weights)
    slabs = tuple((2 * w.shape[0], w.shape[1]) for w in shards)
    wholes, gain, down_part, kept = gather_all(dims, own_gains, shards, tile, rows, cotangent[0])
    shares = reduce_all(dims, slabs, own_gains, wholes, down_part, cotangent[0], gain, rows, kept)
    gain_share = shares[6][: own_gains // 48, :48].reshape(own_gains)
    return (shares[1][None], shares[0][None], *shares[2:6], gain_share)


def fits(mesh, dims):
    chips = dims[0] * dims[1] * dims[2]
    rows = (15 * D, 5 * D, 3 * D, 3 * FF)
    return dims[:2] == (2, 2) and dims[2] > 3 and all(r % (chips * ROWS) == 0 for r in rows) and (10 * D) % (2 * chips * 48) == 0 and 10 * D // (2 * chips) <= 384


def solution(mesh):
    seq, tm = mesh.shape["seq"], mesh.shape["tm"]
    dims = (2, seq // 2, tm // 2)
    body = functools.partial(per_device, dims) if fits(mesh, dims) else plain_device
    placed = (
        P("seq", "tm", None),
        P("seq", "tm", None),
        P(("seq", "tm"), None),
        P(("seq", "tm"), None),
        P(("seq", "tm"), None),
        P(("seq", "tm"), None),
        P(("seq", "tm")),
    )
    return jax.shard_map(body, mesh=mesh, in_specs=placed, out_specs=placed, check_vma=False)
```
